32 devices in a mesh: fsdp: 8 (over y, x, core), replica: 4 (over z).
Axes of the slice: x: 2, y: 2, z: 4, core: 2. Of those that a mesh axis runs over, the one named last changes fastest.
Arguments:
- tokens: bfloat16 [8192, 1152], P(('fsdp', 'replica')), may hold values from -6 to 6
- cond: bfloat16 [16, 1152], replicated, may hold values from -6 to 6
- latent_len: int32 [16], replicated, may hold values from 1 to 1024, 8192 in all
- first_ada_weight: bfloat16 [1152, 6912], P('fsdp'), may hold values from -0.1875 to 0.1875
- first_ada_bias: bfloat16 [6912], P('fsdp'), may hold values from -6 to 6
- first_qkv_weight: bfloat16 [1152, 3456], P('fsdp'), may hold values from -0.1875 to 0.1875
- first_qkv_bias: bfloat16 [2304], P('fsdp'), may hold values from -3.5 to 3.5
- first_out_weight: bfloat16 [1152, 1152], P('fsdp'), may hold values from -1.5 to 1.5
- first_out_bias: bfloat16 [1152], P('fsdp'), may hold values from -6 to 6
- first_up_weight: bfloat16 [1152, 4608], P('fsdp'), may hold values from -0.1875 to 0.1875
- first_up_bias: bfloat16 [4608], P('fsdp'), may hold values from -6 to 6
- first_down_weight: bfloat16 [4608, 1152], P('fsdp'), may hold values from -0.09375 to 0.09375
- first_down_bias: bfloat16 [1152], P('fsdp'), may hold values from -6 to 6
- second_ada_weight: bfloat16 [1152, 6912], P('fsdp'), may hold values from -0.1875 to 0.1875
- second_ada_bias: bfloat16 [6912], P('fsdp'), may hold values from -6 to 6
- second_qkv_weight: bfloat16 [1152, 3456], P('fsdp'), may hold values from -0.1875 to 0.1875
- second_qkv_bias: bfloat16 [2304], P('fsdp'), may hold values from -3.5 to 3.5
- second_out_weight: bfloat16 [1152, 1152], P('fsdp'), may hold values from -1.5 to 1.5
- second_out_bias: bfloat16 [1152], P('fsdp'), may hold values from -6 to 6
- second_up_weight: bfloat16 [1152, 4608], P('fsdp'), may hold values from -0.1875 to 0.1875
- second_up_bias: bfloat16 [4608], P('fsdp'), may hold values from -6 to 6
- second_down_weight: bfloat16 [4608, 1152], P('fsdp'), may hold values from -0.09375 to 0.09375
- second_down_bias: bfloat16 [1152], P('fsdp'), may hold values from -6 to 6
- cotangent: bfloat16 [8192, 1152], P(('fsdp', 'replica')), may hold values from -6 to 6
Outputs:
- output: bfloat16 [8192, 1152], P(('fsdp', 'replica'))
- token_grad: float32 [8192, 1152], P(('fsdp', 'replica'))
- cond_grad: float32 [16, 1152], P(None, 'fsdp')
- grad_first_ada_weight: float32 [1152, 6912], P('fsdp')
- grad_first_ada_bias: float32 [6912], P('fsdp')
- grad_first_qkv_weight: float32 [1152, 3456], P('fsdp')
- grad_first_qkv_bias: float32 [2304], P('fsdp')
- grad_first_out_weight: float32 [1152, 1152], P('fsdp')
- grad_first_out_bias: float32 [1152], P('fsdp')
- grad_first_up_weight: float32 [1152, 4608], P('fsdp')
- grad_first_up_bias: float32 [4608], P('fsdp')
- grad_first_down_weight: float32 [4608, 1152], P('fsdp')
- grad_first_down_bias: float32 [1152], P('fsdp')
- grad_second_ada_weight: float32 [1152, 6912], P('fsdp')
- grad_second_ada_bias: float32 [6912], P('fsdp')
- grad_second_qkv_weight: float32 [1152, 3456], P('fsdp')
- grad_second_qkv_bias: float32 [2304], P('fsdp')
- grad_second_out_weight: float32 [1152, 1152], P('fsdp')
- grad_second_out_bias: float32 [1152], P('fsdp')
- grad_second_up_weight: float32 [1152, 4608], P('fsdp')
- grad_second_up_bias: float32 [4608], P('fsdp')
- grad_second_down_weight: float32 [4608, 1152], P('fsdp')
- grad_second_down_bias: float32 [1152], P('fsdp')
The draws below stay inside these ranges and needn't reach their ends.
Inputs may be any that keep to these rules, and one draw needn't show every extreme that they name: `latent_len`: the latents lie end to end and their lengths sum to 8192; the longest holds exactly 1024 tokens.
All inputs are finite; a program needn't handle non-finite values.
Results may differ from the reference program's by a relative error of at most 0.02.
Values may be sent and summed in bfloat16 or wider, within the bound.
A program may use at most 448 MiB of HBM per device.

```python
import math
import jax
import jax.numpy as jnp
import numpy as np
from jax import lax

D = 1152
HEADS = 16
FF = 4608
HEAD_DIM = 72
MAXLEN = 1024
TOKENS = 8192
LATENTS = 16


def shard_levels(stream_key, dims, cuts, low, high):
    level, own = 1.0, jax.random.fold_in(stream_key, 6)
    for axis_at, blocks in cuts:
        steps = jnp.exp(jax.random.uniform(jax.random.fold_in(own, axis_at), (blocks,), jnp.float32, low / len(cuts), high / len(cuts)))
        level = level * jnp.repeat(steps, dims[axis_at] // blocks).reshape([-1 if axis == axis_at else 1 for axis in range(len(dims))])
    return level


def split_up(count, total, limit, slope):
    portions = [(1 << 20) // math.isqrt(standing ** slope) + 1 for standing in range(2, count + 1)]
    spare, counts = total - limit - (count - 1), [1] * (count - 1)
    while spare > 0:
        movable = [i for i in range(count - 1) if counts[i] < limit]
        pool, remaining = sum([portions[i] for i in movable]), spare
        for i in movable:
            addition = min(limit - counts[i], max(1, remaining * portions[i] // pool), spare)
            counts[i] = counts[i] + addition
            spare = spare - addition
    return np.array([limit] + counts)


def ragged(key, amount, total, bound, skew):
    if amount == 2:
        one = jax.random.randint(key, (), max(1, total - bound), min(bound, total - 1) + 1)
        return jnp.stack([one, total - one])
    tallies = jnp.asarray(split_up(amount, total, bound, skew), jnp.int32)
    pairs = (amount - 1) // 2
    source_of, taker = tallies[1:1 + 2 * pairs:2], tallies[2:2 + 2 * pairs:2]
    slack = jnp.minimum(source_of - 1, bound - taker)
    shifted = jax.random.randint(jax.random.fold_in(key, 1), (pairs,), 0, 1 << 20) % (slack + 1)
    tallies = tallies.at[1:1 + 2 * pairs:2].set(source_of - shifted).at[2:2 + 2 * pairs:2].set(taker + shifted)
    return tallies[jax.random.permutation(jax.random.fold_in(key, 2), amount)]


def gaussian(key, dims, scale, bound, cuts=(), held_as=jnp.bfloat16):
    values = jax.random.normal(key, dims, jnp.float32) * scale
    if len(cuts) > 0:
        values = shard_levels(key, dims, cuts, -0.22, 0.18) * values
    return jnp.clip(values, min=-bound, max=bound).astype(held_as)


def setup_inputs(seed: int = 0) -> dict:
    splits = jax.random.split(jax.random.key(seed), 25)
    tokens = gaussian(splits[0], (TOKENS, D), 1.0, 6.0, ((0, 32),))
    cond = gaussian(splits[1], (LATENTS, D), 1.0, 6.0)
    latent_len = ragged(splits[2], LATENTS, TOKENS, MAXLEN, 2).astype(jnp.int32)
    first_ada_weight = gaussian(splits[3], (D, 6 * D), D ** -0.5, 0.1875, ((0, 8),))
    first_ada_bias = gaussian(splits[4], (6 * D,), 1.0, 6.0, ((0, 8),))
    first_qkv_weight = gaussian(splits[5], (D, 3 * D), D ** -0.5, 0.1875, ((0, 8),))
    first_qkv_bias = gaussian(splits[6], (2 * D,), 0.6, 3.5, ((0, 8),))
    first_out_weight = gaussian(splits[7], (D, D), (max(D // 64, 1)) ** -0.5, 1.5, ((0, 8),))
    first_out_bias = gaussian(splits[8], (D,), 1.0, 6.0, ((0, 8),))
    first_up_weight = gaussian(splits[9], (D, FF), D ** -0.5, 0.1875, ((0, 8),))
    first_up_bias = gaussian(splits[10], (FF,), 1.0, 6.0, ((0, 8),))
    first_down_weight = gaussian(splits[11], (FF, D), FF ** -0.5, 0.09375, ((0, 8),))
    first_down_bias = gaussian(splits[12], (D,), 1.0, 6.0, ((0, 8),))
    second_ada_weight = gaussian(splits[13], (D, 6 * D), D ** -0.5, 0.1875, ((0, 8),))
    second_ada_bias = gaussian(splits[14], (6 * D,), 1.0, 6.0, ((0, 8),))
    second_qkv_weight = gaussian(splits[15], (D, 3 * D), D ** -0.5, 0.1875, ((0, 8),))
    second_qkv_bias = gaussian(splits[16], (2 * D,), 0.6, 3.5, ((0, 8),))
    second_out_weight = gaussian(splits[17], (D, D), (max(D // 64, 1)) ** -0.5, 1.5, ((0, 8),))
    second_out_bias = gaussian(splits[18], (D,), 1.0, 6.0, ((0, 8),))
    second_up_weight = gaussian(splits[19], (D, FF), D ** -0.5, 0.1875, ((0, 8),))
    second_up_bias = gaussian(splits[20], (FF,), 1.0, 6.0, ((0, 8),))
    second_down_weight = gaussian(splits[21], (FF, D), FF ** -0.5, 0.09375, ((0, 8),))
    second_down_bias = gaussian(splits[22], (D,), 1.0, 6.0, ((0, 8),))
    cotangent = gaussian(splits[23], (TOKENS, D), 1.0, 6.0, ((0, 32),))
    return dict(tokens=tokens, cond=cond, latent_len=latent_len, first_ada_weight=first_ada_weight, first_ada_bias=first_ada_bias, first_qkv_weight=first_qkv_weight, first_qkv_bias=first_qkv_bias, first_out_weight=first_out_weight, first_out_bias=first_out_bias, first_up_weight=first_up_weight, first_up_bias=first_up_bias, first_down_weight=first_down_weight, first_down_bias=first_down_bias, second_ada_weight=second_ada_weight, second_ada_bias=second_ada_bias, second_qkv_weight=second_qkv_weight, second_qkv_bias=second_qkv_bias, second_out_weight=second_out_weight, second_out_bias=second_out_bias, second_up_weight=second_up_weight, second_up_bias=second_up_bias, second_down_weight=second_down_weight, second_down_bias=second_down_bias, cotangent=cotangent)


@jax.custom_vjp
def low(v):
    return lax.optimization_barrier(v.astype(jnp.bfloat16)).astype(jnp.float32)

@jax.custom_vjp
def low_back(v):
    return v

def low_keep(v):
    return (low(v), None)

def low_pass(kept, grad):
    return (grad,)

def back_keep(v):
    return (v, None)

def back_low(kept, grad):
    return (low(grad),)
low.defvjp(low_keep, low_pass)
low_back.defvjp(back_keep, back_low)
NORM_EPS = 1e-06
HIGH = lax.Precision.HIGHEST

def mat_mul(left, right):
    return jnp.dot(left, right, precision=HIGH, preferred_element_type=jnp.float32)

def pre_norm(stream, shift, scale):
    centred = stream - lax.optimization_barrier(jnp.mean(stream, axis=-1, keepdims=True))
    spread = lax.optimization_barrier(jnp.mean(centred * centred, axis=-1, keepdims=True))
    return centred * lax.rsqrt(spread + NORM_EPS) * (1.0 + scale) + shift

def latent_ids(latent_len, positions, token_total):
    starts = (jnp.cumsum(latent_len) - latent_len).astype(jnp.int32)
    found = lax.optimization_barrier(jnp.sum((starts[None, :] <= positions[:, None]).astype(jnp.int32), axis=1)) - 1
    inside = (positions >= 0) & (positions < token_total)
    return jnp.where(inside, found, -1).astype(jnp.int32)

def attend(query, key, value, token_ids):
    token_count = query.shape[0]
    block = math.gcd(token_count, 1024)
    key_pad = jnp.pad(key, ((MAXLEN, MAXLEN), (0, 0)))
    value_pad = jnp.pad(value, ((MAXLEN, MAXLEN), (0, 0)))
    ids_pad = jnp.pad(token_ids, (MAXLEN, MAXLEN), constant_values=-1)
    span = block + 2 * MAXLEN
    scale = 1.0 / math.sqrt(HEAD_DIM)

    def one_block(start):
        q_block = lax.dynamic_slice_in_dim(query, start, block, 0).reshape(block, HEADS, HEAD_DIM)
        k_block = lax.dynamic_slice_in_dim(key_pad, start, span, 0).reshape(span, HEADS, HEAD_DIM)
        v_block = lax.dynamic_slice_in_dim(value_pad, start, span, 0).reshape(span, HEADS, HEAD_DIM)
        q_ids = lax.dynamic_slice_in_dim(token_ids, start, block, 0)
        k_ids = lax.dynamic_slice_in_dim(ids_pad, start, span, 0)
        scores = low_back(jnp.einsum('thd,whd->htw', q_block, k_block, precision=HIGH) * scale)
        same = (q_ids[:, None] == k_ids[None, :])[None, :, :]
        scores = jnp.where(same, scores, -1e+30)
        probs = low(jax.nn.softmax(scores, axis=-1))
        mixed = jnp.einsum('htw,whd->thd', probs, v_block, precision=HIGH)
        return mixed.reshape(block, HEADS * HEAD_DIM)
    starts = jnp.arange(token_count // block, dtype=jnp.int32) * block
    return lax.map(jax.checkpoint(one_block), starts).reshape(token_count, HEADS * HEAD_DIM)

def block_layer(stream, silu_cond, params, token_ids):
    ada_w, ada_b, qkv_w, qkv_b, out_w, out_b, up_w, up_b, down_w, down_b = params
    width = stream.shape[1]
    mod = low_back(mat_mul(silu_cond, ada_w) + ada_b)
    mod_tok = mod[token_ids]
    shift_one, scale_one, gate_one, shift_two, scale_two, gate_two = jnp.split(mod_tok, 6, axis=1)
    normed = low(pre_norm(stream, shift_one, scale_one))
    bias_full = jnp.concatenate([qkv_b[:width], jnp.zeros((width,), jnp.float32), qkv_b[width:]])
    projected = mat_mul(normed, qkv_w) + bias_full
    query = low_back(low(projected[:, :width]))
    key = low_back(low(projected[:, width:2 * width]))
    value = low_back(low(projected[:, 2 * width:]))
    mixed = low_back(low(attend(query, key, value, token_ids)))
    branch = low_back(mat_mul(mixed, out_w) + out_b)
    middle = stream + gate_one * branch
    normed_two = low(pre_norm(middle, shift_two, scale_two))
    hidden = low_back(mat_mul(normed_two, up_w) + up_b)
    active = low(jax.nn.gelu(hidden, approximate=True))
    result = low_back(mat_mul(active, down_w) + down_b)
    return middle + gate_two * result

def reference(tokens, cond, latent_len, first_ada_weight, first_ada_bias, first_qkv_weight, first_qkv_bias, first_out_weight, first_out_bias, first_up_weight, first_up_bias, first_down_weight, first_down_bias, second_ada_weight, second_ada_bias, second_qkv_weight, second_qkv_bias, second_out_weight, second_out_bias, second_up_weight, second_up_bias, second_down_weight, second_down_bias, cotangent):
    token_count = tokens.shape[0]
    positions = jnp.arange(token_count, dtype=jnp.int32)
    token_ids = latent_ids(latent_len, positions, token_count)
    first = (first_ada_weight.astype(jnp.float32), first_ada_bias.astype(jnp.float32), first_qkv_weight.astype(jnp.float32), first_qkv_bias.astype(jnp.float32), first_out_weight.astype(jnp.float32), first_out_bias.astype(jnp.float32), first_up_weight.astype(jnp.float32), first_up_bias.astype(jnp.float32), first_down_weight.astype(jnp.float32), first_down_bias.astype(jnp.float32))
    second = (second_ada_weight.astype(jnp.float32), second_ada_bias.astype(jnp.float32), second_qkv_weight.astype(jnp.float32), second_qkv_bias.astype(jnp.float32), second_out_weight.astype(jnp.float32), second_out_bias.astype(jnp.float32), second_up_weight.astype(jnp.float32), second_up_bias.astype(jnp.float32), second_down_weight.astype(jnp.float32), second_down_bias.astype(jnp.float32))

    def forward(stream, cond_float, first_params, second_params):
        silu_cond = low(jax.nn.silu(cond_float))
        stream = block_layer(stream, silu_cond, first_params, token_ids)
        return block_layer(stream, silu_cond, second_params, token_ids)
    result, pullback = jax.vjp(forward, tokens.astype(jnp.float32), cond.astype(jnp.float32), first, second)
    grad_tokens, grad_cond, grad_first, grad_second = pullback(cotangent.astype(jnp.float32))
    return (result.astype(jnp.bfloat16), grad_tokens, grad_cond, grad_first[0], grad_first[1], grad_first[2], grad_first[3], grad_first[4], grad_first[5], grad_first[6], grad_first[7], grad_first[8], grad_first[9], grad_second[0], grad_second[1], grad_second[2], grad_second[3], grad_second[4], grad_second[5], grad_second[6], grad_second[7], grad_second[8], grad_second[9])
```

```python
import functools
import math

import jax
import jax.numpy as jnp
from jax import lax
from jax.experimental import pallas as pl
from jax.experimental.pallas import tpu as pltpu
from jax.sharding import PartitionSpec as P

HEADS = 16
MAXLEN = 1024
NORM_EPS = 1e-06
HIGH = lax.Precision.HIGHEST
BQ = 256
BK = 256
LANES = 128
NEG = -1e30
VM = pl.BlockSpec(memory_space=pltpu.VMEM)
SM = pl.BlockSpec(memory_space=pltpu.SMEM)
HB = pl.BlockSpec(memory_space=pl.ANY)
VMEM_LIMIT = 56 * 1024 * 1024


def pad_to(size, unit):
    return -(-size // unit) * unit


def take_head(ref, rows, at, dim):
    first, off = at // LANES * LANES, at % LANES
    wide = LANES if off + dim <= LANES else 2 * LANES
    block = ref[rows, first : first + wide].astype(jnp.float32)
    if off:
        block = pltpu.roll(block, wide - off, 1)
    block = block[:, :LANES]
    lane = lax.broadcasted_iota(jnp.int32, block.shape, 1)
    return jnp.where(lane < dim, block, 0.0)


def put_heads(blocks, places, width):
    tiles = [None] * (width // LANES)
    for block, at in zip(blocks, places):
        first, off = at // LANES, at % LANES
        wide = jnp.concatenate([block, jnp.zeros_like(block)], axis=1)
        if off:
            wide = pltpu.roll(wide, off, 1)
        for step in range(2):
            part = wide[:, step * LANES : (step + 1) * LANES]
            if first + step < len(tiles):
                old = tiles[first + step]
                tiles[first + step] = part if old is None else old + part
    rows = blocks[0].shape[0]
    return jnp.concatenate(
        [jnp.zeros((rows, LANES), jnp.float32) if t is None else t for t in tiles], axis=1
    )


def nt_dot(left, right):
    return lax.dot_general(left, right, (((1,), (1,)), ((), ())), preferred_element_type=jnp.float32)


def nn_dot(left, right):
    return jnp.dot(left, right, preferred_element_type=jnp.float32)


def rows_at(block, size):
    return pl.ds(pl.multiple_of(block * size, size), size)


def over_window(lo, hi, prev, own, after, action):
    edge, mid = prev.shape[0] // BK, own.shape[0] // BK

    def run(ref, first, count):
        def body(at, carry):
            action(ref, at - first, at)
            return carry

        lax.fori_loop(jnp.clip(lo, first, first + count), jnp.clip(hi, first, first + count), body, 0)

    run(prev, 0, edge)
    run(own, edge, mid)
    run(after, edge + mid, edge)


def attend_kernel(nh, hd, lo, hi, prev, own, after, kid, qid, o_ref, ot_ref, lse_ref, kh, vt, qh, acc, ml):
    dim = hd // nh
    width = o_ref.shape[1]
    count = own.shape[0] // BQ
    scale = math.log2(math.e) / math.sqrt(dim)

    def load(ref, at, to):
        for h in range(nh):
            kh[h, rows_at(to, BK), :] = take_head(ref, rows_at(at, BK), h * dim, dim).astype(jnp.bfloat16)
            vt[h, :, rows_at(to, BK)] = take_head(ref, rows_at(at, BK), hd + h * dim, dim).T.astype(jnp.bfloat16)

    over_window(lo[0], hi[count - 1], prev, own, after, load)
    lse_ref[...] = jnp.zeros_like(lse_ref)

    def query_block(qb, carry):
        rows = rows_at(qb, BQ)
        for h in range(nh):
            qh[h] = take_head(own, rows, 2 * hd + h * dim, dim).astype(jnp.bfloat16)
        acc[...] = jnp.zeros_like(acc)
        ml[0] = jnp.full(ml.shape[1:], NEG, jnp.float32)
        ml[1] = jnp.zeros(ml.shape[1:], jnp.float32)
        ids = qid[0:1, rows]

        def key_block(kb, inner):
            keys = rows_at(kb, BK)
            lanes = kid[keys, :]
            same = jnp.concatenate([lanes] * (BQ // LANES), axis=1) == ids
            for h in range(nh):
                s = jnp.where(same, nt_dot(kh[h, keys, :], qh[h]) * scale, NEG)
                old = ml[0, h : h + 1, :]
                top = jnp.maximum(old, jnp.max(s, axis=0, keepdims=True))
                p = jnp.exp2(s - top)
                alpha = jnp.exp2(old - top)
                ml[0, h : h + 1, :] = top
                ml[1, h : h + 1, :] = ml[1, h : h + 1, :] * alpha + jnp.sum(p, axis=0, keepdims=True)
                acc[h] = acc[h] * alpha + nn_dot(vt[h, :, keys], p.astype(jnp.bfloat16))
            return inner

        lax.fori_loop(lo[qb], hi[qb], key_block, 0)
        parts = []
        for h in range(nh):
            total = ml[1, h : h + 1, :]
            out = acc[h, :dim, :] / total
            parts.append(out)
            lse_ref[h : h + 1, rows] = ml[0, h : h + 1, :] + jnp.log2(total)
        parts.append(jnp.zeros((width - hd, BQ), jnp.float32))
        heads = jnp.concatenate(parts, axis=0)
        ot_ref[:, rows] = heads
        o_ref[rows, :] = heads.T.astype(jnp.bfloat16)
        return carry

    lax.fori_loop(0, count, query_block, 0)


def attend(nh, hd, lo, hi, prev, own, after, kid, qid):
    rows, window = own.shape[0], own.shape[0] + 2 * prev.shape[0]
    width = pad_to(hd, LANES)
    return pl.pallas_call(
        functools.partial(attend_kernel, nh, hd),
        out_shape=(
            jax.ShapeDtypeStruct((rows, width), jnp.bfloat16),
            jax.ShapeDtypeStruct((width, rows), jnp.float32),
            jax.ShapeDtypeStruct((8, rows), jnp.float32),
        ),
        in_specs=[SM, SM, VM, VM, VM, VM, VM],
        out_specs=(VM, VM, VM),
        scratch_shapes=[
            pltpu.VMEM((nh, window, LANES), jnp.bfloat16),
            pltpu.VMEM((nh, LANES, window), jnp.bfloat16),
            pltpu.VMEM((nh, BQ, LANES), jnp.bfloat16),
            pltpu.VMEM((nh, LANES, BQ), jnp.float32),
            pltpu.VMEM((2, 8, BQ), jnp.float32),
        ],
        compiler_params=pltpu.CompilerParams(vmem_limit_bytes=VMEM_LIMIT),
        cost_estimate=pl.CostEstimate(
            flops=4 * nh * rows * 1024 * LANES, bytes_accessed=8 << 20, transcendentals=nh * rows * 1024
        ),
    )(lo, hi, prev, own, after, kid, qid)


def attend_back_kernel(
    nh, hd, lo, hi, prev, own, after, kid, qid, do_ref, ot_ref, lse_ref,
    dq_ref, dprev, down, dafter, kh, vh, kt, qh, gh, dk, dv, dqt, delta,
):
    dim = hd // nh
    width = dq_ref.shape[1]
    count = own.shape[0] // BQ
    root = 1.0 / math.sqrt(dim)
    scale = math.log2(math.e) / math.sqrt(dim)

    def load(ref, at, to):
        for h in range(nh):
            k = take_head(ref, rows_at(at, BK), h * dim, dim)
            kh[h, rows_at(to, BK), :] = k.astype(jnp.bfloat16)
            kt[h, :, rows_at(to, BK)] = k.T.astype(jnp.bfloat16)
            vh[h, rows_at(to, BK), :] = take_head(ref, rows_at(at, BK), hd + h * dim, dim).astype(jnp.bfloat16)
            dk[h, rows_at(to, BK), :] = jnp.zeros((BK, LANES), jnp.float32)
            dv[h, rows_at(to, BK), :] = jnp.zeros((BK, LANES), jnp.float32)

    over_window(lo[0], hi[count - 1], prev, own, after, load)

    def query_block(qb, carry):
        rows = rows_at(qb, BQ)
        for h in range(nh):
            qh[h] = take_head(own, rows, 2 * hd + h * dim, dim).astype(jnp.bfloat16)
            gh[h] = take_head(do_ref, rows, h * dim, dim).astype(jnp.bfloat16)
        prod = do_ref[rows, :].astype(jnp.float32).T * ot_ref[:, rows]
        for h in range(nh):
            delta[h : h + 1, :] = jnp.sum(prod[h * dim : (h + 1) * dim], axis=0, keepdims=True)
        dqt[...] = jnp.zeros_like(dqt)
        ids = qid[0:1, rows]

        def key_block(kb, inner):
            keys = rows_at(kb, BK)
            lanes = kid[keys, :]
            same = jnp.concatenate([lanes] * (BQ // LANES), axis=1) == ids
            for h in range(nh):
                s = nt_dot(kh[h, keys, :], qh[h]) * scale - lse_ref[h : h + 1, rows]
                p = jnp.exp2(jnp.where(same, s, NEG))
                dp = nt_dot(vh[h, keys, :], gh[h])
                ds = (p * (dp - delta[h : h + 1, :])).astype(jnp.bfloat16)
                dv[h, keys, :] += nn_dot(p.astype(jnp.bfloat16), gh[h])
                dk[h, keys, :] += nn_dot(ds, qh[h])
                dqt[h] += nn_dot(kt[h, :, keys], ds)
            return inner

        lax.fori_loop(lo[qb], hi[qb], key_block, 0)
        parts = [dqt[h, :dim, :] * root for h in range(nh)]
        parts.append(jnp.zeros((width - hd, BQ), jnp.float32))
        dq_ref[rows, :] = jnp.concatenate(parts, axis=0).T.astype(jnp.bfloat16)
        return carry

    lax.fori_loop(0, count, query_block, 0)
    for ref in (dprev, dafter):
        ref[...] = jnp.zeros_like(ref)

    def store(ref, at, to):
        keys = rows_at(to, BK)
        blocks = [dk[h, keys, :] * root for h in range(nh)] + [dv[h, keys, :] for h in range(nh)]
        ref[rows_at(at, BK), :] = put_heads(blocks, [h * dim for h in range(2 * nh)], ref.shape[1]).astype(ref.dtype)

    over_window(lo[0], hi[count - 1], dprev, down, dafter, store)


def attend_back(nh, hd, lo, hi, prev, own, after, kid, qid, grad, ot, lse):
    rows, edge = own.shape[0], prev.shape[0]
    window = rows + 2 * edge
    width, kv = pad_to(hd, LANES), prev.shape[1]
    heads = lambda size, dtype: pltpu.VMEM((nh, size, LANES), dtype)
    return pl.pallas_call(
        functools.partial(attend_back_kernel, nh, hd),
        out_shape=(
            jax.ShapeDtypeStruct((rows, width), jnp.bfloat16),
            jax.ShapeDtypeStruct((edge, kv), jnp.bfloat16),
            jax.ShapeDtypeStruct((rows, kv), jnp.bfloat16),
            jax.ShapeDtypeStruct((edge, kv), jnp.bfloat16),
        ),
        in_specs=[SM, SM] + [VM] * 8,
        out_specs=(VM,) * 4,
        scratch_shapes=[
            heads(window, jnp.bfloat16),
            heads(window, jnp.bfloat16),
            pltpu.VMEM((nh, LANES, window), jnp.bfloat16),
            heads(BQ, jnp.bfloat16),
            heads(BQ, jnp.bfloat16),
            heads(window, jnp.float32),
            heads(window, jnp.float32),
            pltpu.VMEM((nh, LANES, BQ), jnp.float32),
            pltpu.VMEM((8, BQ), jnp.float32),
        ],
        compiler_params=pltpu.CompilerParams(vmem_limit_bytes=VMEM_LIMIT),
        cost_estimate=pl.CostEstimate(
            flops=10 * nh * rows * 1024 * LANES, bytes_accessed=16 << 20, transcendentals=nh * rows * 1024
        ),
    )(lo, hi, prev, own, after, kid, qid, grad, ot, lse)


MESH = pl.DeviceIdType.MESH


def greet(partners, count):
    barrier = pltpu.get_barrier_semaphore()
    for where, there in partners:
        @pl.when(there)
        def _():
            pl.semaphore_signal(barrier, inc=1, device_id=where, device_id_type=MESH)
    pl.semaphore_wait(barrier, count)


def wait_for(ref, sem):
    pltpu.make_async_copy(ref, ref, sem).wait()


def to_heads_kernel(reps, size, edge, kv, x_ref, own, prev, after, send, recv, edge_send, edge_recv):
    group, me = lax.axis_index("fsdp"), lax.axis_index("replica")
    groups = lax.axis_size("fsdp")
    wide = x_ref.shape[2]
    down, up = group > 0, group < groups - 1
    others = [(group, lax.rem(me + d, reps)) for d in range(1, reps)]
    greet(
        [(place, True) for place in others] + [((group - 1, me), down), ((group + 1, me), up)],
        reps - 1 + down.astype(jnp.int32) + up.astype(jnp.int32),
    )
    spans = [pl.ds(0, kv), pl.ds(kv, wide - kv)] if wide > kv else [pl.ds(0, kv)]

    def exchange(span, part, there):
        return pltpu.make_async_remote_copy(
            src_ref=x_ref.at[there, :, span], dst_ref=own.at[me, :, span], send_sem=send.at[part, there],
            recv_sem=recv.at[part, me], device_id=(group, there), device_id_type=MESH,
        )

    for part, span in enumerate(spans):
        for _, there in others:
            exchange(span, part, there).start()
        pltpu.make_async_copy(x_ref.at[me, :, span], own.at[me, :, span], recv.at[part, me]).start()

    def edges(piece, action):
        lo, hi = piece * size, (piece + 1) * size
        total = reps * size
        if lo >= total - edge:
            @pl.when(up)
            def _():
                action(0, piece, (group + 1, me), prev.at[pl.ds(lo - (total - edge), size), :])
        if hi <= edge:
            @pl.when(down)
            def _():
                action(1, piece, (group - 1, me), after.at[pl.ds(lo, size), :])

    def start_edge(way, piece, where, target):
        pltpu.make_async_remote_copy(
            src_ref=own.at[piece, :, spans[0]], dst_ref=target, send_sem=edge_send.at[way, piece],
            recv_sem=edge_recv.at[way, piece], device_id=where, device_id_type=MESH,
        ).start()

    def end_send(way, piece, where, target):
        wait_for(own.at[piece, :, spans[0]], edge_send.at[way, piece])

    def end_recv(way, piece, where, target):
        wait_for(target, edge_recv.at[way, piece])

    for piece in range(reps):
        wait_for(own.at[piece, :, spans[0]], recv.at[0, piece])
        edges(piece, start_edge)
    if len(spans) > 1:
        for piece in range(reps):
            wait_for(own.at[piece, :, spans[1]], recv.at[1, piece])
    for part, span in enumerate(spans):
        for _, there in others:
            wait_for(x_ref.at[there, :, span], send.at[part, there])
    for piece in range(reps):
        edges(piece, end_send)
        lo, hi = piece * size, (piece + 1) * size
        total = reps * size
        if lo >= total - edge:
            @pl.when(down)
            def _():
                wait_for(prev.at[pl.ds(lo - (total - edge), size), :], edge_recv.at[0, piece])
        if hi <= edge:
            @pl.when(up)
            def _():
                wait_for(after.at[pl.ds(lo, size), :], edge_recv.at[1, piece])


def to_heads(packed, edge, kv, collective_id):
    reps, size, wide = packed.shape
    sems = pltpu.SemaphoreType.DMA((2, reps))
    own, prev, after = pl.pallas_call(
        functools.partial(to_heads_kernel, reps, size, edge, kv),
        out_shape=(
            jax.ShapeDtypeStruct(packed.shape, packed.dtype),
            jax.ShapeDtypeStruct((edge, kv), packed.dtype),
            jax.ShapeDtypeStruct((edge, kv), packed.dtype),
        ),
        in_specs=[HB],
        out_specs=(HB, HB, HB),
        scratch_shapes=[sems, sems, sems, sems],
        compiler_params=pltpu.CompilerParams(collective_id=collective_id, has_side_effects=True),
    )(packed)
    return own.reshape(reps * size, wide), prev, after


def swap_kernel(reps, x_ref, y_ref, send, recv):
    group, me = lax.axis_index("fsdp"), lax.axis_index("replica")
    others = [(group, lax.rem(me + d, reps)) for d in range(1, reps)]
    greet([(place, True) for place in others], reps - 1)
    for _, there in others:
        pltpu.make_async_remote_copy(
            src_ref=x_ref.at[there], dst_ref=y_ref.at[me], send_sem=send.at[there], recv_sem=recv.at[me],
            device_id=(group, there), device_id_type=MESH,
        ).start()
    pltpu.make_async_copy(x_ref.at[me], y_ref.at[me], recv.at[me]).start()
    for piece in range(reps):
        wait_for(y_ref.at[piece], recv.at[piece])
    for _, there in others:
        wait_for(x_ref.at[there], send.at[there])


def swap(packed, collective_id):
    reps = packed.shape[0]
    sems = pltpu.SemaphoreType.DMA((reps,))
    return pl.pallas_call(
        functools.partial(swap_kernel, reps),
        out_shape=jax.ShapeDtypeStruct(packed.shape, packed.dtype),
        in_specs=[HB],
        out_specs=HB,
        scratch_shapes=[sems, sems],
        compiler_params=pltpu.CompilerParams(collective_id=collective_id, has_side_effects=True),
    )(packed)


def from_heads_kernel(reps, size, edge, dprev, own, dafter, dq, out_kv, out_q, from_up, from_down, total, mine, sends, recvs, send, recv):
    group, me = lax.axis_index("fsdp"), lax.axis_index("replica")
    groups = lax.axis_size("fsdp")
    rows = reps * size
    down, up = group > 0, group < groups - 1
    others = [(group, lax.rem(me + d, reps)) for d in range(1, reps)]
    greet(
        [(place, True) for place in others] + [((group - 1, me), down), ((group + 1, me), up)],
        reps - 1 + down.astype(jnp.int32) + up.astype(jnp.int32),
    )
    to_down = pltpu.make_async_remote_copy(
        src_ref=dprev, dst_ref=from_up, send_sem=sends.at[0], recv_sem=recvs.at[0],
        device_id=(group - 1, me), device_id_type=MESH,
    )
    to_up = pltpu.make_async_remote_copy(
        src_ref=dafter, dst_ref=from_down, send_sem=sends.at[1], recv_sem=recvs.at[1],
        device_id=(group + 1, me), device_id_type=MESH,
    )
    pl.when(down)(to_down.start)
    pl.when(up)(to_up.start)
    for _, there in others:
        pltpu.make_async_remote_copy(
            src_ref=dq.at[pl.ds(pl.multiple_of(there * size, size), size), :], dst_ref=out_q.at[me], send_sem=send.at[0, there],
            recv_sem=recv.at[0, me], device_id=(group, there), device_id_type=MESH,
        ).start()
    pltpu.make_async_copy(dq.at[pl.ds(pl.multiple_of(me * size, size), size), :], out_q.at[me], recv.at[0, me]).start()
    step = math.gcd(edge, 256)

    def chunk(at, carry):
        here = pl.ds(pl.multiple_of(at * step, step), step)
        total[here, :] = own[here, :].astype(jnp.float32)
        return carry

    lax.fori_loop(0, rows // step, chunk, 0)

    def add(ref, first):
        def body(at, carry):
            here = pl.ds(pl.multiple_of(first + at * step, step), step)
            there = pl.ds(pl.multiple_of(at * step, step), step)
            total[here, :] += ref[there, :].astype(jnp.float32)
            return carry

        lax.fori_loop(0, edge // step, body, 0)

    @pl.when(down)
    def _():
        wait_for(from_down, recvs.at[1])
        add(from_down, 0)

    @pl.when(up)
    def _():
        wait_for(from_up, recvs.at[0])
        add(from_up, rows - edge)

    def narrow(at, carry):
        here = pl.ds(pl.multiple_of(at * step, step), step)
        mine[here, :] = total[here, :].astype(jnp.bfloat16)
        return carry

    lax.fori_loop(0, rows // step, narrow, 0)
    for _, there in others:
        pltpu.make_async_remote_copy(
            src_ref=mine.at[pl.ds(pl.multiple_of(there * size, size), size), :], dst_ref=out_kv.at[me], send_sem=send.at[1, there],
            recv_sem=recv.at[1, me], device_id=(group, there), device_id_type=MESH,
        ).start()
    pltpu.make_async_copy(mine.at[pl.ds(pl.multiple_of(me * size, size), size), :], out_kv.at[me], recv.at[1, me]).start()
    for piece in range(reps):
        wait_for(out_q.at[piece], recv.at[0, piece])
        wait_for(out_kv.at[piece], recv.at[1, piece])
    for _, there in others:
        wait_for(out_q.at[0], send.at[0, there])
        wait_for(out_kv.at[0], send.at[1, there])
    pl.when(down)(to_down.wait_send)
    pl.when(up)(to_up.wait_send)


def from_heads(reps, dprev, own, dafter, dq, collective_id):
    rows, kv = own.shape
    edge, size = dprev.shape[0], own.shape[0] // reps
    pair, both = pltpu.SemaphoreType.DMA((2,)), pltpu.SemaphoreType.DMA((2, reps))
    return pl.pallas_call(
        functools.partial(from_heads_kernel, reps, size, edge),
        out_shape=(
            jax.ShapeDtypeStruct((reps, size, kv), own.dtype),
            jax.ShapeDtypeStruct((reps, size, dq.shape[1]), dq.dtype),
        ),
        in_specs=[HB, VM, HB, HB],
        out_specs=(HB, HB),
        scratch_shapes=[
            pltpu.VMEM((edge, kv), own.dtype),
            pltpu.VMEM((edge, kv), own.dtype),
            pltpu.VMEM((rows, kv), jnp.float32),
            pltpu.VMEM((rows, kv), own.dtype),
            pair,
            pair,
            both,
            both,
        ],
        compiler_params=pltpu.CompilerParams(
            collective_id=collective_id, has_side_effects=True, vmem_limit_bytes=VMEM_LIMIT
        ),
    )(dprev, own, dafter, dq)


def pre_norm(stream, shift, scale):
    centred = stream - jnp.mean(stream, axis=-1, keepdims=True)
    spread = jnp.mean(centred * centred, axis=-1, keepdims=True)
    return centred * lax.rsqrt(spread + NORM_EPS) * (1.0 + scale) + shift


def gelu_tanh(values):
    return jax.nn.gelu(values, approximate=True)


def latent_ids(latent_len, positions, token_total):
    starts = jnp.cumsum(latent_len) - latent_len
    found = jnp.sum((starts[None, :] <= positions[:, None]).astype(jnp.int32), axis=1) - 1
    inside = (positions >= 0) & (positions < token_total)
    return jnp.where(inside, found, -1)


def low_dot(left, right):
    return jnp.dot(left, right, preferred_element_type=jnp.float32)


def group_heads(matrix, reps):
    return matrix.reshape(matrix.shape[0], reps, -1).transpose(1, 0, 2)


def ungroup_heads(stacked):
    return stacked.transpose(1, 0, 2).reshape(stacked.shape[1], -1)


def widen(stacked, width):
    return jnp.pad(stacked, ((0, 0), (0, 0), (0, width - stacked.shape[2])))


def layer_forward(stream, mod_tok, full, plan):
    qkv_w, qkv_b, out_w, out_b, up_w, up_b, down_w, down_b = full
    reps, edge, bounds, ids = plan
    width = stream.shape[1]
    hd = width // reps
    nh = HEADS // reps
    shift_one, scale_one, gate_one, shift_two, scale_two, gate_two = jnp.split(mod_tok, 6, axis=1)
    normed = pre_norm(stream, shift_one, scale_one).astype(jnp.bfloat16)
    qkv_bias = qkv_b.astype(jnp.float32)
    bias_full = jnp.concatenate(
        [qkv_bias[:width], jnp.zeros((width,), jnp.float32), qkv_bias[width:]]
    )
    projected = (low_dot(normed, qkv_w) + bias_full).astype(jnp.bfloat16)
    query, key, value = (group_heads(part, reps) for part in jnp.split(projected, 3, axis=1))
    packed = widen(jnp.concatenate([key, value, query], axis=2), pad_to(3 * hd, LANES))
    own, prev, after = to_heads(packed, edge, pad_to(2 * hd, LANES), 1)
    mixed, mixed_t, log_norm = attend(nh, hd, *bounds, prev, own, after, *ids)
    mixed = swap(mixed.reshape(reps, -1, mixed.shape[1]), 2)
    mixed = ungroup_heads(mixed[:, :, :hd])
    branch = low_dot(mixed, out_w) + out_b.astype(jnp.float32)
    middle = stream + gate_one * branch
    normed_two = pre_norm(middle, shift_two, scale_two).astype(jnp.bfloat16)
    hidden = low_dot(normed_two, up_w) + up_b.astype(jnp.float32)
    active = gelu_tanh(hidden).astype(jnp.bfloat16)
    result = low_dot(active, down_w) + down_b.astype(jnp.float32)
    saved = (
        normed, (prev, own, after), mixed, (mixed_t, log_norm), branch, middle, normed_two, hidden, active, result,
    )
    return (middle + gate_two * result, saved)


def layer_backward(stream, mod_tok, full, saved, plan, pick, grad_next):
    qkv_w, qkv_b, out_w, out_b, up_w, up_b, down_w, down_b = full
    normed, window, mixed, kept, branch, middle, normed_two, hidden, active, result = saved
    reps, edge, bounds, ids = plan
    width = stream.shape[1]
    hd = width // reps
    nh = HEADS // reps
    shift_one, scale_one, gate_one, shift_two, scale_two, gate_two = jnp.split(mod_tok, 6, axis=1)
    grad_result = (gate_two * grad_next).astype(jnp.bfloat16)
    grad_gate_two = grad_next * result
    grad_down_w = jnp.einsum("tf,td->fd", active, grad_result, preferred_element_type=jnp.float32).astype(jnp.bfloat16)
    grad_down_b = jnp.sum(grad_result.astype(jnp.float32), axis=0)
    grad_active = jnp.einsum("td,fd->tf", grad_result, down_w, preferred_element_type=jnp.float32)
    _, gelu_back = jax.vjp(gelu_tanh, hidden)
    grad_hidden = gelu_back(grad_active)[0].astype(jnp.bfloat16)
    grad_up_w = jnp.einsum("td,tf->df", normed_two, grad_hidden, preferred_element_type=jnp.float32).astype(jnp.bfloat16)
    grad_up_b = jnp.sum(grad_hidden.astype(jnp.float32), axis=0)
    grad_normed_two = jnp.einsum("tf,df->td", grad_hidden, up_w, preferred_element_type=jnp.float32)
    _, norm_back_two = jax.vjp(pre_norm, middle, shift_two, scale_two)
    grad_middle_part, grad_shift_two, grad_scale_two = norm_back_two(grad_normed_two)
    grad_middle = grad_next + grad_middle_part
    grad_branch = (gate_one * grad_middle).astype(jnp.bfloat16)
    grad_gate_one = grad_middle * branch
    grad_out_w = jnp.einsum("td,te->de", mixed, grad_branch, preferred_element_type=jnp.float32).astype(jnp.bfloat16)
    grad_out_b = jnp.sum(grad_branch.astype(jnp.float32), axis=0)
    grad_mixed = jnp.einsum(
        "te,de->td", grad_branch, out_w, preferred_element_type=jnp.float32
    ).astype(jnp.bfloat16)
    grad_heads = swap(widen(group_heads(grad_mixed, reps), pad_to(hd, LANES)), 3)
    prev, own, after = window
    grad_q, grad_prev, grad_own, grad_after = attend_back(
        nh, hd, *bounds, prev, own, after, *ids, grad_heads.reshape(own.shape[0], -1), *kept
    )
    grad_kv, grad_q = from_heads(reps, grad_prev, grad_own, grad_after, grad_q, 4)
    grad_projected = jnp.concatenate(
        [ungroup_heads(grad_q[:, :, :hd]), ungroup_heads(grad_kv[:, :, :hd]), ungroup_heads(grad_kv[:, :, hd : 2 * hd])],
        axis=1,
    )
    grad_qkv_w = jnp.einsum("td,te->de", normed, grad_projected, preferred_element_type=jnp.float32).astype(jnp.bfloat16)
    sums = jnp.sum(grad_projected.astype(jnp.float32), axis=0)
    grad_qkv_b = jnp.concatenate([sums[:width], sums[2 * width :]])
    grad_normed = jnp.einsum("te,de->td", grad_projected, qkv_w, preferred_element_type=jnp.float32)
    _, norm_back_one = jax.vjp(pre_norm, stream, shift_one, scale_one)
    grad_stream_part, grad_shift_one, grad_scale_one = norm_back_one(grad_normed)
    grad_stream = grad_middle + grad_stream_part
    grad_mod = jnp.concatenate(
        [
            jnp.einsum("tl,tm->lm", pick, part, precision=HIGH, preferred_element_type=jnp.float32)
            for part in (
                grad_shift_one, grad_scale_one, grad_gate_one, grad_shift_two, grad_scale_two, grad_gate_two,
            )
        ],
        axis=1,
    )
    return (
        grad_stream, grad_mod, (grad_qkv_w, grad_out_w, grad_up_w, grad_down_w),
        (grad_qkv_b, grad_out_b, grad_up_b, grad_down_b),
    )


def gather_layer(params):
    rows = lambda value: lax.all_gather(value, "fsdp", axis=0, tiled=True)
    biases = jnp.concatenate([params[3], params[5], params[7], params[9]])
    biases = lax.all_gather(biases, "fsdp", axis=0)
    cuts = [0]
    for at in (3, 5, 7, 9):
        cuts.append(cuts[-1] + params[at].shape[0])
    qkv_b, out_b, up_b, down_b = (biases[:, a:b].reshape(-1) for a, b in zip(cuts[:-1], cuts[1:]))
    return (rows(params[2]), qkv_b, rows(params[4]), out_b, rows(params[6]), up_b, rows(params[8]), down_b)


def owner_sums(local_grads):
    shares = []
    for grad in local_grads:
        part = lax.psum_scatter(grad, "fsdp", scatter_dimension=0, tiled=True)
        shares.append(lax.psum(part, "replica").astype(jnp.float32))
    return shares


def attention_plan(latent_len, tok_rows, reps, device_at):
    column = tok_rows * reps
    edge = MAXLEN
    total = jnp.sum(latent_len)
    first = lax.axis_index("fsdp") * column
    positions = first - edge + jnp.arange(column + 2 * edge, dtype=jnp.int32)
    ends = jnp.cumsum(latent_len)
    ids = jnp.sum((ends[None, :] <= positions[:, None]).astype(jnp.int32), axis=1)
    ids = jnp.where(positions < 0, -1, ids)
    own = ids[edge : edge + column]
    count = column // BQ
    firsts, lasts = own[::BQ], own[BQ - 1 :: BQ]
    pick = lambda at: (at[:, None] == jnp.arange(latent_len.shape[0], dtype=jnp.int32)[None, :]).astype(jnp.int32)
    low = jnp.sum(pick(firsts) * (ends - latent_len)[None, :], axis=1) - (first - edge)
    high = jnp.sum(pick(lasts) * ends[None, :], axis=1) - (first - edge)
    bounds = ((low // BK).astype(jnp.int32), ((high + BK - 1) // BK).astype(jnp.int32))
    kid = jnp.broadcast_to(ids[:, None], (ids.shape[0], LANES))
    qid = jnp.broadcast_to(own[None, :], (8, column))
    return (reps, edge, bounds, (kid, qid))


def shards(
    tokens,
    cond,
    latent_len,
    first_ada_weight,
    first_ada_bias,
    first_qkv_weight,
    first_qkv_bias,
    first_out_weight,
    first_out_bias,
    first_up_weight,
    first_up_bias,
    first_down_weight,
    first_down_bias,
    second_ada_weight,
    second_ada_bias,
    second_qkv_weight,
    second_qkv_bias,
    second_out_weight,
    second_out_bias,
    second_up_weight,
    second_up_bias,
    second_down_weight,
    second_down_bias,
    cotangent,
):
    tok_rows = tokens.shape[0]
    group_place = lax.axis_index("fsdp")
    device_at = lax.axis_index(("fsdp", "replica"))
    token_total = tok_rows * lax.axis_size(("fsdp", "replica"))
    latent_count = cond.shape[0]
    local_pos = jnp.arange(tok_rows, dtype=jnp.int32)
    own_ids = latent_ids(latent_len, device_at * tok_rows + local_pos, token_total)
    pick = (own_ids[:, None] == jnp.arange(latent_count, dtype=jnp.int32)[None, :]).astype(
        jnp.float32
    )
    plan = attention_plan(latent_len, tok_rows, lax.axis_size("replica"), device_at)
    layers = (
        (
            first_ada_weight,
            first_ada_bias,
            first_qkv_weight,
            first_qkv_bias,
            first_out_weight,
            first_out_bias,
            first_up_weight,
            first_up_bias,
            first_down_weight,
            first_down_bias,
        ),
        (
            second_ada_weight,
            second_ada_bias,
            second_qkv_weight,
            second_qkv_bias,
            second_out_weight,
            second_out_bias,
            second_up_weight,
            second_up_bias,
            second_down_weight,
            second_down_bias,
        ),
    )
    col_width = first_ada_weight.shape[0]
    own_cond = lax.dynamic_slice_in_dim(
        cond.astype(jnp.float32), group_place * col_width, col_width, 1
    )
    own_silu = jax.nn.silu(own_cond).astype(jnp.bfloat16)
    partial_terms = []
    for params in layers:
        term = low_dot(own_silu, params[0])
        bias_share = params[1].astype(jnp.float32)
        spread = lax.dynamic_update_slice_in_dim(
            jnp.zeros((term.shape[1],), jnp.float32),
            bias_share,
            group_place * bias_share.shape[0],
            0,
        )
        partial_terms.append(term + spread[None, :])
    mod_first, mod_second = lax.psum((partial_terms[0], partial_terms[1]), "fsdp")
    mod_tokens = (
        jnp.dot(pick, mod_first, precision=HIGH, preferred_element_type=jnp.float32),
        jnp.dot(pick, mod_second, precision=HIGH, preferred_element_type=jnp.float32),
    )
    stream = tokens.astype(jnp.float32)
    inputs = []
    kept = []
    fulls = [gather_layer(params) for params in layers]
    for layer_at in range(2):
        inputs.append(stream)
        stream, saved = layer_forward(stream, mod_tokens[layer_at], fulls[layer_at], plan)
        kept.append(saved)
    output = stream.astype(jnp.bfloat16)
    grad_stream = cotangent.astype(jnp.float32)
    weight_grads = [None, None]
    mod_grads = [None, None]
    bias_grads = [None, None]
    for layer_at in (1, 0):
        grad_stream, grad_mod, local_grads, local_biases = layer_backward(
            inputs[layer_at], mod_tokens[layer_at], fulls[layer_at], kept[layer_at], plan, pick, grad_stream
        )
        weight_grads[layer_at] = owner_sums(local_grads)
        mod_grads[layer_at] = grad_mod
        bias_grads[layer_at] = local_biases
    flat = jnp.concatenate([part for grads in bias_grads for part in grads])
    grad_mod_first, grad_mod_second, flat = lax.psum((mod_grads[0], mod_grads[1], flat), ("fsdp", "replica"))
    place = 0
    bias_sums = []
    for grads in bias_grads:
        for part in grads:
            share = part.shape[0] // lax.axis_size("fsdp")
            bias_sums.append(lax.dynamic_slice_in_dim(flat, place + group_place * share, share, 0))
            place += part.shape[0]
    grad_silu = jnp.zeros(own_cond.shape, jnp.float32)
    ada_grads = []
    for params, grad_mod in zip(layers, (grad_mod_first, grad_mod_second)):
        low_mod = grad_mod.astype(jnp.bfloat16)
        weight_grad = jnp.einsum("ld,lm->dm", own_silu, low_mod, preferred_element_type=jnp.float32)
        column_sums = jnp.sum(low_mod.astype(jnp.float32), axis=0)
        bias_rows = params[1].shape[0]
        bias_grad = lax.dynamic_slice_in_dim(column_sums, group_place * bias_rows, bias_rows, 0)
        grad_silu = grad_silu + jnp.einsum(
            "lm,dm->ld", low_mod, params[0], preferred_element_type=jnp.float32
        )
        ada_grads.append((weight_grad, bias_grad))
    _, silu_back = jax.vjp(jax.nn.silu, own_cond)
    cond_grad = silu_back(grad_silu)[0]
    outs = [output, grad_stream, cond_grad]
    for layer_at in range(2):
        outs += list(ada_grads[layer_at])
        for weight, bias in zip(weight_grads[layer_at], bias_sums[4 * layer_at : 4 * layer_at + 4]):
            outs += [weight, bias]
    return tuple(outs)


def solution(mesh):
    in_specs = (
        P(("fsdp", "replica"), None),
        P(),
        P(),
        P("fsdp", None),
        P("fsdp"),
        P("fsdp", None),
        P("fsdp"),
        P("fsdp", None),
        P("fsdp"),
        P("fsdp", None),
        P("fsdp"),
        P("fsdp", None),
        P("fsdp"),
        P("fsdp", None),
        P("fsdp"),
        P("fsdp", None),
        P("fsdp"),
        P("fsdp", None),
        P("fsdp"),
        P("fsdp", None),
        P("fsdp"),
        P("fsdp", None),
        P("fsdp"),
        P(("fsdp", "replica"), None),
    )
    out_specs = (
        P(("fsdp", "replica"), None),
        P(("fsdp", "replica"), None),
        P(None, "fsdp"),
        P("fsdp", None),
        P("fsdp"),
        P("fsdp", None),
        P("fsdp"),
        P("fsdp", None),
        P("fsdp"),
        P("fsdp", None),
        P("fsdp"),
        P("fsdp", None),
        P("fsdp"),
        P("fsdp", None),
        P("fsdp"),
        P("fsdp", None),
        P("fsdp"),
        P("fsdp", None),
        P("fsdp"),
        P("fsdp", None),
        P("fsdp"),
        P("fsdp", None),
        P("fsdp"),
    )
    return jax.shard_map(shards, mesh=mesh, in_specs=in_specs, out_specs=out_specs, check_vma=False)
```

```python
import functools
import math

import jax
import jax.numpy as jnp
from jax import lax
from jax.experimental import pallas as pl
from jax.experimental.pallas import tpu as pltpu
from jax.sharding import PartitionSpec as P

HEADS = 16
MAXLEN = 1024
NORM_EPS = 1e-06
HIGH = lax.Precision.HIGHEST
BQ = 256
BK = 256
LANES = 128
NEG = -1e30
VM = pl.BlockSpec(memory_space=pltpu.VMEM)
SM = pl.BlockSpec(memory_space=pltpu.SMEM)
HB = pl.BlockSpec(memory_space=pl.ANY)
VMEM_LIMIT = 56 * 1024 * 1024


def pad_to(size, unit):
    return -(-size // unit) * unit


def take_head(ref, rows, at, dim):
    first, off = at // LANES * LANES, at % LANES
    wide = LANES if off + dim <= LANES else 2 * LANES
    block = ref[rows, first : first + wide].astype(jnp.float32)
    if off:
        block = pltpu.roll(block, wide - off, 1)
    block = block[:, :LANES]
    lane = lax.broadcasted_iota(jnp.int32, block.shape, 1)
    return jnp.where(lane < dim, block, 0.0)


def put_heads(blocks, places, width):
    tiles = [None] * (width // LANES)
    for block, at in zip(blocks, places):
        first, off = at // LANES, at % LANES
        wide = jnp.concatenate([block, jnp.zeros_like(block)], axis=1)
        if off:
            wide = pltpu.roll(wide, off, 1)
        for step in range(2):
            part = wide[:, step * LANES : (step + 1) * LANES]
            if first + step < len(tiles):
                old = tiles[first + step]
                tiles[first + step] = part if old is None else old + part
    rows = blocks[0].shape[0]
    return jnp.concatenate(
        [jnp.zeros((rows, LANES), jnp.float32) if t is None else t for t in tiles], axis=1
    )


def nt_dot(left, right):
    return lax.dot_general(left, right, (((1,), (1,)), ((), ())), preferred_element_type=jnp.float32)


def nn_dot(left, right):
    return jnp.dot(left, right, preferred_element_type=jnp.float32)


def rows_at(block, size):
    return pl.ds(pl.multiple_of(block * size, size), size)


def over_window(lo, hi, prev, own, after, action):
    edge, mid = prev.shape[0] // BK, own.shape[0] // BK

    def run(ref, first, count):
        def body(at, carry):
            action(ref, at - first, at)
            return carry

        lax.fori_loop(jnp.clip(lo, first, first + count), jnp.clip(hi, first, first + count), body, 0)

    run(prev, 0, edge)
    run(own, edge, mid)
    run(after, edge + mid, edge)


def attend_kernel(nh, hd, lo, hi, prev, own, after, kid, qid, o_ref, ot_ref, lse_ref, kh, vt, qh, acc, ml):
    dim = hd // nh
    width = o_ref.shape[1]
    count = own.shape[0] // BQ
    scale = math.log2(math.e) / math.sqrt(dim)

    def load(ref, at, to):
        for h in range(nh):
            kh[h, rows_at(to, BK), :] = take_head(ref, rows_at(at, BK), h * dim, dim).astype(jnp.bfloat16)
            vt[h, :, rows_at(to, BK)] = take_head(ref, rows_at(at, BK), hd + h * dim, dim).T.astype(jnp.bfloat16)

    over_window(lo[0], hi[count - 1], prev, own, after, load)
    lse_ref[...] = jnp.zeros_like(lse_ref)

    def query_block(qb, carry):
        rows = rows_at(qb, BQ)
        for h in range(nh):
            qh[h] = take_head(own, rows, 2 * hd + h * dim, dim).astype(jnp.bfloat16)
        acc[...] = jnp.zeros_like(acc)
        ml[0] = jnp.full(ml.shape[1:], NEG, jnp.float32)
        ml[1] = jnp.zeros(ml.shape[1:], jnp.float32)
        ids = qid[0:1, rows]

        def key_block(kb, inner):
            keys = rows_at(kb, BK)
            lanes = kid[keys, :]
            same = jnp.concatenate([lanes] * (BQ // LANES), axis=1) == ids
            for h in range(nh):
                s = jnp.where(same, nt_dot(kh[h, keys, :], qh[h]) * scale, NEG)
                old = ml[0, h : h + 1, :]
                top = jnp.maximum(old, jnp.max(s, axis=0, keepdims=True))
                p = jnp.exp2(s - top)
                alpha = jnp.exp2(old - top)
                ml[0, h : h + 1, :] = top
                ml[1, h : h + 1, :] = ml[1, h : h + 1, :] * alpha + jnp.sum(p, axis=0, keepdims=True)
                acc[h] = acc[h] * alpha + nn_dot(vt[h, :, keys], p.astype(jnp.bfloat16))
            return inner

        lax.fori_loop(lo[qb], hi[qb], key_block, 0)
        parts = []
        for h in range(nh):
            total = ml[1, h : h + 1, :]
            out = acc[h, :dim, :] / total
            parts.append(out)
            lse_ref[h : h + 1, rows] = ml[0, h : h + 1, :] + jnp.log2(total)
        parts.append(jnp.zeros((width - hd, BQ), jnp.float32))
        heads = jnp.concatenate(parts, axis=0)
        ot_ref[:, rows] = heads
        o_ref[rows, :] = heads.T.astype(jnp.bfloat16)
        return carry

    lax.fori_loop(0, count, query_block, 0)


def attend(nh, hd, lo, hi, prev, own, after, kid, qid):
    rows, window = own.shape[0], own.shape[0] + 2 * prev.shape[0]
    width = pad_to(hd, LANES)
    return pl.pallas_call(
        functools.partial(attend_kernel, nh, hd),
        out_shape=(
            jax.ShapeDtypeStruct((rows, width), jnp.bfloat16),
            jax.ShapeDtypeStruct((width, rows), jnp.float32),
            jax.ShapeDtypeStruct((8, rows), jnp.float32),
        ),
        in_specs=[SM, SM, VM, VM, VM, VM, VM],
        out_specs=(VM, VM, VM),
        scratch_shapes=[
            pltpu.VMEM((nh, window, LANES), jnp.bfloat16),
            pltpu.VMEM((nh, LANES, window), jnp.bfloat16),
            pltpu.VMEM((nh, BQ, LANES), jnp.bfloat16),
            pltpu.VMEM((nh, LANES, BQ), jnp.float32),
            pltpu.VMEM((2, 8, BQ), jnp.float32),
        ],
        compiler_params=pltpu.CompilerParams(vmem_limit_bytes=VMEM_LIMIT),
        cost_estimate=pl.CostEstimate(
            flops=4 * nh * rows * 1024 * LANES, bytes_accessed=8 << 20, transcendentals=nh * rows * 1024
        ),
    )(lo, hi, prev, own, after, kid, qid)


def attend_back_kernel(
    nh, hd, lo, hi, prev, own, after, kid, qid, do_ref, ot_ref, lse_ref,
    dq_ref, dprev, down, dafter, kh, vh, kt, qh, gh, dk, dv, dqt, delta,
):
    dim = hd // nh
    width = dq_ref.shape[1]
    count = own.shape[0] // BQ
    root = 1.0 / math.sqrt(dim)
    scale = math.log2(math.e) / math.sqrt(dim)

    def load(ref, at, to):
        for h in range(nh):
            k = take_head(ref, rows_at(at, BK), h * dim, dim)
            kh[h, rows_at(to, BK), :] = k.astype(jnp.bfloat16)
            kt[h, :, rows_at(to, BK)] = k.T.astype(jnp.bfloat16)
            vh[h, rows_at(to, BK), :] = take_head(ref, rows_at(at, BK), hd + h * dim, dim).astype(jnp.bfloat16)
            dk[h, rows_at(to, BK), :] = jnp.zeros((BK, LANES), jnp.float32)
            dv[h, rows_at(to, BK), :] = jnp.zeros((BK, LANES), jnp.float32)

    over_window(lo[0], hi[count - 1], prev, own, after, load)

    def query_block(qb, carry):
        rows = rows_at(qb, BQ)
        for h in range(nh):
            qh[h] = take_head(own, rows, 2 * hd + h * dim, dim).astype(jnp.bfloat16)
            gh[h] = take_head(do_ref, rows, h * dim, dim).astype(jnp.bfloat16)
        prod = do_ref[rows, :].astype(jnp.float32).T * ot_ref[:, rows]
        for h in range(nh):
            delta[h : h + 1, :] = jnp.sum(prod[h * dim : (h + 1) * dim], axis=0, keepdims=True)
        dqt[...] = jnp.zeros_like(dqt)
        ids = qid[0:1, rows]

        def key_block(kb, inner):
            keys = rows_at(kb, BK)
            lanes = kid[keys, :]
            same = jnp.concatenate([lanes] * (BQ // LANES), axis=1) == ids
            for h in range(nh):
                s = nt_dot(kh[h, keys, :], qh[h]) * scale - lse_ref[h : h + 1, rows]
                p = jnp.exp2(jnp.where(same, s, NEG))
                dp = nt_dot(vh[h, keys, :], gh[h])
                ds = (p * (dp - delta[h : h + 1, :])).astype(jnp.bfloat16)
                dv[h, keys, :] += nn_dot(p.astype(jnp.bfloat16), gh[h])
                dk[h, keys, :] += nn_dot(ds, qh[h])
                dqt[h] += nn_dot(kt[h, :, keys], ds)
            return inner

        lax.fori_loop(lo[qb], hi[qb], key_block, 0)
        parts = [dqt[h, :dim, :] * root for h in range(nh)]
        parts.append(jnp.zeros((width - hd, BQ), jnp.float32))
        dq_ref[rows, :] = jnp.concatenate(parts, axis=0).T.astype(jnp.bfloat16)
        return carry

    lax.fori_loop(0, count, query_block, 0)
    for ref in (dprev, dafter):
        ref[...] = jnp.zeros_like(ref)

    def store(ref, at, to):
        keys = rows_at(to, BK)
        blocks = [dk[h, keys, :] * root for h in range(nh)] + [dv[h, keys, :] for h in range(nh)]
        ref[rows_at(at, BK), :] = put_heads(blocks, [h * dim for h in range(2 * nh)], ref.shape[1]).astype(ref.dtype)

    over_window(lo[0], hi[count - 1], dprev, down, dafter, store)


def attend_back(nh, hd, lo, hi, prev, own, after, kid, qid, grad, ot, lse):
    rows, edge = own.shape[0], prev.shape[0]
    window = rows + 2 * edge
    width, kv = pad_to(hd, LANES), prev.shape[1]
    heads = lambda size, dtype: pltpu.VMEM((nh, size, LANES), dtype)
    return pl.pallas_call(
        functools.partial(attend_back_kernel, nh, hd),
        out_shape=(
            jax.ShapeDtypeStruct((rows, width), jnp.bfloat16),
            jax.ShapeDtypeStruct((edge, kv), jnp.bfloat16),
            jax.ShapeDtypeStruct((rows, kv), jnp.bfloat16),
            jax.ShapeDtypeStruct((edge, kv), jnp.bfloat16),
        ),
        in_specs=[SM, SM] + [VM] * 8,
        out_specs=(VM,) * 4,
        scratch_shapes=[
            heads(window, jnp.bfloat16),
            heads(window, jnp.bfloat16),
            pltpu.VMEM((nh, LANES, window), jnp.bfloat16),
            heads(BQ, jnp.bfloat16),
            heads(BQ, jnp.bfloat16),
            heads(window, jnp.float32),
            heads(window, jnp.float32),
            pltpu.VMEM((nh, LANES, BQ), jnp.float32),
            pltpu.VMEM((8, BQ), jnp.float32),
        ],
        compiler_params=pltpu.CompilerParams(vmem_limit_bytes=VMEM_LIMIT),
        cost_estimate=pl.CostEstimate(
            flops=10 * nh * rows * 1024 * LANES, bytes_accessed=16 << 20, transcendentals=nh * rows * 1024
        ),
    )(lo, hi, prev, own, after, kid, qid, grad, ot, lse)


MESH = pl.DeviceIdType.MESH


def greet(partners, count):
    barrier = pltpu.get_barrier_semaphore()
    for where, there in partners:
        @pl.when(there)
        def _():
            pl.semaphore_signal(barrier, inc=1, device_id=where, device_id_type=MESH)
    pl.semaphore_wait(barrier, count)


def wait_for(ref, sem):
    pltpu.make_async_copy(ref, ref, sem).wait()


def to_heads_kernel(reps, size, edge, kv, x_ref, own, prev, after, send, recv, edge_send, edge_recv):
    group, me = lax.axis_index("fsdp"), lax.axis_index("replica")
    groups = lax.axis_size("fsdp")
    wide = x_ref.shape[2]
    down, up = group > 0, group < groups - 1
    others = [(group, lax.rem(me + d, reps)) for d in range(1, reps)]
    greet(
        [(place, True) for place in others] + [((group - 1, me), down), ((group + 1, me), up)],
        reps - 1 + down.astype(jnp.int32) + up.astype(jnp.int32),
    )
    spans = [pl.ds(0, kv), pl.ds(kv, wide - kv)] if wide > kv else [pl.ds(0, kv)]

    def exchange(span, part, there):
        return pltpu.make_async_remote_copy(
            src_ref=x_ref.at[there, :, span], dst_ref=own.at[me, :, span], send_sem=send.at[part, there],
            recv_sem=recv.at[part, me], device_id=(group, there), device_id_type=MESH,
        )

    for part, span in enumerate(spans):
        for _, there in others:
            exchange(span, part, there).start()
        pltpu.make_async_copy(x_ref.at[me, :, span], own.at[me, :, span], recv.at[part, me]).start()

    def edges(piece, action):
        lo, hi = piece * size, (piece + 1) * size
        total = reps * size
        if lo >= total - edge:
            @pl.when(up)
            def _():
                action(0, piece, (group + 1, me), prev.at[pl.ds(lo - (total - edge), size), :])
        if hi <= edge:
            @pl.when(down)
            def _():
                action(1, piece, (group - 1, me), after.at[pl.ds(lo, size), :])

    def start_edge(way, piece, where, target):
        pltpu.make_async_remote_copy(
            src_ref=own.at[piece, :, spans[0]], dst_ref=target, send_sem=edge_send.at[way, piece],
            recv_sem=edge_recv.at[way, piece], device_id=where, device_id_type=MESH,
        ).start()

    def end_send(way, piece, where, target):
        wait_for(own.at[piece, :, spans[0]], edge_send.at[way, piece])

    def end_recv(way, piece, where, target):
        wait_for(target, edge_recv.at[way, piece])

    for piece in range(reps):
        wait_for(own.at[piece, :, spans[0]], recv.at[0, piece])
        edges(piece, start_edge)
    if len(spans) > 1:
        for piece in range(reps):
            wait_for(own.at[piece, :, spans[1]], recv.at[1, piece])
    for part, span in enumerate(spans):
        for _, there in others:
            wait_for(x_ref.at[there, :, span], send.at[part, there])
    for piece in range(reps):
        edges(piece, end_send)
        lo, hi = piece * size, (piece + 1) * size
        total = reps * size
        if lo >= total - edge:
            @pl.when(down)
            def _():
                wait_for(prev.at[pl.ds(lo - (total - edge), size), :], edge_recv.at[0, piece])
        if hi <= edge:
            @pl.when(up)
            def _():
                wait_for(after.at[pl.ds(lo, size), :], edge_recv.at[1, piece])


def to_heads(packed, edge, kv, collective_id):
    reps, size, wide = packed.shape
    sems = pltpu.SemaphoreType.DMA((2, reps))
    own, prev, after = pl.pallas_call(
        functools.partial(to_heads_kernel, reps, size, edge, kv),
        out_shape=(
            jax.ShapeDtypeStruct(packed.shape, packed.dtype),
            jax.ShapeDtypeStruct((edge, kv), packed.dtype),
            jax.ShapeDtypeStruct((edge, kv), packed.dtype),
        ),
        in_specs=[HB],
        out_specs=(HB, HB, HB),
        scratch_shapes=[sems, sems, sems, sems],
        compiler_params=pltpu.CompilerParams(collective_id=collective_id, has_side_effects=True),
    )(packed)
    return own.reshape(reps * size, wide), prev, after


def swap_kernel(reps, x_ref, y_ref, send, recv):
    group, me = lax.axis_index("fsdp"), lax.axis_index("replica")
    others = [(group, lax.rem(me + d, reps)) for d in range(1, reps)]
    greet([(place, True) for place in others], reps - 1)
    for _, there in others:
        pltpu.make_async_remote_copy(
            src_ref=x_ref.at[there], dst_ref=y_ref.at[me], send_sem=send.at[there], recv_sem=recv.at[me],
            device_id=(group, there), device_id_type=MESH,
        ).start()
    pltpu.make_async_copy(x_ref.at[me], y_ref.at[me], recv.at[me]).start()
    for piece in range(reps):
        wait_for(y_ref.at[piece], recv.at[piece])
    for _, there in others:
        wait_for(x_ref.at[there], send.at[there])


def swap(packed, collective_id):
    reps = packed.shape[0]
    sems = pltpu.SemaphoreType.DMA((reps,))
    return pl.pallas_call(
        functools.partial(swap_kernel, reps),
        out_shape=jax.ShapeDtypeStruct(packed.shape, packed.dtype),
        in_specs=[HB],
        out_specs=HB,
        scratch_shapes=[sems, sems],
        compiler_params=pltpu.CompilerParams(collective_id=collective_id, has_side_effects=True),
    )(packed)


def from_heads_kernel(reps, size, edge, dprev, own, dafter, dq, out_kv, out_q, from_up, from_down, total, mine, sends, recvs, send, recv):
    group, me = lax.axis_index("fsdp"), lax.axis_index("replica")
    groups = lax.axis_size("fsdp")
    rows = reps * size
    down, up = group > 0, group < groups - 1
    others = [(group, lax.rem(me + d, reps)) for d in range(1, reps)]
    greet(
        [(place, True) for place in others] + [((group - 1, me), down), ((group + 1, me), up)],
        reps - 1 + down.astype(jnp.int32) + up.astype(jnp.int32),
    )
    to_down = pltpu.make_async_remote_copy(
        src_ref=dprev, dst_ref=from_up, send_sem=sends.at[0], recv_sem=recvs.at[0],
        device_id=(group - 1, me), device_id_type=MESH,
    )
    to_up = pltpu.make_async_remote_copy(
        src_ref=dafter, dst_ref=from_down, send_sem=sends.at[1], recv_sem=recvs.at[1],
        device_id=(group + 1, me), device_id_type=MESH,
    )
    pl.when(down)(to_down.start)
    pl.when(up)(to_up.start)
    for _, there in others:
        pltpu.make_async_remote_copy(
            src_ref=dq.at[pl.ds(pl.multiple_of(there * size, size), size), :], dst_ref=out_q.at[me], send_sem=send.at[0, there],
            recv_sem=recv.at[0, me], device_id=(group, there), device_id_type=MESH,
        ).start()
    pltpu.make_async_copy(dq.at[pl.ds(pl.multiple_of(me * size, size), size), :], out_q.at[me], recv.at[0, me]).start()
    step = math.gcd(edge, 256)

    def chunk(at, carry):
        here = pl.ds(pl.multiple_of(at * step, step), step)
        total[here, :] = own[here, :].astype(jnp.float32)
        return carry

    lax.fori_loop(0, rows // step, chunk, 0)

    def add(ref, first):
        def body(at, carry):
            here = pl.ds(pl.multiple_of(first + at * step, step), step)
            there = pl.ds(pl.multiple_of(at * step, step), step)
            total[here, :] += ref[there, :].astype(jnp.float32)
            return carry

        lax.fori_loop(0, edge // step, body, 0)

    @pl.when(down)
    def _():
        wait_for(from_down, recvs.at[1])
        add(from_down, 0)

    @pl.when(up)
    def _():
        wait_for(from_up, recvs.at[0])
        add(from_up, rows - edge)

    def narrow(at, carry):
        here = pl.ds(pl.multiple_of(at * step, step), step)
        mine[here, :] = total[here, :].astype(jnp.bfloat16)
        return carry

    lax.fori_loop(0, rows // step, narrow, 0)
    for _, there in others:
        pltpu.make_async_remote_copy(
            src_ref=mine.at[pl.ds(pl.multiple_of(there * size, size), size), :], dst_ref=out_kv.at[me], send_sem=send.at[1, there],
            recv_sem=recv.at[1, me], device_id=(group, there), device_id_type=MESH,
        ).start()
    pltpu.make_async_copy(mine.at[pl.ds(pl.multiple_of(me * size, size), size), :], out_kv.at[me], recv.at[1, me]).start()
    for piece in range(reps):
        wait_for(out_q.at[piece], recv.at[0, piece])
        wait_for(out_kv.at[piece], recv.at[1, piece])
    for _, there in others:
        wait_for(out_q.at[0], send.at[0, there])
        wait_for(out_kv.at[0], send.at[1, there])
    pl.when(down)(to_down.wait_send)
    pl.when(up)(to_up.wait_send)


def from_heads(reps, dprev, own, dafter, dq, collective_id):
    rows, kv = own.shape
    edge, size = dprev.shape[0], own.shape[0] // reps
    pair, both = pltpu.SemaphoreType.DMA((2,)), pltpu.SemaphoreType.DMA((2, reps))
    return pl.pallas_call(
        functools.partial(from_heads_kernel, reps, size, edge),
        out_shape=(
            jax.ShapeDtypeStruct((reps, size, kv), own.dtype),
            jax.ShapeDtypeStruct((reps, size, dq.shape[1]), dq.dtype),
        ),
        in_specs=[HB, VM, HB, HB],
        out_specs=(HB, HB),
        scratch_shapes=[
            pltpu.VMEM((edge, kv), own.dtype),
            pltpu.VMEM((edge, kv), own.dtype),
            pltpu.VMEM((rows, kv), jnp.float32),
            pltpu.VMEM((rows, kv), own.dtype),
            pair,
            pair,
            both,
            both,
        ],
        compiler_params=pltpu.CompilerParams(
            collective_id=collective_id, has_side_effects=True, vmem_limit_bytes=VMEM_LIMIT
        ),
    )(dprev, own, dafter, dq)


UNITS = 12
LEFT_ROWS = 4


def reduce_kernel(layers, width, half, *refs):
    count = layers * UNITS
    ins, refs = refs[: 8 * layers], refs[8 * layers :]
    (out, left, right, csend, crecv, own, xs, xr, ys, yr, tx, ty, x2s, x2r, y2s, y2r, zs, z1r, z2s, z2r, fin,
     load_sem, core_s, core_r, x_s, x_r, y_s, y_r, x2_s, x2_r, y2_s, y2_r, z1_s, z1_r, z2_s, z2_r, fin_l, fin_s, fin_r,
     credit) = refs
    f, r = lax.axis_index("fsdp"), lax.axis_index("replica")
    rows = own.shape[1]
    tokens = left.shape[1]
    c, x, y = lax.rem(f, 2), lax.rem(f // 2, 2), f // 4
    core_at, x_at, y_at = f + 1 - 2 * c, f + 2 - 4 * x, f + 4 - 8 * y
    inner = jnp.logical_and(r > 0, r < 3)
    outer = jnp.logical_not(inner)
    z_at = r + 1 - 2 * lax.rem(r, 2)
    greet(
        [((core_at, r), True), ((x_at, r), True), ((y_at, r), True), ((f, r - 1), r > 0), ((f, r + 1), r < 3)],
        3 + (r > 0).astype(jnp.int32) + (r < 3).astype(jnp.int32),
    )
    loads = []
    for layer in range(layers):
        place = layer * (LEFT_ROWS + 3) * width
        for at in range(4):
            src = ins[8 * layer + at]
            loads.append((src, left.at[pl.ds(place, src.shape[0]), :]))
            place += src.shape[0]
        slot = layer * 9
        for at in range(4):
            src = ins[8 * layer + 4 + at]
            for part in range(src.shape[1] // width):
                loads.append((src.at[:, pl.ds(part * width, width)], right.at[slot]))
                slot += 1
    for at, (src, dst) in enumerate(loads):
        pltpu.make_async_copy(src, dst, load_sem.at[at]).start()
    for at, (src, dst) in enumerate(loads):
        pltpu.make_async_copy(src, dst, load_sem.at[at]).wait()

    def send(src, dst, s_sem, r_sem, where):
        return pltpu.make_async_remote_copy(
            src_ref=src, dst_ref=dst, send_sem=s_sem, recv_sem=r_sem, device_id=where, device_id_type=MESH
        )

    def term(u, core, mx, my):
        layer, w = u // UNITS, lax.rem(u, UNITS)
        block = ((y + my * (1 - 2 * y)) * 2 + (x + mx * (1 - 2 * x))) * 2 + (c + core * (1 - 2 * c))
        inside = jnp.where(
            w < 4, rows * w, LEFT_ROWS * width + jnp.where(w < 8, 0, jnp.where(w < 9, width, 2 * width))
        )
        stride = jnp.where(w < 4, 4 * rows, rows)
        start = pl.multiple_of(layer * ((LEFT_ROWS + 3) * width) + inside + stride * block, 16)
        other = layer * 9 + jnp.maximum(w - 3, 0)
        return nn_dot(left[pl.ds(start, rows), :], right[other])

    places = ((0, 0), (1, 0), (0, 1), (1, 1))
    top, low = pl.ds(0, half), pl.ds(half, rows - half)

    def core_copy(slot):
        return send(csend.at[slot], crecv.at[slot], core_s.at[slot], core_r.at[slot], (core_at, r))

    def x_copy(slot):
        return send(xs.at[slot], xr.at[slot], x_s.at[slot], x_r.at[slot], (x_at, r))

    def y_copy(slot):
        return send(ys.at[slot], yr.at[slot], y_s.at[slot], y_r.at[slot], (y_at, r))

    def x2_copy(slot):
        return send(x2s.at[slot], x2r.at[slot], x2_s.at[slot], x2_r.at[slot], (x_at, r))

    def y2_copy(slot):
        return send(y2s.at[slot], y2r.at[slot], y2_s.at[slot], y2_r.at[slot], (y_at, r))

    def z1_copy(slot, to):
        return send(zs.at[slot], z1r.at[to], z1_s.at[slot], z1_r.at[to], (f, z_at))

    def z2_copy(slot):
        return send(z2s.at[slot], z2r.at[slot], z2_s.at[slot], z2_r.at[slot], (f, 3 - r))

    def fin_copy(slot, u):
        return send(fin.at[slot], out.at[u], fin_s.at[slot], fin_r.at[u], (f, z_at))

    def keep_copy(slot, u):
        return pltpu.make_async_copy(fin.at[slot], out.at[u], fin_l.at[slot])

    f32, bf16 = jnp.float32, jnp.bfloat16
    z_slots = z1r.shape[0]

    def stage(u, condition, body):
        live = jnp.logical_and(u >= 0, u < count)
        pl.when(live if condition is None else jnp.logical_and(live, condition))(lambda: body(u))

    def close(u):
        slot = lax.rem(u, 4)
        fin_copy(slot, u).wait_send()
        keep_copy(slot, u).wait()

    def arrive(u):
        fin_copy(lax.rem(u, 4), u).wait_recv()

    def finish(u):
        slot = lax.rem(u, 4)
        z2_copy(slot).wait()
        fin[slot] = (z2s[slot].astype(f32) + z2r[slot].astype(f32)).astype(bf16)
        fin_copy(slot, u).start()
        keep_copy(slot, u).start()

    def middle(u):
        slot, z_slot, at = lax.rem(u, 4), lax.rem(u, z_slots), lax.rem(u, own.shape[0])
        z1_copy(slot, z_slot).wait_recv()
        z2s[slot] = (own[at] + z1r[z_slot].astype(f32)).astype(bf16)
        z2_copy(slot).start()

        @pl.when(u + z_slots < count)
        def _():
            pl.semaphore_signal(credit, inc=1, device_id=(f, z_at), device_id_type=MESH)

    def sent(u):
        z1_copy(lax.rem(u, 4), lax.rem(u, z_slots)).wait_send()

    def plane(u):
        slot, at = lax.rem(u, 4), lax.rem(u, own.shape[0])
        x2_copy(slot).wait()
        y2_copy(slot).wait()
        own[at, top, :] += y2r[slot].astype(f32)
        own[at, low, :] += x2r[slot].astype(f32)

        @pl.when(outer)
        def _():
            zs[slot] = own[at].astype(bf16)

            @pl.when(u >= z_slots)
            def _():
                pl.semaphore_wait(credit, 1)

            z1_copy(slot, lax.rem(u, z_slots)).start()

    def cross(u):
        slot, at = lax.rem(u, 4), lax.rem(u, own.shape[0])
        x_copy(slot).wait()
        y_copy(slot).wait()
        y2s[slot] = (ty[slot] + xr[slot, 1].astype(f32)).astype(bf16)
        y2_copy(slot).start()
        x2s[slot] = (tx[slot] + yr[slot, 1].astype(f32)).astype(bf16)
        x2_copy(slot).start()
        own[at, top, :] += xr[slot, 0].astype(f32)
        own[at, low, :] += yr[slot, 0].astype(f32)

    def chip(u):
        slot, pair, at = lax.rem(u, 4), lax.rem(u, 2), lax.rem(u, own.shape[0])
        core_copy(pair).wait()
        total = term(u, 0, 1, 1) + crecv[pair, 3].astype(f32)
        xs[slot, 1] = total[:half].astype(bf16)
        ys[slot, 1] = total[half:].astype(bf16)
        total = term(u, 0, 1, 0) + crecv[pair, 1].astype(f32)
        xs[slot, 0] = total[:half].astype(bf16)
        tx[slot] = total[half:]
        x_copy(slot).start()
        total = term(u, 0, 0, 1) + crecv[pair, 2].astype(f32)
        ys[slot, 0] = total[half:].astype(bf16)
        ty[slot] = total[:half]
        y_copy(slot).start()
        own[at] = term(u, 0, 0, 0) + crecv[pair, 0].astype(f32)

    def open_unit(u):
        pair = lax.rem(u, 2)
        for m, (mx, my) in enumerate(places):
            csend[pair, m] = term(u, 1, mx, my).astype(bf16)
        core_copy(pair).start()

    def step(t, carry):
        stage(t - 11, inner, close)
        stage(t - 11, outer, arrive)
        stage(t - 9, inner, finish)
        stage(t - 7, inner, middle)
        stage(t - 7, outer, sent)
        stage(t - 5, None, plane)
        stage(t - 3, None, cross)
        stage(t - 1, None, chip)
        stage(t, None, open_unit)
        return carry

    lax.fori_loop(0, count + 11, step, 0)


def reduce_grads(pairs):
    layers = len(pairs)
    width, tokens = pairs[0][0][1].shape
    rows = width // 8
    half = pad_to(rows // 2, 16)
    ins = [part for lefts, rights in pairs for part in (*lefts, *rights)]
    count = layers * UNITS
    bf16, f32 = jnp.bfloat16, jnp.float32
    buf = lambda dtype, *shape: pltpu.VMEM((*shape, width), dtype)
    sem = lambda size: pltpu.SemaphoreType.DMA((size,))
    z_slots = 8
    return pl.pallas_call(
        functools.partial(reduce_kernel, layers, width, half),
        out_shape=jax.ShapeDtypeStruct((count, rows, width), bf16),
        in_specs=[HB] * len(ins),
        out_specs=HB,
        scratch_shapes=[
            pltpu.VMEM((layers * (LEFT_ROWS + 3) * width, tokens), bf16),
            buf(bf16, layers * 9, tokens),
            buf(bf16, 2, 4, rows), buf(bf16, 2, 4, rows), buf(f32, 9, rows),
            buf(bf16, 4, 2, half), buf(bf16, 4, 2, half), buf(bf16, 4, 2, rows - half), buf(bf16, 4, 2, rows - half),
            buf(f32, 4, rows - half), buf(f32, 4, half),
            buf(bf16, 4, rows - half), buf(bf16, 4, rows - half), buf(bf16, 4, half), buf(bf16, 4, half),
            buf(bf16, 4, rows), buf(bf16, z_slots, rows), buf(bf16, 4, rows), buf(bf16, 4, rows), buf(bf16, 4, rows),
            sem(13 * layers), sem(2), sem(2), sem(4), sem(4), sem(4), sem(4), sem(4), sem(4), sem(4), sem(4),
            sem(4), sem(z_slots), sem(4), sem(4), sem(4), sem(4), sem(count), pltpu.SemaphoreType.REGULAR,
        ],
        compiler_params=pltpu.CompilerParams(
            collective_id=5, has_side_effects=True, vmem_limit_bytes=60 * 1024 * 1024
        ),
        cost_estimate=pl.CostEstimate(
            flops=2 * count * 8 * rows * tokens * width, bytes_accessed=100 << 20, transcendentals=0
        ),
    )(*ins)


def pre_norm(stream, shift, scale):
    centred = stream - jnp.mean(stream, axis=-1, keepdims=True)
    spread = jnp.mean(centred * centred, axis=-1, keepdims=True)
    return centred * lax.rsqrt(spread + NORM_EPS) * (1.0 + scale) + shift


def gelu_tanh(values):
    return jax.nn.gelu(values, approximate=True)


def latent_ids(latent_len, positions, token_total):
    starts = jnp.cumsum(latent_len) - latent_len
    found = jnp.sum((starts[None, :] <= positions[:, None]).astype(jnp.int32), axis=1) - 1
    inside = (positions >= 0) & (positions < token_total)
    return jnp.where(inside, found, -1)


def low_dot(left, right):
    return jnp.dot(left, right, preferred_element_type=jnp.float32)


def group_heads(matrix, reps):
    return matrix.reshape(matrix.shape[0], reps, -1).transpose(1, 0, 2)


def ungroup_heads(stacked):
    return stacked.transpose(1, 0, 2).reshape(stacked.shape[1], -1)


def widen(stacked, width):
    return jnp.pad(stacked, ((0, 0), (0, 0), (0, width - stacked.shape[2])))


def layer_forward(stream, mod_tok, full, plan):
    qkv_w, qkv_b, out_w, out_b, up_w, up_b, down_w, down_b = full
    reps, edge, bounds, ids = plan
    width = stream.shape[1]
    hd = width // reps
    nh = HEADS // reps
    shift_one, scale_one, gate_one, shift_two, scale_two, gate_two = jnp.split(mod_tok, 6, axis=1)
    normed = pre_norm(stream, shift_one, scale_one).astype(jnp.bfloat16)
    qkv_bias = qkv_b.astype(jnp.float32)
    bias_full = jnp.concatenate(
        [qkv_bias[:width], jnp.zeros((width,), jnp.float32), qkv_bias[width:]]
    )
    projected = (low_dot(normed, qkv_w) + bias_full).astype(jnp.bfloat16)
    query, key, value = (group_heads(part, reps) for part in jnp.split(projected, 3, axis=1))
    packed = widen(jnp.concatenate([key, value, query], axis=2), pad_to(3 * hd, LANES))
    own, prev, after = to_heads(packed, edge, pad_to(2 * hd, LANES), 1)
    mixed, mixed_t, log_norm = attend(nh, hd, *bounds, prev, own, after, *ids)
    mixed = swap(mixed.reshape(reps, -1, mixed.shape[1]), 2)
    mixed = ungroup_heads(mixed[:, :, :hd])
    branch = low_dot(mixed, out_w) + out_b.astype(jnp.float32)
    middle = stream + gate_one * branch
    normed_two = pre_norm(middle, shift_two, scale_two).astype(jnp.bfloat16)
    hidden = low_dot(normed_two, up_w) + up_b.astype(jnp.float32)
    active = gelu_tanh(hidden).astype(jnp.bfloat16)
    result = low_dot(active, down_w) + down_b.astype(jnp.float32)
    saved = (
        normed, (prev, own, after), mixed, (mixed_t, log_norm), branch, middle, normed_two, hidden, active, result,
    )
    return (middle + gate_two * result, saved)


def layer_backward(stream, mod_tok, full, saved, plan, pick, grad_next):
    qkv_w, qkv_b, out_w, out_b, up_w, up_b, down_w, down_b = full
    normed, window, mixed, kept, branch, middle, normed_two, hidden, active, result = saved
    reps, edge, bounds, ids = plan
    width = stream.shape[1]
    hd = width // reps
    nh = HEADS // reps
    shift_one, scale_one, gate_one, shift_two, scale_two, gate_two = jnp.split(mod_tok, 6, axis=1)
    grad_result = (gate_two * grad_next).astype(jnp.bfloat16)
    grad_gate_two = grad_next * result
    grad_down_b = jnp.sum(grad_result.astype(jnp.float32), axis=0)
    grad_active = jnp.einsum("td,fd->tf", grad_result, down_w, preferred_element_type=jnp.float32)
    _, gelu_back = jax.vjp(gelu_tanh, hidden)
    grad_hidden = gelu_back(grad_active)[0].astype(jnp.bfloat16)
    grad_up_b = jnp.sum(grad_hidden.astype(jnp.float32), axis=0)
    grad_normed_two = jnp.einsum("tf,df->td", grad_hidden, up_w, preferred_element_type=jnp.float32)
    _, norm_back_two = jax.vjp(pre_norm, middle, shift_two, scale_two)
    grad_middle_part, grad_shift_two, grad_scale_two = norm_back_two(grad_normed_two)
    grad_middle = grad_next + grad_middle_part
    grad_branch = (gate_one * grad_middle).astype(jnp.bfloat16)
    grad_gate_one = grad_middle * branch
    grad_out_b = jnp.sum(grad_branch.astype(jnp.float32), axis=0)
    grad_mixed = jnp.einsum(
        "te,de->td", grad_branch, out_w, preferred_element_type=jnp.float32
    ).astype(jnp.bfloat16)
    grad_heads = swap(widen(group_heads(grad_mixed, reps), pad_to(hd, LANES)), 3)
    prev, own, after = window
    grad_q, grad_prev, grad_own, grad_after = attend_back(
        nh, hd, *bounds, prev, own, after, *ids, grad_heads.reshape(own.shape[0], -1), *kept
    )
    grad_kv, grad_q = from_heads(reps, grad_prev, grad_own, grad_after, grad_q, 4)
    grad_projected = jnp.concatenate(
        [ungroup_heads(grad_q[:, :, :hd]), ungroup_heads(grad_kv[:, :, :hd]), ungroup_heads(grad_kv[:, :, hd : 2 * hd])],
        axis=1,
    )
    sums = jnp.sum(grad_projected.astype(jnp.float32), axis=0)
    grad_qkv_b = jnp.concatenate([sums[:width], sums[2 * width :]])
    grad_normed = jnp.einsum("te,de->td", grad_projected, qkv_w, preferred_element_type=jnp.float32)
    _, norm_back_one = jax.vjp(pre_norm, stream, shift_one, scale_one)
    grad_stream_part, grad_shift_one, grad_scale_one = norm_back_one(grad_normed)
    grad_stream = grad_middle + grad_stream_part
    grad_mod = jnp.concatenate(
        [
            jnp.einsum("tl,tm->lm", pick, part, precision=HIGH, preferred_element_type=jnp.float32)
            for part in (
                grad_shift_one, grad_scale_one, grad_gate_one, grad_shift_two, grad_scale_two, grad_gate_two,
            )
        ],
        axis=1,
    )
    return (
        grad_stream, grad_mod,
        ((active.T, normed_two.T, mixed.T, normed.T), (grad_result, grad_hidden, grad_branch, grad_projected)),
        (grad_qkv_b, grad_out_b, grad_up_b, grad_down_b),
    )


def gather_layer(params):
    rows = lambda value: lax.all_gather(value, "fsdp", axis=0, tiled=True)
    biases = jnp.concatenate([params[3], params[5], params[7], params[9]])
    biases = lax.all_gather(biases, "fsdp", axis=0)
    cuts = [0]
    for at in (3, 5, 7, 9):
        cuts.append(cuts[-1] + params[at].shape[0])
    qkv_b, out_b, up_b, down_b = (biases[:, a:b].reshape(-1) for a, b in zip(cuts[:-1], cuts[1:]))
    return (rows(params[2]), qkv_b, rows(params[4]), out_b, rows(params[6]), up_b, rows(params[8]), down_b)


def owner_sums(pairs):
    if lax.axis_size("fsdp") == 8 and lax.axis_size("replica") == 4:
        units = reduce_grads(pairs).reshape(len(pairs), UNITS, -1, pairs[0][0][1].shape[0])
        rows, width = units.shape[2:]
        across = lambda part: part.transpose(1, 0, 2).reshape(rows, -1).astype(jnp.float32)
        return [
            (
                across(unit[9:12]), across(unit[8:9]), across(unit[4:8]),
                unit[0:4].reshape(-1, width).astype(jnp.float32),
            )
            for unit in units
        ]
    shares = []
    for lefts, rights in pairs:
        grads = []
        for left, right in zip(lefts, rights):
            grad = low_dot(left, right).astype(jnp.bfloat16)
            part = lax.psum_scatter(grad, "fsdp", scatter_dimension=0, tiled=True)
            grads.append(lax.psum(part, "replica").astype(jnp.float32))
        shares.append(grads[::-1])
    return shares


def attention_plan(latent_len, tok_rows, reps, device_at):
    column = tok_rows * reps
    edge = MAXLEN
    total = jnp.sum(latent_len)
    first = lax.axis_index("fsdp") * column
    positions = first - edge + jnp.arange(column + 2 * edge, dtype=jnp.int32)
    ends = jnp.cumsum(latent_len)
    ids = jnp.sum((ends[None, :] <= positions[:, None]).astype(jnp.int32), axis=1)
    ids = jnp.where(positions < 0, -1, ids)
    own = ids[edge : edge + column]
    count = column // BQ
    firsts, lasts = own[::BQ], own[BQ - 1 :: BQ]
    pick = lambda at: (at[:, None] == jnp.arange(latent_len.shape[0], dtype=jnp.int32)[None, :]).astype(jnp.int32)
    low = jnp.sum(pick(firsts) * (ends - latent_len)[None, :], axis=1) - (first - edge)
    high = jnp.sum(pick(lasts) * ends[None, :], axis=1) - (first - edge)
    bounds = ((low // BK).astype(jnp.int32), ((high + BK - 1) // BK).astype(jnp.int32))
    kid = jnp.broadcast_to(ids[:, None], (ids.shape[0], LANES))
    qid = jnp.broadcast_to(own[None, :], (8, column))
    return (reps, edge, bounds, (kid, qid))


def shards(
    tokens,
    cond,
    latent_len,
    first_ada_weight,
    first_ada_bias,
    first_qkv_weight,
    first_qkv_bias,
    first_out_weight,
    first_out_bias,
    first_up_weight,
    first_up_bias,
    first_down_weight,
    first_down_bias,
    second_ada_weight,
    second_ada_bias,
    second_qkv_weight,
    second_qkv_bias,
    second_out_weight,
    second_out_bias,
    second_up_weight,
    second_up_bias,
    second_down_weight,
    second_down_bias,
    cotangent,
):
    tok_rows = tokens.shape[0]
    group_place = lax.axis_index("fsdp")
    device_at = lax.axis_index(("fsdp", "replica"))
    token_total = tok_rows * lax.axis_size(("fsdp", "replica"))
    latent_count = cond.shape[0]
    local_pos = jnp.arange(tok_rows, dtype=jnp.int32)
    own_ids = latent_ids(latent_len, device_at * tok_rows + local_pos, token_total)
    pick = (own_ids[:, None] == jnp.arange(latent_count, dtype=jnp.int32)[None, :]).astype(
        jnp.float32
    )
    plan = attention_plan(latent_len, tok_rows, lax.axis_size("replica"), device_at)
    layers = (
        (
            first_ada_weight,
            first_ada_bias,
            first_qkv_weight,
            first_qkv_bias,
            first_out_weight,
            first_out_bias,
            first_up_weight,
            first_up_bias,
            first_down_weight,
            first_down_bias,
        ),
        (
            second_ada_weight,
            second_ada_bias,
            second_qkv_weight,
            second_qkv_bias,
            second_out_weight,
            second_out_bias,
            second_up_weight,
            second_up_bias,
            second_down_weight,
            second_down_bias,
        ),
    )
    col_width = first_ada_weight.shape[0]
    own_cond = lax.dynamic_slice_in_dim(
        cond.astype(jnp.float32), group_place * col_width, col_width, 1
    )
    own_silu = jax.nn.silu(own_cond).astype(jnp.bfloat16)
    partial_terms = []
    for params in layers:
        term = low_dot(own_silu, params[0])
        bias_share = params[1].astype(jnp.float32)
        spread = lax.dynamic_update_slice_in_dim(
            jnp.zeros((term.shape[1],), jnp.float32),
            bias_share,
            group_place * bias_share.shape[0],
            0,
        )
        partial_terms.append(term + spread[None, :])
    mod_first, mod_second = lax.psum((partial_terms[0], partial_terms[1]), "fsdp")
    mod_tokens = (
        jnp.dot(pick, mod_first, precision=HIGH, preferred_element_type=jnp.float32),
        jnp.dot(pick, mod_second, precision=HIGH, preferred_element_type=jnp.float32),
    )
    stream = tokens.astype(jnp.float32)
    inputs = []
    kept = []
    fulls = [gather_layer(params) for params in layers]
    for layer_at in range(2):
        inputs.append(stream)
        stream, saved = layer_forward(stream, mod_tokens[layer_at], fulls[layer_at], plan)
        kept.append(saved)
    output = stream.astype(jnp.bfloat16)
    grad_stream = cotangent.astype(jnp.float32)
    weight_pairs = [None, None]
    mod_grads = [None, None]
    bias_grads = [None, None]
    for layer_at in (1, 0):
        grad_stream, grad_mod, local_grads, local_biases = layer_backward(
            inputs[layer_at], mod_tokens[layer_at], fulls[layer_at], kept[layer_at], plan, pick, grad_stream
        )
        weight_pairs[layer_at] = local_grads
        mod_grads[layer_at] = grad_mod
        bias_grads[layer_at] = local_biases
    weight_grads = owner_sums(weight_pairs)
    flat = jnp.concatenate([part for grads in bias_grads for part in grads])
    grad_mod_first, grad_mod_second, flat = lax.psum((mod_grads[0], mod_grads[1], flat), ("fsdp", "replica"))
    place = 0
    bias_sums = []
    for grads in bias_grads:
        for part in grads:
            share = part.shape[0] // lax.axis_size("fsdp")
            bias_sums.append(lax.dynamic_slice_in_dim(flat, place + group_place * share, share, 0))
            place += part.shape[0]
    grad_silu = jnp.zeros(own_cond.shape, jnp.float32)
    ada_grads = []
    for params, grad_mod in zip(layers, (grad_mod_first, grad_mod_second)):
        low_mod = grad_mod.astype(jnp.bfloat16)
        weight_grad = jnp.einsum("ld,lm->dm", own_silu, low_mod, preferred_element_type=jnp.float32)
        column_sums = jnp.sum(low_mod.astype(jnp.float32), axis=0)
        bias_rows = params[1].shape[0]
        bias_grad = lax.dynamic_slice_in_dim(column_sums, group_place * bias_rows, bias_rows, 0)
        grad_silu = grad_silu + jnp.einsum(
            "lm,dm->ld", low_mod, params[0], preferred_element_type=jnp.float32
        )
        ada_grads.append((weight_grad, bias_grad))
    _, silu_back = jax.vjp(jax.nn.silu, own_cond)
    cond_grad = silu_back(grad_silu)[0]
    outs = [output, grad_stream, cond_grad]
    for layer_at in range(2):
        outs += list(ada_grads[layer_at])
        for weight, bias in zip(weight_grads[layer_at], bias_sums[4 * layer_at : 4 * layer_at + 4]):
            outs += [weight, bias]
    return tuple(outs)


def solution(mesh):
    in_specs = (
        P(("fsdp", "replica"), None),
        P(),
        P(),
        P("fsdp", None),
        P("fsdp"),
        P("fsdp", None),
        P("fsdp"),
        P("fsdp", None),
        P("fsdp"),
        P("fsdp", None),
        P("fsdp"),
        P("fsdp", None),
        P("fsdp"),
        P("fsdp", None),
        P("fsdp"),
        P("fsdp", None),
        P("fsdp"),
        P("fsdp", None),
        P("fsdp"),
        P("fsdp", None),
        P("fsdp"),
        P("fsdp", None),
        P("fsdp"),
        P(("fsdp", "replica"), None),
    )
    out_specs = (
        P(("fsdp", "replica"), None),
        P(("fsdp", "replica"), None),
        P(None, "fsdp"),
        P("fsdp", None),
        P("fsdp"),
        P("fsdp", None),
        P("fsdp"),
        P("fsdp", None),
        P("fsdp"),
        P("fsdp", None),
        P("fsdp"),
        P("fsdp", None),
        P("fsdp"),
        P("fsdp", None),
        P("fsdp"),
        P("fsdp", None),
        P("fsdp"),
        P("fsdp", None),
        P("fsdp"),
        P("fsdp", None),
        P("fsdp"),
        P("fsdp", None),
        P("fsdp"),
    )
    return jax.shard_map(shards, mesh=mesh, in_specs=in_specs, out_specs=out_specs, check_vma=False)
```

```python
import functools
import math

import jax
import jax.numpy as jnp
from jax import lax
from jax.experimental import pallas as pl
from jax.experimental.pallas import tpu as pltpu
from jax.sharding import PartitionSpec as P

HEADS = 16
MAXLEN = 1024
NORM_EPS = 1e-06
HIGH = lax.Precision.HIGHEST
BQ = 256
BK = 256
LANES = 128
NEG = -1e30
VM = pl.BlockSpec(memory_space=pltpu.VMEM)
SM = pl.BlockSpec(memory_space=pltpu.SMEM)
HB = pl.BlockSpec(memory_space=pl.ANY)
VMEM_LIMIT = 56 * 1024 * 1024


def pad_to(size, unit):
    return -(-size // unit) * unit


def take_head(ref, rows, at, dim):
    first, off = at // LANES * LANES, at % LANES
    wide = LANES if off + dim <= LANES else 2 * LANES
    block = ref[rows, first : first + wide].astype(jnp.float32)
    if off:
        block = pltpu.roll(block, wide - off, 1)
    block = block[:, :LANES]
    lane = lax.broadcasted_iota(jnp.int32, block.shape, 1)
    return jnp.where(lane < dim, block, 0.0)


def put_heads(blocks, places, width):
    tiles = [None] * (width // LANES)
    for block, at in zip(blocks, places):
        first, off = at // LANES, at % LANES
        wide = jnp.concatenate([block, jnp.zeros_like(block)], axis=1)
        if off:
            wide = pltpu.roll(wide, off, 1)
        for step in range(2):
            part = wide[:, step * LANES : (step + 1) * LANES]
            if first + step < len(tiles):
                old = tiles[first + step]
                tiles[first + step] = part if old is None else old + part
    rows = blocks[0].shape[0]
    return jnp.concatenate(
        [jnp.zeros((rows, LANES), jnp.float32) if t is None else t for t in tiles], axis=1
    )


def nt_dot(left, right):
    return lax.dot_general(left, right, (((1,), (1,)), ((), ())), preferred_element_type=jnp.float32)


def nn_dot(left, right):
    return jnp.dot(left, right, preferred_element_type=jnp.float32)


def rows_at(block, size):
    return pl.ds(pl.multiple_of(block * size, size), size)


def over_window(lo, hi, prev, own, after, action):
    edge, mid = prev.shape[0] // BK, own.shape[0] // BK

    def run(ref, first, count):
        def body(at, carry):
            action(ref, at - first, at)
            return carry

        lax.fori_loop(jnp.clip(lo, first, first + count), jnp.clip(hi, first, first + count), body, 0)

    run(prev, 0, edge)
    run(own, edge, mid)
    run(after, edge + mid, edge)


def attend_kernel(nh, hd, lo, hi, prev, own, after, kid, qid, o_ref, ot_ref, lse_ref, kh, vt, qh, acc, ml):
    dim = hd // nh
    width = o_ref.shape[1]
    count = own.shape[0] // BQ
    scale = math.log2(math.e) / math.sqrt(dim)

    def load(ref, at, to):
        for h in range(nh):
            kh[h, rows_at(to, BK), :] = take_head(ref, rows_at(at, BK), h * dim, dim).astype(jnp.bfloat16)
            vt[h, :, rows_at(to, BK)] = take_head(ref, rows_at(at, BK), hd + h * dim, dim).T.astype(jnp.bfloat16)

    over_window(lo[0], hi[count - 1], prev, own, after, load)
    lse_ref[...] = jnp.zeros_like(lse_ref)

    def query_block(qb, carry):
        rows = rows_at(qb, BQ)
        for h in range(nh):
            qh[h] = take_head(own, rows, 2 * hd + h * dim, dim).astype(jnp.bfloat16)
        acc[...] = jnp.zeros_like(acc)
        ml[0] = jnp.full(ml.shape[1:], NEG, jnp.float32)
        ml[1] = jnp.zeros(ml.shape[1:], jnp.float32)
        ids = qid[0:1, rows]

        def key_block(kb, inner):
            keys = rows_at(kb, BK)
            lanes = kid[keys, :]
            same = jnp.concatenate([lanes] * (BQ // LANES), axis=1) == ids
            for h in range(nh):
                s = jnp.where(same, nt_dot(kh[h, keys, :], qh[h]) * scale, NEG)
                old = ml[0, h : h + 1, :]
                top = jnp.maximum(old, jnp.max(s, axis=0, keepdims=True))
                p = jnp.exp2(s - top)
                alpha = jnp.exp2(old - top)
                ml[0, h : h + 1, :] = top
                ml[1, h : h + 1, :] = ml[1, h : h + 1, :] * alpha + jnp.sum(p, axis=0, keepdims=True)
                acc[h] = acc[h] * alpha + nn_dot(vt[h, :, keys], p.astype(jnp.bfloat16))
            return inner

        lax.fori_loop(lo[qb], hi[qb], key_block, 0)
        parts = []
        for h in range(nh):
            total = ml[1, h : h + 1, :]
            out = acc[h, :dim, :] / total
            parts.append(out)
            lse_ref[h : h + 1, rows] = ml[0, h : h + 1, :] + jnp.log2(total)
        parts.append(jnp.zeros((width - hd, BQ), jnp.float32))
        heads = jnp.concatenate(parts, axis=0)
        ot_ref[:, rows] = heads
        o_ref[rows, :] = heads.T.astype(jnp.bfloat16)
        return carry

    lax.fori_loop(0, count, query_block, 0)


def attend(nh, hd, lo, hi, prev, own, after, kid, qid):
    rows, window = own.shape[0], own.shape[0] + 2 * prev.shape[0]
    width = pad_to(hd, LANES)
    return pl.pallas_call(
        functools.partial(attend_kernel, nh, hd),
        out_shape=(
            jax.ShapeDtypeStruct((rows, width), jnp.bfloat16),
            jax.ShapeDtypeStruct((width, rows), jnp.float32),
            jax.ShapeDtypeStruct((8, rows), jnp.float32),
        ),
        in_specs=[SM, SM, VM, VM, VM, VM, VM],
        out_specs=(VM, VM, VM),
        scratch_shapes=[
            pltpu.VMEM((nh, window, LANES), jnp.bfloat16),
            pltpu.VMEM((nh, LANES, window), jnp.bfloat16),
            pltpu.VMEM((nh, BQ, LANES), jnp.bfloat16),
            pltpu.VMEM((nh, LANES, BQ), jnp.float32),
            pltpu.VMEM((2, 8, BQ), jnp.float32),
        ],
        compiler_params=pltpu.CompilerParams(vmem_limit_bytes=VMEM_LIMIT),
        cost_estimate=pl.CostEstimate(
            flops=4 * nh * rows * 1024 * LANES, bytes_accessed=8 << 20, transcendentals=nh * rows * 1024
        ),
    )(lo, hi, prev, own, after, kid, qid)


def attend_back_kernel(
    nh, hd, lo, hi, prev, own, after, kid, qid, do_ref, ot_ref, lse_ref,
    dq_ref, dprev, down, dafter, kh, vh, kt, qh, gh, dk, dv, dqt, delta,
):
    dim = hd // nh
    width = dq_ref.shape[1]
    count = own.shape[0] // BQ
    root = 1.0 / math.sqrt(dim)
    scale = math.log2(math.e) / math.sqrt(dim)

    def load(ref, at, to):
        for h in range(nh):
            k = take_head(ref, rows_at(at, BK), h * dim, dim)
            kh[h, rows_at(to, BK), :] = k.astype(jnp.bfloat16)
            kt[h, :, rows_at(to, BK)] = k.T.astype(jnp.bfloat16)
            vh[h, rows_at(to, BK), :] = take_head(ref, rows_at(at, BK), hd + h * dim, dim).astype(jnp.bfloat16)
            dk[h, rows_at(to, BK), :] = jnp.zeros((BK, LANES), jnp.float32)
            dv[h, rows_at(to, BK), :] = jnp.zeros((BK, LANES), jnp.float32)

    over_window(lo[0], hi[count - 1], prev, own, after, load)

    def query_block(qb, carry):
        rows = rows_at(qb, BQ)
        for h in range(nh):
            qh[h] = take_head(own, rows, 2 * hd + h * dim, dim).astype(jnp.bfloat16)
            gh[h] = take_head(do_ref, rows, h * dim, dim).astype(jnp.bfloat16)
        prod = do_ref[rows, :].astype(jnp.float32).T * ot_ref[:, rows]
        for h in range(nh):
            delta[h : h + 1, :] = jnp.sum(prod[h * dim : (h + 1) * dim], axis=0, keepdims=True)
        dqt[...] = jnp.zeros_like(dqt)
        ids = qid[0:1, rows]

        def key_block(kb, inner):
            keys = rows_at(kb, BK)
            lanes = kid[keys, :]
            same = jnp.concatenate([lanes] * (BQ // LANES), axis=1) == ids
            for h in range(nh):
                s = nt_dot(kh[h, keys, :], qh[h]) * scale - lse_ref[h : h + 1, rows]
                p = jnp.exp2(jnp.where(same, s, NEG))
                dp = nt_dot(vh[h, keys, :], gh[h])
                ds = (p * (dp - delta[h : h + 1, :])).astype(jnp.bfloat16)
                dv[h, keys, :] += nn_dot(p.astype(jnp.bfloat16), gh[h])
                dk[h, keys, :] += nn_dot(ds, qh[h])
                dqt[h] += nn_dot(kt[h, :, keys], ds)
            return inner

        lax.fori_loop(lo[qb], hi[qb], key_block, 0)
        parts = [dqt[h, :dim, :] * root for h in range(nh)]
        parts.append(jnp.zeros((width - hd, BQ), jnp.float32))
        dq_ref[rows, :] = jnp.concatenate(parts, axis=0).T.astype(jnp.bfloat16)
        return carry

    lax.fori_loop(0, count, query_block, 0)
    for ref in (dprev, dafter):
        ref[...] = jnp.zeros_like(ref)

    def store(ref, at, to):
        keys = rows_at(to, BK)
        blocks = [dk[h, keys, :] * root for h in range(nh)] + [dv[h, keys, :] for h in range(nh)]
        ref[rows_at(at, BK), :] = put_heads(blocks, [h * dim for h in range(2 * nh)], ref.shape[1]).astype(ref.dtype)

    over_window(lo[0], hi[count - 1], dprev, down, dafter, store)


def attend_back(nh, hd, lo, hi, prev, own, after, kid, qid, grad, ot, lse):
    rows, edge = own.shape[0], prev.shape[0]
    window = rows + 2 * edge
    width, kv = pad_to(hd, LANES), prev.shape[1]
    heads = lambda size, dtype: pltpu.VMEM((nh, size, LANES), dtype)
    return pl.pallas_call(
        functools.partial(attend_back_kernel, nh, hd),
        out_shape=(
            jax.ShapeDtypeStruct((rows, width), jnp.bfloat16),
            jax.ShapeDtypeStruct((edge, kv), jnp.bfloat16),
            jax.ShapeDtypeStruct((rows, kv), jnp.bfloat16),
            jax.ShapeDtypeStruct((edge, kv), jnp.bfloat16),
        ),
        in_specs=[SM, SM] + [VM] * 8,
        out_specs=(VM,) * 4,
        scratch_shapes=[
            heads(window, jnp.bfloat16),
            heads(window, jnp.bfloat16),
            pltpu.VMEM((nh, LANES, window), jnp.bfloat16),
            heads(BQ, jnp.bfloat16),
            heads(BQ, jnp.bfloat16),
            heads(window, jnp.float32),
            heads(window, jnp.float32),
            pltpu.VMEM((nh, LANES, BQ), jnp.float32),
            pltpu.VMEM((8, BQ), jnp.float32),
        ],
        compiler_params=pltpu.CompilerParams(vmem_limit_bytes=VMEM_LIMIT),
        cost_estimate=pl.CostEstimate(
            flops=10 * nh * rows * 1024 * LANES, bytes_accessed=16 << 20, transcendentals=nh * rows * 1024
        ),
    )(lo, hi, prev, own, after, kid, qid, grad, ot, lse)


MESH = pl.DeviceIdType.MESH


def greet(partners, count):
    barrier = pltpu.get_barrier_semaphore()
    for where, there in partners:
        @pl.when(there)
        def _():
            pl.semaphore_signal(barrier, inc=1, device_id=where, device_id_type=MESH)
    pl.semaphore_wait(barrier, count)


def wait_for(ref, sem):
    pltpu.make_async_copy(ref, ref, sem).wait()


class Gather:
    COPIES = 9

    def __init__(self, shards, fulls, halves, send, recv, load, store, *held):
        self.shards, self.fulls, self.halves, self.held = shards, fulls, halves, held
        self.send, self.recv, self.load, self.store = send, recv, load, store
        self.f, self.r = lax.axis_index("fsdp"), lax.axis_index("replica")
        f = self.f
        c, x, y = lax.rem(f, 2), lax.rem(f // 2, 2), f // 4
        self.core, self.x, self.y = f + 1 - 2 * c, f + 2 - 4 * x, f + 4 - 8 * y
        self.xy = self.x + 4 - 8 * y

    def rows(self, at, which):
        rows, half = self.shards[at][0].shape[0], self.halves[at]
        return {"all": (0, rows), "top": (0, half), "low": (half, rows - half)}[which]

    def part(self, at, place, which):
        first, size = self.rows(at, which)
        rows = self.shards[at][0].shape[0]
        return self.fulls[at].at[pl.ds(pl.multiple_of(place * rows + first, 16), size), :]

    def remote(self, at, kind, src, dst, to):
        return pltpu.make_async_remote_copy(
            src_ref=src, dst_ref=dst, send_sem=self.send.at[at, kind],
            recv_sem=self.recv.at[at, kind], device_id=(to, self.r), device_id_type=MESH,
        )

    def copy(self, at, kind, place, which, to, source=None):
        dst = self.part(at, place, which)
        src = dst if source is None else self.held[at].at[source, pl.ds(*self.rows(at, which)), :]
        return self.remote(at, kind, src, dst, to)

    def hop(self, at, source):
        return self.remote(at, 6 + source, self.held[at].at[0], self.held[at].at[source], (self.x, self.y)[source - 1])

    def keep(self, at, source):
        place = (self.f, self.x, self.y)[source]
        return pltpu.make_async_copy(self.held[at].at[source], self.part(at, place, "all"), self.store.at[at, source])

    def fetch(self, at, source):
        return pltpu.make_async_copy(self.shards[at][source], self.held[at].at[source], self.load.at[at, source])

    def pass_on(self, at, source):
        place = (self.f, self.x, self.y)[source]
        self.copy(at, 2 + source, place, "all", self.core, source).start()
        self.keep(at, source).start()

    def begin(self):
        places = range(len(self.shards))
        for at in places:
            for source in range(len(self.shards[at])):
                self.fetch(at, source).start()
        for at in places:
            self.fetch(at, 0).wait()
            if len(self.shards[at]) == 1:
                self.hop(at, 1).start()
                self.hop(at, 2).start()
        for at in places:
            self.pass_on(at, 0)

    def onward(self, at):
        ahead = len(self.shards[at]) == 3
        self.fetch(at, 1).wait() if ahead else self.hop(at, 1).wait_recv()
        self.copy(at, 0, self.x, "top", self.y, 1).start()
        self.fetch(at, 2).wait() if ahead else self.hop(at, 2).wait_recv()
        self.copy(at, 1, self.y, "low", self.x, 2).start()
        self.pass_on(at, 1)
        self.pass_on(at, 2)

    def across(self, at):
        self.copy(at, 0, self.xy, "top", self.y).wait_recv()
        self.copy(at, 5, self.xy, "top", self.core).start()
        self.copy(at, 1, self.xy, "low", self.x).wait_recv()
        self.copy(at, 6, self.xy, "low", self.core).start()

    def end(self, at):
        for source in range(3):
            self.keep(at, source).wait()
            if source and len(self.shards[at]) == 1:
                self.hop(at, source).wait_send()
        for kind, which in ((0, "top"), (1, "low"), (2, "all"), (3, "all"), (4, "all"), (5, "top"), (6, "low")):
            self.copy(at, kind, self.f, which, self.core).wait_send()
            if kind >= 2:
                self.copy(at, kind, self.f, which, self.core).wait_recv()


def sent_ahead(shards, after):
    shards, _ = lax.optimization_barrier((shards, after))
    hop = lambda shard, step: lax.ppermute(shard, "fsdp", [(at, at ^ step) for at in range(8)])
    return [(shard, hop(shard, 2), hop(shard, 4)) for shard in shards]


def split_shards(refs, sizes):
    shards = []
    for size in sizes:
        shards.append(refs[:size])
        refs = refs[size:]
    return shards, refs


def gather_scratch(shards):
    count = len(shards)
    if not count:
        return []
    return [
        pltpu.SemaphoreType.DMA((count, Gather.COPIES)),
        pltpu.SemaphoreType.DMA((count, Gather.COPIES)),
        pltpu.SemaphoreType.DMA((count, 3)),
        pltpu.SemaphoreType.DMA((count, 3)),
    ] + [pltpu.VMEM((3, *part.shape), part.dtype) for part, *_ in shards]


def gathered_shapes(shards):
    return tuple(jax.ShapeDtypeStruct((8 * part.shape[0], part.shape[1]), part.dtype) for part, *_ in shards)


def halves_of(shards):
    halves, ahead = [], 0
    for part, *_ in shards:
        rows, size = part.shape
        half = rows // 32 * 16
        if rows % 32 and ahead <= 0:
            half += 16
        ahead += (2 * half - rows) * size
        halves.append(half)
    return tuple(halves), tuple(len(shard) for shard in shards)


def start_kernel(plan, part_in, bias_in, *refs):
    halves, sizes = plan
    count = len(halves)
    shards, refs = split_shards(refs, sizes)
    (mod, bias), fulls, refs = refs[:2], refs[2 : count + 2], refs[count + 2 :]
    terms, total, m_s, m_r, b_s, b_r, t_s, t_r, keep, *sems = refs
    f, r = lax.axis_index("fsdp"), lax.axis_index("replica")
    others = [lax.rem(f + d, 8) for d in range(1, 8)]
    greet([((there, r), True) for there in others], 7)

    def remote(src, dst, s_sem, r_sem, there):
        return pltpu.make_async_remote_copy(
            src_ref=src, dst_ref=dst, send_sem=s_sem, recv_sem=r_sem, device_id=(there, r), device_id_type=MESH
        )

    def term_copy(block, source, there):
        return remote(part_in.at[block], terms.at[source], t_s.at[there], t_r.at[source], there)

    def bias_copy(source, there):
        return remote(bias_in, bias.at[source], b_s.at[there], b_r.at[source], there)

    def mod_copy(source, there):
        return remote(total, mod.at[source], m_s.at[there], m_r.at[source], there)

    gather = Gather(shards, fulls, halves, *sems)
    for there in others:
        term_copy(there, f, there).start()
    mine = pltpu.make_async_copy(part_in.at[f], terms.at[f], keep.at[0])
    mine.start()
    gather.begin()
    for there in others:
        bias_copy(f, there).start()
    own_bias = pltpu.make_async_copy(bias_in, bias.at[f], keep.at[1])
    own_bias.start()
    mine.wait()
    for there in others:
        term_copy(f, there, there).wait_recv()
    total[...] = functools.reduce(lambda a, b: a + b, [terms[j] for j in range(8)])
    for there in others:
        mod_copy(f, there).start()
    own_mod = pltpu.make_async_copy(total, mod.at[f], keep.at[2])
    own_mod.start()
    for at in range(count):
        gather.onward(at)
    for at in range(count):
        gather.across(at)
    for at in range(count):
        gather.end(at)
    own_bias.wait()
    own_mod.wait()
    for there in others:
        term_copy(there, f, there).wait_send()
        bias_copy(f, there).wait_send()
        mod_copy(f, there).wait_send()
        bias_copy(there, there).wait_recv()
        mod_copy(there, there).wait_recv()


def start(parts, biases, shards, collective_id):
    sem = lambda: pltpu.SemaphoreType.DMA((8,))
    return pl.pallas_call(
        functools.partial(start_kernel, halves_of(shards)),
        out_shape=(
            jax.ShapeDtypeStruct(parts.shape, parts.dtype),
            jax.ShapeDtypeStruct((8, *biases.shape), biases.dtype),
            *gathered_shapes(shards),
        ),
        in_specs=[HB] * (2 + sum(len(shard) for shard in shards)),
        out_specs=(HB,) * (2 + len(shards)),
        scratch_shapes=[
            pltpu.VMEM(parts.shape, parts.dtype), pltpu.VMEM(parts.shape[1:], parts.dtype),
            sem(), sem(), sem(), sem(), sem(), sem(), pltpu.SemaphoreType.DMA((3,)), *gather_scratch(shards),
        ],
        compiler_params=pltpu.CompilerParams(
            collective_id=collective_id, has_side_effects=True, vmem_limit_bytes=VMEM_LIMIT
        ),
    )(parts, biases, *(part for shard in shards for part in shard))


def to_heads_kernel(reps, size, edge, kv, plan, x_ref, *refs):
    halves, sizes = plan
    count = len(halves)
    shards, refs = split_shards(refs, sizes)
    (own, prev, after), fulls, refs = refs[:3], refs[3 : count + 3], refs[count + 3 :]
    send, recv, edge_send, edge_recv, *sems = refs
    gather = Gather(shards, fulls, halves, *sems) if count else None
    group, me = lax.axis_index("fsdp"), lax.axis_index("replica")
    groups = lax.axis_size("fsdp")
    wide = x_ref.shape[2]
    down, up = group > 0, group < groups - 1
    others = [(group, lax.rem(me + d, reps)) for d in range(1, reps)]
    greet(
        [(place, True) for place in others] + [((group - 1, me), down), ((group + 1, me), up)]
        + ([((there, me), True) for there in (gather.core, gather.x, gather.y)] if count else []),
        reps - 1 + down.astype(jnp.int32) + up.astype(jnp.int32) + (3 if count else 0),
    )
    spans = [pl.ds(0, kv), pl.ds(kv, wide - kv)] if wide > kv else [pl.ds(0, kv)]

    def exchange(span, part, there):
        return pltpu.make_async_remote_copy(
            src_ref=x_ref.at[there, :, span], dst_ref=own.at[me, :, span], send_sem=send.at[part, there],
            recv_sem=recv.at[part, me], device_id=(group, there), device_id_type=MESH,
        )

    for part, span in enumerate(spans):
        for _, there in others:
            exchange(span, part, there).start()
        pltpu.make_async_copy(x_ref.at[me, :, span], own.at[me, :, span], recv.at[part, me]).start()

    if count:
        gather.begin()
    for at in range(count):
        gather.onward(at)

    def edges(piece, action):
        lo, hi = piece * size, (piece + 1) * size
        total = reps * size
        if lo >= total - edge:
            @pl.when(up)
            def _():
                action(0, piece, (group + 1, me), prev.at[pl.ds(lo - (total - edge), size), :])
        if hi <= edge:
            @pl.when(down)
            def _():
                action(1, piece, (group - 1, me), after.at[pl.ds(lo, size), :])

    def start_edge(way, piece, where, target):
        pltpu.make_async_remote_copy(
            src_ref=own.at[piece, :, spans[0]], dst_ref=target, send_sem=edge_send.at[way, piece],
            recv_sem=edge_recv.at[way, piece], device_id=where, device_id_type=MESH,
        ).start()

    def end_send(way, piece, where, target):
        wait_for(own.at[piece, :, spans[0]], edge_send.at[way, piece])

    def end_recv(way, piece, where, target):
        wait_for(target, edge_recv.at[way, piece])

    for piece in range(reps):
        wait_for(own.at[piece, :, spans[0]], recv.at[0, piece])
        edges(piece, start_edge)
    if len(spans) > 1:
        for piece in range(reps):
            wait_for(own.at[piece, :, spans[1]], recv.at[1, piece])
    for at in range(count):
        gather.across(at)
    for part, span in enumerate(spans):
        for _, there in others:
            wait_for(x_ref.at[there, :, span], send.at[part, there])
    for piece in range(reps):
        edges(piece, end_send)
        lo, hi = piece * size, (piece + 1) * size
        total = reps * size
        if lo >= total - edge:
            @pl.when(down)
            def _():
                wait_for(prev.at[pl.ds(lo - (total - edge), size), :], edge_recv.at[0, piece])
        if hi <= edge:
            @pl.when(up)
            def _():
                wait_for(after.at[pl.ds(lo, size), :], edge_recv.at[1, piece])
    for at in range(count):
        gather.end(at)


def to_heads(packed, edge, kv, shards, collective_id):
    reps, size, wide = packed.shape
    sems = pltpu.SemaphoreType.DMA((2, reps))
    own, prev, after, *fulls = pl.pallas_call(
        functools.partial(to_heads_kernel, reps, size, edge, kv, halves_of(shards)),
        out_shape=(
            jax.ShapeDtypeStruct(packed.shape, packed.dtype),
            jax.ShapeDtypeStruct((edge, kv), packed.dtype),
            jax.ShapeDtypeStruct((edge, kv), packed.dtype),
            *gathered_shapes(shards),
        ),
        in_specs=[HB] * (1 + sum(len(shard) for shard in shards)),
        out_specs=(HB,) * (3 + len(shards)),
        scratch_shapes=[sems, sems, sems, sems, *gather_scratch(shards)],
        compiler_params=pltpu.CompilerParams(
            collective_id=collective_id, has_side_effects=True, vmem_limit_bytes=VMEM_LIMIT
        ),
    )(packed, *(part for shard in shards for part in shard))
    return own.reshape(reps * size, wide), prev, after, fulls


def swap_kernel(reps, plan, x_ref, *refs):
    halves, sizes = plan
    count = len(halves)
    shards, refs = split_shards(refs, sizes)
    y_ref, fulls, (send, recv, *sems) = refs[0], refs[1 : count + 1], refs[count + 1 :]
    gather = Gather(shards, fulls, halves, *sems) if count else None
    group, me = lax.axis_index("fsdp"), lax.axis_index("replica")
    others = [(group, lax.rem(me + d, reps)) for d in range(1, reps)]
    planar = [(there, me) for there in (gather.core, gather.x, gather.y)] if count else []
    greet([(place, True) for place in others + planar], reps - 1 + len(planar))
    for _, there in others:
        pltpu.make_async_remote_copy(
            src_ref=x_ref.at[there], dst_ref=y_ref.at[me], send_sem=send.at[there], recv_sem=recv.at[me],
            device_id=(group, there), device_id_type=MESH,
        ).start()
    pltpu.make_async_copy(x_ref.at[me], y_ref.at[me], recv.at[me]).start()
    if count:
        gather.begin()
    for at in range(count):
        gather.onward(at)
    for at in range(count):
        gather.across(at)
    for piece in range(reps):
        wait_for(y_ref.at[piece], recv.at[piece])
    for _, there in others:
        wait_for(x_ref.at[there], send.at[there])
    for at in range(count):
        gather.end(at)


def swap(packed, shards, collective_id):
    reps = packed.shape[0]
    sems = pltpu.SemaphoreType.DMA((reps,))
    swapped, *fulls = pl.pallas_call(
        functools.partial(swap_kernel, reps, halves_of(shards)),
        out_shape=(jax.ShapeDtypeStruct(packed.shape, packed.dtype), *gathered_shapes(shards)),
        in_specs=[HB] * (1 + sum(len(shard) for shard in shards)),
        out_specs=(HB,) * (1 + len(shards)),
        scratch_shapes=[sems, sems, *gather_scratch(shards)],
        compiler_params=pltpu.CompilerParams(
            collective_id=collective_id, has_side_effects=True, vmem_limit_bytes=VMEM_LIMIT
        ),
    )(packed, *(part for shard in shards for part in shard))
    return swapped, fulls


def from_heads_kernel(reps, size, edge, dprev, own, dafter, dq, out_kv, out_q, from_up, from_down, total, mine, sends, recvs, send, recv):
    group, me = lax.axis_index("fsdp"), lax.axis_index("replica")
    groups = lax.axis_size("fsdp")
    rows = reps * size
    down, up = group > 0, group < groups - 1
    others = [(group, lax.rem(me + d, reps)) for d in range(1, reps)]
    greet(
        [(place, True) for place in others] + [((group - 1, me), down), ((group + 1, me), up)],
        reps - 1 + down.astype(jnp.int32) + up.astype(jnp.int32),
    )
    to_down = pltpu.make_async_remote_copy(
        src_ref=dprev, dst_ref=from_up, send_sem=sends.at[0], recv_sem=recvs.at[0],
        device_id=(group - 1, me), device_id_type=MESH,
    )
    to_up = pltpu.make_async_remote_copy(
        src_ref=dafter, dst_ref=from_down, send_sem=sends.at[1], recv_sem=recvs.at[1],
        device_id=(group + 1, me), device_id_type=MESH,
    )
    pl.when(down)(to_down.start)
    pl.when(up)(to_up.start)
    for _, there in others:
        pltpu.make_async_remote_copy(
            src_ref=dq.at[pl.ds(pl.multiple_of(there * size, size), size), :], dst_ref=out_q.at[me], send_sem=send.at[0, there],
            recv_sem=recv.at[0, me], device_id=(group, there), device_id_type=MESH,
        ).start()
    pltpu.make_async_copy(dq.at[pl.ds(pl.multiple_of(me * size, size), size), :], out_q.at[me], recv.at[0, me]).start()
    step = math.gcd(edge, 256)

    def chunk(at, carry):
        here = pl.ds(pl.multiple_of(at * step, step), step)
        total[here, :] = own[here, :].astype(jnp.float32)
        return carry

    lax.fori_loop(0, rows // step, chunk, 0)

    def add(ref, first):
        def body(at, carry):
            here = pl.ds(pl.multiple_of(first + at * step, step), step)
            there = pl.ds(pl.multiple_of(at * step, step), step)
            total[here, :] += ref[there, :].astype(jnp.float32)
            return carry

        lax.fori_loop(0, edge // step, body, 0)

    @pl.when(down)
    def _():
        wait_for(from_down, recvs.at[1])
        add(from_down, 0)

    @pl.when(up)
    def _():
        wait_for(from_up, recvs.at[0])
        add(from_up, rows - edge)

    def narrow(at, carry):
        here = pl.ds(pl.multiple_of(at * step, step), step)
        mine[here, :] = total[here, :].astype(jnp.bfloat16)
        return carry

    lax.fori_loop(0, rows // step, narrow, 0)
    for _, there in others:
        pltpu.make_async_remote_copy(
            src_ref=mine.at[pl.ds(pl.multiple_of(there * size, size), size), :], dst_ref=out_kv.at[me], send_sem=send.at[1, there],
            recv_sem=recv.at[1, me], device_id=(group, there), device_id_type=MESH,
        ).start()
    pltpu.make_async_copy(mine.at[pl.ds(pl.multiple_of(me * size, size), size), :], out_kv.at[me], recv.at[1, me]).start()
    for piece in range(reps):
        wait_for(out_q.at[piece], recv.at[0, piece])
        wait_for(out_kv.at[piece], recv.at[1, piece])
    for _, there in others:
        wait_for(out_q.at[0], send.at[0, there])
        wait_for(out_kv.at[0], send.at[1, there])
    pl.when(down)(to_down.wait_send)
    pl.when(up)(to_up.wait_send)


def from_heads(reps, dprev, own, dafter, dq, collective_id):
    rows, kv = own.shape
    edge, size = dprev.shape[0], own.shape[0] // reps
    pair, both = pltpu.SemaphoreType.DMA((2,)), pltpu.SemaphoreType.DMA((2, reps))
    return pl.pallas_call(
        functools.partial(from_heads_kernel, reps, size, edge),
        out_shape=(
            jax.ShapeDtypeStruct((reps, size, kv), own.dtype),
            jax.ShapeDtypeStruct((reps, size, dq.shape[1]), dq.dtype),
        ),
        in_specs=[HB, VM, HB, HB],
        out_specs=(HB, HB),
        scratch_shapes=[
            pltpu.VMEM((edge, kv), own.dtype),
            pltpu.VMEM((edge, kv), own.dtype),
            pltpu.VMEM((rows, kv), jnp.float32),
            pltpu.VMEM((rows, kv), own.dtype),
            pair,
            pair,
            both,
            both,
        ],
        compiler_params=pltpu.CompilerParams(
            collective_id=collective_id, has_side_effects=True, vmem_limit_bytes=VMEM_LIMIT
        ),
    )(dprev, own, dafter, dq)


UNITS = 12
LEFT_ROWS = 4


def reduce_kernel(layers, width, half, *refs):
    count = layers * UNITS + 1
    ins, extra_in, refs = refs[: 8 * layers], refs[8 * layers], refs[8 * layers + 1 :]
    (out, shared, extra, share_s, share_r, left, right, csend, crecv, own, xs, xr, ys, yr, tx, ty, x2s, x2r, y2s, y2r, zs, z1r, z2s, z2r, fin,
     load_sem, core_s, core_r, x_s, x_r, y_s, y_r, x2_s, x2_r, y2_s, y2_r, z1_s, z1_r, z2_s, z2_r, fin_l, fin_s, fin_r,
     credit) = refs
    f, r = lax.axis_index("fsdp"), lax.axis_index("replica")
    rows = own.shape[1]
    tokens = left.shape[1]
    c, x, y = lax.rem(f, 2), lax.rem(f // 2, 2), f // 4
    core_at, x_at, y_at = f + 1 - 2 * c, f + 2 - 4 * x, f + 4 - 8 * y
    inner = jnp.logical_and(r > 0, r < 3)
    outer = jnp.logical_not(inner)
    z_at = r + 1 - 2 * lax.rem(r, 2)
    others = [lax.rem(f + d, 8) for d in range(1, 8)]
    greet(
        [((there, r), True) for there in others] + [((f, r - 1), r > 0), ((f, r + 1), r < 3)],
        7 + (r > 0).astype(jnp.int32) + (r < 3).astype(jnp.int32),
    )
    few = extra.shape[1]
    loads = [(extra_in, extra)]
    for layer in range(layers):
        place = layer * (LEFT_ROWS + 3) * width
        for at in range(4):
            src = ins[8 * layer + at]
            loads.append((src, left.at[pl.ds(place, src.shape[0]), :]))
            place += src.shape[0]
        slot = layer * 9
        for at in range(4):
            src = ins[8 * layer + 4 + at]
            for part in range(src.shape[1] // width):
                loads.append((src.at[:, pl.ds(part * width, width)], right.at[slot]))
                slot += 1
    for at, (src, dst) in enumerate(loads):
        pltpu.make_async_copy(src, dst, load_sem.at[at]).start()
    for at, (src, dst) in enumerate(loads):
        pltpu.make_async_copy(src, dst, load_sem.at[at]).wait()

    def send(src, dst, s_sem, r_sem, where):
        return pltpu.make_async_remote_copy(
            src_ref=src, dst_ref=dst, send_sem=s_sem, recv_sem=r_sem, device_id=where, device_id_type=MESH
        )

    def place_of(core, mx, my):
        return ((y + my * (1 - 2 * y)) * 2 + (x + mx * (1 - 2 * x))) * 2 + (c + core * (1 - 2 * c))

    def term(u, core, mx, my):
        layer, w = (u - 1) // UNITS, lax.rem(u - 1, UNITS)
        block = place_of(core, mx, my)
        inside = jnp.where(
            w < 4, rows * w, LEFT_ROWS * width + jnp.where(w < 8, 0, jnp.where(w < 9, width, 2 * width))
        )
        stride = jnp.where(w < 4, 4 * rows, rows)
        start = pl.multiple_of(layer * ((LEFT_ROWS + 3) * width) + inside + stride * block, 16)
        other = layer * 9 + jnp.maximum(w - 3, 0)
        return nn_dot(left[pl.ds(start, rows), :], right[other])

    places = ((0, 0), (1, 0), (0, 1), (1, 1))
    top, low = pl.ds(0, half), pl.ds(half, rows - half)

    def core_copy(slot):
        return send(csend.at[slot], crecv.at[slot], core_s.at[slot], core_r.at[slot], (core_at, r))

    def x_copy(slot):
        return send(xs.at[slot], xr.at[slot], x_s.at[slot], x_r.at[slot], (x_at, r))

    def y_copy(slot):
        return send(ys.at[slot], yr.at[slot], y_s.at[slot], y_r.at[slot], (y_at, r))

    def x2_copy(slot):
        return send(x2s.at[slot], x2r.at[slot], x2_s.at[slot], x2_r.at[slot], (x_at, r))

    def y2_copy(slot):
        return send(y2s.at[slot], y2r.at[slot], y2_s.at[slot], y2_r.at[slot], (y_at, r))

    def z1_copy(slot, to):
        return send(zs.at[slot], z1r.at[to], z1_s.at[slot], z1_r.at[to], (f, z_at))

    def z2_copy(slot):
        return send(z2s.at[slot], z2r.at[slot], z2_s.at[slot], z2_r.at[slot], (f, 3 - r))

    def fin_copy(slot, u):
        return send(fin.at[slot], out.at[u], fin_s.at[slot], fin_r.at[u], (f, z_at))

    def keep_copy(slot, u):
        return pltpu.make_async_copy(fin.at[slot], out.at[u], fin_l.at[slot])

    f32, bf16 = jnp.float32, jnp.bfloat16
    z_slots = z1r.shape[0]

    def stage(u, condition, body):
        live = jnp.logical_and(u >= 0, u < count)
        pl.when(live if condition is None else jnp.logical_and(live, condition))(lambda: body(u))

    def close(u):
        slot = lax.rem(u, 4)
        fin_copy(slot, u).wait_send()
        keep_copy(slot, u).wait()

    def arrive(u):
        fin_copy(lax.rem(u, 4), u).wait_recv()

    def finish(u):
        slot = lax.rem(u, 4)
        z2_copy(slot).wait()
        fin[slot] = (z2s[slot].astype(f32) + z2r[slot].astype(f32)).astype(bf16)
        fin_copy(slot, u).start()
        keep_copy(slot, u).start()

    def middle(u):
        slot, z_slot, at = lax.rem(u, 4), lax.rem(u, z_slots), lax.rem(u, own.shape[0])
        z1_copy(slot, z_slot).wait_recv()
        z2s[slot] = (own[at] + z1r[z_slot].astype(f32)).astype(bf16)
        z2_copy(slot).start()

        @pl.when(u + z_slots < count)
        def _():
            pl.semaphore_signal(credit, inc=1, device_id=(f, z_at), device_id_type=MESH)

    def sent(u):
        z1_copy(lax.rem(u, 4), lax.rem(u, z_slots)).wait_send()

    def plane(u):
        slot, at = lax.rem(u, 4), lax.rem(u, own.shape[0])
        x2_copy(slot).wait()
        y2_copy(slot).wait()
        own[at, top, :] += y2r[slot].astype(f32)
        own[at, low, :] += x2r[slot].astype(f32)

        @pl.when(outer)
        def _():
            zs[slot] = own[at].astype(bf16)

            @pl.when(u >= z_slots)
            def _():
                pl.semaphore_wait(credit, 1)

            z1_copy(slot, lax.rem(u, z_slots)).start()

    def cross(u):
        slot, at = lax.rem(u, 4), lax.rem(u, own.shape[0])
        x_copy(slot).wait()
        y_copy(slot).wait()
        y2s[slot] = (ty[slot] + xr[slot, 1].astype(f32)).astype(bf16)
        y2_copy(slot).start()
        x2s[slot] = (tx[slot] + yr[slot, 1].astype(f32)).astype(bf16)
        x2_copy(slot).start()
        own[at, top, :] += xr[slot, 0].astype(f32)
        own[at, low, :] += yr[slot, 0].astype(f32)

    def chip_extra(u):
        core_copy(0).wait()
        for m, (mx, my) in enumerate(places):
            total = extra[place_of(0, mx, my)] + crecv[0, m, :few, :].astype(f32)
            if m == 0:
                own[0, :few, :] = total
            elif m == 2:
                ty[0, :few, :] = total
            else:
                xs[0, m // 2, :few, :] = total.astype(bf16)
        x_copy(0).start()
        y_copy(0).start()

    def chip(u):
        slot, pair, at = lax.rem(u, 4), lax.rem(u, 2), lax.rem(u, own.shape[0])
        core_copy(pair).wait()
        total = term(u, 0, 1, 1) + crecv[pair, 3].astype(f32)
        xs[slot, 1] = total[:half].astype(bf16)
        ys[slot, 1] = total[half:].astype(bf16)
        total = term(u, 0, 1, 0) + crecv[pair, 1].astype(f32)
        xs[slot, 0] = total[:half].astype(bf16)
        tx[slot] = total[half:]
        x_copy(slot).start()
        total = term(u, 0, 0, 1) + crecv[pair, 2].astype(f32)
        ys[slot, 0] = total[half:].astype(bf16)
        ty[slot] = total[:half]
        y_copy(slot).start()
        own[at] = term(u, 0, 0, 0) + crecv[pair, 0].astype(f32)

    def open_extra(u):
        for m, (mx, my) in enumerate(places):
            csend[0, m, :few, :] = extra[place_of(1, mx, my)].astype(bf16)
        core_copy(0).start()

    def share_copy(there, where):
        return send(out.at[0, pl.ds(0, few), :], shared.at[there], share_s.at[where], share_r.at[there], (where, r))

    def share(u):
        for there in others:
            share_copy(f, there).start()

    def open_unit(u):
        pair = lax.rem(u, 2)
        for m, (mx, my) in enumerate(places):
            csend[pair, m] = term(u, 1, mx, my).astype(bf16)
        core_copy(pair).start()

    def step(t, carry):
        pl.when(t == 12)(lambda: share(t))
        stage(t - 11, inner, close)
        stage(t - 11, outer, arrive)
        stage(t - 9, inner, finish)
        stage(t - 7, inner, middle)
        stage(t - 7, outer, sent)
        stage(t - 5, None, plane)
        stage(t - 3, None, cross)
        stage(t - 1, t > 1, chip)
        pl.when(t == 1)(lambda: chip_extra(t - 1))
        stage(t, t > 0, open_unit)
        pl.when(t == 0)(lambda: open_extra(t))
        return carry

    lax.fori_loop(0, count + 11, step, 0)
    for there in others:
        share_copy(f, there).wait_send()
        share_copy(there, there).wait_recv()


def reduce_grads(pairs, extra):
    layers = len(pairs)
    width, tokens = pairs[0][0][1].shape
    rows = width // 8
    half = pad_to(rows // 2, 16)
    ins = [part for lefts, rights in pairs for part in (*lefts, *rights)] + [extra]
    count = layers * UNITS + 1
    bf16, f32 = jnp.bfloat16, jnp.float32
    buf = lambda dtype, *shape: pltpu.VMEM((*shape, width), dtype)
    sem = lambda size: pltpu.SemaphoreType.DMA((size,))
    z_slots = 8
    return pl.pallas_call(
        functools.partial(reduce_kernel, layers, width, half),
        out_shape=(
            jax.ShapeDtypeStruct((count, rows, width), bf16),
            jax.ShapeDtypeStruct(extra.shape, bf16),
        ),
        in_specs=[HB] * len(ins),
        out_specs=(HB, HB),
        scratch_shapes=[
            buf(f32, *extra.shape[:2]), sem(8), sem(8),
            pltpu.VMEM((layers * (LEFT_ROWS + 3) * width, tokens), bf16),
            buf(bf16, layers * 9, tokens),
            buf(bf16, 2, 4, rows), buf(bf16, 2, 4, rows), buf(f32, 9, rows),
            buf(bf16, 4, 2, half), buf(bf16, 4, 2, half), buf(bf16, 4, 2, rows - half), buf(bf16, 4, 2, rows - half),
            buf(f32, 4, rows - half), buf(f32, 4, half),
            buf(bf16, 4, rows - half), buf(bf16, 4, rows - half), buf(bf16, 4, half), buf(bf16, 4, half),
            buf(bf16, 4, rows), buf(bf16, z_slots, rows), buf(bf16, 4, rows), buf(bf16, 4, rows), buf(bf16, 4, rows),
            sem(13 * layers + 1), sem(2), sem(2), sem(4), sem(4), sem(4), sem(4), sem(4), sem(4), sem(4), sem(4),
            sem(4), sem(z_slots), sem(4), sem(4), sem(4), sem(4), sem(count), pltpu.SemaphoreType.REGULAR,
        ],
        compiler_params=pltpu.CompilerParams(
            collective_id=5, has_side_effects=True, vmem_limit_bytes=60 * 1024 * 1024
        ),
        cost_estimate=pl.CostEstimate(
            flops=2 * count * 8 * rows * tokens * width, bytes_accessed=100 << 20, transcendentals=0
        ),
    )(*ins)


def pre_norm(stream, shift, scale):
    centred = stream - jnp.mean(stream, axis=-1, keepdims=True)
    spread = jnp.mean(centred * centred, axis=-1, keepdims=True)
    return centred * lax.rsqrt(spread + NORM_EPS) * (1.0 + scale) + shift


def gelu_tanh(values):
    return jax.nn.gelu(values, approximate=True)


def latent_ids(latent_len, positions, token_total):
    starts = jnp.cumsum(latent_len) - latent_len
    found = jnp.sum((starts[None, :] <= positions[:, None]).astype(jnp.int32), axis=1) - 1
    inside = (positions >= 0) & (positions < token_total)
    return jnp.where(inside, found, -1)


def low_dot(left, right):
    return jnp.dot(left, right, preferred_element_type=jnp.float32)


def group_heads(matrix, reps):
    return matrix.reshape(matrix.shape[0], reps, -1).transpose(1, 0, 2)


def ungroup_heads(stacked):
    return stacked.transpose(1, 0, 2).reshape(stacked.shape[1], -1)


def widen(stacked, width):
    return jnp.pad(stacked, ((0, 0), (0, 0), (0, width - stacked.shape[2])))


def layer_forward(stream, mod_tok, full, plan, in_first, shards_second, shards_ahead, collective_id):
    qkv_w, qkv_b, out_w, out_b, up_w, up_b, down_w, down_b = full
    reps, edge, bounds, ids = plan
    width = stream.shape[1]
    hd = width // reps
    nh = HEADS // reps
    shift_one, scale_one, gate_one, shift_two, scale_two, gate_two = jnp.split(mod_tok, 6, axis=1)
    normed = pre_norm(stream, shift_one, scale_one).astype(jnp.bfloat16)
    qkv_bias = qkv_b.astype(jnp.float32)
    bias_full = jnp.concatenate(
        [qkv_bias[:width], jnp.zeros((width,), jnp.float32), qkv_bias[width:]]
    )
    projected = (low_dot(normed, qkv_w) + bias_full).astype(jnp.bfloat16)
    query, key, value = (group_heads(part, reps) for part in jnp.split(projected, 3, axis=1))
    packed = widen(jnp.concatenate([key, value, query], axis=2), pad_to(3 * hd, LANES))
    own, prev, after, fulls = to_heads(packed, edge, pad_to(2 * hd, LANES), in_first, collective_id)
    first_gathered = fulls
    in_second = sent_ahead(shards_second, own) if shards_second else ()
    mixed, mixed_t, log_norm = attend(nh, hd, *bounds, prev, own, after, *ids)
    mixed, fulls = swap(mixed.reshape(reps, -1, mixed.shape[1]), in_second, collective_id + 1)
    up_w, down_w = first_gathered or (up_w, down_w)
    in_next = sent_ahead(shards_ahead, mixed) if shards_ahead else ()
    mixed = ungroup_heads(mixed[:, :, :hd])
    branch = low_dot(mixed, out_w) + out_b.astype(jnp.float32)
    middle = stream + gate_one * branch
    normed_two = pre_norm(middle, shift_two, scale_two).astype(jnp.bfloat16)
    hidden = low_dot(normed_two, up_w) + up_b.astype(jnp.float32)
    active = gelu_tanh(hidden).astype(jnp.bfloat16)
    result = low_dot(active, down_w) + down_b.astype(jnp.float32)
    saved = (
        normed, (prev, own, after), mixed, (mixed_t, log_norm), branch, middle, normed_two, hidden, active, result,
    )
    full = (qkv_w, qkv_b, out_w, out_b, up_w, up_b, down_w, down_b)
    return (middle + gate_two * result, saved, full, fulls, in_next)


def layer_backward(stream, mod_tok, full, saved, plan, pick, grad_next):
    qkv_w, qkv_b, out_w, out_b, up_w, up_b, down_w, down_b = full
    normed, window, mixed, kept, branch, middle, normed_two, hidden, active, result = saved
    reps, edge, bounds, ids = plan
    width = stream.shape[1]
    hd = width // reps
    nh = HEADS // reps
    shift_one, scale_one, gate_one, shift_two, scale_two, gate_two = jnp.split(mod_tok, 6, axis=1)
    grad_result = (gate_two * grad_next).astype(jnp.bfloat16)
    grad_gate_two = grad_next * result
    grad_down_b = jnp.sum(grad_result.astype(jnp.float32), axis=0)
    grad_active = jnp.einsum("td,fd->tf", grad_result, down_w, preferred_element_type=jnp.float32)
    _, gelu_back = jax.vjp(gelu_tanh, hidden)
    grad_hidden = gelu_back(grad_active)[0].astype(jnp.bfloat16)
    grad_up_b = jnp.sum(grad_hidden.astype(jnp.float32), axis=0)
    grad_normed_two = jnp.einsum("tf,df->td", grad_hidden, up_w, preferred_element_type=jnp.float32)
    _, norm_back_two = jax.vjp(pre_norm, middle, shift_two, scale_two)
    grad_middle_part, grad_shift_two, grad_scale_two = norm_back_two(grad_normed_two)
    grad_middle = grad_next + grad_middle_part
    grad_branch = (gate_one * grad_middle).astype(jnp.bfloat16)
    grad_gate_one = grad_middle * branch
    grad_out_b = jnp.sum(grad_branch.astype(jnp.float32), axis=0)
    grad_mixed = jnp.einsum(
        "te,de->td", grad_branch, out_w, preferred_element_type=jnp.float32
    ).astype(jnp.bfloat16)
    grad_heads, _ = swap(widen(group_heads(grad_mixed, reps), pad_to(hd, LANES)), (), 3)
    prev, own, after = window
    grad_q, grad_prev, grad_own, grad_after = attend_back(
        nh, hd, *bounds, prev, own, after, *ids, grad_heads.reshape(own.shape[0], -1), *kept
    )
    grad_kv, grad_q = from_heads(reps, grad_prev, grad_own, grad_after, grad_q, 4)
    grad_projected = jnp.concatenate(
        [ungroup_heads(grad_q[:, :, :hd]), ungroup_heads(grad_kv[:, :, :hd]), ungroup_heads(grad_kv[:, :, hd : 2 * hd])],
        axis=1,
    )
    sums = jnp.sum(grad_projected.astype(jnp.float32), axis=0)
    grad_qkv_b = jnp.concatenate([sums[:width], sums[2 * width :]])
    grad_normed = jnp.einsum("te,de->td", grad_projected, qkv_w, preferred_element_type=jnp.float32)
    _, norm_back_one = jax.vjp(pre_norm, stream, shift_one, scale_one)
    grad_stream_part, grad_shift_one, grad_scale_one = norm_back_one(grad_normed)
    grad_stream = grad_middle + grad_stream_part
    grad_mod = jnp.concatenate(
        [
            jnp.einsum("tl,tm->lm", pick, part, precision=HIGH, preferred_element_type=jnp.float32)
            for part in (
                grad_shift_one, grad_scale_one, grad_gate_one, grad_shift_two, grad_scale_two, grad_gate_two,
            )
        ],
        axis=1,
    )
    return (
        grad_stream, grad_mod,
        ((active.T, normed_two.T, mixed.T, normed.T), (grad_result, grad_hidden, grad_branch, grad_projected)),
        (grad_qkv_b, grad_out_b, grad_up_b, grad_down_b),
    )


def bias_parts(stacked, params):
    cuts = [0]
    for at in (3, 5, 7, 9):
        cuts.append(cuts[-1] + params[at].shape[0])
    return [stacked[:, a:b].reshape(-1) for a, b in zip(cuts[:-1], cuts[1:])]


def modulation(partial_terms, layers):
    shares = jnp.stack([jnp.concatenate([params[at] for at in (3, 5, 7, 9)]) for params in layers])
    if not on_planes():
        mods = lax.psum(tuple(partial_terms), "fsdp")
        stacked = lax.all_gather(shares, "fsdp", axis=0)
        fulls = [lax.all_gather(layers[0][at], "fsdp", axis=0, tiled=True) for at in (2, 4)]
    else:
        width = layers[0][4].shape[1]
        parts = jnp.stack(partial_terms).reshape(8, -1, width)
        mod, stacked, *fulls = start(
            parts, jnp.pad(shares, ((0, 16 - shares.shape[0]), (0, 0))), [(layers[0][at],) for at in (2, 4)], 6
        )
        mods = mod.reshape(len(layers), -1, partial_terms[0].shape[1])
    return mods, [bias_parts(stacked[:, at], params) for at, params in enumerate(layers)], fulls


def on_planes():
    return lax.axis_size("fsdp") == 8 and lax.axis_size("replica") == 4


def owner_sums(pairs, grad_mods, grad_biases):
    groups = lax.axis_size("fsdp")
    width = pairs[0][0][1].shape[0]
    if on_planes():
        mods = jnp.stack(grad_mods).reshape(groups, -1, width)
        biases = jnp.stack(
            [jnp.concatenate([part.reshape(groups, -1) for part in parts], axis=1) for parts in grad_biases], axis=1
        )
        extra = jnp.concatenate([mods, biases], axis=1)
        used = extra.shape[1]
        extra = jnp.pad(extra, ((0, 0), (0, pad_to(used, 16) - used), (0, 0)))
        out, shared = reduce_grads(pairs, extra)
        shared = lax.dynamic_update_slice_in_dim(
            shared, out[None, 0, : extra.shape[1]], lax.axis_index("fsdp"), 0
        )
        mods = shared[:, : mods.shape[1]].reshape(len(pairs), -1, grad_mods[0].shape[1])
        units = out[1:].reshape(len(pairs), UNITS, -1, width)
        rows = units.shape[2]
        across = lambda part: part.transpose(1, 0, 2).reshape(rows, -1).astype(jnp.float32)
        results = []
        for layer_at, unit in enumerate(units):
            share = out[0, used - len(pairs) + layer_at].astype(jnp.float32)
            cuts = [0]
            for part in grad_biases[layer_at]:
                cuts.append(cuts[-1] + part.shape[0] // groups)
            weights = (
                across(unit[9:12]), across(unit[8:9]), across(unit[4:8]),
                unit[0:4].reshape(-1, width).astype(jnp.float32),
            )
            results.append((weights, [share[i:j] for i, j in zip(cuts[:-1], cuts[1:])]))
        return results, mods
    flat = jnp.concatenate([part for parts in grad_biases for part in parts])
    *mods, flat = lax.psum((*grad_mods, flat), ("fsdp", "replica"))
    results, place = [], 0
    for (lefts, rights), parts in zip(pairs, grad_biases):
        grads, biases = [], []
        for left, right in zip(lefts, rights):
            grad = low_dot(left, right).astype(jnp.bfloat16)
            part = lax.psum_scatter(grad, "fsdp", scatter_dimension=0, tiled=True)
            grads.append(lax.psum(part, "replica").astype(jnp.float32))
        for part in parts:
            share = part.shape[0] // groups
            biases.append(lax.dynamic_slice_in_dim(flat, place + lax.axis_index("fsdp") * share, share, 0))
            place += part.shape[0]
        results.append((grads[::-1], biases))
    return results, mods


def attention_plan(latent_len, tok_rows, reps, device_at):
    column = tok_rows * reps
    edge = MAXLEN
    total = jnp.sum(latent_len)
    first = lax.axis_index("fsdp") * column
    positions = first - edge + jnp.arange(column + 2 * edge, dtype=jnp.int32)
    ends = jnp.cumsum(latent_len)
    ids = jnp.sum((ends[None, :] <= positions[:, None]).astype(jnp.int32), axis=1)
    ids = jnp.where(positions < 0, -1, ids)
    own = ids[edge : edge + column]
    count = column // BQ
    firsts, lasts = own[::BQ], own[BQ - 1 :: BQ]
    pick = lambda at: (at[:, None] == jnp.arange(latent_len.shape[0], dtype=jnp.int32)[None, :]).astype(jnp.int32)
    low = jnp.sum(pick(firsts) * (ends - latent_len)[None, :], axis=1) - (first - edge)
    high = jnp.sum(pick(lasts) * ends[None, :], axis=1) - (first - edge)
    bounds = ((low // BK).astype(jnp.int32), ((high + BK - 1) // BK).astype(jnp.int32))
    kid = jnp.broadcast_to(ids[:, None], (ids.shape[0], LANES))
    qid = jnp.broadcast_to(own[None, :], (8, column))
    return (reps, edge, bounds, (kid, qid))


def shards(
    tokens,
    cond,
    latent_len,
    first_ada_weight,
    first_ada_bias,
    first_qkv_weight,
    first_qkv_bias,
    first_out_weight,
    first_out_bias,
    first_up_weight,
    first_up_bias,
    first_down_weight,
    first_down_bias,
    second_ada_weight,
    second_ada_bias,
    second_qkv_weight,
    second_qkv_bias,
    second_out_weight,
    second_out_bias,
    second_up_weight,
    second_up_bias,
    second_down_weight,
    second_down_bias,
    cotangent,
):
    tok_rows = tokens.shape[0]
    group_place = lax.axis_index("fsdp")
    device_at = lax.axis_index(("fsdp", "replica"))
    token_total = tok_rows * lax.axis_size(("fsdp", "replica"))
    latent_count = cond.shape[0]
    local_pos = jnp.arange(tok_rows, dtype=jnp.int32)
    own_ids = latent_ids(latent_len, device_at * tok_rows + local_pos, token_total)
    pick = (own_ids[:, None] == jnp.arange(latent_count, dtype=jnp.int32)[None, :]).astype(
        jnp.float32
    )
    plan = attention_plan(latent_len, tok_rows, lax.axis_size("replica"), device_at)
    layers = (
        (
            first_ada_weight,
            first_ada_bias,
            first_qkv_weight,
            first_qkv_bias,
            first_out_weight,
            first_out_bias,
            first_up_weight,
            first_up_bias,
            first_down_weight,
            first_down_bias,
        ),
        (
            second_ada_weight,
            second_ada_bias,
            second_qkv_weight,
            second_qkv_bias,
            second_out_weight,
            second_out_bias,
            second_up_weight,
            second_up_bias,
            second_down_weight,
            second_down_bias,
        ),
    )
    col_width = first_ada_weight.shape[0]
    own_cond = lax.dynamic_slice_in_dim(
        cond.astype(jnp.float32), group_place * col_width, col_width, 1
    )
    own_silu = jax.nn.silu(own_cond).astype(jnp.bfloat16)
    partial_terms = []
    for params in layers:
        term = low_dot(own_silu, params[0])
        bias_share = params[1].astype(jnp.float32)
        spread = lax.dynamic_update_slice_in_dim(
            jnp.zeros((term.shape[1],), jnp.float32),
            bias_share,
            group_place * bias_share.shape[0],
            0,
        )
        partial_terms.append(term + spread[None, :])
    (mod_first, mod_second), biases, attention_weights = modulation(partial_terms, layers)
    mod_tokens = (
        jnp.dot(pick, mod_first, precision=HIGH, preferred_element_type=jnp.float32),
        jnp.dot(pick, mod_second, precision=HIGH, preferred_element_type=jnp.float32),
    )
    stream = tokens.astype(jnp.float32)
    inputs = []
    kept = []
    whole = lambda value: lax.all_gather(value, "fsdp", axis=0, tiled=True)
    fulls = []
    in_first = sent_ahead((first_up_weight, first_down_weight), mod_first) if on_planes() else ()
    for layer_at, params in enumerate(layers):
        inputs.append(stream)
        ahead = layers[layer_at + 1] if layer_at + 1 < len(layers) else None
        qkv_w, out_w = attention_weights
        qkv_b, out_b, up_b, down_b = biases[layer_at]
        shards_second, shards_ahead, up_w, down_w = (), (), None, None
        if on_planes():
            shards_second = () if ahead is None else (ahead[2], ahead[4])
            shards_ahead = () if ahead is None else (ahead[6], ahead[8])
        else:
            up_w, down_w = whole(params[6]), whole(params[8])
        full = (qkv_w, qkv_b, out_w, out_b, up_w, up_b, down_w, down_b)
        stream, saved, full, attention_weights, in_first = layer_forward(
            stream, mod_tokens[layer_at], full, plan, in_first, shards_second, shards_ahead, 7 + 2 * layer_at
        )
        fulls.append(full)
        if ahead is not None and not on_planes():
            attention_weights = [whole(ahead[at]) for at in (2, 4)]
        kept.append(saved)
    output = stream.astype(jnp.bfloat16)
    grad_stream = cotangent.astype(jnp.float32)
    weight_pairs = [None, None]
    mod_grads = [None, None]
    bias_grads = [None, None]
    for layer_at in (1, 0):
        grad_stream, grad_mod, local_grads, local_biases = layer_backward(
            inputs[layer_at], mod_tokens[layer_at], fulls[layer_at], kept[layer_at], plan, pick, grad_stream
        )
        weight_pairs[layer_at] = local_grads
        mod_grads[layer_at] = grad_mod
        bias_grads[layer_at] = local_biases
    sums, (grad_mod_first, grad_mod_second) = owner_sums(weight_pairs, mod_grads, bias_grads)
    grad_silu = jnp.zeros(own_cond.shape, jnp.float32)
    ada_grads = []
    for params, grad_mod in zip(layers, (grad_mod_first, grad_mod_second)):
        low_mod = grad_mod.astype(jnp.bfloat16)
        weight_grad = jnp.einsum("ld,lm->dm", own_silu, low_mod, preferred_element_type=jnp.float32)
        column_sums = jnp.sum(low_mod.astype(jnp.float32), axis=0)
        bias_rows = params[1].shape[0]
        bias_grad = lax.dynamic_slice_in_dim(column_sums, group_place * bias_rows, bias_rows, 0)
        grad_silu = grad_silu + jnp.einsum(
            "lm,dm->ld", low_mod, params[0], preferred_element_type=jnp.float32
        )
        ada_grads.append((weight_grad, bias_grad))
    _, silu_back = jax.vjp(jax.nn.silu, own_cond)
    cond_grad = silu_back(grad_silu)[0]
    outs = [output, grad_stream, cond_grad]
    for layer_at in range(2):
        outs += list(ada_grads[layer_at])
        for weight, bias in zip(*sums[layer_at]):
            outs += [weight, bias]
    return tuple(outs)


def solution(mesh):
    in_specs = (
        P(("fsdp", "replica"), None),
        P(),
        P(),
        P("fsdp", None),
        P("fsdp"),
        P("fsdp", None),
        P("fsdp"),
        P("fsdp", None),
        P("fsdp"),
        P("fsdp", None),
        P("fsdp"),
        P("fsdp", None),
        P("fsdp"),
        P("fsdp", None),
        P("fsdp"),
        P("fsdp", None),
        P("fsdp"),
        P("fsdp", None),
        P("fsdp"),
        P("fsdp", None),
        P("fsdp"),
        P("fsdp", None),
        P("fsdp"),
        P(("fsdp", "replica"), None),
    )
    out_specs = (
        P(("fsdp", "replica"), None),
        P(("fsdp", "replica"), None),
        P(None, "fsdp"),
        P("fsdp", None),
        P("fsdp"),
        P("fsdp", None),
        P("fsdp"),
        P("fsdp", None),
        P("fsdp"),
        P("fsdp", None),
        P("fsdp"),
        P("fsdp", None),
        P("fsdp"),
        P("fsdp", None),
        P("fsdp"),
        P("fsdp", None),
        P("fsdp"),
        P("fsdp", None),
        P("fsdp"),
        P("fsdp", None),
        P("fsdp"),
        P("fsdp", None),
        P("fsdp"),
    )
    return jax.shard_map(shards, mesh=mesh, in_specs=in_specs, out_specs=out_specs, check_vma=False)
```

```python
import functools
import math

import jax
import jax.numpy as jnp
from jax import lax
from jax.experimental import pallas as pl
from jax.experimental.pallas import tpu as pltpu
from jax.sharding import PartitionSpec as P

HEADS = 16
HEAD_DIM = 72
MAXLEN = 1024
NORM_EPS = 1e-06
HIGH = lax.Precision.HIGHEST
BQ = 256
BK = 256
LANES = 128
NEG = -1e30
VM = pl.BlockSpec(memory_space=pltpu.VMEM)
SM = pl.BlockSpec(memory_space=pltpu.SMEM)
HB = pl.BlockSpec(memory_space=pl.ANY)
VMEM_LIMIT = 56 * 1024 * 1024


def pad_to(size, unit):
    return -(-size // unit) * unit


def take_head(ref, rows, at, dim):
    first, off = at // LANES * LANES, at % LANES
    wide = LANES if off + dim <= LANES else 2 * LANES
    block = ref[rows, first : first + wide].astype(jnp.float32)
    if off:
        block = pltpu.roll(block, wide - off, 1)
    block = block[:, :LANES]
    lane = lax.broadcasted_iota(jnp.int32, block.shape, 1)
    return jnp.where(lane < dim, block, 0.0)


def put_heads(blocks, places, width):
    tiles = [None] * (width // LANES)
    for block, at in zip(blocks, places):
        first, off = at // LANES, at % LANES
        wide = jnp.concatenate([block, jnp.zeros_like(block)], axis=1)
        if off:
            wide = pltpu.roll(wide, off, 1)
        for step in range(2):
            part = wide[:, step * LANES : (step + 1) * LANES]
            if first + step < len(tiles):
                old = tiles[first + step]
                tiles[first + step] = part if old is None else old + part
    rows = blocks[0].shape[0]
    return jnp.concatenate(
        [jnp.zeros((rows, LANES), jnp.float32) if t is None else t for t in tiles], axis=1
    )


def nt_dot(left, right):
    return lax.dot_general(left, right, (((1,), (1,)), ((), ())), preferred_element_type=jnp.float32)


def nn_dot(left, right):
    return jnp.dot(left, right, preferred_element_type=jnp.float32)


def rows_at(block, size):
    return pl.ds(pl.multiple_of(block * size, size), size)


def over_window(lo, hi, prev, own, after, action):
    edge, mid = prev.shape[0] // BK, own.shape[0] // BK

    def run(ref, first, count):
        def body(at, carry):
            action(ref, at - first, at)
            return carry

        lax.fori_loop(jnp.clip(lo, first, first + count), jnp.clip(hi, first, first + count), body, 0)

    run(prev, 0, edge)
    run(own, edge, mid)
    run(after, edge + mid, edge)


def attend_kernel(nh, hd, lo, hi, prev, own, after, kid, qid, o_ref, ot_ref, lse_ref, kh, vt, qh, acc, ml):
    dim = hd // nh
    width = o_ref.shape[1]
    count = own.shape[0] // BQ
    scale = math.log2(math.e) / math.sqrt(dim)

    def load(ref, at, to):
        for h in range(nh):
            kh[h, rows_at(to, BK), :] = take_head(ref, rows_at(at, BK), h * dim, dim).astype(jnp.bfloat16)
            vt[h, :, rows_at(to, BK)] = take_head(ref, rows_at(at, BK), hd + h * dim, dim).T.astype(jnp.bfloat16)

    over_window(lo[0], hi[count - 1], prev, own, after, load)
    lse_ref[...] = jnp.zeros_like(lse_ref)

    def query_block(qb, carry):
        rows = rows_at(qb, BQ)
        for h in range(nh):
            qh[h] = take_head(own, rows, 2 * hd + h * dim, dim).astype(jnp.bfloat16)
        acc[...] = jnp.zeros_like(acc)
        ml[0] = jnp.full(ml.shape[1:], NEG, jnp.float32)
        ml[1] = jnp.zeros(ml.shape[1:], jnp.float32)
        ids = qid[0:1, rows]

        def key_block(kb, inner):
            keys = rows_at(kb, BK)
            lanes = kid[keys, :]
            same = jnp.concatenate([lanes] * (BQ // LANES), axis=1) == ids
            scores = [jnp.where(same, nt_dot(kh[h, keys, :], qh[h]) * scale, NEG) for h in range(nh)]
            olds = [ml[0, h : h + 1, :] for h in range(nh)]
            tops = [jnp.maximum(old, jnp.max(s, axis=0, keepdims=True)) for old, s in zip(olds, scores)]
            probs = [jnp.exp2(s - top) for s, top in zip(scores, tops)]
            outs = [nn_dot(vt[h, :, keys], probs[h].astype(jnp.bfloat16)) for h in range(nh)]
            for h in range(nh):
                alpha = jnp.exp2(olds[h] - tops[h])
                ml[0, h : h + 1, :] = tops[h]
                ml[1, h : h + 1, :] = ml[1, h : h + 1, :] * alpha + jnp.sum(probs[h], axis=0, keepdims=True)
                acc[h] = acc[h] * alpha + outs[h]
            return inner

        lax.fori_loop(lo[qb], hi[qb], key_block, 0)
        parts = []
        for h in range(nh):
            total = ml[1, h : h + 1, :]
            out = acc[h, :dim, :] / total
            parts.append(out)
            lse_ref[h : h + 1, rows] = ml[0, h : h + 1, :] + jnp.log2(total)
        parts.append(jnp.zeros((width - hd, BQ), jnp.float32))
        heads = jnp.concatenate(parts, axis=0)
        ot_ref[:, rows] = heads
        o_ref[rows, :] = heads.T.astype(jnp.bfloat16)
        return carry

    lax.fori_loop(0, count, query_block, 0)


def attend(nh, hd, lo, hi, prev, own, after, kid, qid):
    rows, window = own.shape[0], own.shape[0] + 2 * prev.shape[0]
    width = pad_to(hd, LANES)
    return pl.pallas_call(
        functools.partial(attend_kernel, nh, hd),
        out_shape=(
            jax.ShapeDtypeStruct((rows, width), jnp.bfloat16),
            jax.ShapeDtypeStruct((width, rows), jnp.float32),
            jax.ShapeDtypeStruct((8, rows), jnp.float32),
        ),
        in_specs=[SM, SM, VM, VM, VM, VM, VM],
        out_specs=(VM, VM, VM),
        scratch_shapes=[
            pltpu.VMEM((nh, window, LANES), jnp.bfloat16),
            pltpu.VMEM((nh, LANES, window), jnp.bfloat16),
            pltpu.VMEM((nh, BQ, LANES), jnp.bfloat16),
            pltpu.VMEM((nh, LANES, BQ), jnp.float32),
            pltpu.VMEM((2, 8, BQ), jnp.float32),
        ],
        compiler_params=pltpu.CompilerParams(vmem_limit_bytes=VMEM_LIMIT),
        cost_estimate=pl.CostEstimate(
            flops=4 * nh * rows * 1024 * LANES, bytes_accessed=8 << 20, transcendentals=nh * rows * 1024
        ),
    )(lo, hi, prev, own, after, kid, qid)


def attend_back_kernel(
    nh, hd, lo, hi, prev, own, after, kid, qid, do_ref, ot_ref, lse_ref,
    dq_ref, dprev, down, dafter, kh, vh, kt, qh, gh, dk, dv, dqt, delta,
):
    dim = hd // nh
    width = dq_ref.shape[1]
    count = own.shape[0] // BQ
    root = 1.0 / math.sqrt(dim)
    scale = math.log2(math.e) / math.sqrt(dim)

    def load(ref, at, to):
        for h in range(nh):
            k = take_head(ref, rows_at(at, BK), h * dim, dim)
            kh[h, rows_at(to, BK), :] = k.astype(jnp.bfloat16)
            kt[h, :, rows_at(to, BK)] = k.T.astype(jnp.bfloat16)
            vh[h, rows_at(to, BK), :] = take_head(ref, rows_at(at, BK), hd + h * dim, dim).astype(jnp.bfloat16)
            dk[h, rows_at(to, BK), :] = jnp.zeros((BK, LANES), jnp.float32)
            dv[h, rows_at(to, BK), :] = jnp.zeros((BK, LANES), jnp.float32)

    over_window(lo[0], hi[count - 1], prev, own, after, load)

    def query_block(qb, carry):
        rows = rows_at(qb, BQ)
        for h in range(nh):
            qh[h] = take_head(own, rows, 2 * hd + h * dim, dim).astype(jnp.bfloat16)
            gh[h] = take_head(do_ref, rows, h * dim, dim).astype(jnp.bfloat16)
        prod = do_ref[rows, :].astype(jnp.float32).T * ot_ref[:, rows]
        for h in range(nh):
            delta[h : h + 1, :] = jnp.sum(prod[h * dim : (h + 1) * dim], axis=0, keepdims=True)
        dqt[...] = jnp.zeros_like(dqt)
        ids = qid[0:1, rows]

        def key_block(kb, inner):
            keys = rows_at(kb, BK)
            lanes = kid[keys, :]
            same = jnp.concatenate([lanes] * (BQ // LANES), axis=1) == ids
            hs = range(nh)
            scores = [nt_dot(kh[h, keys, :], qh[h]) * scale - lse_ref[h : h + 1, rows] for h in hs]
            dps = [nt_dot(vh[h, keys, :], gh[h]) - delta[h : h + 1, :] for h in hs]
            probs = [jnp.exp2(jnp.where(same, s, NEG)) for s in scores]
            dss = [(p * dp).astype(jnp.bfloat16) for p, dp in zip(probs, dps)]
            lows = [p.astype(jnp.bfloat16) for p in probs]
            for h in hs:
                dv[h, keys, :] += nn_dot(lows[h], gh[h])
            for h in hs:
                dk[h, keys, :] += nn_dot(dss[h], qh[h])
            for h in hs:
                dqt[h] += nn_dot(kt[h, :, keys], dss[h])
            return inner

        lax.fori_loop(lo[qb], hi[qb], key_block, 0)
        parts = [dqt[h, :dim, :] * root for h in range(nh)]
        parts.append(jnp.zeros((width - hd, BQ), jnp.float32))
        dq_ref[rows, :] = jnp.concatenate(parts, axis=0).T.astype(jnp.bfloat16)
        return carry

    lax.fori_loop(0, count, query_block, 0)
    for ref in (dprev, dafter):
        ref[...] = jnp.zeros_like(ref)

    def store(ref, at, to):
        keys = rows_at(to, BK)
        blocks = [dk[h, keys, :] * root for h in range(nh)] + [dv[h, keys, :] for h in range(nh)]
        ref[rows_at(at, BK), :] = put_heads(blocks, [h * dim for h in range(2 * nh)], ref.shape[1]).astype(ref.dtype)

    over_window(lo[0], hi[count - 1], dprev, down, dafter, store)


def attend_back(nh, hd, lo, hi, prev, own, after, kid, qid, grad, ot, lse):
    rows, edge = own.shape[0], prev.shape[0]
    window = rows + 2 * edge
    width, kv = pad_to(hd, LANES), prev.shape[1]
    heads = lambda size, dtype: pltpu.VMEM((nh, size, LANES), dtype)
    return pl.pallas_call(
        functools.partial(attend_back_kernel, nh, hd),
        out_shape=(
            jax.ShapeDtypeStruct((rows, width), jnp.bfloat16),
            jax.ShapeDtypeStruct((edge, kv), jnp.bfloat16),
            jax.ShapeDtypeStruct((rows, kv), jnp.bfloat16),
            jax.ShapeDtypeStruct((edge, kv), jnp.bfloat16),
        ),
        in_specs=[SM, SM] + [VM] * 8,
        out_specs=(VM,) * 4,
        scratch_shapes=[
            heads(window, jnp.bfloat16),
            heads(window, jnp.bfloat16),
            pltpu.VMEM((nh, LANES, window), jnp.bfloat16),
            heads(BQ, jnp.bfloat16),
            heads(BQ, jnp.bfloat16),
            heads(window, jnp.float32),
            heads(window, jnp.float32),
            pltpu.VMEM((nh, LANES, BQ), jnp.float32),
            pltpu.VMEM((8, BQ), jnp.float32),
        ],
        compiler_params=pltpu.CompilerParams(vmem_limit_bytes=VMEM_LIMIT),
        cost_estimate=pl.CostEstimate(
            flops=10 * nh * rows * 1024 * LANES, bytes_accessed=16 << 20, transcendentals=nh * rows * 1024
        ),
    )(lo, hi, prev, own, after, kid, qid, grad, ot, lse)


MESH = pl.DeviceIdType.MESH


def greet(partners, count):
    barrier = pltpu.get_barrier_semaphore()
    for where, there in partners:
        @pl.when(there)
        def _():
            pl.semaphore_signal(barrier, inc=1, device_id=where, device_id_type=MESH)
    pl.semaphore_wait(barrier, count)


def wait_for(ref, sem):
    pltpu.make_async_copy(ref, ref, sem).wait()


def assemble(rows, width, pieces):
    tiles = [None] * (width // LANES)
    for ref, src, dst, count in pieces:
        off, to = src % LANES, dst % LANES
        wide = max(off + count, to + count)
        wide, have = pad_to(wide, LANES), pad_to(off + count, LANES)
        first = src // LANES * LANES
        block = ref[rows, first : first + have].astype(jnp.float32)
        lane = lax.broadcasted_iota(jnp.int32, block.shape, 1)
        block = jnp.where(jnp.logical_and(lane >= off, lane < off + count), block, 0.0)
        if wide > have:
            block = jnp.concatenate([block, jnp.zeros((block.shape[0], wide - have), jnp.float32)], axis=1)
        if off != to:
            block = pltpu.roll(block, (to - off) % wide, 1)
        for step in range(pad_to(to + count, LANES) // LANES):
            part = block[:, step * LANES : (step + 1) * LANES]
            at = dst // LANES + step
            tiles[at] = part if tiles[at] is None else tiles[at] + part
    size = next(t for t in tiles if t is not None).shape
    return jnp.concatenate([jnp.zeros(size, jnp.float32) if t is None else t for t in tiles], axis=1)


def by_rows(size, action, step=64):
    def body(at, carry):
        action(pl.ds(pl.multiple_of(at * step, step), step))
        return carry

    lax.fori_loop(0, size // step, body, 0)


class Gather:
    COPIES = 9

    def __init__(self, shards, fulls, halves, send, recv, load, store, *held):
        self.shards, self.fulls, self.halves, self.held = shards, fulls, halves, held
        self.send, self.recv, self.load, self.store = send, recv, load, store
        self.f, self.r = lax.axis_index("fsdp"), lax.axis_index("replica")
        f = self.f
        c, x, y = lax.rem(f, 2), lax.rem(f // 2, 2), f // 4
        self.core, self.x, self.y = f + 1 - 2 * c, f + 2 - 4 * x, f + 4 - 8 * y
        self.xy = self.x + 4 - 8 * y

    def rows(self, at, which):
        rows, half = self.shards[at][0].shape[0], self.halves[at]
        return {"all": (0, rows), "top": (0, half), "low": (half, rows - half)}[which]

    def part(self, at, place, which):
        first, size = self.rows(at, which)
        rows = self.shards[at][0].shape[0]
        return self.fulls[at].at[pl.ds(pl.multiple_of(place * rows + first, 16), size), :]

    def remote(self, at, kind, src, dst, to):
        return pltpu.make_async_remote_copy(
            src_ref=src, dst_ref=dst, send_sem=self.send.at[at, kind],
            recv_sem=self.recv.at[at, kind], device_id=(to, self.r), device_id_type=MESH,
        )

    def copy(self, at, kind, place, which, to, source=None):
        dst = self.part(at, place, which)
        src = dst if source is None else self.held[at].at[source, pl.ds(*self.rows(at, which)), :]
        return self.remote(at, kind, src, dst, to)

    def hop(self, at, source):
        return self.remote(at, 6 + source, self.held[at].at[0], self.held[at].at[source], (self.x, self.y)[source - 1])

    def keep(self, at, source):
        place = (self.f, self.x, self.y)[source]
        return pltpu.make_async_copy(self.held[at].at[source], self.part(at, place, "all"), self.store.at[at, source])

    def fetch(self, at, source):
        return pltpu.make_async_copy(self.shards[at][source], self.held[at].at[source], self.load.at[at, source])

    def pass_on(self, at, source):
        place = (self.f, self.x, self.y)[source]
        self.copy(at, 2 + source, place, "all", self.core, source).start()
        self.keep(at, source).start()

    def begin(self):
        places = range(len(self.shards))
        for at in places:
            for source in range(len(self.shards[at])):
                self.fetch(at, source).start()
        for at in places:
            self.fetch(at, 0).wait()
            if len(self.shards[at]) == 1:
                self.hop(at, 1).start()
                self.hop(at, 2).start()
        for at in places:
            self.pass_on(at, 0)

    def onward(self, at):
        ahead = len(self.shards[at]) == 3
        self.fetch(at, 1).wait() if ahead else self.hop(at, 1).wait_recv()
        self.copy(at, 0, self.x, "top", self.y, 1).start()
        self.fetch(at, 2).wait() if ahead else self.hop(at, 2).wait_recv()
        self.copy(at, 1, self.y, "low", self.x, 2).start()
        self.pass_on(at, 1)
        self.pass_on(at, 2)

    def across(self, at):
        self.copy(at, 0, self.xy, "top", self.y).wait_recv()
        self.copy(at, 5, self.xy, "top", self.core).start()
        self.copy(at, 1, self.xy, "low", self.x).wait_recv()
        self.copy(at, 6, self.xy, "low", self.core).start()

    def end(self, at):
        for source in range(3):
            self.keep(at, source).wait()
            if source and len(self.shards[at]) == 1:
                self.hop(at, source).wait_send()
        for kind, which in ((0, "top"), (1, "low"), (2, "all"), (3, "all"), (4, "all"), (5, "top"), (6, "low")):
            self.copy(at, kind, self.f, which, self.core).wait_send()
            if kind >= 2:
                self.copy(at, kind, self.f, which, self.core).wait_recv()


def sent_ahead(shards, after):
    shards, _ = lax.optimization_barrier((shards, after))
    hop = lambda shard, step: lax.ppermute(shard, "fsdp", [(at, at ^ step) for at in range(8)])
    return [(shard, hop(shard, 2), hop(shard, 4)) for shard in shards]


def split_shards(refs, sizes):
    shards = []
    for size in sizes:
        shards.append(refs[:size])
        refs = refs[size:]
    return shards, refs


def gather_scratch(shards):
    count = len(shards)
    if not count:
        return []
    return [
        pltpu.SemaphoreType.DMA((count, Gather.COPIES)),
        pltpu.SemaphoreType.DMA((count, Gather.COPIES)),
        pltpu.SemaphoreType.DMA((count, 3)),
        pltpu.SemaphoreType.DMA((count, 3)),
    ] + [pltpu.VMEM((3, *part.shape), part.dtype) for part, *_ in shards]


def gathered_shapes(shards):
    return tuple(jax.ShapeDtypeStruct((8 * part.shape[0], part.shape[1]), part.dtype) for part, *_ in shards)


def halves_of(shards):
    halves, ahead = [], 0
    for part, *_ in shards:
        rows, size = part.shape
        half = rows // 32 * 16
        if rows % 32 and ahead <= 0:
            half += 16
        ahead += (2 * half - rows) * size
        halves.append(half)
    return tuple(halves), tuple(len(shard) for shard in shards)


def start_kernel(plan, part_in, bias_in, *refs):
    halves, sizes = plan
    count = len(halves)
    shards, refs = split_shards(refs, sizes)
    (mod, bias), fulls, refs = refs[:2], refs[2 : count + 2], refs[count + 2 :]
    terms, total, m_s, m_r, b_s, b_r, t_s, t_r, keep, *sems = refs
    f, r = lax.axis_index("fsdp"), lax.axis_index("replica")
    others = [lax.rem(f + d, 8) for d in range(1, 8)]
    greet([((there, r), True) for there in others], 7)

    def remote(src, dst, s_sem, r_sem, there):
        return pltpu.make_async_remote_copy(
            src_ref=src, dst_ref=dst, send_sem=s_sem, recv_sem=r_sem, device_id=(there, r), device_id_type=MESH
        )

    def term_copy(block, source, there):
        return remote(part_in.at[block], terms.at[source], t_s.at[there], t_r.at[source], there)

    def bias_copy(source, there):
        return remote(bias_in, bias.at[source], b_s.at[there], b_r.at[source], there)

    def mod_copy(source, there):
        return remote(total, mod.at[source], m_s.at[there], m_r.at[source], there)

    gather = Gather(shards, fulls, halves, *sems)
    for there in others:
        term_copy(there, f, there).start()
    mine = pltpu.make_async_copy(part_in.at[f], terms.at[f], keep.at[0])
    mine.start()
    gather.begin()
    for there in others:
        bias_copy(f, there).start()
    own_bias = pltpu.make_async_copy(bias_in, bias.at[f], keep.at[1])
    own_bias.start()
    mine.wait()
    for there in others:
        term_copy(f, there, there).wait_recv()
    total[...] = functools.reduce(lambda a, b: a + b, [terms[j] for j in range(8)])
    for there in others:
        mod_copy(f, there).start()
    own_mod = pltpu.make_async_copy(total, mod.at[f], keep.at[2])
    own_mod.start()
    for at in range(count):
        gather.onward(at)
    for at in range(count):
        gather.across(at)
    for at in range(count):
        gather.end(at)
    own_bias.wait()
    own_mod.wait()
    for there in others:
        term_copy(there, f, there).wait_send()
        bias_copy(f, there).wait_send()
        mod_copy(f, there).wait_send()
        bias_copy(there, there).wait_recv()
        mod_copy(there, there).wait_recv()


def start(parts, biases, shards, collective_id):
    sem = lambda: pltpu.SemaphoreType.DMA((8,))
    return pl.pallas_call(
        functools.partial(start_kernel, halves_of(shards)),
        out_shape=(
            jax.ShapeDtypeStruct(parts.shape, parts.dtype),
            jax.ShapeDtypeStruct((8, *biases.shape), biases.dtype),
            *gathered_shapes(shards),
        ),
        in_specs=[HB] * (2 + sum(len(shard) for shard in shards)),
        out_specs=(HB,) * (2 + len(shards)),
        scratch_shapes=[
            pltpu.VMEM(parts.shape, parts.dtype), pltpu.VMEM(parts.shape[1:], parts.dtype),
            sem(), sem(), sem(), sem(), sem(), sem(), pltpu.SemaphoreType.DMA((3,)), *gather_scratch(shards),
        ],
        compiler_params=pltpu.CompilerParams(
            collective_id=collective_id, has_side_effects=True, vmem_limit_bytes=VMEM_LIMIT
        ),
    )(parts, biases, *(part for shard in shards for part in shard))


def to_heads_kernel(reps, size, edge, kv, plan, qkv, *refs):
    halves, sizes = plan
    count = len(halves)
    shards, refs = split_shards(refs, sizes)
    (own, prev, after), fulls, refs = refs[:3], refs[3 : count + 3], refs[count + 3 :]
    x_ref, send, recv, edge_send, edge_recv, *sems = refs
    gather = Gather(shards, fulls, halves, *sems) if count else None
    group, me = lax.axis_index("fsdp"), lax.axis_index("replica")
    groups = lax.axis_size("fsdp")
    wide = x_ref.shape[2]
    width = qkv.shape[1] // 3
    hd = width // reps
    for place in range(reps):
        def pack(rows, place=place):
            at = place * hd
            pieces = [(qkv, width + at, 0, hd), (qkv, 2 * width + at, hd, hd), (qkv, at, 2 * hd, hd)]
            x_ref[place, rows, :] = assemble(rows, wide, pieces).astype(jnp.bfloat16)

        by_rows(size, pack)
    down, up = group > 0, group < groups - 1
    others = [(group, lax.rem(me + d, reps)) for d in range(1, reps)]
    greet(
        [(place, True) for place in others] + [((group - 1, me), down), ((group + 1, me), up)]
        + ([((there, me), True) for there in (gather.core, gather.x, gather.y)] if count else []),
        reps - 1 + down.astype(jnp.int32) + up.astype(jnp.int32) + (3 if count else 0),
    )
    spans = [pl.ds(0, kv), pl.ds(kv, wide - kv)] if wide > kv else [pl.ds(0, kv)]

    def exchange(span, part, there):
        return pltpu.make_async_remote_copy(
            src_ref=x_ref.at[there, :, span], dst_ref=own.at[me, :, span], send_sem=send.at[part, there],
            recv_sem=recv.at[part, me], device_id=(group, there), device_id_type=MESH,
        )

    for part, span in enumerate(spans):
        for _, there in others:
            exchange(span, part, there).start()
        pltpu.make_async_copy(x_ref.at[me, :, span], own.at[me, :, span], recv.at[part, me]).start()

    if count:
        gather.begin()
    for at in range(count):
        gather.onward(at)

    def edges(piece, action):
        lo, hi = piece * size, (piece + 1) * size
        total = reps * size
        if lo >= total - edge:
            @pl.when(up)
            def _():
                action(0, piece, (group + 1, me), prev.at[pl.ds(lo - (total - edge), size), :])
        if hi <= edge:
            @pl.when(down)
            def _():
                action(1, piece, (group - 1, me), after.at[pl.ds(lo, size), :])

    def start_edge(way, piece, where, target):
        pltpu.make_async_remote_copy(
            src_ref=own.at[piece, :, spans[0]], dst_ref=target, send_sem=edge_send.at[way, piece],
            recv_sem=edge_recv.at[way, piece], device_id=where, device_id_type=MESH,
        ).start()

    def end_send(way, piece, where, target):
        wait_for(own.at[piece, :, spans[0]], edge_send.at[way, piece])

    def end_recv(way, piece, where, target):
        wait_for(target, edge_recv.at[way, piece])

    for piece in range(reps):
        wait_for(own.at[piece, :, spans[0]], recv.at[0, piece])
        edges(piece, start_edge)
    if len(spans) > 1:
        for piece in range(reps):
            wait_for(own.at[piece, :, spans[1]], recv.at[1, piece])
    for at in range(count):
        gather.across(at)
    for part, span in enumerate(spans):
        for _, there in others:
            wait_for(x_ref.at[there, :, span], send.at[part, there])
    for piece in range(reps):
        edges(piece, end_send)
        lo, hi = piece * size, (piece + 1) * size
        total = reps * size
        if lo >= total - edge:
            @pl.when(down)
            def _():
                wait_for(prev.at[pl.ds(lo - (total - edge), size), :], edge_recv.at[0, piece])
        if hi <= edge:
            @pl.when(up)
            def _():
                wait_for(after.at[pl.ds(lo, size), :], edge_recv.at[1, piece])
    for at in range(count):
        gather.end(at)


def to_heads(qkv, reps, edge, kv, shards, collective_id):
    size, wide = qkv.shape[0], pad_to(qkv.shape[1] // reps, LANES)
    sems = pltpu.SemaphoreType.DMA((2, reps))
    own, prev, after, *fulls = pl.pallas_call(
        functools.partial(to_heads_kernel, reps, size, edge, kv, halves_of(shards)),
        out_shape=(
            jax.ShapeDtypeStruct((reps, size, wide), qkv.dtype),
            jax.ShapeDtypeStruct((edge, kv), qkv.dtype),
            jax.ShapeDtypeStruct((edge, kv), qkv.dtype),
            *gathered_shapes(shards),
        ),
        in_specs=[VM] + [HB] * sum(len(shard) for shard in shards),
        out_specs=(HB,) * (3 + len(shards)),
        scratch_shapes=[pltpu.VMEM((reps, size, wide), qkv.dtype), sems, sems, sems, sems, *gather_scratch(shards)],
        compiler_params=pltpu.CompilerParams(
            collective_id=collective_id, has_side_effects=True, vmem_limit_bytes=VMEM_LIMIT
        ),
    )(qkv, *(part for shard in shards for part in shard))
    return own.reshape(reps * size, wide), prev, after, fulls


def swap_kernel(reps, out, plan, x_ref, *refs):
    halves, sizes = plan
    count = len(halves)
    shards, refs = split_shards(refs, sizes)
    y_ref, fulls, (held, send, recv, *sems) = refs[0], refs[1 : count + 1], refs[count + 1 :]
    gather = Gather(shards, fulls, halves, *sems) if count else None
    group, me = lax.axis_index("fsdp"), lax.axis_index("replica")
    others = [(group, lax.rem(me + d, reps)) for d in range(1, reps)]
    planar = [(there, me) for there in (gather.core, gather.x, gather.y)] if count else []
    size, lanes = held.shape[1:]
    if out:
        src, dst = x_ref, held
        hd = y_ref.shape[1] // reps
    else:
        src, dst = held, y_ref
        hd = x_ref.shape[1] // reps
        for place in range(reps):
            def pack(rows, place=place):
                held[place, rows, :] = assemble(rows, lanes, [(x_ref, place * hd, 0, hd)]).astype(jnp.bfloat16)

            by_rows(size, pack)
    greet([(place, True) for place in others + planar], reps - 1 + len(planar))
    for _, there in others:
        pltpu.make_async_remote_copy(
            src_ref=src.at[there], dst_ref=dst.at[me], send_sem=send.at[there], recv_sem=recv.at[me],
            device_id=(group, there), device_id_type=MESH,
        ).start()
    pltpu.make_async_copy(src.at[me], dst.at[me], recv.at[me]).start()
    if count:
        gather.begin()
    for at in range(count):
        gather.onward(at)
    for at in range(count):
        gather.across(at)
    for piece in range(reps):
        wait_for(dst.at[piece], recv.at[piece])
    if out:
        def unpack(rows):
            pieces = [(held.at[place], 0, place * hd, hd) for place in range(reps)]
            y_ref[rows, :] = assemble(rows, y_ref.shape[1], pieces).astype(jnp.bfloat16)

        by_rows(size, unpack)
    for _, there in others:
        wait_for(src.at[there], send.at[there])
    for at in range(count):
        gather.end(at)


def swap(x, reps, out, shards, collective_id):
    if out:
        size, lanes = x.shape[0] // reps, x.shape[1]
        x = x.reshape(reps, size, lanes)
        shape = (size, HEADS * HEAD_DIM)
    else:
        size, lanes = x.shape[0], pad_to(x.shape[1] // reps, LANES)
        shape = (reps, size, lanes)
    sems = pltpu.SemaphoreType.DMA((reps,))
    swapped, *fulls = pl.pallas_call(
        functools.partial(swap_kernel, reps, out, halves_of(shards)),
        out_shape=(jax.ShapeDtypeStruct(shape, x.dtype), *gathered_shapes(shards)),
        in_specs=[HB if out else VM] + [HB] * sum(len(shard) for shard in shards),
        out_specs=(VM if out else HB,) + (HB,) * len(shards),
        scratch_shapes=[pltpu.VMEM((reps, size, lanes), x.dtype), sems, sems, *gather_scratch(shards)],
        compiler_params=pltpu.CompilerParams(
            collective_id=collective_id, has_side_effects=True, vmem_limit_bytes=VMEM_LIMIT
        ),
    )(x, *(part for shard in shards for part in shard))
    return swapped, fulls


def from_heads_kernel(reps, size, edge, dprev, own, dafter, dq, out, out_kv, out_q, from_up, from_down, total, mine, sends, recvs, send, recv):
    group, me = lax.axis_index("fsdp"), lax.axis_index("replica")
    groups = lax.axis_size("fsdp")
    rows = reps * size
    down, up = group > 0, group < groups - 1
    others = [(group, lax.rem(me + d, reps)) for d in range(1, reps)]
    greet(
        [(place, True) for place in others] + [((group - 1, me), down), ((group + 1, me), up)],
        reps - 1 + down.astype(jnp.int32) + up.astype(jnp.int32),
    )
    to_down = pltpu.make_async_remote_copy(
        src_ref=dprev, dst_ref=from_up, send_sem=sends.at[0], recv_sem=recvs.at[0],
        device_id=(group - 1, me), device_id_type=MESH,
    )
    to_up = pltpu.make_async_remote_copy(
        src_ref=dafter, dst_ref=from_down, send_sem=sends.at[1], recv_sem=recvs.at[1],
        device_id=(group + 1, me), device_id_type=MESH,
    )
    pl.when(down)(to_down.start)
    pl.when(up)(to_up.start)
    for _, there in others:
        pltpu.make_async_remote_copy(
            src_ref=dq.at[pl.ds(pl.multiple_of(there * size, size), size), :], dst_ref=out_q.at[me], send_sem=send.at[0, there],
            recv_sem=recv.at[0, me], device_id=(group, there), device_id_type=MESH,
        ).start()
    pltpu.make_async_copy(dq.at[pl.ds(pl.multiple_of(me * size, size), size), :], out_q.at[me], recv.at[0, me]).start()
    step = math.gcd(edge, 256)

    def chunk(at, carry):
        here = pl.ds(pl.multiple_of(at * step, step), step)
        total[here, :] = own[here, :].astype(jnp.float32)
        return carry

    lax.fori_loop(0, rows // step, chunk, 0)

    def add(ref, first):
        def body(at, carry):
            here = pl.ds(pl.multiple_of(first + at * step, step), step)
            there = pl.ds(pl.multiple_of(at * step, step), step)
            total[here, :] += ref[there, :].astype(jnp.float32)
            return carry

        lax.fori_loop(0, edge // step, body, 0)

    @pl.when(down)
    def _():
        wait_for(from_down, recvs.at[1])
        add(from_down, 0)

    @pl.when(up)
    def _():
        wait_for(from_up, recvs.at[0])
        add(from_up, rows - edge)

    def narrow(at, carry):
        here = pl.ds(pl.multiple_of(at * step, step), step)
        mine[here, :] = total[here, :].astype(jnp.bfloat16)
        return carry

    lax.fori_loop(0, rows // step, narrow, 0)
    for _, there in others:
        pltpu.make_async_remote_copy(
            src_ref=mine.at[pl.ds(pl.multiple_of(there * size, size), size), :], dst_ref=out_kv.at[me], send_sem=send.at[1, there],
            recv_sem=recv.at[1, me], device_id=(group, there), device_id_type=MESH,
        ).start()
    pltpu.make_async_copy(mine.at[pl.ds(pl.multiple_of(me * size, size), size), :], out_kv.at[me], recv.at[1, me]).start()
    width = out.shape[1] // 3
    hd = width // reps

    def unpack(ref, first, section):
        def body(rows):
            pieces = [(ref.at[place], first, place * hd, hd) for place in range(reps)]
            out[rows, section * width : (section + 1) * width] = assemble(rows, width, pieces).astype(jnp.bfloat16)

        by_rows(size, body)

    for piece in range(reps):
        wait_for(out_q.at[piece], recv.at[0, piece])
    unpack(out_q, 0, 0)
    for piece in range(reps):
        wait_for(out_kv.at[piece], recv.at[1, piece])
    unpack(out_kv, 0, 1)
    unpack(out_kv, hd, 2)
    for _, there in others:
        wait_for(out_q.at[0], send.at[0, there])
        wait_for(out_kv.at[0], send.at[1, there])
    pl.when(down)(to_down.wait_send)
    pl.when(up)(to_up.wait_send)


def from_heads(reps, width, dprev, own, dafter, dq, collective_id):
    rows, kv = own.shape
    edge, size = dprev.shape[0], own.shape[0] // reps
    pair, both = pltpu.SemaphoreType.DMA((2,)), pltpu.SemaphoreType.DMA((2, reps))
    return pl.pallas_call(
        functools.partial(from_heads_kernel, reps, size, edge),
        out_shape=jax.ShapeDtypeStruct((size, 3 * width), own.dtype),
        in_specs=[HB, VM, HB, HB],
        out_specs=VM,
        scratch_shapes=[
            pltpu.VMEM((reps, size, kv), own.dtype),
            pltpu.VMEM((reps, size, dq.shape[1]), own.dtype),
            pltpu.VMEM((edge, kv), own.dtype),
            pltpu.VMEM((edge, kv), own.dtype),
            pltpu.VMEM((rows, kv), jnp.float32),
            pltpu.VMEM((rows, kv), own.dtype),
            pair,
            pair,
            both,
            both,
        ],
        compiler_params=pltpu.CompilerParams(
            collective_id=collective_id, has_side_effects=True, vmem_limit_bytes=VMEM_LIMIT
        ),
    )(dprev, own, dafter, dq)


UNITS = 12
LEFT_ROWS = 4


def reduce_kernel(layers, width, half, *refs):
    count = layers * UNITS + 1
    ins, extra_in, refs = refs[: 8 * layers], refs[8 * layers], refs[8 * layers + 1 :]
    (out, shared, extra, share_s, share_r, left, right, csend, crecv, own, xs, xr, ys, yr, tx, ty, x2s, x2r, y2s, y2r, zs, z1r, z2s, z2r, fin,
     load_sem, core_s, core_r, x_s, x_r, y_s, y_r, x2_s, x2_r, y2_s, y2_r, z1_s, z1_r, z2_s, z2_r, fin_l, fin_s, fin_r,
     credit) = refs
    f, r = lax.axis_index("fsdp"), lax.axis_index("replica")
    rows = own.shape[1]
    tokens = left.shape[1]
    c, x, y = lax.rem(f, 2), lax.rem(f // 2, 2), f // 4
    core_at, x_at, y_at = f + 1 - 2 * c, f + 2 - 4 * x, f + 4 - 8 * y
    inner = jnp.logical_and(r > 0, r < 3)
    outer = jnp.logical_not(inner)
    z_at = r + 1 - 2 * lax.rem(r, 2)
    others = [lax.rem(f + d, 8) for d in range(1, 8)]
    greet(
        [((there, r), True) for there in others] + [((f, r - 1), r > 0), ((f, r + 1), r < 3)],
        7 + (r > 0).astype(jnp.int32) + (r < 3).astype(jnp.int32),
    )
    few = extra.shape[1]
    loads = [(extra_in, extra)]
    for layer in range(layers):
        place = layer * (LEFT_ROWS + 3) * width
        for at in range(4):
            src = ins[8 * layer + at]
            loads.append((src, left.at[pl.ds(place, src.shape[0]), :]))
            place += src.shape[0]
        slot = layer * 9
        for at in range(4):
            src = ins[8 * layer + 4 + at]
            for part in range(src.shape[1] // width):
                loads.append((src.at[:, pl.ds(part * width, width)], right.at[slot]))
                slot += 1
    for at, (src, dst) in enumerate(loads):
        pltpu.make_async_copy(src, dst, load_sem.at[at]).start()
    for at, (src, dst) in enumerate(loads):
        pltpu.make_async_copy(src, dst, load_sem.at[at]).wait()

    def send(src, dst, s_sem, r_sem, where):
        return pltpu.make_async_remote_copy(
            src_ref=src, dst_ref=dst, send_sem=s_sem, recv_sem=r_sem, device_id=where, device_id_type=MESH
        )

    def place_of(core, mx, my):
        return ((y + my * (1 - 2 * y)) * 2 + (x + mx * (1 - 2 * x))) * 2 + (c + core * (1 - 2 * c))

    def term(u, core, mx, my):
        layer, w = (u - 1) // UNITS, lax.rem(u - 1, UNITS)
        block = place_of(core, mx, my)
        inside = jnp.where(
            w < 4, rows * w, LEFT_ROWS * width + jnp.where(w < 8, 0, jnp.where(w < 9, width, 2 * width))
        )
        stride = jnp.where(w < 4, 4 * rows, rows)
        start = pl.multiple_of(layer * ((LEFT_ROWS + 3) * width) + inside + stride * block, 16)
        other = layer * 9 + jnp.maximum(w - 3, 0)
        return nn_dot(left[pl.ds(start, rows), :], right[other])

    places = ((0, 0), (1, 0), (0, 1), (1, 1))
    top, low = pl.ds(0, half), pl.ds(half, rows - half)

    def core_copy(slot):
        return send(csend.at[slot], crecv.at[slot], core_s.at[slot], core_r.at[slot], (core_at, r))

    def x_copy(slot):
        return send(xs.at[slot], xr.at[slot], x_s.at[slot], x_r.at[slot], (x_at, r))

    def y_copy(slot):
        return send(ys.at[slot], yr.at[slot], y_s.at[slot], y_r.at[slot], (y_at, r))

    def x2_copy(slot):
        return send(x2s.at[slot], x2r.at[slot], x2_s.at[slot], x2_r.at[slot], (x_at, r))

    def y2_copy(slot):
        return send(y2s.at[slot], y2r.at[slot], y2_s.at[slot], y2_r.at[slot], (y_at, r))

    def z1_copy(slot, to):
        return send(zs.at[slot], z1r.at[to], z1_s.at[slot], z1_r.at[to], (f, z_at))

    def z2_copy(slot):
        return send(z2s.at[slot], z2r.at[slot], z2_s.at[slot], z2_r.at[slot], (f, 3 - r))

    def fin_copy(slot, u):
        return send(fin.at[slot], out.at[u], fin_s.at[slot], fin_r.at[u], (f, z_at))

    def keep_copy(slot, u):
        return pltpu.make_async_copy(fin.at[slot], out.at[u], fin_l.at[slot])

    f32, bf16 = jnp.float32, jnp.bfloat16
    z_slots = z1r.shape[0]

    def stage(u, condition, body):
        live = jnp.logical_and(u >= 0, u < count)
        pl.when(live if condition is None else jnp.logical_and(live, condition))(lambda: body(u))

    def close(u):
        slot = lax.rem(u, 4)
        fin_copy(slot, u).wait_send()
        keep_copy(slot, u).wait()

    def arrive(u):
        fin_copy(lax.rem(u, 4), u).wait_recv()

    def finish(u):
        slot = lax.rem(u, 4)
        z2_copy(slot).wait()
        fin[slot] = (z2s[slot].astype(f32) + z2r[slot].astype(f32)).astype(bf16)
        fin_copy(slot, u).start()
        keep_copy(slot, u).start()

    def middle(u):
        slot, z_slot, at = lax.rem(u, 4), lax.rem(u, z_slots), lax.rem(u, own.shape[0])
        z1_copy(slot, z_slot).wait_recv()
        z2s[slot] = (own[at] + z1r[z_slot].astype(f32)).astype(bf16)
        z2_copy(slot).start()

        @pl.when(u + z_slots < count)
        def _():
            pl.semaphore_signal(credit, inc=1, device_id=(f, z_at), device_id_type=MESH)

    def sent(u):
        z1_copy(lax.rem(u, 4), lax.rem(u, z_slots)).wait_send()

    def plane(u):
        slot, at = lax.rem(u, 4), lax.rem(u, own.shape[0])
        x2_copy(slot).wait()
        y2_copy(slot).wait()
        own[at, top, :] += y2r[slot].astype(f32)
        own[at, low, :] += x2r[slot].astype(f32)

        @pl.when(outer)
        def _():
            zs[slot] = own[at].astype(bf16)

            @pl.when(u >= z_slots)
            def _():
                pl.semaphore_wait(credit, 1)

            z1_copy(slot, lax.rem(u, z_slots)).start()

    def cross(u):
        slot, at = lax.rem(u, 4), lax.rem(u, own.shape[0])
        x_copy(slot).wait()
        y_copy(slot).wait()
        y2s[slot] = (ty[slot] + xr[slot, 1].astype(f32)).astype(bf16)
        y2_copy(slot).start()
        x2s[slot] = (tx[slot] + yr[slot, 1].astype(f32)).astype(bf16)
        x2_copy(slot).start()
        own[at, top, :] += xr[slot, 0].astype(f32)
        own[at, low, :] += yr[slot, 0].astype(f32)

    def chip_extra(u):
        core_copy(0).wait()
        for m, (mx, my) in enumerate(places):
            total = extra[place_of(0, mx, my)] + crecv[0, m, :few, :].astype(f32)
            if m == 0:
                own[0, :few, :] = total
            elif m == 2:
                ty[0, :few, :] = total
            else:
                xs[0, m // 2, :few, :] = total.astype(bf16)
        x_copy(0).start()
        y_copy(0).start()

    def chip(u):
        slot, pair, at = lax.rem(u, 4), lax.rem(u, 2), lax.rem(u, own.shape[0])
        core_copy(pair).wait()
        total = term(u, 0, 1, 1) + crecv[pair, 3].astype(f32)
        xs[slot, 1] = total[:half].astype(bf16)
        ys[slot, 1] = total[half:].astype(bf16)
        total = term(u, 0, 1, 0) + crecv[pair, 1].astype(f32)
        xs[slot, 0] = total[:half].astype(bf16)
        tx[slot] = total[half:]
        x_copy(slot).start()
        total = term(u, 0, 0, 1) + crecv[pair, 2].astype(f32)
        ys[slot, 0] = total[half:].astype(bf16)
        ty[slot] = total[:half]
        y_copy(slot).start()
        own[at] = term(u, 0, 0, 0) + crecv[pair, 0].astype(f32)

    def open_extra(u):
        for m, (mx, my) in enumerate(places):
            csend[0, m, :few, :] = extra[place_of(1, mx, my)].astype(bf16)
        core_copy(0).start()

    def share_copy(there, where):
        return send(out.at[0, pl.ds(0, few), :], shared.at[there], share_s.at[where], share_r.at[there], (where, r))

    def share(u):
        for there in others:
            share_copy(f, there).start()

    def open_unit(u):
        pair = lax.rem(u, 2)
        for m, (mx, my) in enumerate(places):
            csend[pair, m] = term(u, 1, mx, my).astype(bf16)
        core_copy(pair).start()

    def step(t, carry):
        pl.when(t == 12)(lambda: share(t))
        stage(t - 11, inner, close)
        stage(t - 11, outer, arrive)
        stage(t - 9, inner, finish)
        stage(t - 7, inner, middle)
        stage(t - 7, outer, sent)
        stage(t - 5, None, plane)
        stage(t - 3, None, cross)
        stage(t - 1, t > 1, chip)
        pl.when(t == 1)(lambda: chip_extra(t - 1))
        stage(t, t > 0, open_unit)
        pl.when(t == 0)(lambda: open_extra(t))
        return carry

    lax.fori_loop(0, count + 11, step, 0)
    for there in others:
        share_copy(f, there).wait_send()
        share_copy(there, there).wait_recv()


def reduce_grads(pairs, extra):
    layers = len(pairs)
    width, tokens = pairs[0][0][1].shape
    rows = width // 8
    half = pad_to(rows // 2, 16)
    ins = [part for lefts, rights in pairs for part in (*lefts, *rights)] + [extra]
    count = layers * UNITS + 1
    bf16, f32 = jnp.bfloat16, jnp.float32
    buf = lambda dtype, *shape: pltpu.VMEM((*shape, width), dtype)
    sem = lambda size: pltpu.SemaphoreType.DMA((size,))
    z_slots = 8
    return pl.pallas_call(
        functools.partial(reduce_kernel, layers, width, half),
        out_shape=(
            jax.ShapeDtypeStruct((count, rows, width), bf16),
            jax.ShapeDtypeStruct(extra.shape, bf16),
        ),
        in_specs=[HB] * len(ins),
        out_specs=(HB, HB),
        scratch_shapes=[
            buf(f32, *extra.shape[:2]), sem(8), sem(8),
            pltpu.VMEM((layers * (LEFT_ROWS + 3) * width, tokens), bf16),
            buf(bf16, layers * 9, tokens),
            buf(bf16, 2, 4, rows), buf(bf16, 2, 4, rows), buf(f32, 9, rows),
            buf(bf16, 4, 2, half), buf(bf16, 4, 2, half), buf(bf16, 4, 2, rows - half), buf(bf16, 4, 2, rows - half),
            buf(f32, 4, rows - half), buf(f32, 4, half),
            buf(bf16, 4, rows - half), buf(bf16, 4, rows - half), buf(bf16, 4, half), buf(bf16, 4, half),
            buf(bf16, 4, rows), buf(bf16, z_slots, rows), buf(bf16, 4, rows), buf(bf16, 4, rows), buf(bf16, 4, rows),
            sem(13 * layers + 1), sem(2), sem(2), sem(4), sem(4), sem(4), sem(4), sem(4), sem(4), sem(4), sem(4),
            sem(4), sem(z_slots), sem(4), sem(4), sem(4), sem(4), sem(count), pltpu.SemaphoreType.REGULAR,
        ],
        compiler_params=pltpu.CompilerParams(
            collective_id=5, has_side_effects=True, vmem_limit_bytes=60 * 1024 * 1024
        ),
        cost_estimate=pl.CostEstimate(
            flops=2 * count * 8 * rows * tokens * width, bytes_accessed=100 << 20, transcendentals=0
        ),
    )(*ins)


def pre_norm(stream, shift, scale):
    centred = stream - jnp.mean(stream, axis=-1, keepdims=True)
    spread = jnp.mean(centred * centred, axis=-1, keepdims=True)
    return centred * lax.rsqrt(spread + NORM_EPS) * (1.0 + scale) + shift


def gelu_tanh(values):
    return jax.nn.gelu(values, approximate=True)


def latent_ids(latent_len, positions, token_total):
    starts = jnp.cumsum(latent_len) - latent_len
    found = jnp.sum((starts[None, :] <= positions[:, None]).astype(jnp.int32), axis=1) - 1
    inside = (positions >= 0) & (positions < token_total)
    return jnp.where(inside, found, -1)


def low_dot(left, right):
    return jnp.dot(left, right, preferred_element_type=jnp.float32)


def layer_forward(stream, mod_tok, full, plan, in_first, shards_first, shards_second, shards_ahead, collective_id):
    qkv_w, qkv_b, out_w, out_b, up_w, up_b, down_w, down_b = full
    reps, edge, bounds, ids = plan
    width = stream.shape[1]
    hd = width // reps
    nh = HEADS // reps
    shift_one, scale_one, gate_one, shift_two, scale_two, gate_two = jnp.split(mod_tok, 6, axis=1)
    normed = pre_norm(stream, shift_one, scale_one).astype(jnp.bfloat16)
    qkv_bias = qkv_b.astype(jnp.float32)
    bias_full = jnp.concatenate(
        [qkv_bias[:width], jnp.zeros((width,), jnp.float32), qkv_bias[width:]]
    )
    projected = (low_dot(normed, qkv_w) + bias_full).astype(jnp.bfloat16)
    in_second = sent_ahead(shards_first, projected) if shards_first else []
    own, prev, after, fulls = to_heads(projected, reps, edge, pad_to(2 * hd, LANES), in_first, collective_id)
    first_gathered = fulls
    in_second += sent_ahead(shards_second, own) if shards_second else []
    mixed, mixed_t, log_norm = attend(nh, hd, *bounds, prev, own, after, *ids)
    mixed, fulls = swap(mixed, reps, True, in_second, collective_id + 1)
    if in_first:
        (up_w,), (down_w, *fulls) = first_gathered, fulls
    in_next = sent_ahead(shards_ahead, mixed) if shards_ahead else ()
    branch = low_dot(mixed, out_w) + out_b.astype(jnp.float32)
    middle = stream + gate_one * branch
    normed_two = pre_norm(middle, shift_two, scale_two).astype(jnp.bfloat16)
    hidden = low_dot(normed_two, up_w) + up_b.astype(jnp.float32)
    active = gelu_tanh(hidden).astype(jnp.bfloat16)
    result = low_dot(active, down_w) + down_b.astype(jnp.float32)
    saved = (
        normed, (prev, own, after), mixed, (mixed_t, log_norm), branch, middle, normed_two, hidden, active, result,
    )
    full = (qkv_w, qkv_b, out_w, out_b, up_w, up_b, down_w, down_b)
    return (middle + gate_two * result, saved, full, fulls, in_next)


def layer_backward(stream, mod_tok, full, saved, plan, pick, grad_next):
    qkv_w, qkv_b, out_w, out_b, up_w, up_b, down_w, down_b = full
    normed, window, mixed, kept, branch, middle, normed_two, hidden, active, result = saved
    reps, edge, bounds, ids = plan
    width = stream.shape[1]
    hd = width // reps
    nh = HEADS // reps
    shift_one, scale_one, gate_one, shift_two, scale_two, gate_two = jnp.split(mod_tok, 6, axis=1)
    grad_result = (gate_two * grad_next).astype(jnp.bfloat16)
    grad_gate_two = grad_next * result
    grad_down_b = jnp.sum(grad_result.astype(jnp.float32), axis=0)
    grad_active = jnp.einsum("td,fd->tf", grad_result, down_w, preferred_element_type=jnp.float32)
    _, gelu_back = jax.vjp(gelu_tanh, hidden)
    grad_hidden = gelu_back(grad_active)[0].astype(jnp.bfloat16)
    grad_up_b = jnp.sum(grad_hidden.astype(jnp.float32), axis=0)
    grad_normed_two = jnp.einsum("tf,df->td", grad_hidden, up_w, preferred_element_type=jnp.float32)
    _, norm_back_two = jax.vjp(pre_norm, middle, shift_two, scale_two)
    grad_middle_part, grad_shift_two, grad_scale_two = norm_back_two(grad_normed_two)
    grad_middle = grad_next + grad_middle_part
    grad_branch = (gate_one * grad_middle).astype(jnp.bfloat16)
    grad_gate_one = grad_middle * branch
    grad_out_b = jnp.sum(grad_branch.astype(jnp.float32), axis=0)
    grad_mixed = jnp.einsum(
        "te,de->td", grad_branch, out_w, preferred_element_type=jnp.float32
    ).astype(jnp.bfloat16)
    grad_heads, _ = swap(grad_mixed, reps, False, (), 3)
    prev, own, after = window
    grad_q, grad_prev, grad_own, grad_after = attend_back(
        nh, hd, *bounds, prev, own, after, *ids, grad_heads.reshape(own.shape[0], -1), *kept
    )
    grad_projected = from_heads(reps, width, grad_prev, grad_own, grad_after, grad_q, 4)
    sums = jnp.sum(grad_projected.astype(jnp.float32), axis=0)
    grad_qkv_b = jnp.concatenate([sums[:width], sums[2 * width :]])
    grad_normed = jnp.einsum("te,de->td", grad_projected, qkv_w, preferred_element_type=jnp.float32)
    _, norm_back_one = jax.vjp(pre_norm, stream, shift_one, scale_one)
    grad_stream_part, grad_shift_one, grad_scale_one = norm_back_one(grad_normed)
    grad_stream = grad_middle + grad_stream_part
    grad_mod = jnp.concatenate(
        [
            jnp.einsum("tl,tm->lm", pick, part, precision=HIGH, preferred_element_type=jnp.float32)
            for part in (
                grad_shift_one, grad_scale_one, grad_gate_one, grad_shift_two, grad_scale_two, grad_gate_two,
            )
        ],
        axis=1,
    )
    return (
        grad_stream, grad_mod,
        ((active.T, normed_two.T, mixed.T, normed.T), (grad_result, grad_hidden, grad_branch, grad_projected)),
        (grad_qkv_b, grad_out_b, grad_up_b, grad_down_b),
    )


def bias_parts(stacked, params):
    cuts = [0]
    for at in (3, 5, 7, 9):
        cuts.append(cuts[-1] + params[at].shape[0])
    return [stacked[:, a:b].reshape(-1) for a, b in zip(cuts[:-1], cuts[1:])]


def modulation(partial_terms, layers):
    shares = jnp.stack([jnp.concatenate([params[at] for at in (3, 5, 7, 9)]) for params in layers])
    if not on_planes():
        mods = lax.psum(tuple(partial_terms), "fsdp")
        stacked = lax.all_gather(shares, "fsdp", axis=0)
        fulls = [lax.all_gather(layers[0][at], "fsdp", axis=0, tiled=True) for at in (2, 4)]
    else:
        width = layers[0][4].shape[1]
        parts = jnp.stack(partial_terms).reshape(8, -1, width)
        mod, stacked, *fulls = start(
            parts, jnp.pad(shares, ((0, 16 - shares.shape[0]), (0, 0))), [(layers[0][at],) for at in (2, 4)], 6
        )
        mods = mod.reshape(len(layers), -1, partial_terms[0].shape[1])
    return mods, [bias_parts(stacked[:, at], params) for at, params in enumerate(layers)], fulls


def on_planes():
    return lax.axis_size("fsdp") == 8 and lax.axis_size("replica") == 4


def owner_sums(pairs, grad_mods, grad_biases):
    groups = lax.axis_size("fsdp")
    width = pairs[0][0][1].shape[0]
    if on_planes():
        mods = jnp.stack(grad_mods).reshape(groups, -1, width)
        biases = jnp.stack(
            [jnp.concatenate([part.reshape(groups, -1) for part in parts], axis=1) for parts in grad_biases], axis=1
        )
        extra = jnp.concatenate([mods, biases], axis=1)
        used = extra.shape[1]
        extra = jnp.pad(extra, ((0, 0), (0, pad_to(used, 16) - used), (0, 0)))
        out, shared = reduce_grads(pairs, extra)
        shared = lax.dynamic_update_slice_in_dim(
            shared, out[None, 0, : extra.shape[1]], lax.axis_index("fsdp"), 0
        )
        mods = shared[:, : mods.shape[1]].reshape(len(pairs), -1, grad_mods[0].shape[1])
        units = out[1:].reshape(len(pairs), UNITS, -1, width)
        rows = units.shape[2]
        across = lambda part: part.transpose(1, 0, 2).reshape(rows, -1).astype(jnp.float32)
        results = []
        for layer_at, unit in enumerate(units):
            share = out[0, used - len(pairs) + layer_at].astype(jnp.float32)
            cuts = [0]
            for part in grad_biases[layer_at]:
                cuts.append(cuts[-1] + part.shape[0] // groups)
            weights = (
                across(unit[9:12]), across(unit[8:9]), across(unit[4:8]),
                unit[0:4].reshape(-1, width).astype(jnp.float32),
            )
            results.append((weights, [share[i:j] for i, j in zip(cuts[:-1], cuts[1:])]))
        return results, mods
    flat = jnp.concatenate([part for parts in grad_biases for part in parts])
    *mods, flat = lax.psum((*grad_mods, flat), ("fsdp", "replica"))
    results, place = [], 0
    for (lefts, rights), parts in zip(pairs, grad_biases):
        grads, biases = [], []
        for left, right in zip(lefts, rights):
            grad = low_dot(left, right).astype(jnp.bfloat16)
            part = lax.psum_scatter(grad, "fsdp", scatter_dimension=0, tiled=True)
            grads.append(lax.psum(part, "replica").astype(jnp.float32))
        for part in parts:
            share = part.shape[0] // groups
            biases.append(lax.dynamic_slice_in_dim(flat, place + lax.axis_index("fsdp") * share, share, 0))
            place += part.shape[0]
        results.append((grads[::-1], biases))
    return results, mods


def attention_plan(latent_len, tok_rows, reps, device_at):
    column = tok_rows * reps
    edge = MAXLEN
    total = jnp.sum(latent_len)
    first = lax.axis_index("fsdp") * column
    positions = first - edge + jnp.arange(column + 2 * edge, dtype=jnp.int32)
    ends = jnp.cumsum(latent_len)
    ids = jnp.sum((ends[None, :] <= positions[:, None]).astype(jnp.int32), axis=1)
    ids = jnp.where(positions < 0, -1, ids)
    own = ids[edge : edge + column]
    count = column // BQ
    firsts, lasts = own[::BQ], own[BQ - 1 :: BQ]
    pick = lambda at: (at[:, None] == jnp.arange(latent_len.shape[0], dtype=jnp.int32)[None, :]).astype(jnp.int32)
    low = jnp.sum(pick(firsts) * (ends - latent_len)[None, :], axis=1) - (first - edge)
    high = jnp.sum(pick(lasts) * ends[None, :], axis=1) - (first - edge)
    bounds = ((low // BK).astype(jnp.int32), ((high + BK - 1) // BK).astype(jnp.int32))
    kid = jnp.broadcast_to(ids[:, None], (ids.shape[0], LANES))
    qid = jnp.broadcast_to(own[None, :], (8, column))
    return (reps, edge, bounds, (kid, qid))


def shards(
    tokens,
    cond,
    latent_len,
    first_ada_weight,
    first_ada_bias,
    first_qkv_weight,
    first_qkv_bias,
    first_out_weight,
    first_out_bias,
    first_up_weight,
    first_up_bias,
    first_down_weight,
    first_down_bias,
    second_ada_weight,
    second_ada_bias,
    second_qkv_weight,
    second_qkv_bias,
    second_out_weight,
    second_out_bias,
    second_up_weight,
    second_up_bias,
    second_down_weight,
    second_down_bias,
    cotangent,
):
    tok_rows = tokens.shape[0]
    group_place = lax.axis_index("fsdp")
    device_at = lax.axis_index(("fsdp", "replica"))
    token_total = tok_rows * lax.axis_size(("fsdp", "replica"))
    latent_count = cond.shape[0]
    local_pos = jnp.arange(tok_rows, dtype=jnp.int32)
    own_ids = latent_ids(latent_len, device_at * tok_rows + local_pos, token_total)
    pick = (own_ids[:, None] == jnp.arange(latent_count, dtype=jnp.int32)[None, :]).astype(
        jnp.float32
    )
    plan = attention_plan(latent_len, tok_rows, lax.axis_size("replica"), device_at)
    layers = (
        (
            first_ada_weight,
            first_ada_bias,
            first_qkv_weight,
            first_qkv_bias,
            first_out_weight,
            first_out_bias,
            first_up_weight,
            first_up_bias,
            first_down_weight,
            first_down_bias,
        ),
        (
            second_ada_weight,
            second_ada_bias,
            second_qkv_weight,
            second_qkv_bias,
            second_out_weight,
            second_out_bias,
            second_up_weight,
            second_up_bias,
            second_down_weight,
            second_down_bias,
        ),
    )
    col_width = first_ada_weight.shape[0]
    own_cond = lax.dynamic_slice_in_dim(
        cond.astype(jnp.float32), group_place * col_width, col_width, 1
    )
    own_silu = jax.nn.silu(own_cond).astype(jnp.bfloat16)
    partial_terms = []
    for params in layers:
        term = low_dot(own_silu, params[0])
        bias_share = params[1].astype(jnp.float32)
        spread = lax.dynamic_update_slice_in_dim(
            jnp.zeros((term.shape[1],), jnp.float32),
            bias_share,
            group_place * bias_share.shape[0],
            0,
        )
        partial_terms.append(term + spread[None, :])
    (mod_first, mod_second), biases, attention_weights = modulation(partial_terms, layers)
    mod_tokens = (
        jnp.dot(pick, mod_first, precision=HIGH, preferred_element_type=jnp.float32),
        jnp.dot(pick, mod_second, precision=HIGH, preferred_element_type=jnp.float32),
    )
    stream = tokens.astype(jnp.float32)
    inputs = []
    kept = []
    whole = lambda value: lax.all_gather(value, "fsdp", axis=0, tiled=True)
    fulls = []
    in_first = sent_ahead((first_up_weight,), mod_first) if on_planes() else ()
    for layer_at, params in enumerate(layers):
        inputs.append(stream)
        ahead = layers[layer_at + 1] if layer_at + 1 < len(layers) else None
        qkv_w, out_w = attention_weights
        qkv_b, out_b, up_b, down_b = biases[layer_at]
        shards_first, shards_second, shards_ahead, up_w, down_w = (), (), (), None, None
        if on_planes():
            shards_first = (params[8],)
            shards_second = () if ahead is None else (ahead[2], ahead[4])
            shards_ahead = () if ahead is None else (ahead[6],)
        else:
            up_w, down_w = whole(params[6]), whole(params[8])
        full = (qkv_w, qkv_b, out_w, out_b, up_w, up_b, down_w, down_b)
        stream, saved, full, attention_weights, in_first = layer_forward(
            stream, mod_tokens[layer_at], full, plan, in_first, shards_first, shards_second, shards_ahead, 7 + 2 * layer_at
        )
        fulls.append(full)
        if ahead is not None and not on_planes():
            attention_weights = [whole(ahead[at]) for at in (2, 4)]
        kept.append(saved)
    output = stream.astype(jnp.bfloat16)
    grad_stream = cotangent.astype(jnp.float32)
    weight_pairs = [None, None]
    mod_grads = [None, None]
    bias_grads = [None, None]
    for layer_at in (1, 0):
        grad_stream, grad_mod, local_grads, local_biases = layer_backward(
            inputs[layer_at], mod_tokens[layer_at], fulls[layer_at], kept[layer_at], plan, pick, grad_stream
        )
        weight_pairs[layer_at] = local_grads
        mod_grads[layer_at] = grad_mod
        bias_grads[layer_at] = local_biases
    sums, (grad_mod_first, grad_mod_second) = owner_sums(weight_pairs, mod_grads, bias_grads)
    grad_silu = jnp.zeros(own_cond.shape, jnp.float32)
    ada_grads = []
    for params, grad_mod in zip(layers, (grad_mod_first, grad_mod_second)):
        low_mod = grad_mod.astype(jnp.bfloat16)
        weight_grad = jnp.einsum("ld,lm->dm", own_silu, low_mod, preferred_element_type=jnp.float32)
        column_sums = jnp.sum(low_mod.astype(jnp.float32), axis=0)
        bias_rows = params[1].shape[0]
        bias_grad = lax.dynamic_slice_in_dim(column_sums, group_place * bias_rows, bias_rows, 0)
        grad_silu = grad_silu + jnp.einsum(
            "lm,dm->ld", low_mod, params[0], preferred_element_type=jnp.float32
        )
        ada_grads.append((weight_grad, bias_grad))
    _, silu_back = jax.vjp(jax.nn.silu, own_cond)
    cond_grad = silu_back(grad_silu)[0]
    outs = [output, grad_stream, cond_grad]
    for layer_at in range(2):
        outs += list(ada_grads[layer_at])
        for weight, bias in zip(*sums[layer_at]):
            outs += [weight, bias]
    return tuple(outs)


def solution(mesh):
    in_specs = (
        P(("fsdp", "replica"), None),
        P(),
        P(),
        P("fsdp", None),
        P("fsdp"),
        P("fsdp", None),
        P("fsdp"),
        P("fsdp", None),
        P("fsdp"),
        P("fsdp", None),
        P("fsdp"),
        P("fsdp", None),
        P("fsdp"),
        P("fsdp", None),
        P("fsdp"),
        P("fsdp", None),
        P("fsdp"),
        P("fsdp", None),
        P("fsdp"),
        P("fsdp", None),
        P("fsdp"),
        P("fsdp", None),
        P("fsdp"),
        P(("fsdp", "replica"), None),
    )
    out_specs = (
        P(("fsdp", "replica"), None),
        P(("fsdp", "replica"), None),
        P(None, "fsdp"),
        P("fsdp", None),
        P("fsdp"),
        P("fsdp", None),
        P("fsdp"),
        P("fsdp", None),
        P("fsdp"),
        P("fsdp", None),
        P("fsdp"),
        P("fsdp", None),
        P("fsdp"),
        P("fsdp", None),
        P("fsdp"),
        P("fsdp", None),
        P("fsdp"),
        P("fsdp", None),
        P("fsdp"),
        P("fsdp", None),
        P("fsdp"),
        P("fsdp", None),
        P("fsdp"),
    )
    return jax.shard_map(shards, mesh=mesh, in_specs=in_specs, out_specs=out_specs, check_vma=False)
```

```python
import functools
import math

import jax
import jax.numpy as jnp
from jax import lax
from jax.experimental import pallas as pl
from jax.experimental.pallas import tpu as pltpu
from jax.sharding import PartitionSpec as P

HEADS = 16
HEAD_DIM = 72
MAXLEN = 1024
NORM_EPS = 1e-06
HIGH = lax.Precision.HIGHEST
BQ = 256
BK = 256
LANES = 128
NEG = -1e30
VM = pl.BlockSpec(memory_space=pltpu.VMEM)
SM = pl.BlockSpec(memory_space=pltpu.SMEM)
HB = pl.BlockSpec(memory_space=pl.ANY)
VMEM_LIMIT = 56 * 1024 * 1024


def pad_to(size, unit):
    return -(-size // unit) * unit


def take_head(ref, rows, at, dim):
    first, off = at // LANES * LANES, at % LANES
    wide = LANES if off + dim <= LANES else 2 * LANES
    block = ref[rows, first : first + wide].astype(jnp.float32)
    if off:
        block = pltpu.roll(block, wide - off, 1)
    block = block[:, :LANES]
    lane = lax.broadcasted_iota(jnp.int32, block.shape, 1)
    return jnp.where(lane < dim, block, 0.0)


def put_heads(blocks, places, width):
    tiles = [None] * (width // LANES)
    for block, at in zip(blocks, places):
        first, off = at // LANES, at % LANES
        wide = jnp.concatenate([block, jnp.zeros_like(block)], axis=1)
        if off:
            wide = pltpu.roll(wide, off, 1)
        for step in range(2):
            part = wide[:, step * LANES : (step + 1) * LANES]
            if first + step < len(tiles):
                old = tiles[first + step]
                tiles[first + step] = part if old is None else old + part
    rows = blocks[0].shape[0]
    return jnp.concatenate(
        [jnp.zeros((rows, LANES), jnp.float32) if t is None else t for t in tiles], axis=1
    )


def nt_dot(left, right):
    return lax.dot_general(left, right, (((1,), (1,)), ((), ())), preferred_element_type=jnp.float32)


def nn_dot(left, right):
    return jnp.dot(left, right, preferred_element_type=jnp.float32)


def rows_at(block, size):
    return pl.ds(pl.multiple_of(block * size, size), size)


def over_window(lo, hi, prev, own, after, action):
    edge, mid = prev.shape[0] // BK, own.shape[0] // BK

    def run(ref, first, count):
        def body(at, carry):
            action(ref, at - first, at)
            return carry

        lax.fori_loop(jnp.clip(lo, first, first + count), jnp.clip(hi, first, first + count), body, 0)

    run(prev, 0, edge)
    run(own, edge, mid)
    run(after, edge + mid, edge)


def attend_kernel(nh, hd, lo, hi, prev, own, after, kid, qid, o_ref, ot_ref, lse_ref, kh, vt, qh, acc, ml):
    dim = hd // nh
    width = o_ref.shape[1]
    count = own.shape[0] // BQ
    scale = math.log2(math.e) / math.sqrt(dim)

    def load(ref, at, to):
        for h in range(nh):
            kh[h, rows_at(to, BK), :] = take_head(ref, rows_at(at, BK), h * dim, dim).astype(jnp.bfloat16)
            vt[h, :, rows_at(to, BK)] = take_head(ref, rows_at(at, BK), hd + h * dim, dim).T.astype(jnp.bfloat16)

    over_window(lo[0], hi[count - 1], prev, own, after, load)
    lse_ref[...] = jnp.zeros_like(lse_ref)

    def query_block(qb, carry):
        rows = rows_at(qb, BQ)
        for h in range(nh):
            qh[h] = take_head(own, rows, 2 * hd + h * dim, dim).astype(jnp.bfloat16)
        acc[...] = jnp.zeros_like(acc)
        ml[0] = jnp.full(ml.shape[1:], NEG, jnp.float32)
        ml[1] = jnp.zeros(ml.shape[1:], jnp.float32)
        ids = qid[0:1, rows]

        def key_block(kb, inner):
            keys = rows_at(kb, BK)
            lanes = kid[keys, :]
            same = jnp.concatenate([lanes] * (BQ // LANES), axis=1) == ids
            scores = [jnp.where(same, nt_dot(kh[h, keys, :], qh[h]) * scale, NEG) for h in range(nh)]
            olds = [ml[0, h : h + 1, :] for h in range(nh)]
            tops = [jnp.maximum(old, jnp.max(s, axis=0, keepdims=True)) for old, s in zip(olds, scores)]
            probs = [jnp.exp2(s - top) for s, top in zip(scores, tops)]
            outs = [nn_dot(vt[h, :, keys], probs[h].astype(jnp.bfloat16)) for h in range(nh)]
            for h in range(nh):
                alpha = jnp.exp2(olds[h] - tops[h])
                ml[0, h : h + 1, :] = tops[h]
                ml[1, h : h + 1, :] = ml[1, h : h + 1, :] * alpha + jnp.sum(probs[h], axis=0, keepdims=True)
                acc[h] = acc[h] * alpha + outs[h]
            return inner

        lax.fori_loop(lo[qb], hi[qb], key_block, 0)
        parts = []
        for h in range(nh):
            total = ml[1, h : h + 1, :]
            out = acc[h, :dim, :] / total
            parts.append(out)
            lse_ref[h : h + 1, rows] = ml[0, h : h + 1, :] + jnp.log2(total)
        parts.append(jnp.zeros((width - hd, BQ), jnp.float32))
        heads = jnp.concatenate(parts, axis=0)
        ot_ref[:, rows] = heads
        o_ref[rows, :] = heads.T.astype(jnp.bfloat16)
        return carry

    lax.fori_loop(0, count, query_block, 0)


def attend(nh, hd, lo, hi, prev, own, after, kid, qid):
    rows, window = own.shape[0], own.shape[0] + 2 * prev.shape[0]
    width = pad_to(hd, LANES)
    return pl.pallas_call(
        functools.partial(attend_kernel, nh, hd),
        out_shape=(
            jax.ShapeDtypeStruct((rows, width), jnp.bfloat16),
            jax.ShapeDtypeStruct((width, rows), jnp.float32),
            jax.ShapeDtypeStruct((8, rows), jnp.float32),
        ),
        in_specs=[SM, SM, VM, VM, VM, VM, VM],
        out_specs=(VM, VM, VM),
        scratch_shapes=[
            pltpu.VMEM((nh, window, LANES), jnp.bfloat16),
            pltpu.VMEM((nh, LANES, window), jnp.bfloat16),
            pltpu.VMEM((nh, BQ, LANES), jnp.bfloat16),
            pltpu.VMEM((nh, LANES, BQ), jnp.float32),
            pltpu.VMEM((2, 8, BQ), jnp.float32),
        ],
        compiler_params=pltpu.CompilerParams(vmem_limit_bytes=VMEM_LIMIT),
    )(lo, hi, prev, own, after, kid, qid)


def attend_back_kernel(
    nh, hd, lo, hi, prev, own, after, kid, qid, do_ref, ot_ref, lse_ref,
    dq_ref, dprev, down, dafter, kh, vh, kt, qh, gh, dk, dv, dqt, delta,
):
    dim = hd // nh
    width = dq_ref.shape[1]
    count = own.shape[0] // BQ
    root = 1.0 / math.sqrt(dim)
    scale = math.log2(math.e) / math.sqrt(dim)

    def load(ref, at, to):
        for h in range(nh):
            k = take_head(ref, rows_at(at, BK), h * dim, dim)
            kh[h, rows_at(to, BK), :] = k.astype(jnp.bfloat16)
            kt[h, :, rows_at(to, BK)] = k.T.astype(jnp.bfloat16)
            vh[h, rows_at(to, BK), :] = take_head(ref, rows_at(at, BK), hd + h * dim, dim).astype(jnp.bfloat16)
            dk[h, rows_at(to, BK), :] = jnp.zeros((BK, LANES), jnp.float32)
            dv[h, rows_at(to, BK), :] = jnp.zeros((BK, LANES), jnp.float32)

    over_window(lo[0], hi[count - 1], prev, own, after, load)

    def query_block(qb, carry):
        rows = rows_at(qb, BQ)
        for h in range(nh):
            qh[h] = take_head(own, rows, 2 * hd + h * dim, dim).astype(jnp.bfloat16)
            gh[h] = take_head(do_ref, rows, h * dim, dim).astype(jnp.bfloat16)
        prod = do_ref[rows, :].astype(jnp.float32).T * ot_ref[:, rows]
        for h in range(nh):
            delta[h : h + 1, :] = jnp.sum(prod[h * dim : (h + 1) * dim], axis=0, keepdims=True)
        dqt[...] = jnp.zeros_like(dqt)
        ids = qid[0:1, rows]

        def key_block(kb, inner):
            keys = rows_at(kb, BK)
            lanes = kid[keys, :]
            same = jnp.concatenate([lanes] * (BQ // LANES), axis=1) == ids
            hs = range(nh)
            scores = [nt_dot(kh[h, keys, :], qh[h]) * scale - lse_ref[h : h + 1, rows] for h in hs]
            dps = [nt_dot(vh[h, keys, :], gh[h]) - delta[h : h + 1, :] for h in hs]
            probs = [jnp.exp2(jnp.where(same, s, NEG)) for s in scores]
            dss = [(p * dp).astype(jnp.bfloat16) for p, dp in zip(probs, dps)]
            lows = [p.astype(jnp.bfloat16) for p in probs]
            for h in hs:
                dv[h, keys, :] += nn_dot(lows[h], gh[h])
            for h in hs:
                dk[h, keys, :] += nn_dot(dss[h], qh[h])
            for h in hs:
                dqt[h] += nn_dot(kt[h, :, keys], dss[h])
            return inner

        lax.fori_loop(lo[qb], hi[qb], key_block, 0)
        parts = [dqt[h, :dim, :] * root for h in range(nh)]
        parts.append(jnp.zeros((width - hd, BQ), jnp.float32))
        dq_ref[rows, :] = jnp.concatenate(parts, axis=0).T.astype(jnp.bfloat16)
        return carry

    lax.fori_loop(0, count, query_block, 0)
    for ref in (dprev, dafter):
        ref[...] = jnp.zeros_like(ref)

    def store(ref, at, to):
        keys = rows_at(to, BK)
        blocks = [dk[h, keys, :] * root for h in range(nh)] + [dv[h, keys, :] for h in range(nh)]
        ref[rows_at(at, BK), :] = put_heads(blocks, [h * dim for h in range(2 * nh)], ref.shape[1]).astype(ref.dtype)

    over_window(lo[0], hi[count - 1], dprev, down, dafter, store)


def attend_back(nh, hd, lo, hi, prev, own, after, kid, qid, grad, ot, lse):
    rows, edge = own.shape[0], prev.shape[0]
    window = rows + 2 * edge
    width, kv = pad_to(hd, LANES), prev.shape[1]
    heads = lambda size, dtype: pltpu.VMEM((nh, size, LANES), dtype)
    return pl.pallas_call(
        functools.partial(attend_back_kernel, nh, hd),
        out_shape=(
            jax.ShapeDtypeStruct((rows, width), jnp.bfloat16),
            jax.ShapeDtypeStruct((edge, kv), jnp.bfloat16),
            jax.ShapeDtypeStruct((rows, kv), jnp.bfloat16),
            jax.ShapeDtypeStruct((edge, kv), jnp.bfloat16),
        ),
        in_specs=[SM, SM] + [VM] * 8,
        out_specs=(VM,) * 4,
        scratch_shapes=[
            heads(window, jnp.bfloat16),
            heads(window, jnp.bfloat16),
            pltpu.VMEM((nh, LANES, window), jnp.bfloat16),
            heads(BQ, jnp.bfloat16),
            heads(BQ, jnp.bfloat16),
            heads(window, jnp.float32),
            heads(window, jnp.float32),
            pltpu.VMEM((nh, LANES, BQ), jnp.float32),
            pltpu.VMEM((8, BQ), jnp.float32),
        ],
        compiler_params=pltpu.CompilerParams(vmem_limit_bytes=VMEM_LIMIT),
    )(lo, hi, prev, own, after, kid, qid, grad, ot, lse)


MESH = pl.DeviceIdType.MESH


def greet(partners, count):
    barrier = pltpu.get_barrier_semaphore()
    for where, there in partners:
        @pl.when(there)
        def _():
            pl.semaphore_signal(barrier, inc=1, device_id=where, device_id_type=MESH)
    pl.semaphore_wait(barrier, count)


def wait_for(ref, sem):
    pltpu.make_async_copy(ref, ref, sem).wait()


def assemble(rows, width, pieces):
    tiles = [None] * (width // LANES)
    for ref, src, dst, count in pieces:
        off, to = src % LANES, dst % LANES
        wide = max(off + count, to + count)
        wide, have = pad_to(wide, LANES), pad_to(off + count, LANES)
        first = src // LANES * LANES
        block = ref[rows, first : first + have].astype(jnp.float32)
        lane = lax.broadcasted_iota(jnp.int32, block.shape, 1)
        block = jnp.where(jnp.logical_and(lane >= off, lane < off + count), block, 0.0)
        if wide > have:
            block = jnp.concatenate([block, jnp.zeros((block.shape[0], wide - have), jnp.float32)], axis=1)
        if off != to:
            block = pltpu.roll(block, (to - off) % wide, 1)
        for step in range(pad_to(to + count, LANES) // LANES):
            part = block[:, step * LANES : (step + 1) * LANES]
            at = dst // LANES + step
            tiles[at] = part if tiles[at] is None else tiles[at] + part
    size = next(t for t in tiles if t is not None).shape
    return jnp.concatenate([jnp.zeros(size, jnp.float32) if t is None else t for t in tiles], axis=1)


def by_rows(size, action, step=64):
    def body(at, carry):
        action(pl.ds(pl.multiple_of(at * step, step), step))
        return carry

    lax.fori_loop(0, size // step, body, 0)


class Gather:
    COPIES = 9

    def __init__(self, shards, fulls, halves, send, recv, load, store, *held):
        self.shards, self.fulls, self.halves, self.held = shards, fulls, halves, held
        self.send, self.recv, self.load, self.store = send, recv, load, store
        self.f, self.r = lax.axis_index("fsdp"), lax.axis_index("replica")
        f = self.f
        c, x, y = lax.rem(f, 2), lax.rem(f // 2, 2), f // 4
        self.core, self.x, self.y = f + 1 - 2 * c, f + 2 - 4 * x, f + 4 - 8 * y
        self.xy = self.x + 4 - 8 * y

    def rows(self, at, which):
        rows, half = self.shards[at][0].shape[0], self.halves[at]
        return {"all": (0, rows), "top": (0, half), "low": (half, rows - half)}[which]

    def part(self, at, place, which):
        first, size = self.rows(at, which)
        rows = self.shards[at][0].shape[0]
        return self.fulls[at].at[pl.ds(pl.multiple_of(place * rows + first, 16), size), :]

    def remote(self, at, kind, src, dst, to):
        return pltpu.make_async_remote_copy(
            src_ref=src, dst_ref=dst, send_sem=self.send.at[at, kind],
            recv_sem=self.recv.at[at, kind], device_id=(to, self.r), device_id_type=MESH,
        )

    def copy(self, at, kind, place, which, to, source=None):
        dst = self.part(at, place, which)
        src = dst if source is None else self.held[at].at[source, pl.ds(*self.rows(at, which)), :]
        return self.remote(at, kind, src, dst, to)

    def hop(self, at, source):
        return self.remote(at, 6 + source, self.held[at].at[0], self.held[at].at[source], (self.x, self.y)[source - 1])

    def keep(self, at, source):
        place = (self.f, self.x, self.y)[source]
        return pltpu.make_async_copy(self.held[at].at[source], self.part(at, place, "all"), self.store.at[at, source])

    def fetch(self, at, source):
        return pltpu.make_async_copy(self.shards[at][source], self.held[at].at[source], self.load.at[at, source])

    def pass_on(self, at, source):
        place = (self.f, self.x, self.y)[source]
        self.copy(at, 2 + source, place, "all", self.core, source).start()
        self.keep(at, source).start()

    def begin(self):
        places = range(len(self.shards))
        for at in places:
            for source in range(len(self.shards[at])):
                self.fetch(at, source).start()
        for at in places:
            self.fetch(at, 0).wait()
            if len(self.shards[at]) == 1:
                self.hop(at, 1).start()
                self.hop(at, 2).start()
        for at in places:
            self.pass_on(at, 0)

    def onward(self, at):
        ahead = len(self.shards[at]) == 3
        self.fetch(at, 1).wait() if ahead else self.hop(at, 1).wait_recv()
        self.copy(at, 0, self.x, "top", self.y, 1).start()
        self.fetch(at, 2).wait() if ahead else self.hop(at, 2).wait_recv()
        self.copy(at, 1, self.y, "low", self.x, 2).start()
        self.pass_on(at, 1)
        self.pass_on(at, 2)

    def across(self, at):
        self.copy(at, 0, self.xy, "top", self.y).wait_recv()
        self.copy(at, 5, self.xy, "top", self.core).start()
        self.copy(at, 1, self.xy, "low", self.x).wait_recv()
        self.copy(at, 6, self.xy, "low", self.core).start()

    def end(self, at):
        for source in range(3):
            self.keep(at, source).wait()
            if source and len(self.shards[at]) == 1:
                self.hop(at, source).wait_send()
        for kind, which in ((0, "top"), (1, "low"), (2, "all"), (3, "all"), (4, "all"), (5, "top"), (6, "low")):
            self.copy(at, kind, self.f, which, self.core).wait_send()
            if kind >= 2:
                self.copy(at, kind, self.f, which, self.core).wait_recv()


def sent_ahead(shards, after):
    shards, _ = lax.optimization_barrier((shards, after))
    hop = lambda shard, step: lax.ppermute(shard, "fsdp", [(at, at ^ step) for at in range(8)])
    return [(shard, hop(shard, 2), hop(shard, 4)) for shard in shards]


def split_shards(refs, sizes):
    shards = []
    for size in sizes:
        shards.append(refs[:size])
        refs = refs[size:]
    return shards, refs


def gather_scratch(shards):
    count = len(shards)
    if not count:
        return []
    return [
        pltpu.SemaphoreType.DMA((count, Gather.COPIES)),
        pltpu.SemaphoreType.DMA((count, Gather.COPIES)),
        pltpu.SemaphoreType.DMA((count, 3)),
        pltpu.SemaphoreType.DMA((count, 3)),
    ] + [pltpu.VMEM((3, *part.shape), part.dtype) for part, *_ in shards]


def gathered_shapes(shards):
    return tuple(jax.ShapeDtypeStruct((8 * part.shape[0], part.shape[1]), part.dtype) for part, *_ in shards)


def halves_of(shards):
    halves, ahead = [], 0
    for part, *_ in shards:
        rows, size = part.shape
        half = rows // 32 * 16
        if rows % 32 and ahead <= 0:
            half += 16
        ahead += (2 * half - rows) * size
        halves.append(half)
    return tuple(halves), tuple(len(shard) for shard in shards)


def start_kernel(plan, part_in, bias_in, *refs):
    halves, sizes = plan
    count = len(halves)
    shards, refs = split_shards(refs, sizes)
    (mod, bias), fulls, refs = refs[:2], refs[2 : count + 2], refs[count + 2 :]
    terms, total, m_s, m_r, b_s, b_r, t_s, t_r, keep, *sems = refs
    f, r = lax.axis_index("fsdp"), lax.axis_index("replica")
    others = [lax.rem(f + d, 8) for d in range(1, 8)]
    greet([((there, r), True) for there in others], 7)

    def remote(src, dst, s_sem, r_sem, there):
        return pltpu.make_async_remote_copy(
            src_ref=src, dst_ref=dst, send_sem=s_sem, recv_sem=r_sem, device_id=(there, r), device_id_type=MESH
        )

    def term_copy(block, source, there):
        return remote(part_in.at[block], terms.at[source], t_s.at[there], t_r.at[source], there)

    def bias_copy(source, there):
        return remote(bias_in, bias.at[source], b_s.at[there], b_r.at[source], there)

    def mod_copy(source, there):
        return remote(total, mod.at[source], m_s.at[there], m_r.at[source], there)

    gather = Gather(shards, fulls, halves, *sems)
    for there in others:
        term_copy(there, f, there).start()
    mine = pltpu.make_async_copy(part_in.at[f], terms.at[f], keep.at[0])
    mine.start()
    gather.begin()
    for there in others:
        bias_copy(f, there).start()
    own_bias = pltpu.make_async_copy(bias_in, bias.at[f], keep.at[1])
    own_bias.start()
    mine.wait()
    for there in others:
        term_copy(f, there, there).wait_recv()
    total[...] = functools.reduce(lambda a, b: a + b, [terms[j] for j in range(8)])
    for there in others:
        mod_copy(f, there).start()
    own_mod = pltpu.make_async_copy(total, mod.at[f], keep.at[2])
    own_mod.start()
    for at in range(count):
        gather.onward(at)
    for at in range(count):
        gather.across(at)
    for at in range(count):
        gather.end(at)
    own_bias.wait()
    own_mod.wait()
    for there in others:
        term_copy(there, f, there).wait_send()
        bias_copy(f, there).wait_send()
        mod_copy(f, there).wait_send()
        bias_copy(there, there).wait_recv()
        mod_copy(there, there).wait_recv()


def start(parts, biases, shards, collective_id):
    sem = lambda: pltpu.SemaphoreType.DMA((8,))
    return pl.pallas_call(
        functools.partial(start_kernel, halves_of(shards)),
        out_shape=(
            jax.ShapeDtypeStruct(parts.shape, parts.dtype),
            jax.ShapeDtypeStruct((8, *biases.shape), biases.dtype),
            *gathered_shapes(shards),
        ),
        in_specs=[HB] * (2 + sum(len(shard) for shard in shards)),
        out_specs=(HB,) * (2 + len(shards)),
        scratch_shapes=[
            pltpu.VMEM(parts.shape, parts.dtype), pltpu.VMEM(parts.shape[1:], parts.dtype),
            sem(), sem(), sem(), sem(), sem(), sem(), pltpu.SemaphoreType.DMA((3,)), *gather_scratch(shards),
        ],
        compiler_params=pltpu.CompilerParams(
            collective_id=collective_id, has_side_effects=True, vmem_limit_bytes=VMEM_LIMIT
        ),
    )(parts, biases, *(part for shard in shards for part in shard))


def to_heads_kernel(reps, size, edge, kv, plan, qkv, *refs):
    halves, sizes = plan
    count = len(halves)
    shards, refs = split_shards(refs, sizes)
    (own, prev, after), fulls, refs = refs[:3], refs[3 : count + 3], refs[count + 3 :]
    x_ref, send, recv, edge_send, edge_recv, *sems = refs
    gather = Gather(shards, fulls, halves, *sems) if count else None
    group, me = lax.axis_index("fsdp"), lax.axis_index("replica")
    groups = lax.axis_size("fsdp")
    wide = x_ref.shape[2]
    width = qkv.shape[1] // 3
    hd = width // reps
    for place in range(reps):
        def pack(rows, place=place):
            at = place * hd
            pieces = [(qkv, width + at, 0, hd), (qkv, 2 * width + at, hd, hd), (qkv, at, 2 * hd, hd)]
            x_ref[place, rows, :] = assemble(rows, wide, pieces).astype(jnp.bfloat16)

        by_rows(size, pack)
    down, up = group > 0, group < groups - 1
    others = [(group, lax.rem(me + d, reps)) for d in range(1, reps)]
    greet(
        [(place, True) for place in others] + [((group - 1, me), down), ((group + 1, me), up)]
        + ([((there, me), True) for there in (gather.core, gather.x, gather.y)] if count else []),
        reps - 1 + down.astype(jnp.int32) + up.astype(jnp.int32) + (3 if count else 0),
    )
    spans = [pl.ds(0, kv), pl.ds(kv, wide - kv)] if wide > kv else [pl.ds(0, kv)]

    def exchange(span, part, there):
        return pltpu.make_async_remote_copy(
            src_ref=x_ref.at[there, :, span], dst_ref=own.at[me, :, span], send_sem=send.at[part, there],
            recv_sem=recv.at[part, me], device_id=(group, there), device_id_type=MESH,
        )

    for part, span in enumerate(spans):
        for _, there in others:
            exchange(span, part, there).start()
        pltpu.make_async_copy(x_ref.at[me, :, span], own.at[me, :, span], recv.at[part, me]).start()

    if count:
        gather.begin()
    for at in range(count):
        gather.onward(at)

    def edges(piece, action):
        lo, hi = piece * size, (piece + 1) * size
        total = reps * size
        if lo >= total - edge:
            @pl.when(up)
            def _():
                action(0, piece, (group + 1, me), prev.at[pl.ds(lo - (total - edge), size), :])
        if hi <= edge:
            @pl.when(down)
            def _():
                action(1, piece, (group - 1, me), after.at[pl.ds(lo, size), :])

    def start_edge(way, piece, where, target):
        pltpu.make_async_remote_copy(
            src_ref=own.at[piece, :, spans[0]], dst_ref=target, send_sem=edge_send.at[way, piece],
            recv_sem=edge_recv.at[way, piece], device_id=where, device_id_type=MESH,
        ).start()

    def end_send(way, piece, where, target):
        wait_for(own.at[piece, :, spans[0]], edge_send.at[way, piece])

    def end_recv(way, piece, where, target):
        wait_for(target, edge_recv.at[way, piece])

    for piece in range(reps):
        wait_for(own.at[piece, :, spans[0]], recv.at[0, piece])
        edges(piece, start_edge)
    if len(spans) > 1:
        for piece in range(reps):
            wait_for(own.at[piece, :, spans[1]], recv.at[1, piece])
    for at in range(count):
        gather.across(at)
    for part, span in enumerate(spans):
        for _, there in others:
            wait_for(x_ref.at[there, :, span], send.at[part, there])
    for piece in range(reps):
        edges(piece, end_send)
        lo, hi = piece * size, (piece + 1) * size
        total = reps * size
        if lo >= total - edge:
            @pl.when(down)
            def _():
                wait_for(prev.at[pl.ds(lo - (total - edge), size), :], edge_recv.at[0, piece])
        if hi <= edge:
            @pl.when(up)
            def _():
                wait_for(after.at[pl.ds(lo, size), :], edge_recv.at[1, piece])
    for at in range(count):
        gather.end(at)


def to_heads(qkv, reps, edge, kv, shards, collective_id):
    size, wide = qkv.shape[0], pad_to(qkv.shape[1] // reps, LANES)
    sems = pltpu.SemaphoreType.DMA((2, reps))
    own, prev, after, *fulls = pl.pallas_call(
        functools.partial(to_heads_kernel, reps, size, edge, kv, halves_of(shards)),
        out_shape=(
            jax.ShapeDtypeStruct((reps, size, wide), qkv.dtype),
            jax.ShapeDtypeStruct((edge, kv), qkv.dtype),
            jax.ShapeDtypeStruct((edge, kv), qkv.dtype),
            *gathered_shapes(shards),
        ),
        in_specs=[VM] + [HB] * sum(len(shard) for shard in shards),
        out_specs=(HB,) * (3 + len(shards)),
        scratch_shapes=[pltpu.VMEM((reps, size, wide), qkv.dtype), sems, sems, sems, sems, *gather_scratch(shards)],
        compiler_params=pltpu.CompilerParams(
            collective_id=collective_id, has_side_effects=True, vmem_limit_bytes=VMEM_LIMIT
        ),
    )(qkv, *(part for shard in shards for part in shard))
    return own.reshape(reps * size, wide), prev, after, fulls


def swap_kernel(reps, out, plan, x_ref, *refs):
    halves, sizes = plan
    count = len(halves)
    shards, refs = split_shards(refs, sizes)
    y_ref, fulls, (held, send, recv, *sems) = refs[0], refs[1 : count + 1], refs[count + 1 :]
    gather = Gather(shards, fulls, halves, *sems) if count else None
    group, me = lax.axis_index("fsdp"), lax.axis_index("replica")
    others = [(group, lax.rem(me + d, reps)) for d in range(1, reps)]
    planar = [(there, me) for there in (gather.core, gather.x, gather.y)] if count else []
    size, lanes = held.shape[1:]
    if out:
        src, dst = x_ref, held
        hd = y_ref.shape[1] // reps
    else:
        src, dst = held, y_ref
        hd = x_ref.shape[1] // reps
        for place in range(reps):
            def pack(rows, place=place):
                held[place, rows, :] = assemble(rows, lanes, [(x_ref, place * hd, 0, hd)]).astype(jnp.bfloat16)

            by_rows(size, pack)
    greet([(place, True) for place in others + planar], reps - 1 + len(planar))
    for _, there in others:
        pltpu.make_async_remote_copy(
            src_ref=src.at[there], dst_ref=dst.at[me], send_sem=send.at[there], recv_sem=recv.at[me],
            device_id=(group, there), device_id_type=MESH,
        ).start()
    pltpu.make_async_copy(src.at[me], dst.at[me], recv.at[me]).start()
    if count:
        gather.begin()
    for at in range(count):
        gather.onward(at)
    for at in range(count):
        gather.across(at)
    for piece in range(reps):
        wait_for(dst.at[piece], recv.at[piece])
    if out:
        def unpack(rows):
            pieces = [(held.at[place], 0, place * hd, hd) for place in range(reps)]
            y_ref[rows, :] = assemble(rows, y_ref.shape[1], pieces).astype(jnp.bfloat16)

        by_rows(size, unpack)
    for _, there in others:
        wait_for(src.at[there], send.at[there])
    for at in range(count):
        gather.end(at)


def swap(x, reps, out, shards, collective_id):
    if out:
        size, lanes = x.shape[0] // reps, x.shape[1]
        x = x.reshape(reps, size, lanes)
        shape = (size, HEADS * HEAD_DIM)
    else:
        size, lanes = x.shape[0], pad_to(x.shape[1] // reps, LANES)
        shape = (reps, size, lanes)
    sems = pltpu.SemaphoreType.DMA((reps,))
    swapped, *fulls = pl.pallas_call(
        functools.partial(swap_kernel, reps, out, halves_of(shards)),
        out_shape=(jax.ShapeDtypeStruct(shape, x.dtype), *gathered_shapes(shards)),
        in_specs=[HB if out else VM] + [HB] * sum(len(shard) for shard in shards),
        out_specs=(VM if out else HB,) + (HB,) * len(shards),
        scratch_shapes=[pltpu.VMEM((reps, size, lanes), x.dtype), sems, sems, *gather_scratch(shards)],
        compiler_params=pltpu.CompilerParams(
            collective_id=collective_id, has_side_effects=True, vmem_limit_bytes=VMEM_LIMIT
        ),
    )(x, *(part for shard in shards for part in shard))
    return swapped, fulls


def from_heads_kernel(reps, size, edge, dprev, own, dafter, dq, out, out_kv, out_q, from_up, from_down, total, mine, sends, recvs, send, recv):
    group, me = lax.axis_index("fsdp"), lax.axis_index("replica")
    groups = lax.axis_size("fsdp")
    rows = reps * size
    down, up = group > 0, group < groups - 1
    others = [(group, lax.rem(me + d, reps)) for d in range(1, reps)]
    greet(
        [(place, True) for place in others] + [((group - 1, me), down), ((group + 1, me), up)],
        reps - 1 + down.astype(jnp.int32) + up.astype(jnp.int32),
    )
    to_down = pltpu.make_async_remote_copy(
        src_ref=dprev, dst_ref=from_up, send_sem=sends.at[0], recv_sem=recvs.at[0],
        device_id=(group - 1, me), device_id_type=MESH,
    )
    to_up = pltpu.make_async_remote_copy(
        src_ref=dafter, dst_ref=from_down, send_sem=sends.at[1], recv_sem=recvs.at[1],
        device_id=(group + 1, me), device_id_type=MESH,
    )
    pl.when(down)(to_down.start)
    pl.when(up)(to_up.start)
    for _, there in others:
        pltpu.make_async_remote_copy(
            src_ref=dq.at[pl.ds(pl.multiple_of(there * size, size), size), :], dst_ref=out_q.at[me], send_sem=send.at[0, there],
            recv_sem=recv.at[0, me], device_id=(group, there), device_id_type=MESH,
        ).start()
    pltpu.make_async_copy(dq.at[pl.ds(pl.multiple_of(me * size, size), size), :], out_q.at[me], recv.at[0, me]).start()
    step = math.gcd(edge, 256)

    def chunk(at, carry):
        here = pl.ds(pl.multiple_of(at * step, step), step)
        total[here, :] = own[here, :].astype(jnp.float32)
        return carry

    lax.fori_loop(0, rows // step, chunk, 0)

    def add(ref, first):
        def body(at, carry):
            here = pl.ds(pl.multiple_of(first + at * step, step), step)
            there = pl.ds(pl.multiple_of(at * step, step), step)
            total[here, :] += ref[there, :].astype(jnp.float32)
            return carry

        lax.fori_loop(0, edge // step, body, 0)

    @pl.when(down)
    def _():
        wait_for(from_down, recvs.at[1])
        add(from_down, 0)

    @pl.when(up)
    def _():
        wait_for(from_up, recvs.at[0])
        add(from_up, rows - edge)

    def narrow(at, carry):
        here = pl.ds(pl.multiple_of(at * step, step), step)
        mine[here, :] = total[here, :].astype(jnp.bfloat16)
        return carry

    lax.fori_loop(0, rows // step, narrow, 0)
    for _, there in others:
        pltpu.make_async_remote_copy(
            src_ref=mine.at[pl.ds(pl.multiple_of(there * size, size), size), :], dst_ref=out_kv.at[me], send_sem=send.at[1, there],
            recv_sem=recv.at[1, me], device_id=(group, there), device_id_type=MESH,
        ).start()
    pltpu.make_async_copy(mine.at[pl.ds(pl.multiple_of(me * size, size), size), :], out_kv.at[me], recv.at[1, me]).start()
    width = out.shape[1] // 3
    hd = width // reps

    def unpack(ref, first, section):
        def body(rows):
            pieces = [(ref.at[place], first, place * hd, hd) for place in range(reps)]
            out[rows, section * width : (section + 1) * width] = assemble(rows, width, pieces).astype(jnp.bfloat16)

        by_rows(size, body)

    for piece in range(reps):
        wait_for(out_q.at[piece], recv.at[0, piece])
    unpack(out_q, 0, 0)
    for piece in range(reps):
        wait_for(out_kv.at[piece], recv.at[1, piece])
    unpack(out_kv, 0, 1)
    unpack(out_kv, hd, 2)
    for _, there in others:
        wait_for(out_q.at[0], send.at[0, there])
        wait_for(out_kv.at[0], send.at[1, there])
    pl.when(down)(to_down.wait_send)
    pl.when(up)(to_up.wait_send)


def from_heads(reps, width, dprev, own, dafter, dq, collective_id):
    rows, kv = own.shape
    edge, size = dprev.shape[0], own.shape[0] // reps
    pair, both = pltpu.SemaphoreType.DMA((2,)), pltpu.SemaphoreType.DMA((2, reps))
    return pl.pallas_call(
        functools.partial(from_heads_kernel, reps, size, edge),
        out_shape=jax.ShapeDtypeStruct((size, 3 * width), own.dtype),
        in_specs=[HB, VM, HB, HB],
        out_specs=VM,
        scratch_shapes=[
            pltpu.VMEM((reps, size, kv), own.dtype),
            pltpu.VMEM((reps, size, dq.shape[1]), own.dtype),
            pltpu.VMEM((edge, kv), own.dtype),
            pltpu.VMEM((edge, kv), own.dtype),
            pltpu.VMEM((rows, kv), jnp.float32),
            pltpu.VMEM((rows, kv), own.dtype),
            pair,
            pair,
            both,
            both,
        ],
        compiler_params=pltpu.CompilerParams(
            collective_id=collective_id, has_side_effects=True, vmem_limit_bytes=VMEM_LIMIT
        ),
    )(dprev, own, dafter, dq)


MATRICES = 12
UNIT_WIDTH = 1152
LEFT_ROWS = 4
PLACES = ((0, 0), (1, 0), (0, 1), (1, 1))


class Terms:
    def __init__(self, ins, left, right, rows, width, load_sem):
        self.left, self.right, self.rows, self.width = left, right, rows, width
        self.unit = right.shape[2]
        self.parts = width // self.unit
        f = lax.axis_index("fsdp")
        self.c, self.x, self.y = lax.rem(f, 2), lax.rem(f // 2, 2), f // 4
        self.core_at, self.x_at, self.y_at = f + 1 - 2 * self.c, f + 2 - 4 * self.x, f + 4 - 8 * self.y
        self.loads, place, slot = [], 0, 0
        for src in ins[:4]:
            self.loads.append((src, left.at[pl.ds(place, src.shape[0]), :]))
            place += src.shape[0]
        for src in ins[4:]:
            for part in range(src.shape[1] // self.unit):
                self.loads.append((src.at[:, pl.ds(part * self.unit, self.unit)], right.at[slot]))
                slot += 1
        self.load_sem = load_sem

    def start(self):
        for at, (src, dst) in enumerate(self.loads):
            pltpu.make_async_copy(src, dst, self.load_sem.at[at]).start()

    def wait(self):
        for at, (src, dst) in enumerate(self.loads):
            pltpu.make_async_copy(src, dst, self.load_sem.at[at]).wait()

    def block(self, core, mx, my):
        x, y = self.x + mx * (1 - 2 * self.x), self.y + my * (1 - 2 * self.y)
        return (y * 2 + x) * 2 + (self.c + core * (1 - 2 * self.c))

    def stack(self, u, core):
        rows, width = self.rows, self.width
        m, part = u // self.parts, lax.rem(u, self.parts)
        inside = jnp.where(
            m < 4, rows * m, LEFT_ROWS * width + jnp.where(m < 8, 0, jnp.where(m < 9, width, 2 * width))
        )
        stride = jnp.where(m < 4, 4 * rows, rows)
        other = jnp.maximum(m - 3, 0) * self.parts + part
        blocks = []
        for mx, my in PLACES:
            start = pl.multiple_of(inside + stride * self.block(core, mx, my), 16)
            blocks.append(self.left[pl.ds(start, rows), :])
        return nn_dot(jnp.concatenate(blocks, axis=0), self.right[other])


def term_scratch(ins, unit):
    width, tokens = ins[1].shape
    parts = width // unit
    return [
        pltpu.VMEM(((LEFT_ROWS + 3) * width, tokens), jnp.bfloat16),
        pltpu.VMEM((9 * parts, tokens, unit), jnp.bfloat16),
        pltpu.SemaphoreType.DMA((4 + 9 * parts,)),
    ]


def remote_copy(src, dst, s_sem, r_sem, where):
    return pltpu.make_async_remote_copy(
        src_ref=src, dst_ref=dst, send_sem=s_sem, recv_sem=r_sem, device_id=where, device_id_type=MESH
    )


def chip_kernel(width, half, *refs):
    ins, (own, xs, ys, tx, ty), refs = refs[:8], refs[8:13], refs[13:]
    left, right, load_sem, csend, crecv, own_b, xs_b, ys_b, tx_b, ty_b, core_s, core_r, out_sem = refs
    r = lax.axis_index("replica")
    count, rows = own.shape[:2]
    terms = Terms(ins, left, right, rows, width, load_sem)
    where = (terms.core_at, r)
    greet([(where, True)], 1)
    terms.start()
    terms.wait()
    bf16, f32 = jnp.bfloat16, jnp.float32

    def core_copy(u):
        pair, four = lax.rem(u, 2), lax.rem(u, 4)
        return remote_copy(csend.at[pair], crecv.at[four], core_s.at[pair], core_r.at[four], where)

    def stores(u):
        pair = lax.rem(u, 2)
        buffers = ((own_b, own), (xs_b, xs), (ys_b, ys), (tx_b, tx), (ty_b, ty))
        return [
            pltpu.make_async_copy(src.at[pair], dst.at[u], out_sem.at[at, pair]) for at, (src, dst) in enumerate(buffers)
        ]

    def close(u):
        for copy in stores(u):
            copy.wait()

    def chip(u):
        pair, four = lax.rem(u, 2), lax.rem(u, 4)
        stacked = terms.stack(u, 0)
        core_copy(u).wait()
        totals = [stacked[m * rows : (m + 1) * rows] + crecv[four, m].astype(f32) for m in range(4)]
        mine, along_x, along_y, opposite = [total.astype(bf16) for total in totals]
        own_b[pair] = mine
        xs_b[pair, 0] = along_x[:half]
        tx_b[pair] = along_x[half:]
        ty_b[pair] = along_y[:half]
        ys_b[pair, 0] = along_y[half:]
        xs_b[pair, 1] = opposite[:half]
        ys_b[pair, 1] = opposite[half:]
        for copy in stores(u):
            copy.start()

    def open_unit(u):
        pair = lax.rem(u, 2)
        csend[pair] = terms.stack(u, 1).astype(bf16).reshape(csend.shape[1:])
        core_copy(u).start()

    def step(t, carry):
        pl.when(t < count)(lambda: open_unit(t))
        pl.when(t >= 3)(lambda: close(t - 3))
        pl.when(jnp.logical_and(t >= 1, t <= count))(lambda: chip(t - 1))
        return carry

    lax.fori_loop(0, count + 3, step, 0)


def chip_sums(lefts, rights, collective_id):
    ins = (*lefts, *rights)
    width, tokens = lefts[1].shape
    rows, unit = width // 8, UNIT_WIDTH
    half = pad_to(rows // 2, 16)
    count = MATRICES * (width // unit)
    bf16 = jnp.bfloat16
    shapes = ((rows, unit), (2, half, unit), (2, rows - half, unit), (rows - half, unit), (half, unit))
    pair = pltpu.SemaphoreType.DMA((2,))
    return pl.pallas_call(
        functools.partial(chip_kernel, width, half),
        out_shape=tuple(jax.ShapeDtypeStruct((count, *shape), bf16) for shape in shapes),
        in_specs=[HB] * 8,
        out_specs=(HB,) * 5,
        scratch_shapes=[
            *term_scratch(ins, unit),
            pltpu.VMEM((2, 4, rows, unit), bf16),
            pltpu.VMEM((4, 4, rows, unit), bf16),
            *(pltpu.VMEM((2, *shape), bf16) for shape in shapes),
            pair,
            pltpu.SemaphoreType.DMA((4,)),
            pltpu.SemaphoreType.DMA((5, 2)),
        ],
        compiler_params=pltpu.CompilerParams(
            collective_id=collective_id, has_side_effects=True, vmem_limit_bytes=VMEM_LIMIT
        ),
        cost_estimate=pl.CostEstimate(flops=2 * 64 * width * width * tokens, bytes_accessed=40 << 20, transcendentals=0),
    )(*ins)


def reduce_kernel(width, half, *refs):
    ins, (extra_in, own_in, xr_in, yr_in, tx_in, ty_in), (out, mine, shared), refs = refs[:8], refs[8:14], refs[14:17], refs[17:]
    (left, right, load_sem, extra, extra_sem, cx_s, cx_r, cxs_sem, cxr_sem, share_s, share_r,
     csend, crecv, own, xs, xr, ys, yr, tx, ty, x2s, x2r, y2s, y2r, zs, z1r, z2s, z2r, fin,
     own_l, xr_l, yr_l, tx_l, ty_l, ready_sem,
     core_s, core_r, x_s, x_r, y_s, y_r, x2_s, x2_r, y2_s, y2_r, z1_s, z1_r, z2_s, z2_r, fin_l, fin_s, fin_r,
     credit) = refs
    f, r = lax.axis_index("fsdp"), lax.axis_index("replica")
    rows = own.shape[1]
    extras = extra.shape[0]
    count = extras + 2 * own_in.shape[0]
    unit = own.shape[2]
    terms = Terms(ins, left, right, rows, width, load_sem)
    core_at, x_at, y_at = terms.core_at, terms.x_at, terms.y_at
    inner = jnp.logical_and(r > 0, r < 3)
    outer = jnp.logical_not(inner)
    z_at = r + 1 - 2 * lax.rem(r, 2)
    others = [lax.rem(f + d, 8) for d in range(1, 8)]
    greet(
        [((there, r), True) for there in others] + [((f, r - 1), r > 0), ((f, r + 1), r < 3)],
        7 + (r > 0).astype(jnp.int32) + (r < 3).astype(jnp.int32),
    )
    few = extra.shape[2]
    extra_load = pltpu.make_async_copy(extra_in, extra, extra_sem)
    extra_load.start()
    terms.start()
    extra_load.wait()
    send = remote_copy
    top, low = pl.ds(0, half), pl.ds(half, rows - half)

    def core_copy(slot):
        return send(csend.at[slot], crecv.at[slot], core_s.at[slot], core_r.at[slot], (core_at, r))

    def extra_copy(u):
        return send(cx_s.at[u], cx_r.at[u], cxs_sem.at[u], cxr_sem.at[u], (core_at, r))

    def x_copy(slot):
        return send(xs.at[slot], xr.at[slot], x_s.at[slot], x_r.at[slot], (x_at, r))

    def y_copy(slot):
        return send(ys.at[slot], yr.at[slot], y_s.at[slot], y_r.at[slot], (y_at, r))

    def x2_copy(slot):
        return send(x2s.at[slot], x2r.at[slot], x2_s.at[slot], x2_r.at[slot], (x_at, r))

    def y2_copy(slot):
        return send(y2s.at[slot], y2r.at[slot], y2_s.at[slot], y2_r.at[slot], (y_at, r))

    def z1_copy(slot, to):
        return send(zs.at[slot], z1r.at[to], z1_s.at[slot], z1_r.at[to], (f, z_at))

    def z2_copy(slot):
        return send(z2s.at[slot], z2r.at[slot], z2_s.at[slot], z2_r.at[slot], (f, 3 - r))

    def target(u):
        v = u - extras
        first = pl.multiple_of((v // 2) * unit, LANES)
        return out.at[1 - lax.rem(v, 2), :, pl.ds(first, unit)]

    def fin_copy(slot, u):
        return send(fin.at[slot], target(u), fin_s.at[slot], fin_r.at[u], (f, z_at))

    def keep_copy(slot, u):
        return pltpu.make_async_copy(fin.at[slot], target(u), fin_l.at[slot])

    def fin_extra(u):
        slot = lax.rem(u, 4)
        return send(fin.at[slot, pl.ds(0, few), :], mine.at[u], fin_s.at[slot], fin_r.at[u], (f, z_at))

    def keep_extra(u):
        slot = lax.rem(u, 4)
        return pltpu.make_async_copy(fin.at[slot, pl.ds(0, few), :], mine.at[u], fin_l.at[slot])

    def share_copy(u, there, where):
        return send(
            mine.at[u], shared.at[u, there], share_s.at[u, where], share_r.at[u, there], (where, r)
        )

    def ready_copies(u):
        slot = lax.rem(u, 4)
        buffers = ((own_in, own_l), (xr_in, xr_l), (yr_in, yr_l), (tx_in, tx_l), (ty_in, ty_l))
        return [
            pltpu.make_async_copy(src.at[(u - extras) // 2], dst.at[slot], ready_sem.at[at, slot])
            for at, (src, dst) in enumerate(buffers)
        ]

    f32, bf16 = jnp.float32, jnp.bfloat16
    z_slots = z1r.shape[0]

    def stage(u, condition, body, first=0, last=count):
        live = jnp.logical_and(u >= first, u < last)
        pl.when(live if condition is None else jnp.logical_and(live, condition))(lambda: body(u))

    def share(u):
        for there in others:
            share_copy(u, f, there).start()

    def close(u):
        slot = lax.rem(u, 4)
        fin_copy(slot, u).wait_send()
        keep_copy(slot, u).wait()

    def arrive(u):
        fin_copy(lax.rem(u, 4), u).wait_recv()

    def close_extra(u):
        fin_extra(u).wait_send()
        keep_extra(u).wait()

    def arrive_extra(u):
        fin_extra(u).wait_recv()

    def finish(u):
        slot = lax.rem(u, 4)
        z2_copy(slot).wait()
        fin[slot] = (z2s[slot].astype(f32) + z2r[slot].astype(f32)).astype(bf16)

        @pl.when(u >= extras)
        def _():
            fin_copy(slot, u).start()
            keep_copy(slot, u).start()

        @pl.when(u < extras)
        def _():
            fin_extra(u).start()
            keep_extra(u).start()

    def middle(u):
        slot, z_slot, at = lax.rem(u, 4), lax.rem(u, z_slots), lax.rem(u, own.shape[0])
        z1_copy(slot, z_slot).wait_recv()
        z2s[slot] = (own[at] + z1r[z_slot].astype(f32)).astype(bf16)
        z2_copy(slot).start()

        @pl.when(u + z_slots < count)
        def _():
            pl.semaphore_signal(credit, inc=1, device_id=(f, z_at), device_id_type=MESH)

    def sent(u):
        z1_copy(lax.rem(u, 4), lax.rem(u, z_slots)).wait_send()

    def plane(u):
        slot, at = lax.rem(u, 4), lax.rem(u, own.shape[0])
        x2_copy(slot).wait()
        y2_copy(slot).wait()
        own[at, top, :] += y2r[slot].astype(f32)
        own[at, low, :] += x2r[slot].astype(f32)

        @pl.when(outer)
        def _():
            zs[slot] = own[at].astype(bf16)

            @pl.when(u >= z_slots)
            def _():
                pl.semaphore_wait(credit, 1)

            z1_copy(slot, lax.rem(u, z_slots)).start()

    def cross(u):
        slot, at = lax.rem(u, 4), lax.rem(u, own.shape[0])
        x_copy(slot).wait()
        y_copy(slot).wait()
        y2s[slot] = (ty[slot] + xr[slot, 1].astype(f32)).astype(bf16)
        y2_copy(slot).start()
        x2s[slot] = (tx[slot] + yr[slot, 1].astype(f32)).astype(bf16)
        x2_copy(slot).start()
        own[at, top, :] += xr[slot, 0].astype(f32)
        own[at, low, :] += yr[slot, 0].astype(f32)

    def cross_ready(u):
        slot, at = lax.rem(u, 4), lax.rem(u, own.shape[0])
        for copy in ready_copies(u):
            copy.wait()
        y2s[slot] = (ty_l[slot].astype(f32) + xr_l[slot, 1].astype(f32)).astype(bf16)
        y2_copy(slot).start()
        x2s[slot] = (tx_l[slot].astype(f32) + yr_l[slot, 1].astype(f32)).astype(bf16)
        x2_copy(slot).start()
        own[at, top, :] = own_l[slot, top, :].astype(f32) + xr_l[slot, 0].astype(f32)
        own[at, low, :] = own_l[slot, low, :].astype(f32) + yr_l[slot, 0].astype(f32)

    def chip(u):
        slot, at = lax.rem(u, 4), lax.rem(u, own.shape[0])
        w = (u - extras) // 2
        pair = lax.rem(w, 2)
        stacked = terms.stack(w, 0)
        core_copy(pair).wait()
        total = stacked[3 * rows :] + crecv[pair, 3].astype(f32)
        xs[slot, 1] = total[:half].astype(bf16)
        ys[slot, 1] = total[half:].astype(bf16)
        total = stacked[rows : 2 * rows] + crecv[pair, 1].astype(f32)
        xs[slot, 0] = total[:half].astype(bf16)
        tx[slot] = total[half:]
        x_copy(slot).start()
        total = stacked[2 * rows : 3 * rows] + crecv[pair, 2].astype(f32)
        ys[slot, 0] = total[half:].astype(bf16)
        ty[slot] = total[:half]
        y_copy(slot).start()
        own[at] = stacked[:rows] + crecv[pair, 0].astype(f32)

    def chip_extra(u):
        slot, at = lax.rem(u, 4), lax.rem(u, own.shape[0])
        extra_copy(u).wait()
        for m, (mx, my) in enumerate(PLACES):
            total = extra[u, terms.block(0, mx, my)] + cx_r[u, m].astype(f32)
            if m == 0:
                own[at, :few, :] = total
            elif m == 2:
                ty[slot, :few, :] = total
            else:
                xs[slot, m // 2, :few, :] = total.astype(bf16)
        x_copy(slot).start()
        y_copy(slot).start()

    def open_extra(u):
        for m, (mx, my) in enumerate(PLACES):
            cx_s[u, m] = extra[u, terms.block(1, mx, my)].astype(bf16)
        extra_copy(u).start()

    def open_ready(u):
        for copy in ready_copies(u):
            copy.start()

    def open_unit(u):
        w = (u - extras) // 2
        pair = lax.rem(w, 2)
        csend[pair] = terms.stack(w, 1).astype(bf16).reshape(csend.shape[1:])
        core_copy(pair).start()

    def full(u):
        return lax.rem(u - extras, 2) == 1

    def prepared(u):
        return lax.rem(u - extras, 2) == 0

    def step(t, carry):
        stage(t - 13, None, share, 0, extras)
        stage(t - 12, inner, close, extras)
        stage(t - 12, outer, arrive, extras)
        stage(t - 12, inner, close_extra, 0, extras)
        stage(t - 12, outer, arrive_extra, 0, extras)
        stage(t - 10, inner, finish)
        stage(t - 8, inner, middle)
        stage(t - 8, outer, sent)
        stage(t - 6, None, plane)
        stage(t - 4, full(t - 4), cross, extras)
        stage(t - 4, None, cross, 0, extras)
        stage(t - 4, prepared(t - 4), cross_ready, extras)
        stage(t - 2, full(t - 2), chip, extras)
        stage(t - 2, None, chip_extra, 0, extras)
        pl.when(t == extras)(terms.wait)
        stage(t, full(t), open_unit, extras)
        stage(t, prepared(t), open_ready, extras)
        stage(t, None, open_extra, 0, extras)
        return carry

    lax.fori_loop(0, count + 12, step, 0)
    for u in range(extras):
        for there in others:
            share_copy(u, f, there).wait_send()
            share_copy(u, there, there).wait_recv()


def reduce_grads(lefts, rights, ready, extra):
    width, tokens = lefts[1].shape
    rows, unit = width // 8, UNIT_WIDTH
    half = pad_to(rows // 2, 16)
    ins = (*lefts, *rights)
    extras, _, few, _ = extra.shape
    count = extras + ready[0].shape[0] + MATRICES * (width // unit)
    bf16, f32 = jnp.bfloat16, jnp.float32
    buf = lambda dtype, *shape: pltpu.VMEM((*shape, unit), dtype)
    sem = lambda *size: pltpu.SemaphoreType.DMA(size)
    z_slots = 8
    rest = rows - half
    return pl.pallas_call(
        functools.partial(reduce_kernel, width, half),
        out_shape=(
            jax.ShapeDtypeStruct((2, rows, MATRICES * width), bf16),
            jax.ShapeDtypeStruct((extras, few, unit), bf16),
            jax.ShapeDtypeStruct(extra.shape, bf16),
        ),
        in_specs=[HB] * 14,
        out_specs=(HB, HB, HB),
        scratch_shapes=[
            *term_scratch(ins, unit),
            pltpu.VMEM(extra.shape, f32), pltpu.SemaphoreType.DMA, buf(bf16, extras, 4, few), buf(bf16, extras, 4, few),
            sem(extras), sem(extras), sem(extras, 8), sem(extras, 8),
            buf(bf16, 2, 4, rows), buf(bf16, 2, 4, rows), buf(f32, 9, rows),
            buf(bf16, 4, 2, half), buf(bf16, 4, 2, half), buf(bf16, 4, 2, rest), buf(bf16, 4, 2, rest),
            buf(f32, 4, rest), buf(f32, 4, half),
            buf(bf16, 4, rest), buf(bf16, 4, rest), buf(bf16, 4, half), buf(bf16, 4, half),
            buf(bf16, 4, rows), buf(bf16, z_slots, rows), buf(bf16, 4, rows), buf(bf16, 4, rows), buf(bf16, 4, rows),
            buf(bf16, 4, rows), buf(bf16, 4, 2, half), buf(bf16, 4, 2, rest), buf(bf16, 4, rest), buf(bf16, 4, half),
            sem(5, 4),
            sem(2), sem(2), sem(4), sem(4), sem(4), sem(4), sem(4), sem(4), sem(4), sem(4),
            sem(4), sem(z_slots), sem(4), sem(4), sem(4), sem(4), sem(count), pltpu.SemaphoreType.REGULAR,
        ],
        compiler_params=pltpu.CompilerParams(
            collective_id=5, has_side_effects=True, vmem_limit_bytes=60 * 1024 * 1024
        ),
        cost_estimate=pl.CostEstimate(
            flops=2 * 64 * width * width * tokens, bytes_accessed=100 << 20, transcendentals=0
        ),
    )(*ins, extra, *ready)


def pre_norm(stream, shift, scale):
    centred = stream - jnp.mean(stream, axis=-1, keepdims=True)
    spread = jnp.mean(centred * centred, axis=-1, keepdims=True)
    return centred * lax.rsqrt(spread + NORM_EPS) * (1.0 + scale) + shift


def gelu_tanh(values):
    return jax.nn.gelu(values, approximate=True)


def latent_ids(latent_len, positions, token_total):
    starts = jnp.cumsum(latent_len) - latent_len
    found = jnp.sum((starts[None, :] <= positions[:, None]).astype(jnp.int32), axis=1) - 1
    inside = (positions >= 0) & (positions < token_total)
    return jnp.where(inside, found, -1)


def low_dot(left, right):
    return jnp.dot(left, right, preferred_element_type=jnp.float32)


def layer_forward(stream, mod_tok, full, plan, in_first, shards_first, shards_second, shards_ahead, collective_id):
    qkv_w, qkv_b, out_w, out_b, up_w, up_b, down_w, down_b = full
    reps, edge, bounds, ids = plan
    width = stream.shape[1]
    hd = width // reps
    nh = HEADS // reps
    shift_one, scale_one, gate_one, shift_two, scale_two, gate_two = jnp.split(mod_tok, 6, axis=1)
    normed = pre_norm(stream, shift_one, scale_one).astype(jnp.bfloat16)
    qkv_bias = qkv_b.astype(jnp.float32)
    bias_full = jnp.concatenate(
        [qkv_bias[:width], jnp.zeros((width,), jnp.float32), qkv_bias[width:]]
    )
    projected = (low_dot(normed, qkv_w) + bias_full).astype(jnp.bfloat16)
    in_second = sent_ahead(shards_first, projected) if shards_first else []
    own, prev, after, fulls = to_heads(projected, reps, edge, pad_to(2 * hd, LANES), in_first, collective_id)
    first_gathered = fulls
    in_second += sent_ahead(shards_second, own) if shards_second else []
    mixed, mixed_t, log_norm = attend(nh, hd, *bounds, prev, own, after, *ids)
    mixed, fulls = swap(mixed, reps, True, in_second, collective_id + 1)
    if in_first:
        (up_w,), (down_w, *fulls) = first_gathered, fulls
    in_next = sent_ahead(shards_ahead, mixed) if shards_ahead else ()
    branch = low_dot(mixed, out_w) + out_b.astype(jnp.float32)
    middle = stream + gate_one * branch
    normed_two = pre_norm(middle, shift_two, scale_two).astype(jnp.bfloat16)
    hidden = low_dot(normed_two, up_w) + up_b.astype(jnp.float32)
    active = gelu_tanh(hidden).astype(jnp.bfloat16)
    result = low_dot(active, down_w) + down_b.astype(jnp.float32)
    saved = (
        normed, (prev, own, after), mixed, (mixed_t, log_norm), branch, middle, normed_two, hidden, active, result,
    )
    full = (qkv_w, qkv_b, out_w, out_b, up_w, up_b, down_w, down_b)
    return (middle + gate_two * result, saved, full, fulls, in_next)


def layer_backward(stream, mod_tok, full, saved, plan, pick, grad_next, beside):
    qkv_w, qkv_b, out_w, out_b, up_w, up_b, down_w, down_b = full
    normed, window, mixed, kept, branch, middle, normed_two, hidden, active, result = saved
    reps, edge, bounds, ids = plan
    width = stream.shape[1]
    hd = width // reps
    nh = HEADS // reps
    shift_one, scale_one, gate_one, shift_two, scale_two, gate_two = jnp.split(mod_tok, 6, axis=1)
    grad_result = (gate_two * grad_next).astype(jnp.bfloat16)
    grad_gate_two = grad_next * result
    grad_down_b = jnp.sum(grad_result.astype(jnp.float32), axis=0)
    grad_active = jnp.einsum("td,fd->tf", grad_result, down_w, preferred_element_type=jnp.float32)
    _, gelu_back = jax.vjp(gelu_tanh, hidden)
    grad_hidden = gelu_back(grad_active)[0].astype(jnp.bfloat16)
    grad_up_b = jnp.sum(grad_hidden.astype(jnp.float32), axis=0)
    grad_normed_two = jnp.einsum("tf,df->td", grad_hidden, up_w, preferred_element_type=jnp.float32)
    _, norm_back_two = jax.vjp(pre_norm, middle, shift_two, scale_two)
    grad_middle_part, grad_shift_two, grad_scale_two = norm_back_two(grad_normed_two)
    grad_middle = grad_next + grad_middle_part
    grad_branch = (gate_one * grad_middle).astype(jnp.bfloat16)
    grad_gate_one = grad_middle * branch
    grad_out_b = jnp.sum(grad_branch.astype(jnp.float32), axis=0)
    grad_mixed = jnp.einsum(
        "te,de->td", grad_branch, out_w, preferred_element_type=jnp.float32
    ).astype(jnp.bfloat16)
    grad_heads, _ = swap(grad_mixed, reps, False, (), 3)
    prev, own, after = window
    grad_q, grad_prev, grad_own, grad_after = attend_back(
        nh, hd, *bounds, prev, own, after, *ids, grad_heads.reshape(own.shape[0], -1), *kept
    )
    grad_projected = from_heads(reps, width, grad_prev, grad_own, grad_after, grad_q, 4)
    grad_projected, beside = lax.optimization_barrier((grad_projected, beside))
    sums = jnp.sum(grad_projected.astype(jnp.float32), axis=0)
    grad_qkv_b = jnp.concatenate([sums[:width], sums[2 * width :]])
    grad_normed = jnp.einsum("te,de->td", grad_projected, qkv_w, preferred_element_type=jnp.float32)
    _, norm_back_one = jax.vjp(pre_norm, stream, shift_one, scale_one)
    grad_stream_part, grad_shift_one, grad_scale_one = norm_back_one(grad_normed)
    grad_stream = grad_middle + grad_stream_part
    grad_mod = jnp.concatenate(
        [
            jnp.einsum("tl,tm->lm", pick, part, precision=HIGH, preferred_element_type=jnp.float32)
            for part in (
                grad_shift_one, grad_scale_one, grad_gate_one, grad_shift_two, grad_scale_two, grad_gate_two,
            )
        ],
        axis=1,
    )
    return (
        grad_stream, grad_mod,
        ((active.T, normed_two.T, mixed.T, normed.T), (grad_result, grad_hidden, grad_branch, grad_projected)),
        (grad_qkv_b, grad_out_b, grad_up_b, grad_down_b), beside,
    )


def bias_parts(stacked, params):
    cuts = [0]
    for at in (3, 5, 7, 9):
        cuts.append(cuts[-1] + params[at].shape[0])
    return [stacked[:, a:b].reshape(-1) for a, b in zip(cuts[:-1], cuts[1:])]


def modulation(partial_terms, layers):
    shares = jnp.stack([jnp.concatenate([params[at] for at in (3, 5, 7, 9)]) for params in layers])
    if not on_planes():
        mods = lax.psum(tuple(partial_terms), "fsdp")
        stacked = lax.all_gather(shares, "fsdp", axis=0)
        fulls = [lax.all_gather(layers[0][at], "fsdp", axis=0, tiled=True) for at in (2, 4)]
    else:
        width = layers[0][4].shape[1]
        parts = jnp.stack(partial_terms).reshape(8, -1, width)
        mod, stacked, *fulls = start(
            parts, jnp.pad(shares, ((0, 16 - shares.shape[0]), (0, 0))), [(layers[0][at],) for at in (2, 4)], 6
        )
        mods = mod.reshape(len(layers), -1, partial_terms[0].shape[1])
    return mods, [bias_parts(stacked[:, at], params) for at, params in enumerate(layers)], fulls


def on_planes():
    return lax.axis_size("fsdp") == 8 and lax.axis_size("replica") == 4


def first_hop(lefts, rights):
    own, xs, ys, tx, ty = chip_sums(lefts, rights, 11)
    hop = lambda value, step: lax.ppermute(value, "fsdp", [(at, at ^ step) for at in range(8)])
    return (own, hop(xs, 2), hop(ys, 4), tx, ty), own


def owner_sums(pairs, ready, grad_mods, grad_biases):
    groups = lax.axis_size("fsdp")
    width = pairs[0][0][1].shape[0]
    if on_planes():
        mods = jnp.stack(grad_mods).reshape(groups, -1, width)
        biases = jnp.stack(
            [jnp.concatenate([part.reshape(groups, -1) for part in parts], axis=1) for parts in grad_biases], axis=1
        )
        extra = jnp.concatenate([mods, biases], axis=1)
        used, parts = extra.shape[1], width // UNIT_WIDTH
        lines = pad_to(used, 16) * parts
        extras = -(-lines // pad_to(width // 16, 16))
        extra = jnp.pad(extra, ((0, 0), (0, lines // parts - used), (0, 0)))
        extra = extra.reshape(groups, extras, -1, UNIT_WIDTH).transpose(1, 0, 2, 3)
        out, mine, shared = reduce_grads(*pairs[0], ready, extra)
        shared = lax.dynamic_update_slice_in_dim(shared, mine[:, None], lax.axis_index("fsdp"), 1)
        shared = shared.transpose(1, 0, 2, 3).reshape(groups, -1, width)
        mods = shared[:, : mods.shape[1]].reshape(len(pairs), -1, grad_mods[0].shape[1])
        mine = mine.reshape(-1, width)
        columns = lambda layer_at, first, last: out[layer_at, :, first * width : last * width].astype(jnp.float32)
        results = []
        for layer_at in range(2):
            share = mine[used - 2 + layer_at].astype(jnp.float32)
            cuts = [0]
            for part in grad_biases[layer_at]:
                cuts.append(cuts[-1] + part.shape[0] // groups)
            down = jnp.stack([columns(layer_at, m, m + 1) for m in range(4)]).reshape(-1, width)
            weights = (columns(layer_at, 9, 12), columns(layer_at, 8, 9), columns(layer_at, 4, 8), down)
            results.append((weights, [share[i:j] for i, j in zip(cuts[:-1], cuts[1:])]))
        return results, mods
    flat = jnp.concatenate([part for parts in grad_biases for part in parts])
    *mods, flat = lax.psum((*grad_mods, flat), ("fsdp", "replica"))
    results, place = [], 0
    for (lefts, rights), parts in zip(pairs, grad_biases):
        grads, biases = [], []
        for left, right in zip(lefts, rights):
            grad = low_dot(left, right).astype(jnp.bfloat16)
            part = lax.psum_scatter(grad, "fsdp", scatter_dimension=0, tiled=True)
            grads.append(lax.psum(part, "replica").astype(jnp.float32))
        for part in parts:
            share = part.shape[0] // groups
            biases.append(lax.dynamic_slice_in_dim(flat, place + lax.axis_index("fsdp") * share, share, 0))
            place += part.shape[0]
        results.append((grads[::-1], biases))
    return results, mods


def attention_plan(latent_len, tok_rows, reps, device_at):
    column = tok_rows * reps
    edge = MAXLEN
    total = jnp.sum(latent_len)
    first = lax.axis_index("fsdp") * column
    positions = first - edge + jnp.arange(column + 2 * edge, dtype=jnp.int32)
    ends = jnp.cumsum(latent_len)
    ids = jnp.sum((ends[None, :] <= positions[:, None]).astype(jnp.int32), axis=1)
    ids = jnp.where(positions < 0, -1, ids)
    own = ids[edge : edge + column]
    count = column // BQ
    firsts, lasts = own[::BQ], own[BQ - 1 :: BQ]
    pick = lambda at: (at[:, None] == jnp.arange(latent_len.shape[0], dtype=jnp.int32)[None, :]).astype(jnp.int32)
    low = jnp.sum(pick(firsts) * (ends - latent_len)[None, :], axis=1) - (first - edge)
    high = jnp.sum(pick(lasts) * ends[None, :], axis=1) - (first - edge)
    bounds = ((low // BK).astype(jnp.int32), ((high + BK - 1) // BK).astype(jnp.int32))
    kid = jnp.broadcast_to(ids[:, None], (ids.shape[0], LANES))
    qid = jnp.broadcast_to(own[None, :], (8, column))
    return (reps, edge, bounds, (kid, qid))


def shards(
    tokens,
    cond,
    latent_len,
    first_ada_weight,
    first_ada_bias,
    first_qkv_weight,
    first_qkv_bias,
    first_out_weight,
    first_out_bias,
    first_up_weight,
    first_up_bias,
    first_down_weight,
    first_down_bias,
    second_ada_weight,
    second_ada_bias,
    second_qkv_weight,
    second_qkv_bias,
    second_out_weight,
    second_out_bias,
    second_up_weight,
    second_up_bias,
    second_down_weight,
    second_down_bias,
    cotangent,
):
    tok_rows = tokens.shape[0]
    group_place = lax.axis_index("fsdp")
    device_at = lax.axis_index(("fsdp", "replica"))
    token_total = tok_rows * lax.axis_size(("fsdp", "replica"))
    latent_count = cond.shape[0]
    local_pos = jnp.arange(tok_rows, dtype=jnp.int32)
    own_ids = latent_ids(latent_len, device_at * tok_rows + local_pos, token_total)
    pick = (own_ids[:, None] == jnp.arange(latent_count, dtype=jnp.int32)[None, :]).astype(
        jnp.float32
    )
    plan = attention_plan(latent_len, tok_rows, lax.axis_size("replica"), device_at)
    layers = (
        (
            first_ada_weight,
            first_ada_bias,
            first_qkv_weight,
            first_qkv_bias,
            first_out_weight,
            first_out_bias,
            first_up_weight,
            first_up_bias,
            first_down_weight,
            first_down_bias,
        ),
        (
            second_ada_weight,
            second_ada_bias,
            second_qkv_weight,
            second_qkv_bias,
            second_out_weight,
            second_out_bias,
            second_up_weight,
            second_up_bias,
            second_down_weight,
            second_down_bias,
        ),
    )
    col_width = first_ada_weight.shape[0]
    own_cond = lax.dynamic_slice_in_dim(
        cond.astype(jnp.float32), group_place * col_width, col_width, 1
    )
    own_silu = jax.nn.silu(own_cond).astype(jnp.bfloat16)
    partial_terms = []
    for params in layers:
        term = low_dot(own_silu, params[0])
        bias_share = params[1].astype(jnp.float32)
        spread = lax.dynamic_update_slice_in_dim(
            jnp.zeros((term.shape[1],), jnp.float32),
            bias_share,
            group_place * bias_share.shape[0],
            0,
        )
        partial_terms.append(term + spread[None, :])
    (mod_first, mod_second), biases, attention_weights = modulation(partial_terms, layers)
    mod_tokens = (
        jnp.dot(pick, mod_first, precision=HIGH, preferred_element_type=jnp.float32),
        jnp.dot(pick, mod_second, precision=HIGH, preferred_element_type=jnp.float32),
    )
    stream = tokens.astype(jnp.float32)
    inputs = []
    kept = []
    whole = lambda value: lax.all_gather(value, "fsdp", axis=0, tiled=True)
    fulls = []
    in_first = sent_ahead((first_up_weight,), mod_first) if on_planes() else ()
    for layer_at, params in enumerate(layers):
        inputs.append(stream)
        ahead = layers[layer_at + 1] if layer_at + 1 < len(layers) else None
        qkv_w, out_w = attention_weights
        qkv_b, out_b, up_b, down_b = biases[layer_at]
        shards_first, shards_second, shards_ahead, up_w, down_w = (), (), (), None, None
        if on_planes():
            shards_first = (params[8],)
            shards_second = () if ahead is None else (ahead[2], ahead[4])
            shards_ahead = () if ahead is None else (ahead[6],)
        else:
            up_w, down_w = whole(params[6]), whole(params[8])
        full = (qkv_w, qkv_b, out_w, out_b, up_w, up_b, down_w, down_b)
        stream, saved, full, attention_weights, in_first = layer_forward(
            stream, mod_tokens[layer_at], full, plan, in_first, shards_first, shards_second, shards_ahead, 7 + 2 * layer_at
        )
        fulls.append(full)
        if ahead is not None and not on_planes():
            attention_weights = [whole(ahead[at]) for at in (2, 4)]
        kept.append(saved)
    output = stream.astype(jnp.bfloat16)
    grad_stream = cotangent.astype(jnp.float32)
    weight_pairs = [None, None]
    ready = ()
    mod_grads = [None, None]
    bias_grads = [None, None]
    for layer_at in (1, 0):
        grad_stream, grad_mod, local_grads, local_biases, ready = layer_backward(
            inputs[layer_at], mod_tokens[layer_at], fulls[layer_at], kept[layer_at], plan, pick, grad_stream, ready
        )
        weight_pairs[layer_at] = local_grads
        if layer_at == 1 and on_planes():
            ready, own = first_hop(*local_grads)
            grad_stream, _ = lax.optimization_barrier((grad_stream, own))
        mod_grads[layer_at] = grad_mod
        bias_grads[layer_at] = local_biases
    sums, (grad_mod_first, grad_mod_second) = owner_sums(weight_pairs, ready, mod_grads, bias_grads)
    grad_silu = jnp.zeros(own_cond.shape, jnp.float32)
    ada_grads = []
    for params, grad_mod in zip(layers, (grad_mod_first, grad_mod_second)):
        low_mod = grad_mod.astype(jnp.bfloat16)
        weight_grad = jnp.einsum("ld,lm->dm", own_silu, low_mod, preferred_element_type=jnp.float32)
        column_sums = jnp.sum(low_mod.astype(jnp.float32), axis=0)
        bias_rows = params[1].shape[0]
        bias_grad = lax.dynamic_slice_in_dim(column_sums, group_place * bias_rows, bias_rows, 0)
        grad_silu = grad_silu + jnp.einsum(
            "lm,dm->ld", low_mod, params[0], preferred_element_type=jnp.float32
        )
        ada_grads.append((weight_grad, bias_grad))
    _, silu_back = jax.vjp(jax.nn.silu, own_cond)
    cond_grad = silu_back(grad_silu)[0]
    outs = [output, grad_stream, cond_grad]
    for layer_at in range(2):
        outs += list(ada_grads[layer_at])
        for weight, bias in zip(*sums[layer_at]):
            outs += [weight, bias]
    return tuple(outs)


def solution(mesh):
    in_specs = (
        P(("fsdp", "replica"), None),
        P(),
        P(),
        P("fsdp", None),
        P("fsdp"),
        P("fsdp", None),
        P("fsdp"),
        P("fsdp", None),
        P("fsdp"),
        P("fsdp", None),
        P("fsdp"),
        P("fsdp", None),
        P("fsdp"),
        P("fsdp", None),
        P("fsdp"),
        P("fsdp", None),
        P("fsdp"),
        P("fsdp", None),
        P("fsdp"),
        P("fsdp", None),
        P("fsdp"),
        P("fsdp", None),
        P("fsdp"),
        P(("fsdp", "replica"), None),
    )
    out_specs = (
        P(("fsdp", "replica"), None),
        P(("fsdp", "replica"), None),
        P(None, "fsdp"),
        P("fsdp", None),
        P("fsdp"),
        P("fsdp", None),
        P("fsdp"),
        P("fsdp", None),
        P("fsdp"),
        P("fsdp", None),
        P("fsdp"),
        P("fsdp", None),
        P("fsdp"),
        P("fsdp", None),
        P("fsdp"),
        P("fsdp", None),
        P("fsdp"),
        P("fsdp", None),
        P("fsdp"),
        P("fsdp", None),
        P("fsdp"),
        P("fsdp", None),
        P("fsdp"),
    )
    return jax.shard_map(shards, mesh=mesh, in_specs=in_specs, out_specs=out_specs, check_vma=False)
```

```python
import functools
import math

import jax
import jax.numpy as jnp
from jax import lax
from jax.experimental import pallas as pl
from jax.experimental.pallas import tpu as pltpu
from jax.sharding import PartitionSpec as P

HEADS = 16
HEAD_DIM = 72
MAXLEN = 1024
NORM_EPS = 1e-06
HIGH = lax.Precision.HIGHEST
BQ = 256
BK = 256
LANES = 128
NEG = -1e30
VM = pl.BlockSpec(memory_space=pltpu.VMEM)
SM = pl.BlockSpec(memory_space=pltpu.SMEM)
HB = pl.BlockSpec(memory_space=pl.ANY)
VMEM_LIMIT = 56 * 1024 * 1024


def pad_to(size, unit):
    return -(-size // unit) * unit


def take_head(ref, rows, at, dim):
    first, off = at // LANES * LANES, at % LANES
    wide = LANES if off + dim <= LANES else 2 * LANES
    block = ref[rows, first : first + wide].astype(jnp.float32)
    if off:
        block = pltpu.roll(block, wide - off, 1)
    block = block[:, :LANES]
    lane = lax.broadcasted_iota(jnp.int32, block.shape, 1)
    return jnp.where(lane < dim, block, 0.0)


def put_heads(blocks, places, width):
    tiles = [None] * (width // LANES)
    for block, at in zip(blocks, places):
        first, off = at // LANES, at % LANES
        wide = jnp.concatenate([block, jnp.zeros_like(block)], axis=1)
        if off:
            wide = pltpu.roll(wide, off, 1)
        for step in range(2):
            part = wide[:, step * LANES : (step + 1) * LANES]
            if first + step < len(tiles):
                old = tiles[first + step]
                tiles[first + step] = part if old is None else old + part
    rows = blocks[0].shape[0]
    return jnp.concatenate(
        [jnp.zeros((rows, LANES), jnp.float32) if t is None else t for t in tiles], axis=1
    )


def nt_dot(left, right):
    return lax.dot_general(left, right, (((1,), (1,)), ((), ())), preferred_element_type=jnp.float32)


def nn_dot(left, right):
    return jnp.dot(left, right, preferred_element_type=jnp.float32)


def rows_at(block, size):
    return pl.ds(pl.multiple_of(block * size, size), size)


def over_window(lo, hi, prev, own, after, action):
    edge, mid = prev.shape[0] // BK, own.shape[0] // BK

    def run(ref, first, count):
        def body(at, carry):
            action(ref, at - first, at)
            return carry

        lax.fori_loop(jnp.clip(lo, first, first + count), jnp.clip(hi, first, first + count), body, 0)

    run(prev, 0, edge)
    run(own, edge, mid)
    run(after, edge + mid, edge)


def attend_kernel(nh, hd, lo, hi, prev, own, after, kid, qid, o_ref, ot_ref, lse_ref, kh, vt, qh, acc, ml):
    dim = hd // nh
    width = o_ref.shape[1]
    count = own.shape[0] // BQ
    scale = math.log2(math.e) / math.sqrt(dim)

    def load(ref, at, to):
        for h in range(nh):
            kh[h, rows_at(to, BK), :] = take_head(ref, rows_at(at, BK), h * dim, dim).astype(jnp.bfloat16)
            vt[h, :, rows_at(to, BK)] = take_head(ref, rows_at(at, BK), hd + h * dim, dim).T.astype(jnp.bfloat16)

    over_window(lo[0], hi[count - 1], prev, own, after, load)
    lse_ref[...] = jnp.zeros_like(lse_ref)

    def query_block(qb, carry):
        rows = rows_at(qb, BQ)
        for h in range(nh):
            qh[h] = take_head(own, rows, 2 * hd + h * dim, dim).astype(jnp.bfloat16)
        acc[...] = jnp.zeros_like(acc)
        ml[0] = jnp.full(ml.shape[1:], NEG, jnp.float32)
        ml[1] = jnp.zeros(ml.shape[1:], jnp.float32)
        ids = qid[0:1, rows]

        def key_block(kb, inner):
            keys = rows_at(kb, BK)
            lanes = kid[keys, :]
            same = jnp.concatenate([lanes] * (BQ // LANES), axis=1) == ids
            scores = [jnp.where(same, nt_dot(kh[h, keys, :], qh[h]) * scale, NEG) for h in range(nh)]
            olds = [ml[0, h : h + 1, :] for h in range(nh)]
            tops = [jnp.maximum(old, jnp.max(s, axis=0, keepdims=True)) for old, s in zip(olds, scores)]
            probs = [jnp.exp2(s - top) for s, top in zip(scores, tops)]
            outs = [nn_dot(vt[h, :, keys], probs[h].astype(jnp.bfloat16)) for h in range(nh)]
            for h in range(nh):
                alpha = jnp.exp2(olds[h] - tops[h])
                ml[0, h : h + 1, :] = tops[h]
                ml[1, h : h + 1, :] = ml[1, h : h + 1, :] * alpha + jnp.sum(probs[h], axis=0, keepdims=True)
                acc[h] = acc[h] * alpha + outs[h]
            return inner

        lax.fori_loop(lo[qb], hi[qb], key_block, 0)
        parts = []
        for h in range(nh):
            total = ml[1, h : h + 1, :]
            out = acc[h, :dim, :] / total
            parts.append(out)
            lse_ref[h : h + 1, rows] = ml[0, h : h + 1, :] + jnp.log2(total)
        parts.append(jnp.zeros((width - hd, BQ), jnp.float32))
        heads = jnp.concatenate(parts, axis=0)
        ot_ref[:, rows] = heads
        o_ref[rows, :] = heads.T.astype(jnp.bfloat16)
        return carry

    lax.fori_loop(0, count, query_block, 0)


def attend(nh, hd, lo, hi, prev, own, after, kid, qid):
    rows, window = own.shape[0], own.shape[0] + 2 * prev.shape[0]
    width = pad_to(hd, LANES)
    return pl.pallas_call(
        functools.partial(attend_kernel, nh, hd),
        out_shape=(
            jax.ShapeDtypeStruct((rows, width), jnp.bfloat16),
            jax.ShapeDtypeStruct((width, rows), jnp.float32),
            jax.ShapeDtypeStruct((8, rows), jnp.float32),
        ),
        in_specs=[SM, SM, VM, VM, VM, VM, VM],
        out_specs=(VM, VM, VM),
        scratch_shapes=[
            pltpu.VMEM((nh, window, LANES), jnp.bfloat16),
            pltpu.VMEM((nh, LANES, window), jnp.bfloat16),
            pltpu.VMEM((nh, BQ, LANES), jnp.bfloat16),
            pltpu.VMEM((nh, LANES, BQ), jnp.float32),
            pltpu.VMEM((2, 8, BQ), jnp.float32),
        ],
        compiler_params=pltpu.CompilerParams(vmem_limit_bytes=VMEM_LIMIT),
    )(lo, hi, prev, own, after, kid, qid)


def attend_back_kernel(
    nh, hd, lo, hi, prev, own, after, kid, qid, do_ref, ot_ref, lse_ref,
    dq_ref, dprev, down, dafter, kh, vh, kt, qh, gh, dk, dv, dqt, delta,
):
    dim = hd // nh
    width = dq_ref.shape[1]
    count = own.shape[0] // BQ
    root = 1.0 / math.sqrt(dim)
    scale = math.log2(math.e) / math.sqrt(dim)

    def load(ref, at, to):
        for h in range(nh):
            k = take_head(ref, rows_at(at, BK), h * dim, dim)
            kh[h, rows_at(to, BK), :] = k.astype(jnp.bfloat16)
            kt[h, :, rows_at(to, BK)] = k.T.astype(jnp.bfloat16)
            vh[h, rows_at(to, BK), :] = take_head(ref, rows_at(at, BK), hd + h * dim, dim).astype(jnp.bfloat16)
            dk[h, rows_at(to, BK), :] = jnp.zeros((BK, LANES), jnp.float32)
            dv[h, rows_at(to, BK), :] = jnp.zeros((BK, LANES), jnp.float32)

    over_window(lo[0], hi[count - 1], prev, own, after, load)

    def query_block(qb, carry):
        rows = rows_at(qb, BQ)
        for h in range(nh):
            qh[h] = take_head(own, rows, 2 * hd + h * dim, dim).astype(jnp.bfloat16)
            gh[h] = take_head(do_ref, rows, h * dim, dim).astype(jnp.bfloat16)
        prod = do_ref[rows, :].astype(jnp.float32).T * ot_ref[:, rows]
        for h in range(nh):
            delta[h : h + 1, :] = jnp.sum(prod[h * dim : (h + 1) * dim], axis=0, keepdims=True)
        dqt[...] = jnp.zeros_like(dqt)
        ids = qid[0:1, rows]

        def key_block(kb, inner):
            keys = rows_at(kb, BK)
            lanes = kid[keys, :]
            same = jnp.concatenate([lanes] * (BQ // LANES), axis=1) == ids
            hs = range(nh)
            scores = [nt_dot(kh[h, keys, :], qh[h]) * scale - lse_ref[h : h + 1, rows] for h in hs]
            dps = [nt_dot(vh[h, keys, :], gh[h]) - delta[h : h + 1, :] for h in hs]
            probs = [jnp.exp2(jnp.where(same, s, NEG)) for s in scores]
            dss = [(p * dp).astype(jnp.bfloat16) for p, dp in zip(probs, dps)]
            lows = [p.astype(jnp.bfloat16) for p in probs]
            for h in hs:
                dv[h, keys, :] += nn_dot(lows[h], gh[h])
            for h in hs:
                dk[h, keys, :] += nn_dot(dss[h], qh[h])
            for h in hs:
                dqt[h] += nn_dot(kt[h, :, keys], dss[h])
            return inner

        lax.fori_loop(lo[qb], hi[qb], key_block, 0)
        parts = [dqt[h, :dim, :] * root for h in range(nh)]
        parts.append(jnp.zeros((width - hd, BQ), jnp.float32))
        dq_ref[rows, :] = jnp.concatenate(parts, axis=0).T.astype(jnp.bfloat16)
        return carry

    lax.fori_loop(0, count, query_block, 0)
    for ref in (dprev, dafter):
        ref[...] = jnp.zeros_like(ref)

    def store(ref, at, to):
        keys = rows_at(to, BK)
        blocks = [dk[h, keys, :] * root for h in range(nh)] + [dv[h, keys, :] for h in range(nh)]
        ref[rows_at(at, BK), :] = put_heads(blocks, [h * dim for h in range(2 * nh)], ref.shape[1]).astype(ref.dtype)

    over_window(lo[0], hi[count - 1], dprev, down, dafter, store)


def attend_back(nh, hd, lo, hi, prev, own, after, kid, qid, grad, ot, lse):
    rows, edge = own.shape[0], prev.shape[0]
    window = rows + 2 * edge
    width, kv = pad_to(hd, LANES), prev.shape[1]
    heads = lambda size, dtype: pltpu.VMEM((nh, size, LANES), dtype)
    return pl.pallas_call(
        functools.partial(attend_back_kernel, nh, hd),
        out_shape=(
            jax.ShapeDtypeStruct((rows, width), jnp.bfloat16),
            jax.ShapeDtypeStruct((edge, kv), jnp.bfloat16),
            jax.ShapeDtypeStruct((rows, kv), jnp.bfloat16),
            jax.ShapeDtypeStruct((edge, kv), jnp.bfloat16),
        ),
        in_specs=[SM, SM] + [VM] * 8,
        out_specs=(VM,) * 4,
        scratch_shapes=[
            heads(window, jnp.bfloat16),
            heads(window, jnp.bfloat16),
            pltpu.VMEM((nh, LANES, window), jnp.bfloat16),
            heads(BQ, jnp.bfloat16),
            heads(BQ, jnp.bfloat16),
            heads(window, jnp.float32),
            heads(window, jnp.float32),
            pltpu.VMEM((nh, LANES, BQ), jnp.float32),
            pltpu.VMEM((8, BQ), jnp.float32),
        ],
        compiler_params=pltpu.CompilerParams(vmem_limit_bytes=VMEM_LIMIT),
    )(lo, hi, prev, own, after, kid, qid, grad, ot, lse)


MESH = pl.DeviceIdType.MESH


def greet(partners, count):
    barrier = pltpu.get_barrier_semaphore()
    for where, there in partners:
        @pl.when(there)
        def _():
            pl.semaphore_signal(barrier, inc=1, device_id=where, device_id_type=MESH)
    pl.semaphore_wait(barrier, count)


def wait_for(ref, sem):
    pltpu.make_async_copy(ref, ref, sem).wait()


def assemble(rows, width, pieces):
    tiles = [None] * (width // LANES)
    for ref, src, dst, count in pieces:
        off, to = src % LANES, dst % LANES
        wide = max(off + count, to + count)
        wide, have = pad_to(wide, LANES), pad_to(off + count, LANES)
        first = src // LANES * LANES
        block = ref[rows, first : first + have].astype(jnp.float32)
        lane = lax.broadcasted_iota(jnp.int32, block.shape, 1)
        block = jnp.where(jnp.logical_and(lane >= off, lane < off + count), block, 0.0)
        if wide > have:
            block = jnp.concatenate([block, jnp.zeros((block.shape[0], wide - have), jnp.float32)], axis=1)
        if off != to:
            block = pltpu.roll(block, (to - off) % wide, 1)
        for step in range(pad_to(to + count, LANES) // LANES):
            part = block[:, step * LANES : (step + 1) * LANES]
            at = dst // LANES + step
            tiles[at] = part if tiles[at] is None else tiles[at] + part
    size = next(t for t in tiles if t is not None).shape
    return jnp.concatenate([jnp.zeros(size, jnp.float32) if t is None else t for t in tiles], axis=1)


def by_rows(size, action, step=64):
    def body(at, carry):
        action(pl.ds(pl.multiple_of(at * step, step), step))
        return carry

    lax.fori_loop(0, size // step, body, 0)


class Gather:
    COPIES = 9

    def __init__(self, shards, fulls, halves, send, recv, load, store, *held):
        self.shards, self.fulls, self.halves, self.held = shards, fulls, halves, held
        self.send, self.recv, self.load, self.store = send, recv, load, store
        self.f, self.r = lax.axis_index("fsdp"), lax.axis_index("replica")
        f = self.f
        c, x, y = lax.rem(f, 2), lax.rem(f // 2, 2), f // 4
        self.core, self.x, self.y = f + 1 - 2 * c, f + 2 - 4 * x, f + 4 - 8 * y
        self.xy = self.x + 4 - 8 * y

    def rows(self, at, which):
        rows, half = self.shards[at][0].shape[0], self.halves[at]
        return {"all": (0, rows), "top": (0, half), "low": (half, rows - half)}[which]

    def part(self, at, place, which):
        first, size = self.rows(at, which)
        rows = self.shards[at][0].shape[0]
        return self.fulls[at].at[pl.ds(pl.multiple_of(place * rows + first, 16), size), :]

    def remote(self, at, kind, src, dst, to):
        return pltpu.make_async_remote_copy(
            src_ref=src, dst_ref=dst, send_sem=self.send.at[at, kind],
            recv_sem=self.recv.at[at, kind], device_id=(to, self.r), device_id_type=MESH,
        )

    def copy(self, at, kind, place, which, to, source=None):
        dst = self.part(at, place, which)
        src = dst if source is None else self.held[at].at[source, pl.ds(*self.rows(at, which)), :]
        return self.remote(at, kind, src, dst, to)

    def hop(self, at, source):
        return self.remote(at, 6 + source, self.held[at].at[0], self.held[at].at[source], (self.x, self.y)[source - 1])

    def keep(self, at, source):
        place = (self.f, self.x, self.y)[source]
        return pltpu.make_async_copy(self.held[at].at[source], self.part(at, place, "all"), self.store.at[at, source])

    def fetch(self, at, source):
        return pltpu.make_async_copy(self.shards[at][source], self.held[at].at[source], self.load.at[at, source])

    def pass_on(self, at, source):
        place = (self.f, self.x, self.y)[source]
        self.copy(at, 2 + source, place, "all", self.core, source).start()
        self.keep(at, source).start()

    def begin(self):
        places = range(len(self.shards))
        for at in places:
            for source in range(len(self.shards[at])):
                self.fetch(at, source).start()
        for at in places:
            self.fetch(at, 0).wait()
            if len(self.shards[at]) == 1:
                self.hop(at, 1).start()
                self.hop(at, 2).start()
        for at in places:
            self.pass_on(at, 0)

    def onward(self, at):
        ahead = len(self.shards[at]) == 3
        self.fetch(at, 1).wait() if ahead else self.hop(at, 1).wait_recv()
        self.copy(at, 0, self.x, "top", self.y, 1).start()
        self.fetch(at, 2).wait() if ahead else self.hop(at, 2).wait_recv()
        self.copy(at, 1, self.y, "low", self.x, 2).start()
        self.pass_on(at, 1)
        self.pass_on(at, 2)

    def across(self, at):
        self.copy(at, 0, self.xy, "top", self.y).wait_recv()
        self.copy(at, 5, self.xy, "top", self.core).start()
        self.copy(at, 1, self.xy, "low", self.x).wait_recv()
        self.copy(at, 6, self.xy, "low", self.core).start()

    def end(self, at):
        for source in range(3):
            self.keep(at, source).wait()
            if source and len(self.shards[at]) == 1:
                self.hop(at, source).wait_send()
        for kind, which in ((0, "top"), (1, "low"), (2, "all"), (3, "all"), (4, "all"), (5, "top"), (6, "low")):
            self.copy(at, kind, self.f, which, self.core).wait_send()
            if kind >= 2:
                self.copy(at, kind, self.f, which, self.core).wait_recv()


def sent_ahead(shards, after):
    shards, _ = lax.optimization_barrier((shards, after))
    hop = lambda shard, step: lax.ppermute(shard, "fsdp", [(at, at ^ step) for at in range(8)])
    return [(shard, hop(shard, 2), hop(shard, 4)) for shard in shards]


def split_shards(refs, sizes):
    shards = []
    for size in sizes:
        shards.append(refs[:size])
        refs = refs[size:]
    return shards, refs


def gather_scratch(shards):
    count = len(shards)
    if not count:
        return []
    return [
        pltpu.SemaphoreType.DMA((count, Gather.COPIES)),
        pltpu.SemaphoreType.DMA((count, Gather.COPIES)),
        pltpu.SemaphoreType.DMA((count, 3)),
        pltpu.SemaphoreType.DMA((count, 3)),
    ] + [pltpu.VMEM((3, *part.shape), part.dtype) for part, *_ in shards]


def gathered_shapes(shards):
    return tuple(jax.ShapeDtypeStruct((8 * part.shape[0], part.shape[1]), part.dtype) for part, *_ in shards)


def halves_of(shards):
    halves, ahead = [], 0
    for part, *_ in shards:
        rows, size = part.shape
        half = rows // 32 * 16
        if rows % 32 and ahead <= 0:
            half += 16
        ahead += (2 * half - rows) * size
        halves.append(half)
    return tuple(halves), tuple(len(shard) for shard in shards)


def start_kernel(plan, part_in, bias_in, *refs):
    halves, sizes = plan
    count = len(halves)
    shards, refs = split_shards(refs, sizes)
    (mod, bias), fulls, refs = refs[:2], refs[2 : count + 2], refs[count + 2 :]
    terms, total, m_s, m_r, b_s, b_r, t_s, t_r, keep, *sems = refs
    f, r = lax.axis_index("fsdp"), lax.axis_index("replica")
    others = [lax.rem(f + d, 8) for d in range(1, 8)]
    greet([((there, r), True) for there in others], 7)

    def remote(src, dst, s_sem, r_sem, there):
        return pltpu.make_async_remote_copy(
            src_ref=src, dst_ref=dst, send_sem=s_sem, recv_sem=r_sem, device_id=(there, r), device_id_type=MESH
        )

    def term_copy(block, source, there):
        return remote(part_in.at[block], terms.at[source], t_s.at[there], t_r.at[source], there)

    def bias_copy(source, there):
        return remote(bias_in, bias.at[source], b_s.at[there], b_r.at[source], there)

    def mod_copy(source, there):
        return remote(total, mod.at[source], m_s.at[there], m_r.at[source], there)

    gather = Gather(shards, fulls, halves, *sems)
    for there in others:
        term_copy(there, f, there).start()
    mine = pltpu.make_async_copy(part_in.at[f], terms.at[f], keep.at[0])
    mine.start()
    gather.begin()
    for there in others:
        bias_copy(f, there).start()
    own_bias = pltpu.make_async_copy(bias_in, bias.at[f], keep.at[1])
    own_bias.start()
    mine.wait()
    for there in others:
        term_copy(f, there, there).wait_recv()
    total[...] = functools.reduce(lambda a, b: a + b, [terms[j] for j in range(8)])
    for there in others:
        mod_copy(f, there).start()
    own_mod = pltpu.make_async_copy(total, mod.at[f], keep.at[2])
    own_mod.start()
    for at in range(count):
        gather.onward(at)
    for at in range(count):
        gather.across(at)
    for at in range(count):
        gather.end(at)
    own_bias.wait()
    own_mod.wait()
    for there in others:
        term_copy(there, f, there).wait_send()
        bias_copy(f, there).wait_send()
        mod_copy(f, there).wait_send()
        bias_copy(there, there).wait_recv()
        mod_copy(there, there).wait_recv()


def start(parts, biases, shards, collective_id):
    sem = lambda: pltpu.SemaphoreType.DMA((8,))
    return pl.pallas_call(
        functools.partial(start_kernel, halves_of(shards)),
        out_shape=(
            jax.ShapeDtypeStruct(parts.shape, parts.dtype),
            jax.ShapeDtypeStruct((8, *biases.shape), biases.dtype),
            *gathered_shapes(shards),
        ),
        in_specs=[HB] * (2 + sum(len(shard) for shard in shards)),
        out_specs=(HB,) * (2 + len(shards)),
        scratch_shapes=[
            pltpu.VMEM(parts.shape, parts.dtype), pltpu.VMEM(parts.shape[1:], parts.dtype),
            sem(), sem(), sem(), sem(), sem(), sem(), pltpu.SemaphoreType.DMA((3,)), *gather_scratch(shards),
        ],
        compiler_params=pltpu.CompilerParams(
            collective_id=collective_id, has_side_effects=True, vmem_limit_bytes=VMEM_LIMIT
        ),
    )(parts, biases, *(part for shard in shards for part in shard))


def to_heads_kernel(reps, size, edge, kv, plan, qkv, *refs):
    halves, sizes = plan
    count = len(halves)
    shards, refs = split_shards(refs, sizes)
    (own, prev, after), fulls, refs = refs[:3], refs[3 : count + 3], refs[count + 3 :]
    x_ref, send, recv, edge_send, edge_recv, *sems = refs
    gather = Gather(shards, fulls, halves, *sems) if count else None
    group, me = lax.axis_index("fsdp"), lax.axis_index("replica")
    groups = lax.axis_size("fsdp")
    wide = x_ref.shape[2]
    width = qkv.shape[1] // 3
    hd = width // reps
    down, up = group > 0, group < groups - 1
    others = [(group, lax.rem(me + d, reps)) for d in range(1, reps)]
    greet(
        [(place, True) for place in others] + [((group - 1, me), down), ((group + 1, me), up)]
        + ([((there, me), True) for there in (gather.core, gather.x, gather.y)] if count else []),
        reps - 1 + down.astype(jnp.int32) + up.astype(jnp.int32) + (3 if count else 0),
    )
    spans = [pl.ds(0, kv), pl.ds(kv, wide - kv)] if wide > kv else [pl.ds(0, kv)]

    def exchange(span, part, there):
        return pltpu.make_async_remote_copy(
            src_ref=x_ref.at[there, :, span], dst_ref=own.at[me, :, span], send_sem=send.at[part, there],
            recv_sem=recv.at[part, me], device_id=(group, there), device_id_type=MESH,
        )

    def depart(place, part):
        span = spans[part]
        pl.when(me != place)(lambda: exchange(span, part, place).start())
        keep = pltpu.make_async_copy(x_ref.at[place, :, span], own.at[place, :, span], recv.at[part, place])
        pl.when(me == place)(keep.start)

    for place in range(reps):
        def pack(rows, place=place):
            at = place * hd
            pieces = [(qkv, width + at, 0, hd), (qkv, 2 * width + at, hd, hd), (qkv, at, 2 * hd, hd)]
            x_ref[place, rows, :] = assemble(rows, wide, pieces).astype(jnp.bfloat16)

        by_rows(size, pack)
        depart(place, 0)
    for part in range(1, len(spans)):
        for place in range(reps):
            depart(place, part)

    if count:
        gather.begin()
    for at in range(count):
        gather.onward(at)

    def edges(piece, action):
        lo, hi = piece * size, (piece + 1) * size
        total = reps * size
        if lo >= total - edge:
            @pl.when(up)
            def _():
                action(0, piece, (group + 1, me), prev.at[pl.ds(lo - (total - edge), size), :])
        if hi <= edge:
            @pl.when(down)
            def _():
                action(1, piece, (group - 1, me), after.at[pl.ds(lo, size), :])

    def start_edge(way, piece, where, target):
        pltpu.make_async_remote_copy(
            src_ref=own.at[piece, :, spans[0]], dst_ref=target, send_sem=edge_send.at[way, piece],
            recv_sem=edge_recv.at[way, piece], device_id=where, device_id_type=MESH,
        ).start()

    def end_send(way, piece, where, target):
        wait_for(own.at[piece, :, spans[0]], edge_send.at[way, piece])

    def end_recv(way, piece, where, target):
        wait_for(target, edge_recv.at[way, piece])

    for piece in range(reps):
        wait_for(own.at[piece, :, spans[0]], recv.at[0, piece])
        edges(piece, start_edge)
    if len(spans) > 1:
        for piece in range(reps):
            wait_for(own.at[piece, :, spans[1]], recv.at[1, piece])
    for at in range(count):
        gather.across(at)
    for part, span in enumerate(spans):
        for _, there in others:
            wait_for(x_ref.at[there, :, span], send.at[part, there])
    for piece in range(reps):
        edges(piece, end_send)
        lo, hi = piece * size, (piece + 1) * size
        total = reps * size
        if lo >= total - edge:
            @pl.when(down)
            def _():
                wait_for(prev.at[pl.ds(lo - (total - edge), size), :], edge_recv.at[0, piece])
        if hi <= edge:
            @pl.when(up)
            def _():
                wait_for(after.at[pl.ds(lo, size), :], edge_recv.at[1, piece])
    for at in range(count):
        gather.end(at)


def to_heads(qkv, reps, edge, kv, shards, collective_id):
    size, wide = qkv.shape[0], pad_to(qkv.shape[1] // reps, LANES)
    sems = pltpu.SemaphoreType.DMA((2, reps))
    own, prev, after, *fulls = pl.pallas_call(
        functools.partial(to_heads_kernel, reps, size, edge, kv, halves_of(shards)),
        out_shape=(
            jax.ShapeDtypeStruct((reps, size, wide), qkv.dtype),
            jax.ShapeDtypeStruct((edge, kv), qkv.dtype),
            jax.ShapeDtypeStruct((edge, kv), qkv.dtype),
            *gathered_shapes(shards),
        ),
        in_specs=[VM] + [HB] * sum(len(shard) for shard in shards),
        out_specs=(HB,) * (3 + len(shards)),
        scratch_shapes=[pltpu.VMEM((reps, size, wide), qkv.dtype), sems, sems, sems, sems, *gather_scratch(shards)],
        compiler_params=pltpu.CompilerParams(
            collective_id=collective_id, has_side_effects=True, vmem_limit_bytes=VMEM_LIMIT
        ),
    )(qkv, *(part for shard in shards for part in shard))
    return own.reshape(reps * size, wide), prev, after, fulls


def swap_kernel(reps, out, plan, x_ref, *refs):
    halves, sizes = plan
    count = len(halves)
    shards, refs = split_shards(refs, sizes)
    y_ref, fulls, (held, send, recv, *sems) = refs[0], refs[1 : count + 1], refs[count + 1 :]
    gather = Gather(shards, fulls, halves, *sems) if count else None
    group, me = lax.axis_index("fsdp"), lax.axis_index("replica")
    others = [(group, lax.rem(me + d, reps)) for d in range(1, reps)]
    planar = [(there, me) for there in (gather.core, gather.x, gather.y)] if count else []
    size, lanes = held.shape[1:]
    src, dst = (x_ref, held) if out else (held, y_ref)
    hd = (y_ref if out else x_ref).shape[1] // reps
    greet([(place, True) for place in others + planar], reps - 1 + len(planar))
    for place in range(reps):
        if not out:
            def pack(rows, place=place):
                held[place, rows, :] = assemble(rows, lanes, [(x_ref, place * hd, 0, hd)]).astype(jnp.bfloat16)

            by_rows(size, pack)
        leave = pltpu.make_async_remote_copy(
            src_ref=src.at[place], dst_ref=dst.at[me], send_sem=send.at[place], recv_sem=recv.at[me],
            device_id=(group, place), device_id_type=MESH,
        )
        keep = pltpu.make_async_copy(src.at[place], dst.at[place], recv.at[place])
        pl.when(me != place)(leave.start)
        pl.when(me == place)(keep.start)
    if count:
        gather.begin()
    for at in range(count):
        gather.onward(at)
    for at in range(count):
        gather.across(at)
    for piece in range(reps):
        wait_for(dst.at[piece], recv.at[piece])
    if out:
        def unpack(rows):
            pieces = [(held.at[place], 0, place * hd, hd) for place in range(reps)]
            y_ref[rows, :] = assemble(rows, y_ref.shape[1], pieces).astype(jnp.bfloat16)

        by_rows(size, unpack)
    for _, there in others:
        wait_for(src.at[there], send.at[there])
    for at in range(count):
        gather.end(at)


def swap(x, reps, out, shards, collective_id):
    if out:
        size, lanes = x.shape[0] // reps, x.shape[1]
        x = x.reshape(reps, size, lanes)
        shape = (size, HEADS * HEAD_DIM)
    else:
        size, lanes = x.shape[0], pad_to(x.shape[1] // reps, LANES)
        shape = (reps, size, lanes)
    sems = pltpu.SemaphoreType.DMA((reps,))
    swapped, *fulls = pl.pallas_call(
        functools.partial(swap_kernel, reps, out, halves_of(shards)),
        out_shape=(jax.ShapeDtypeStruct(shape, x.dtype), *gathered_shapes(shards)),
        in_specs=[HB if out else VM] + [HB] * sum(len(shard) for shard in shards),
        out_specs=(VM if out else HB,) + (HB,) * len(shards),
        scratch_shapes=[pltpu.VMEM((reps, size, lanes), x.dtype), sems, sems, *gather_scratch(shards)],
        compiler_params=pltpu.CompilerParams(
            collective_id=collective_id, has_side_effects=True, vmem_limit_bytes=VMEM_LIMIT
        ),
    )(x, *(part for shard in shards for part in shard))
    return swapped, fulls


def from_heads_kernel(reps, size, edge, dprev, own, dafter, dq, out, out_kv, out_q, from_up, from_down, total, mine, sends, recvs, send, recv):
    group, me = lax.axis_index("fsdp"), lax.axis_index("replica")
    groups = lax.axis_size("fsdp")
    rows = reps * size
    down, up = group > 0, group < groups - 1
    others = [(group, lax.rem(me + d, reps)) for d in range(1, reps)]
    greet(
        [(place, True) for place in others] + [((group - 1, me), down), ((group + 1, me), up)],
        reps - 1 + down.astype(jnp.int32) + up.astype(jnp.int32),
    )
    to_down = pltpu.make_async_remote_copy(
        src_ref=dprev, dst_ref=from_up, send_sem=sends.at[0], recv_sem=recvs.at[0],
        device_id=(group - 1, me), device_id_type=MESH,
    )
    to_up = pltpu.make_async_remote_copy(
        src_ref=dafter, dst_ref=from_down, send_sem=sends.at[1], recv_sem=recvs.at[1],
        device_id=(group + 1, me), device_id_type=MESH,
    )
    pl.when(down)(to_down.start)
    pl.when(up)(to_up.start)
    for _, there in others:
        pltpu.make_async_remote_copy(
            src_ref=dq.at[pl.ds(pl.multiple_of(there * size, size), size), :], dst_ref=out_q.at[me], send_sem=send.at[0, there],
            recv_sem=recv.at[0, me], device_id=(group, there), device_id_type=MESH,
        ).start()
    pltpu.make_async_copy(dq.at[pl.ds(pl.multiple_of(me * size, size), size), :], out_q.at[me], recv.at[0, me]).start()
    step = math.gcd(edge, 256)

    def chunk(at, carry):
        here = pl.ds(pl.multiple_of(at * step, step), step)
        total[here, :] = own[here, :].astype(jnp.float32)
        return carry

    lax.fori_loop(0, rows // step, chunk, 0)

    def add(ref, first):
        def body(at, carry):
            here = pl.ds(pl.multiple_of(first + at * step, step), step)
            there = pl.ds(pl.multiple_of(at * step, step), step)
            total[here, :] += ref[there, :].astype(jnp.float32)
            return carry

        lax.fori_loop(0, edge // step, body, 0)

    @pl.when(down)
    def _():
        wait_for(from_down, recvs.at[1])
        add(from_down, 0)

    @pl.when(up)
    def _():
        wait_for(from_up, recvs.at[0])
        add(from_up, rows - edge)

    def narrow(at, carry):
        here = pl.ds(pl.multiple_of(at * step, step), step)
        mine[here, :] = total[here, :].astype(jnp.bfloat16)
        return carry

    lax.fori_loop(0, rows // step, narrow, 0)
    for _, there in others:
        pltpu.make_async_remote_copy(
            src_ref=mine.at[pl.ds(pl.multiple_of(there * size, size), size), :], dst_ref=out_kv.at[me], send_sem=send.at[1, there],
            recv_sem=recv.at[1, me], device_id=(group, there), device_id_type=MESH,
        ).start()
    pltpu.make_async_copy(mine.at[pl.ds(pl.multiple_of(me * size, size), size), :], out_kv.at[me], recv.at[1, me]).start()
    width = out.shape[1] // 3
    hd = width // reps

    def unpack(ref, first, section):
        def body(rows):
            pieces = [(ref.at[place], first, place * hd, hd) for place in range(reps)]
            out[rows, section * width : (section + 1) * width] = assemble(rows, width, pieces).astype(jnp.bfloat16)

        by_rows(size, body)

    for piece in range(reps):
        wait_for(out_q.at[piece], recv.at[0, piece])
    unpack(out_q, 0, 0)
    for piece in range(reps):
        wait_for(out_kv.at[piece], recv.at[1, piece])
    unpack(out_kv, 0, 1)
    unpack(out_kv, hd, 2)
    for _, there in others:
        wait_for(out_q.at[0], send.at[0, there])
        wait_for(out_kv.at[0], send.at[1, there])
    pl.when(down)(to_down.wait_send)
    pl.when(up)(to_up.wait_send)


def from_heads(reps, width, dprev, own, dafter, dq, collective_id):
    rows, kv = own.shape
    edge, size = dprev.shape[0], own.shape[0] // reps
    pair, both = pltpu.SemaphoreType.DMA((2,)), pltpu.SemaphoreType.DMA((2, reps))
    return pl.pallas_call(
        functools.partial(from_heads_kernel, reps, size, edge),
        out_shape=jax.ShapeDtypeStruct((size, 3 * width), own.dtype),
        in_specs=[HB, VM, HB, HB],
        out_specs=VM,
        scratch_shapes=[
            pltpu.VMEM((reps, size, kv), own.dtype),
            pltpu.VMEM((reps, size, dq.shape[1]), own.dtype),
            pltpu.VMEM((edge, kv), own.dtype),
            pltpu.VMEM((edge, kv), own.dtype),
            pltpu.VMEM((rows, kv), jnp.float32),
            pltpu.VMEM((rows, kv), own.dtype),
            pair,
            pair,
            both,
            both,
        ],
        compiler_params=pltpu.CompilerParams(
            collective_id=collective_id, has_side_effects=True, vmem_limit_bytes=VMEM_LIMIT
        ),
    )(dprev, own, dafter, dq)


MATRICES = 12
CHIP_WIDTH, UNIT_WIDTH = 1152, 384
LEFT_ROWS = 4
PLACES = ((0, 0), (1, 0), (0, 1), (1, 1))


class Terms:
    def __init__(self, ins, flat, left, right, rows, width, load_sem):
        self.flat, self.left, self.right, self.rows, self.width = flat, left, right, rows, width
        self.unit = right.shape[2]
        self.parts = width // self.unit
        f = lax.axis_index("fsdp")
        self.c, self.x, self.y = lax.rem(f, 2), lax.rem(f // 2, 2), f // 4
        self.core_at, self.x_at, self.y_at = f + 1 - 2 * self.c, f + 2 - 4 * self.x, f + 4 - 8 * self.y
        self.loads, place, slot = [], 0, 0
        for src in ins[:4]:
            self.loads.append((src, flat.at[:, pl.ds(place, src.shape[1])]))
            place += src.shape[1]
        for src in ins[4:]:
            for part in range(src.shape[1] // self.unit):
                self.loads.append((src.at[:, pl.ds(part * self.unit, self.unit)], right.at[slot]))
                slot += 1
        self.load_sem = load_sem

    def start(self):
        for at, (src, dst) in enumerate(self.loads):
            pltpu.make_async_copy(src, dst, self.load_sem.at[at]).start()

    def wait(self):
        for at, (src, dst) in enumerate(self.loads):
            pltpu.make_async_copy(src, dst, self.load_sem.at[at]).wait()

        def turn(at, carry):
            here = pl.ds(pl.multiple_of(at * LANES, LANES), LANES)
            self.left[here, :] = self.flat[:, here].T
            return carry

        lax.fori_loop(0, self.left.shape[0] // LANES, turn, 0)

    def block(self, core, mx, my):
        x, y = self.x + mx * (1 - 2 * self.x), self.y + my * (1 - 2 * self.y)
        return (y * 2 + x) * 2 + (self.c + core * (1 - 2 * self.c))

    def stack(self, u, core):
        rows, width = self.rows, self.width
        m, part = u // self.parts, lax.rem(u, self.parts)
        inside = jnp.where(
            m < 4, rows * m, LEFT_ROWS * width + jnp.where(m < 8, 0, jnp.where(m < 9, width, 2 * width))
        )
        stride = jnp.where(m < 4, 4 * rows, rows)
        other = jnp.maximum(m - 3, 0) * self.parts + part
        blocks = []
        for mx, my in PLACES:
            start = pl.multiple_of(inside + stride * self.block(core, mx, my), 16)
            blocks.append(self.left[pl.ds(start, rows), :])
        return nn_dot(jnp.concatenate(blocks, axis=0), self.right[other])


def term_scratch(ins, unit):
    tokens, width = ins[1].shape
    parts = width // unit
    return [
        pltpu.VMEM((tokens, (LEFT_ROWS + 3) * width), jnp.bfloat16),
        pltpu.VMEM(((LEFT_ROWS + 3) * width, tokens), jnp.bfloat16),
        pltpu.VMEM((9 * parts, tokens, unit), jnp.bfloat16),
        pltpu.SemaphoreType.DMA((4 + 9 * parts,)),
    ]


def remote_copy(src, dst, s_sem, r_sem, where):
    return pltpu.make_async_remote_copy(
        src_ref=src, dst_ref=dst, send_sem=s_sem, recv_sem=r_sem, device_id=where, device_id_type=MESH
    )


def chip_kernel(width, half, *refs):
    ins, (own, xs, ys, tx, ty), refs = refs[:8], refs[8:13], refs[13:]
    flat, left, right, load_sem, csend, crecv, own_b, xs_b, ys_b, tx_b, ty_b, core_s, core_r, out_sem = refs
    r = lax.axis_index("replica")
    count, rows = own.shape[:2]
    terms = Terms(ins, flat, left, right, rows, width, load_sem)
    where = (terms.core_at, r)
    greet([(where, True)], 1)
    terms.start()
    terms.wait()
    bf16, f32 = jnp.bfloat16, jnp.float32

    def core_copy(u):
        pair, four = lax.rem(u, 2), lax.rem(u, 4)
        return remote_copy(csend.at[pair], crecv.at[four], core_s.at[pair], core_r.at[four], where)

    def stores(u):
        pair = lax.rem(u, 2)
        buffers = ((own_b, own), (xs_b, xs), (ys_b, ys), (tx_b, tx), (ty_b, ty))
        return [
            pltpu.make_async_copy(src.at[pair], dst.at[u], out_sem.at[at, pair]) for at, (src, dst) in enumerate(buffers)
        ]

    def close(u):
        for copy in stores(u):
            copy.wait()

    def chip(u):
        pair, four = lax.rem(u, 2), lax.rem(u, 4)
        stacked = terms.stack(u, 0)
        core_copy(u).wait()
        totals = [stacked[m * rows : (m + 1) * rows] + crecv[four, m].astype(f32) for m in range(4)]
        mine, along_x, along_y, opposite = [total.astype(bf16) for total in totals]
        own_b[pair] = mine
        xs_b[pair, 0] = along_x[:half]
        tx_b[pair] = along_x[half:]
        ty_b[pair] = along_y[:half]
        ys_b[pair, 0] = along_y[half:]
        xs_b[pair, 1] = opposite[:half]
        ys_b[pair, 1] = opposite[half:]
        for copy in stores(u):
            copy.start()

    def open_unit(u):
        pair = lax.rem(u, 2)
        csend[pair] = terms.stack(u, 1).astype(bf16).reshape(csend.shape[1:])
        core_copy(u).start()

    def step(t, carry):
        pl.when(t < count)(lambda: open_unit(t))
        pl.when(t >= 3)(lambda: close(t - 3))
        pl.when(jnp.logical_and(t >= 1, t <= count))(lambda: chip(t - 1))
        return carry

    lax.fori_loop(0, count + 3, step, 0)


def chip_sums(lefts, rights, collective_id):
    ins = (*lefts, *rights)
    tokens, width = lefts[1].shape
    rows, unit = width // 8, CHIP_WIDTH
    half = pad_to(rows // 2, 16)
    count = MATRICES * (width // unit)
    bf16 = jnp.bfloat16
    shapes = ((rows, unit), (2, half, unit), (2, rows - half, unit), (rows - half, unit), (half, unit))
    pair = pltpu.SemaphoreType.DMA((2,))
    return pl.pallas_call(
        functools.partial(chip_kernel, width, half),
        out_shape=tuple(jax.ShapeDtypeStruct((count, *shape), bf16) for shape in shapes),
        in_specs=[HB] * 8,
        out_specs=(HB,) * 5,
        scratch_shapes=[
            *term_scratch(ins, unit),
            pltpu.VMEM((2, 4, rows, unit), bf16),
            pltpu.VMEM((4, 4, rows, unit), bf16),
            *(pltpu.VMEM((2, *shape), bf16) for shape in shapes),
            pair,
            pltpu.SemaphoreType.DMA((4,)),
            pltpu.SemaphoreType.DMA((5, 2)),
        ],
        compiler_params=pltpu.CompilerParams(
            collective_id=collective_id, has_side_effects=True, vmem_limit_bytes=VMEM_LIMIT
        ),
        cost_estimate=pl.CostEstimate(flops=2 * 64 * width * width * tokens, bytes_accessed=40 << 20, transcendentals=0),
    )(*ins)


def reduce_kernel(width, half, *refs):
    ins, (extra_in, own_in, xr_in, yr_in, tx_in, ty_in), (out, out_down, mine, shared), refs = refs[:8], refs[8:14], refs[14:18], refs[18:]
    (flat, left, right, load_sem, extra, extra_sem, cx_s, cx_r, cxs_sem, cxr_sem, share_s, share_r,
     csend, crecv, own, xs, xr, ys, yr, tx, ty, x2s, x2r, y2s, y2r, zs, z1r, z2s, z2r, fin,
     own_l, xr_l, yr_l, tx_l, ty_l, ready_sem,
     core_s, core_r, x_s, x_r, y_s, y_r, x2_s, x2_r, y2_s, y2_r, z1_s, z1_r, z2_s, z2_r, fin_l, fin_s, fin_r,
     credit) = refs
    f, r = lax.axis_index("fsdp"), lax.axis_index("replica")
    rows = own.shape[1]
    extras = extra.shape[0]
    unit = own.shape[2]
    count = extras + 2 * MATRICES * (width // unit)
    terms = Terms(ins, flat, left, right, rows, width, load_sem)
    core_at, x_at, y_at = terms.core_at, terms.x_at, terms.y_at
    inner = jnp.logical_and(r > 0, r < 3)
    outer = jnp.logical_not(inner)
    z_at = r + 1 - 2 * lax.rem(r, 2)
    others = [lax.rem(f + d, 8) for d in range(1, 8)]
    greet(
        [((there, r), True) for there in others] + [((f, r - 1), r > 0), ((f, r + 1), r < 3)],
        7 + (r > 0).astype(jnp.int32) + (r < 3).astype(jnp.int32),
    )
    few = extra.shape[2]
    extra_loads = [
        pltpu.make_async_copy(extra_in.at[:, :, pl.ds(at * unit, unit)], extra.at[at], extra_sem.at[at])
        for at in range(extras)
    ]
    for load in extra_loads:
        load.start()
    terms.start()
    for load in extra_loads:
        load.wait()
    send = remote_copy
    top, low = pl.ds(0, half), pl.ds(half, rows - half)

    def core_copy(slot):
        return send(csend.at[slot], crecv.at[slot], core_s.at[slot], core_r.at[slot], (core_at, r))

    def extra_copy(u):
        return send(cx_s.at[u], cx_r.at[u], cxs_sem.at[u], cxr_sem.at[u], (core_at, r))

    def x_copy(slot):
        return send(xs.at[slot], xr.at[slot], x_s.at[slot], x_r.at[slot], (x_at, r))

    def y_copy(slot):
        return send(ys.at[slot], yr.at[slot], y_s.at[slot], y_r.at[slot], (y_at, r))

    def x2_copy(slot):
        return send(x2s.at[slot], x2r.at[slot], x2_s.at[slot], x2_r.at[slot], (x_at, r))

    def y2_copy(slot):
        return send(y2s.at[slot], y2r.at[slot], y2_s.at[slot], y2_r.at[slot], (y_at, r))

    def z1_copy(slot, to):
        return send(zs.at[slot], z1r.at[to], z1_s.at[slot], z1_r.at[to], (f, z_at))

    def z2_copy(slot):
        return send(z2s.at[slot], z2r.at[slot], z2_s.at[slot], z2_r.at[slot], (f, 3 - r))

    def routed(u, action):
        v = u - extras
        w, layer = v // 2, 1 - lax.rem(v, 2)
        parts = width // unit
        m = w // parts

        @pl.when(m < 4)
        def _():
            row = pl.multiple_of(m * rows, 16)
            column = pl.multiple_of(lax.rem(w, parts) * unit, LANES)
            action(out_down.at[layer, pl.ds(row, rows), pl.ds(column, unit)])

        @pl.when(m >= 4)
        def _():
            column = pl.multiple_of((w - 4 * parts) * unit, LANES)
            action(out.at[layer, :, pl.ds(column, unit)])

    def fin_copy(slot, u, to):
        return send(fin.at[slot], to, fin_s.at[slot], fin_r.at[u], (f, z_at))

    def keep_copy(slot, to):
        return pltpu.make_async_copy(fin.at[slot], to, fin_l.at[slot])

    def columns(u):
        return pl.ds(pl.multiple_of(u * unit, LANES), unit)

    def fin_extra(u):
        slot = lax.rem(u, 4)
        return send(fin.at[slot, pl.ds(0, few), :], mine.at[:, columns(u)], fin_s.at[slot], fin_r.at[u], (f, z_at))

    def keep_extra(u):
        slot = lax.rem(u, 4)
        return pltpu.make_async_copy(fin.at[slot, pl.ds(0, few), :], mine.at[:, columns(u)], fin_l.at[slot])

    def share_copy(u, there, where):
        return send(
            mine.at[:, columns(u)], shared.at[there, :, columns(u)], share_s.at[u, where], share_r.at[u, there], (where, r)
        )

    def piece(src, w):
        whole = src.shape[-1]
        here = pl.ds(pl.multiple_of(lax.rem(w, whole // unit) * unit, LANES), unit)
        at = w // (whole // unit)
        return src.at[at, :, here] if len(src.shape) == 3 else src.at[at, :, :, here]

    def ready_copies(u):
        slot = lax.rem(u, 4)
        buffers = ((own_in, own_l), (xr_in, xr_l), (yr_in, yr_l), (tx_in, tx_l), (ty_in, ty_l))
        return [
            pltpu.make_async_copy(piece(src, (u - extras) // 2), dst.at[slot], ready_sem.at[at, slot])
            for at, (src, dst) in enumerate(buffers)
        ]

    f32, bf16 = jnp.float32, jnp.bfloat16
    z_slots = z1r.shape[0]

    def stage(u, condition, body, first=0, last=count):
        live = jnp.logical_and(u >= first, u < last)
        pl.when(live if condition is None else jnp.logical_and(live, condition))(lambda: body(u))

    def share_own(u):
        return pltpu.make_async_copy(mine.at[:, columns(u)], shared.at[f, :, columns(u)], share_r.at[u, f])

    def share(u):
        for there in others:
            share_copy(u, f, there).start()
        share_own(u).start()

    def close(u):
        slot = lax.rem(u, 4)

        def action(to):
            fin_copy(slot, u, to).wait_send()
            keep_copy(slot, to).wait()

        routed(u, action)

    def arrive(u):
        routed(u, lambda to: fin_copy(lax.rem(u, 4), u, to).wait_recv())

    def close_extra(u):
        fin_extra(u).wait_send()
        keep_extra(u).wait()

    def arrive_extra(u):
        fin_extra(u).wait_recv()

    def finish(u):
        slot = lax.rem(u, 4)
        z2_copy(slot).wait()
        fin[slot] = (z2s[slot].astype(f32) + z2r[slot].astype(f32)).astype(bf16)

        @pl.when(u >= extras)
        def _():
            def action(to):
                fin_copy(slot, u, to).start()
                keep_copy(slot, to).start()

            routed(u, action)

        @pl.when(u < extras)
        def _():
            fin_extra(u).start()
            keep_extra(u).start()

    def middle(u):
        slot, z_slot, at = lax.rem(u, 4), lax.rem(u, z_slots), lax.rem(u, own.shape[0])
        z1_copy(slot, z_slot).wait_recv()
        z2s[slot] = (own[at] + z1r[z_slot].astype(f32)).astype(bf16)
        z2_copy(slot).start()

        @pl.when(u + z_slots < count)
        def _():
            pl.semaphore_signal(credit, inc=1, device_id=(f, z_at), device_id_type=MESH)

    def sent(u):
        z1_copy(lax.rem(u, 4), lax.rem(u, z_slots)).wait_send()

    def plane(u):
        slot, at = lax.rem(u, 4), lax.rem(u, own.shape[0])
        x2_copy(slot).wait()
        y2_copy(slot).wait()
        own[at, top, :] += y2r[slot].astype(f32)
        own[at, low, :] += x2r[slot].astype(f32)

        @pl.when(outer)
        def _():
            zs[slot] = own[at].astype(bf16)

            @pl.when(u >= z_slots)
            def _():
                pl.semaphore_wait(credit, 1)

            z1_copy(slot, lax.rem(u, z_slots)).start()

    def cross(u):
        slot, at = lax.rem(u, 4), lax.rem(u, own.shape[0])
        x_copy(slot).wait()
        y_copy(slot).wait()
        y2s[slot] = (ty[slot] + xr[slot, 1].astype(f32)).astype(bf16)
        y2_copy(slot).start()
        x2s[slot] = (tx[slot] + yr[slot, 1].astype(f32)).astype(bf16)
        x2_copy(slot).start()
        own[at, top, :] += xr[slot, 0].astype(f32)
        own[at, low, :] += yr[slot, 0].astype(f32)

    def cross_ready(u):
        slot, at = lax.rem(u, 4), lax.rem(u, own.shape[0])
        for copy in ready_copies(u):
            copy.wait()
        y2s[slot] = (ty_l[slot].astype(f32) + xr_l[slot, 1].astype(f32)).astype(bf16)
        y2_copy(slot).start()
        x2s[slot] = (tx_l[slot].astype(f32) + yr_l[slot, 1].astype(f32)).astype(bf16)
        x2_copy(slot).start()
        own[at, top, :] = own_l[slot, top, :].astype(f32) + xr_l[slot, 0].astype(f32)
        own[at, low, :] = own_l[slot, low, :].astype(f32) + yr_l[slot, 0].astype(f32)

    def chip(u):
        slot, at = lax.rem(u, 4), lax.rem(u, own.shape[0])
        w = (u - extras) // 2
        pair = lax.rem(w, 2)
        stacked = terms.stack(w, 0)
        core_copy(pair).wait()
        total = stacked[3 * rows :] + crecv[pair, 3].astype(f32)
        xs[slot, 1] = total[:half].astype(bf16)
        ys[slot, 1] = total[half:].astype(bf16)
        total = stacked[rows : 2 * rows] + crecv[pair, 1].astype(f32)
        xs[slot, 0] = total[:half].astype(bf16)
        tx[slot] = total[half:]
        x_copy(slot).start()
        total = stacked[2 * rows : 3 * rows] + crecv[pair, 2].astype(f32)
        ys[slot, 0] = total[half:].astype(bf16)
        ty[slot] = total[:half]
        y_copy(slot).start()
        own[at] = stacked[:rows] + crecv[pair, 0].astype(f32)

    def chip_extra(u):
        slot, at = lax.rem(u, 4), lax.rem(u, own.shape[0])
        extra_copy(u).wait()
        for m, (mx, my) in enumerate(PLACES):
            total = extra[u, terms.block(0, mx, my)] + cx_r[u, m].astype(f32)
            if m == 0:
                own[at, :few, :] = total
            elif m == 2:
                ty[slot, :few, :] = total
            else:
                xs[slot, m // 2, :few, :] = total.astype(bf16)
        x_copy(slot).start()
        y_copy(slot).start()

    def open_extra(u):
        for m, (mx, my) in enumerate(PLACES):
            cx_s[u, m] = extra[u, terms.block(1, mx, my)].astype(bf16)
        extra_copy(u).start()

    def open_ready(u):
        for copy in ready_copies(u):
            copy.start()

    def open_unit(u):
        w = (u - extras) // 2
        pair = lax.rem(w, 2)
        csend[pair] = terms.stack(w, 1).astype(bf16).reshape(csend.shape[1:])
        core_copy(pair).start()

    def full(u):
        return lax.rem(u - extras, 2) == 1

    def prepared(u):
        return lax.rem(u - extras, 2) == 0

    def step(t, carry):
        stage(t - 13, None, share, 0, extras)
        stage(t - 12, inner, close, extras)
        stage(t - 12, outer, arrive, extras)
        stage(t - 12, inner, close_extra, 0, extras)
        stage(t - 12, outer, arrive_extra, 0, extras)
        stage(t - 10, inner, finish)
        stage(t - 8, inner, middle)
        stage(t - 8, outer, sent)
        stage(t - 6, None, plane)
        stage(t - 4, full(t - 4), cross, extras)
        stage(t - 4, None, cross, 0, extras)
        stage(t - 4, prepared(t - 4), cross_ready, extras)
        stage(t - 2, full(t - 2), chip, extras)
        stage(t - 2, None, chip_extra, 0, extras)
        pl.when(t == extras)(terms.wait)
        stage(t, full(t), open_unit, extras)
        stage(t, prepared(t), open_ready, extras)
        stage(t, None, open_extra, 0, extras)
        return carry

    lax.fori_loop(0, count + 12, step, 0)
    for u in range(extras):
        for there in others:
            share_copy(u, f, there).wait_send()
            share_copy(u, there, there).wait_recv()
        share_own(u).wait()


def reduce_grads(lefts, rights, ready, extra):
    tokens, width = lefts[1].shape
    rows, unit = width // 8, UNIT_WIDTH
    half = pad_to(rows // 2, 16)
    ins = (*lefts, *rights)
    extras, few = width // unit, extra.shape[1]
    count = extras + 2 * MATRICES * (width // unit)
    bf16, f32 = jnp.bfloat16, jnp.float32
    buf = lambda dtype, *shape: pltpu.VMEM((*shape, unit), dtype)
    sem = lambda *size: pltpu.SemaphoreType.DMA(size)
    z_slots = 8
    rest = rows - half
    return pl.pallas_call(
        functools.partial(reduce_kernel, width, half),
        out_shape=(
            jax.ShapeDtypeStruct((2, rows, (MATRICES - 4) * width), bf16),
            jax.ShapeDtypeStruct((2, 4 * rows, width), bf16),
            jax.ShapeDtypeStruct((few, width), bf16),
            jax.ShapeDtypeStruct(extra.shape, bf16),
        ),
        in_specs=[HB] * 14,
        out_specs=(HB, HB, HB, HB),
        scratch_shapes=[
            *term_scratch(ins, unit),
            buf(f32, extras, 8, few), sem(extras), buf(bf16, extras, 4, few), buf(bf16, extras, 4, few),
            sem(extras), sem(extras), sem(extras, 8), sem(extras, 8),
            buf(bf16, 2, 4, rows), buf(bf16, 2, 4, rows), buf(f32, 9, rows),
            buf(bf16, 4, 2, half), buf(bf16, 4, 2, half), buf(bf16, 4, 2, rest), buf(bf16, 4, 2, rest),
            buf(f32, 4, rest), buf(f32, 4, half),
            buf(bf16, 4, rest), buf(bf16, 4, rest), buf(bf16, 4, half), buf(bf16, 4, half),
            buf(bf16, 4, rows), buf(bf16, z_slots, rows), buf(bf16, 4, rows), buf(bf16, 4, rows), buf(bf16, 4, rows),
            buf(bf16, 4, rows), buf(bf16, 4, 2, half), buf(bf16, 4, 2, rest), buf(bf16, 4, rest), buf(bf16, 4, half),
            sem(5, 4),
            sem(2), sem(2), sem(4), sem(4), sem(4), sem(4), sem(4), sem(4), sem(4), sem(4),
            sem(4), sem(z_slots), sem(4), sem(4), sem(4), sem(4), sem(count), pltpu.SemaphoreType.REGULAR,
        ],
        compiler_params=pltpu.CompilerParams(
            collective_id=5, has_side_effects=True, vmem_limit_bytes=60 * 1024 * 1024
        ),
        cost_estimate=pl.CostEstimate(
            flops=2 * 64 * width * width * tokens, bytes_accessed=100 << 20, transcendentals=0
        ),
    )(*ins, extra, *ready)


def pre_norm(stream, shift, scale):
    centred = stream - jnp.mean(stream, axis=-1, keepdims=True)
    spread = jnp.mean(centred * centred, axis=-1, keepdims=True)
    return centred * lax.rsqrt(spread + NORM_EPS) * (1.0 + scale) + shift


def latent_ids(latent_len, positions, token_total):
    starts = jnp.cumsum(latent_len) - latent_len
    found = jnp.sum((starts[None, :] <= positions[:, None]).astype(jnp.int32), axis=1) - 1
    inside = (positions >= 0) & (positions < token_total)
    return jnp.where(inside, found, -1)


def low_dot(left, right):
    return jnp.dot(left, right, preferred_element_type=jnp.float32)


TILE = 512
GELU_ROOT = math.sqrt(2.0 / math.pi)


def thirds(values):
    high = values.astype(jnp.bfloat16)
    rest = values - high.astype(jnp.float32)
    middle = rest.astype(jnp.bfloat16)
    return high, middle, (rest - middle.astype(jnp.float32)).astype(jnp.bfloat16)


def halves_across(width):
    first = pad_to(width // 2, LANES)
    return (pl.ds(0, first), pl.ds(first, width - first))


def at_tile(at, size=TILE):
    return pl.ds(pl.multiple_of(at * size, size), size)


def tiles(count, body):
    def run(at, carry):
        body(at)
        return carry

    lax.fori_loop(0, count, run, 0)


def norm_parts(stream):
    centred = stream - jnp.mean(stream, axis=1, keepdims=True)
    root = lax.rsqrt(jnp.mean(centred * centred, axis=1, keepdims=True) + NORM_EPS)
    return centred * root, root


class FeedForward:
    def __init__(self, pick, mod, weights, held, sems):
        self.pick, self.mod = pick, mod
        self.out_w, self.up_w, self.down_w = held
        self.width, self.hidden = held[1].shape
        self.pieces = sems.shape[0] // 2
        self.piece = self.hidden // self.pieces
        cuts = [pl.ds(at * self.piece, self.piece) for at in range(self.pieces)]
        copy = pltpu.make_async_copy
        self.out_copy = copy(weights[0], held[0], sems.at[0])
        self.up_copies = [copy(weights[1].at[:, cut], held[1].at[:, cut], sems.at[1 + at]) for at, cut in enumerate(cuts)]
        self.down_copies = [
            copy(weights[2].at[cut, :], held[2].at[cut, :], sems.at[1 + self.pieces + at]) for at, cut in enumerate(cuts)
        ]

    def start(self, forth):
        order = [self.out_copy, *self.up_copies, *self.down_copies]
        for part in order if forth else [*self.down_copies, *self.up_copies, self.out_copy]:
            part.start()

    def vector(self, rows, at):
        return nn_dot(self.pick[rows, :], self.mod[:, at * self.width : (at + 1) * self.width])

    def forward(self, stream, mixed, biases, branch, middle, normed, hidden, active, result, after):
        out_b, up_b, down_b = biases
        size, width = stream.shape
        self.out_copy.wait()
        for here in halves_across(width):
            branch[:, here] = nn_dot(mixed[...], self.out_w[:, here]) + out_b[:, here].astype(jnp.float32)

        def first_norm(rows):
            total = stream[rows, :] + self.vector(rows, 2) * branch[rows, :]
            middle[rows, :] = total
            unit, _ = norm_parts(total)
            normed[rows, :] = (unit * (1.0 + self.vector(rows, 4)) + self.vector(rows, 3)).astype(jnp.bfloat16)

        by_rows(size, first_norm)
        for piece in range(self.pieces):
            self.up_copies[piece].wait()

            def widen(at, piece=piece):
                here = at_tile(piece * (self.piece // TILE) + at)
                values = nn_dot(normed[...], self.up_w[:, here]) + up_b[:, here].astype(jnp.float32)
                hidden[:, here] = values
                inner = GELU_ROOT * (values + 0.044715 * values * values * values)
                active[:, here] = (0.5 * values * (1.0 + jnp.tanh(inner))).astype(jnp.bfloat16)

            tiles(self.piece // TILE, widen)
        for part in self.down_copies:
            part.wait()
        for here in halves_across(width):
            result[:, here] = nn_dot(active[...], self.down_w[:, here]) + down_b[:, here].astype(jnp.float32)

        def leave(rows):
            after[rows, :] = (middle[rows, :] + self.vector(rows, 5) * result[rows, :]).astype(after.dtype)

        by_rows(size, leave)

    def backward(self, grad, branch, middle, hidden, result, outs, work, fresh):
        low_result, low_hidden, low_branch, low_mixed, grad_middle, grad_mod, out_sum, up_sum, down_sum = outs
        size, width = middle.shape
        grad_mod[...] = jnp.zeros_like(grad_mod)
        for ref in (out_sum, up_sum, down_sum):
            ref[...] = jnp.zeros_like(ref)

        latents = grad_mod.shape[0] // 4

        def collect(rows, at, values):
            here = slice(at * latents, (at + 1) * latents)
            ones = self.pick[rows, :latents]
            for part in thirds(values)[:2]:
                grad_mod[here, :] += lax.dot_general(
                    ones, part, (((0,), (0,)), ((), ())), preferred_element_type=jnp.float32
                )

        def total(values):
            return jnp.sum(values.astype(jnp.float32), axis=0, keepdims=True)

        def enter(rows):
            values = grad[rows, :].astype(jnp.float32)
            low = (self.vector(rows, 5) * values).astype(jnp.bfloat16)
            low_result[rows, :] = low
            down_sum[...] += total(low)
            collect(rows, 3, values * result[rows, :])

        by_rows(size, enter)

        def widen(at):
            here = at_tile(at)
            values = hidden[:, here]
            square = values * values
            bent = jnp.tanh(GELU_ROOT * (values + 0.044715 * values * square))
            slope = 0.5 * (1.0 + bent) + 0.5 * values * (1.0 - bent * bent) * (GELU_ROOT * (1.0 + 3 * 0.044715 * square))
            low = (nt_dot(low_result[...], self.down_w[here, :]) * slope).astype(jnp.bfloat16)
            low_hidden[:, here] = low
            up_sum[:, here] = total(low)

        for part in self.down_copies if fresh else ():
            part.wait()
        tiles(self.hidden // TILE, widen)
        for part in self.up_copies if fresh else ():
            part.wait()
        for here in halves_across(width):
            work[:, here] = nt_dot(low_hidden[...], self.up_w[here, :])

        def norm_back(rows):
            unit, root = norm_parts(middle[rows, :])
            values = work[rows, :]
            collect(rows, 1, values)
            collect(rows, 2, values * unit)
            scaled = values * (1.0 + self.vector(rows, 4))
            inside = scaled - jnp.mean(scaled, axis=1, keepdims=True)
            inside = inside - unit * jnp.mean(scaled * unit, axis=1, keepdims=True)
            here = grad[rows, :].astype(jnp.float32) + root * inside
            grad_middle[rows, :] = here
            low = (self.vector(rows, 2) * here).astype(jnp.bfloat16)
            low_branch[rows, :] = low
            out_sum[...] += total(low)
            collect(rows, 0, here * branch[rows, :])

        by_rows(size, norm_back)

        if fresh:
            self.out_copy.wait()
        for here in halves_across(width):
            low_mixed[:, here] = nt_dot(low_branch[...], self.out_w[here, :]).astype(jnp.bfloat16)


def feed_kernel(forth, back, *refs):
    pick, mod, out_w, up_w, down_w, out_b, up_b, down_b, *refs = refs
    weights, biases = (out_w, up_w, down_w), (out_b, up_b, down_b)
    if forth and not back:
        stream, mixed, branch, middle, normed, hidden, active, result, after, *refs = refs
        held, sems = refs[:3], refs[3]
    elif back and not forth:
        grad, branch, middle, hidden, result, *refs = refs
        outs, (*held, sems, work) = refs[:9], refs[9:]
    else:
        stream, mixed, grad, normed, active, after, *refs = refs
        outs, (*held, sems, work, branch, middle, hidden, result) = refs[:9], refs[9:]
    feed = FeedForward(pick, mod, weights, held, sems)
    feed.start(forth)
    if forth:
        feed.forward(stream, mixed, biases, branch, middle, normed, hidden, active, result, after)
    if back:
        feed.backward(grad, branch, middle, hidden, result, outs, work, not forth)


def feed_call(forth, back, ins, full, pick, mod, dtype):
    qkv_w, qkv_b, out_w, out_b, up_w, up_b, down_w, down_b = full
    size, latents = pick.shape
    width, hidden = up_w.shape
    bf16, f32 = jnp.bfloat16, jnp.float32
    shape = lambda columns, dtype, rows=size: jax.ShapeDtypeStruct((rows, columns), dtype)
    saved = (shape(width, f32), shape(width, f32), shape(width, bf16), shape(hidden, f32), shape(hidden, bf16), shape(width, f32))
    after = shape(width, dtype)
    outs = (
        shape(width, bf16), shape(hidden, bf16), shape(width, bf16), shape(width, bf16), shape(width, f32),
        shape(width, f32, 4 * latents), shape(width, f32, 1), shape(hidden, f32, 1), shape(width, f32, 1),
    )
    scratch = [pltpu.VMEM(part.shape, part.dtype) for part in (out_w, up_w, down_w)]
    scratch.append(pltpu.SemaphoreType.DMA((1 + 2 * (hidden // (3 * TILE)),)))
    if back:
        scratch.append(pltpu.VMEM((size, width), f32))
    if forth and back:
        scratch += [pltpu.VMEM((size, columns), f32) for columns in (width, width, hidden, width)]
        shapes = (saved[2], saved[4], after, *outs)
    else:
        shapes = (*saved, after) if forth else outs
    return pl.pallas_call(
        functools.partial(feed_kernel, forth, back),
        out_shape=shapes,
        in_specs=[VM, VM, HB, HB, HB, VM, VM, VM] + [VM] * len(ins),
        out_specs=(VM,) * len(shapes),
        scratch_shapes=scratch,
        compiler_params=pltpu.CompilerParams(vmem_limit_bytes=60 * 1024 * 1024),
    )(
        jnp.concatenate([pick.astype(bf16)] * 3, axis=1), jnp.concatenate(thirds(mod), axis=0), out_w, up_w, down_w,
        out_b[None], up_b[None], down_b[None], *ins,
    )


def layer_forward(stream, modulation, full, plan, in_first, shards_first, shards_second, shards_ahead, collective_id):
    qkv_w, qkv_b, out_w, out_b, up_w, up_b, down_w, down_b = full
    reps, edge, bounds, ids = plan
    width = stream.shape[1]
    hd = width // reps
    nh = HEADS // reps
    mod, pick, front = modulation
    shift_one, scale_one = jnp.split(front, 2, axis=1)
    normed = pre_norm(stream, shift_one, scale_one).astype(jnp.bfloat16)
    qkv_bias = qkv_b.astype(jnp.float32)
    bias_full = jnp.concatenate(
        [qkv_bias[:width], jnp.zeros((width,), jnp.float32), qkv_bias[width:]]
    )
    projected = (low_dot(normed, qkv_w) + bias_full).astype(jnp.bfloat16)
    in_second = sent_ahead(shards_first, projected) if shards_first else []
    own, prev, after, fulls = to_heads(projected, reps, edge, pad_to(2 * hd, LANES), in_first, collective_id)
    first_gathered = fulls
    in_second += sent_ahead(shards_second, own) if shards_second else []
    mixed, mixed_t, log_norm = attend(nh, hd, *bounds, prev, own, after, *ids)
    mixed, fulls = swap(mixed, reps, True, in_second, collective_id + 1)
    if in_first:
        (up_w,), (down_w, *fulls) = first_gathered, fulls
    in_next = sent_ahead(shards_ahead, mixed) if shards_ahead else ()
    full = (qkv_w, qkv_b, out_w, out_b, up_w, up_b, down_w, down_b)
    saved = (normed, (prev, own, after), mixed, (mixed_t, log_norm))
    return (saved, full, fulls, in_next)


def layer_backward(stream, modulation, full, saved, feed_grads, plan, beside):
    qkv_w = full[0]
    normed, window, mixed, kept = saved
    normed_two, active, grad_result, grad_hidden, grad_branch, grad_mixed, grad_middle, grad_mod, *bias_sums = feed_grads
    reps, edge, bounds, ids = plan
    width = stream.shape[1]
    hd = width // reps
    nh = HEADS // reps
    mod, pick, front = modulation
    shift_one, scale_one = jnp.split(front, 2, axis=1)
    grad_heads, _ = swap(grad_mixed, reps, False, (), 3)
    prev, own, after = window
    grad_q, grad_prev, grad_own, grad_after = attend_back(
        nh, hd, *bounds, prev, own, after, *ids, grad_heads.reshape(own.shape[0], -1), *kept
    )
    grad_projected = from_heads(reps, width, grad_prev, grad_own, grad_after, grad_q, 4)
    grad_projected, beside = lax.optimization_barrier((grad_projected, beside))
    sums = jnp.sum(grad_projected.astype(jnp.float32), axis=0)
    grad_qkv_b = jnp.concatenate([sums[:width], sums[2 * width :]])
    grad_normed = jnp.einsum("te,de->td", grad_projected, qkv_w, preferred_element_type=jnp.float32)
    _, norm_back_one = jax.vjp(pre_norm, stream, shift_one, scale_one)
    grad_stream_part, grad_shift_one, grad_scale_one = norm_back_one(grad_normed)
    grad_stream = grad_middle + grad_stream_part
    grad_mod = jnp.concatenate(
        [
            jnp.einsum("tl,tm->lm", pick, part, precision=HIGH, preferred_element_type=jnp.float32)
            for part in (grad_shift_one, grad_scale_one)
        ]
        + [grad_mod],
    )
    return (
        grad_stream, grad_mod,
        ((active, normed_two, mixed, normed), (grad_result, grad_hidden, grad_branch, grad_projected)),
        (grad_qkv_b, *(part[0] for part in bias_sums)), beside,
    )


def bias_parts(stacked, params):
    return [stacked[:, row, : params[at].shape[0]].reshape(-1) for row, at in enumerate((3, 5, 7, 9))]


def modulation(partial_terms, layers):
    longest = pad_to(max(params[at].shape[0] for params in layers for at in (3, 5, 7, 9)), LANES)
    shares = jnp.stack(
        [jnp.pad(params[at], (0, longest - params[at].shape[0])) for params in layers for at in (3, 5, 7, 9)]
    )
    if not on_planes():
        mods = lax.psum(tuple(partial_terms), "fsdp")
        stacked = lax.all_gather(shares, "fsdp", axis=0)
        fulls = [lax.all_gather(layers[0][at], "fsdp", axis=0, tiled=True) for at in (2, 4)]
    else:
        width = layers[0][4].shape[1]
        parts = partial_terms[0].reshape(8, -1, width)
        some = parts.shape[1]
        parts = jnp.pad(parts, ((0, 0), (0, pad_to(some, 8) - some), (0, 0)))
        mod, stacked, *fulls = start(
            parts, jnp.pad(shares, ((0, 16 - shares.shape[0]), (0, 0))), [(layers[0][at],) for at in (2, 4)], 6
        )
        mods = [mod[:, :some].reshape(partial_terms[0].shape)] + [lax.psum(term, "fsdp") for term in partial_terms[1:]]
    return mods, [bias_parts(stacked[:, 4 * at : 4 * at + 4], params) for at, params in enumerate(layers)], fulls


def on_planes():
    return lax.axis_size("fsdp") == 8 and lax.axis_size("replica") == 4


def first_hop(lefts, rights):
    own, xs, ys, tx, ty = chip_sums(lefts, rights, 11)
    hop = lambda value, step: lax.ppermute(value, "fsdp", [(at, at ^ step) for at in range(8)])
    return (own, hop(xs, 2), hop(ys, 4), tx, ty), own


def owner_sums(pairs, ready, grad_mods, grad_biases):
    groups = lax.axis_size("fsdp")
    width = pairs[0][0][1].shape[1]
    if on_planes():
        mods = jnp.concatenate(grad_mods).reshape(groups, -1, width)
        biases = jnp.stack(
            [jnp.concatenate([part.reshape(groups, -1) for part in parts], axis=1) for parts in grad_biases], axis=1
        )
        used, lines = mods.shape[1], pad_to(mods.shape[1] + 2, 16)
        biases = jnp.pad(biases, ((0, 0), (0, lines - used - 2), (0, 0)))
        out, out_down, mine, shared = reduce_grads(*pairs[0], ready, jnp.concatenate([mods, biases], axis=1))
        mods = shared[:, :used].reshape(2, -1, width)
        shares = mine[used : used + 2].astype(jnp.float32)
        results = []
        for layer_at in range(2):
            columns = lambda first, last: out[layer_at, :, (first - 4) * width : (last - 4) * width].astype(jnp.float32)
            cuts = [0]
            for part in grad_biases[layer_at]:
                cuts.append(cuts[-1] + part.shape[0] // groups)
            weights = (columns(9, 12), columns(8, 9), columns(4, 8), out_down[layer_at].astype(jnp.float32))
            results.append((weights, [shares[layer_at, i:j] for i, j in zip(cuts[:-1], cuts[1:])]))
        return results, mods
    flat = jnp.concatenate([part for parts in grad_biases for part in parts])
    *mods, flat = lax.psum((*grad_mods, flat), ("fsdp", "replica"))
    results, place = [], 0
    for (lefts, rights), parts in zip(pairs, grad_biases):
        grads, biases = [], []
        for left, right in zip(lefts, rights):
            grad = low_dot(left.T, right).astype(jnp.bfloat16)
            part = lax.psum_scatter(grad, "fsdp", scatter_dimension=0, tiled=True)
            grads.append(lax.psum(part, "replica").astype(jnp.float32))
        for part in parts:
            share = part.shape[0] // groups
            biases.append(lax.dynamic_slice_in_dim(flat, place + lax.axis_index("fsdp") * share, share, 0))
            place += part.shape[0]
        results.append((grads[::-1], biases))
    return results, mods


def attention_plan(latent_len, tok_rows, reps, device_at):
    column = tok_rows * reps
    edge = MAXLEN
    total = jnp.sum(latent_len)
    first = lax.axis_index("fsdp") * column
    positions = first - edge + jnp.arange(column + 2 * edge, dtype=jnp.int32)
    ends = jnp.cumsum(latent_len)
    ids = jnp.sum((ends[None, :] <= positions[:, None]).astype(jnp.int32), axis=1)
    ids = jnp.where(positions < 0, -1, ids)
    own = ids[edge : edge + column]
    count = column // BQ
    firsts, lasts = own[::BQ], own[BQ - 1 :: BQ]
    pick = lambda at: (at[:, None] == jnp.arange(latent_len.shape[0], dtype=jnp.int32)[None, :]).astype(jnp.int32)
    low = jnp.sum(pick(firsts) * (ends - latent_len)[None, :], axis=1) - (first - edge)
    high = jnp.sum(pick(lasts) * ends[None, :], axis=1) - (first - edge)
    bounds = ((low // BK).astype(jnp.int32), ((high + BK - 1) // BK).astype(jnp.int32))
    kid = jnp.broadcast_to(ids[:, None], (ids.shape[0], LANES))
    qid = jnp.broadcast_to(own[None, :], (8, column))
    return (reps, edge, bounds, (kid, qid))


def shards(
    tokens,
    cond,
    latent_len,
    first_ada_weight,
    first_ada_bias,
    first_qkv_weight,
    first_qkv_bias,
    first_out_weight,
    first_out_bias,
    first_up_weight,
    first_up_bias,
    first_down_weight,
    first_down_bias,
    second_ada_weight,
    second_ada_bias,
    second_qkv_weight,
    second_qkv_bias,
    second_out_weight,
    second_out_bias,
    second_up_weight,
    second_up_bias,
    second_down_weight,
    second_down_bias,
    cotangent,
):
    tok_rows = tokens.shape[0]
    group_place = lax.axis_index("fsdp")
    device_at = lax.axis_index(("fsdp", "replica"))
    token_total = tok_rows * lax.axis_size(("fsdp", "replica"))
    latent_count = cond.shape[0]
    local_pos = jnp.arange(tok_rows, dtype=jnp.int32)
    own_ids = latent_ids(latent_len, device_at * tok_rows + local_pos, token_total)
    pick = (own_ids[:, None] == jnp.arange(latent_count, dtype=jnp.int32)[None, :]).astype(
        jnp.float32
    )
    plan = attention_plan(latent_len, tok_rows, lax.axis_size("replica"), device_at)
    layers = (
        (
            first_ada_weight,
            first_ada_bias,
            first_qkv_weight,
            first_qkv_bias,
            first_out_weight,
            first_out_bias,
            first_up_weight,
            first_up_bias,
            first_down_weight,
            first_down_bias,
        ),
        (
            second_ada_weight,
            second_ada_bias,
            second_qkv_weight,
            second_qkv_bias,
            second_out_weight,
            second_out_bias,
            second_up_weight,
            second_up_bias,
            second_down_weight,
            second_down_bias,
        ),
    )
    col_width = first_ada_weight.shape[0]
    own_cond = lax.dynamic_slice_in_dim(
        cond.astype(jnp.float32), group_place * col_width, col_width, 1
    )
    own_silu = jax.nn.silu(own_cond).astype(jnp.bfloat16)
    partial_terms = []
    for params in layers:
        term = low_dot(own_silu, params[0])
        bias_share = params[1].astype(jnp.float32)
        spread = lax.dynamic_update_slice_in_dim(
            jnp.zeros((term.shape[1],), jnp.float32),
            bias_share,
            group_place * bias_share.shape[0],
            0,
        )
        partial_terms.append(term + spread[None, :])
    (mod_first, mod_second), biases, attention_weights = modulation(partial_terms, layers)
    mod_tokens = tuple(
        (mod, pick, jnp.dot(pick, mod[:, : 2 * tokens.shape[1]], precision=HIGH, preferred_element_type=jnp.float32))
        for mod in (mod_first, mod_second)
    )
    stream = tokens.astype(jnp.float32)
    inputs = []
    kept = []
    whole = lambda value: lax.all_gather(value, "fsdp", axis=0, tiled=True)
    fulls = []
    in_first = sent_ahead((first_up_weight,), mod_first) if on_planes() else ()
    for layer_at, params in enumerate(layers):
        inputs.append(stream)
        ahead = layers[layer_at + 1] if layer_at + 1 < len(layers) else None
        qkv_w, out_w = attention_weights
        qkv_b, out_b, up_b, down_b = biases[layer_at]
        shards_first, shards_second, shards_ahead, up_w, down_w = (), (), (), None, None
        if on_planes():
            shards_first = (params[8],)
            shards_second = () if ahead is None else (ahead[2], ahead[4])
            shards_ahead = () if ahead is None else (ahead[6],)
        else:
            up_w, down_w = whole(params[6]), whole(params[8])
        full = (qkv_w, qkv_b, out_w, out_b, up_w, up_b, down_w, down_b)
        saved, full, attention_weights, in_first = layer_forward(
            stream, mod_tokens[layer_at], full, plan, in_first, shards_first, shards_second, shards_ahead, 7 + 2 * layer_at
        )
        if layer_at == 0:
            *feed_saved, stream = feed_call(
                True, False, (stream, saved[2]), full, pick, mod_tokens[0][0], jnp.float32
            )
        else:
            normed_two, active, output, *feed_grads = feed_call(
                True, True, (stream, saved[2], cotangent), full, pick, mod_tokens[1][0], jnp.bfloat16
            )
            feed_grads = [normed_two, active, *feed_grads]
        fulls.append(full)
        if ahead is not None and not on_planes():
            attention_weights = [whole(ahead[at]) for at in (2, 4)]
        kept.append(saved)
    weight_pairs = [None, None]
    ready = ()
    mod_grads = [None, None]
    bias_grads = [None, None]
    for layer_at in (1, 0):
        if layer_at == 0:
            branch, middle, normed_two, hidden, active, result = feed_saved
            feed_grads = feed_call(
                False, True, (grad_stream, branch, middle, hidden, result), fulls[0], pick, mod_tokens[0][0], jnp.float32
            )
            feed_grads = [normed_two, active, *feed_grads]
        grad_stream, grad_mod, local_grads, local_biases, ready = layer_backward(
            inputs[layer_at], mod_tokens[layer_at], fulls[layer_at], kept[layer_at], feed_grads, plan, ready
        )
        weight_pairs[layer_at] = local_grads
        if layer_at == 1 and on_planes():
            ready, own = first_hop(*local_grads)
            grad_stream, _ = lax.optimization_barrier((grad_stream, own))
        mod_grads[layer_at] = grad_mod
        bias_grads[layer_at] = local_biases
    sums, (grad_mod_first, grad_mod_second) = owner_sums(weight_pairs, ready, mod_grads, bias_grads)
    grad_silu = jnp.zeros(own_cond.shape, jnp.float32)
    ada_grads = []
    for params, grad_mod in zip(layers, (grad_mod_first, grad_mod_second)):
        low_mod = grad_mod.astype(jnp.bfloat16).reshape(6, latent_count, -1).transpose(1, 0, 2).reshape(latent_count, -1)
        weight_grad = jnp.einsum("ld,lm->dm", own_silu, low_mod, preferred_element_type=jnp.float32)
        column_sums = jnp.sum(low_mod.astype(jnp.float32), axis=0)
        bias_rows = params[1].shape[0]
        bias_grad = lax.dynamic_slice_in_dim(column_sums, group_place * bias_rows, bias_rows, 0)
        grad_silu = grad_silu + jnp.einsum(
            "lm,dm->ld", low_mod, params[0], preferred_element_type=jnp.float32
        )
        ada_grads.append((weight_grad, bias_grad))
    _, silu_back = jax.vjp(jax.nn.silu, own_cond)
    cond_grad = silu_back(grad_silu)[0]
    outs = [output, grad_stream, cond_grad]
    for layer_at in range(2):
        outs += list(ada_grads[layer_at])
        for weight, bias in zip(*sums[layer_at]):
            outs += [weight, bias]
    return tuple(outs)


def solution(mesh):
    in_specs = (
        P(("fsdp", "replica"), None),
        P(),
        P(),
        P("fsdp", None),
        P("fsdp"),
        P("fsdp", None),
        P("fsdp"),
        P("fsdp", None),
        P("fsdp"),
        P("fsdp", None),
        P("fsdp"),
        P("fsdp", None),
        P("fsdp"),
        P("fsdp", None),
        P("fsdp"),
        P("fsdp", None),
        P("fsdp"),
        P("fsdp", None),
        P("fsdp"),
        P("fsdp", None),
        P("fsdp"),
        P("fsdp", None),
        P("fsdp"),
        P(("fsdp", "replica"), None),
    )
    out_specs = (
        P(("fsdp", "replica"), None),
        P(("fsdp", "replica"), None),
        P(None, "fsdp"),
        P("fsdp", None),
        P("fsdp"),
        P("fsdp", None),
        P("fsdp"),
        P("fsdp", None),
        P("fsdp"),
        P("fsdp", None),
        P("fsdp"),
        P("fsdp", None),
        P("fsdp"),
        P("fsdp", None),
        P("fsdp"),
        P("fsdp", None),
        P("fsdp"),
        P("fsdp", None),
        P("fsdp"),
        P("fsdp", None),
        P("fsdp"),
        P("fsdp", None),
        P("fsdp"),
    )
    return jax.shard_map(shards, mesh=mesh, in_specs=in_specs, out_specs=out_specs, check_vma=False)
```

```python
import functools
import math

import jax
import jax.numpy as jnp
from jax import lax
from jax.experimental import pallas as pl
from jax.experimental.pallas import tpu as pltpu
from jax.sharding import PartitionSpec as P

HEADS = 16
HEAD_DIM = 72
MAXLEN = 1024
NORM_EPS = 1e-06
HIGH = lax.Precision.HIGHEST
BQ = 256
BK = 256
LANES = 128
NEG = -1e30
VM = pl.BlockSpec(memory_space=pltpu.VMEM)
SM = pl.BlockSpec(memory_space=pltpu.SMEM)
HB = pl.BlockSpec(memory_space=pl.ANY)
VMEM_LIMIT = 56 * 1024 * 1024


def pad_to(size, unit):
    return -(-size // unit) * unit


def take_head(ref, rows, at, dim):
    first, off = at // LANES * LANES, at % LANES
    wide = LANES if off + dim <= LANES else 2 * LANES
    block = ref[rows, first : first + wide].astype(jnp.float32)
    if off:
        block = pltpu.roll(block, wide - off, 1)
    block = block[:, :LANES]
    lane = lax.broadcasted_iota(jnp.int32, block.shape, 1)
    return jnp.where(lane < dim, block, 0.0)


def put_heads(blocks, places, width):
    tiles = [None] * (width // LANES)
    for block, at in zip(blocks, places):
        first, off = at // LANES, at % LANES
        wide = jnp.concatenate([block, jnp.zeros_like(block)], axis=1)
        if off:
            wide = pltpu.roll(wide, off, 1)
        for step in range(2):
            part = wide[:, step * LANES : (step + 1) * LANES]
            if first + step < len(tiles):
                old = tiles[first + step]
                tiles[first + step] = part if old is None else old + part
    rows = blocks[0].shape[0]
    return jnp.concatenate(
        [jnp.zeros((rows, LANES), jnp.float32) if t is None else t for t in tiles], axis=1
    )


def nt_dot(left, right):
    return lax.dot_general(left, right, (((1,), (1,)), ((), ())), preferred_element_type=jnp.float32)


def nn_dot(left, right):
    return jnp.dot(left, right, preferred_element_type=jnp.float32)


def rows_at(block, size):
    return pl.ds(pl.multiple_of(block * size, size), size)


def over_window(lo, hi, prev, own, after, action):
    edge, mid = prev.shape[0] // BK, own.shape[0] // BK

    def run(ref, first, count):
        def body(at, carry):
            action(ref, at - first, at)
            return carry

        lax.fori_loop(jnp.clip(lo, first, first + count), jnp.clip(hi, first, first + count), body, 0)

    run(prev, 0, edge)
    run(own, edge, mid)
    run(after, edge + mid, edge)


def attend_kernel(nh, hd, lo, hi, prev, own, after, kid, qid, o_ref, ot_ref, lse_ref, kh, vt, qh, acc, ml):
    dim = hd // nh
    width = o_ref.shape[1]
    count = own.shape[0] // BQ
    scale = math.log2(math.e) / math.sqrt(dim)

    def load(ref, at, to):
        for h in range(nh):
            kh[h, rows_at(to, BK), :] = take_head(ref, rows_at(at, BK), h * dim, dim).astype(jnp.bfloat16)
            vt[h, :, rows_at(to, BK)] = take_head(ref, rows_at(at, BK), hd + h * dim, dim).T.astype(jnp.bfloat16)

    over_window(lo[0], hi[count - 1], prev, own, after, load)
    lse_ref[...] = jnp.zeros_like(lse_ref)

    def query_block(qb, carry):
        rows = rows_at(qb, BQ)
        for h in range(nh):
            qh[h] = take_head(own, rows, 2 * hd + h * dim, dim).astype(jnp.bfloat16)
        acc[...] = jnp.zeros_like(acc)
        ml[0] = jnp.full(ml.shape[1:], NEG, jnp.float32)
        ml[1] = jnp.zeros(ml.shape[1:], jnp.float32)
        ids = qid[0:1, rows]

        def key_block(kb, inner):
            keys = rows_at(kb, BK)
            lanes = kid[keys, :]
            same = jnp.concatenate([lanes] * (BQ // LANES), axis=1) == ids
            scores = [jnp.where(same, nt_dot(kh[h, keys, :], qh[h]) * scale, NEG) for h in range(nh)]
            olds = [ml[0, h : h + 1, :] for h in range(nh)]
            tops = [jnp.maximum(old, jnp.max(s, axis=0, keepdims=True)) for old, s in zip(olds, scores)]
            probs = [jnp.exp2(s - top) for s, top in zip(scores, tops)]
            outs = [nn_dot(vt[h, :, keys], probs[h].astype(jnp.bfloat16)) for h in range(nh)]
            for h in range(nh):
                alpha = jnp.exp2(olds[h] - tops[h])
                ml[0, h : h + 1, :] = tops[h]
                ml[1, h : h + 1, :] = ml[1, h : h + 1, :] * alpha + jnp.sum(probs[h], axis=0, keepdims=True)
                acc[h] = acc[h] * alpha + outs[h]
            return inner

        lax.fori_loop(lo[qb], hi[qb], key_block, 0)
        parts = []
        for h in range(nh):
            total = ml[1, h : h + 1, :]
            out = acc[h, :dim, :] / total
            parts.append(out)
            lse_ref[h : h + 1, rows] = ml[0, h : h + 1, :] + jnp.log2(total)
        parts.append(jnp.zeros((width - hd, BQ), jnp.float32))
        heads = jnp.concatenate(parts, axis=0)
        ot_ref[:, rows] = heads
        o_ref[rows, :] = heads.T.astype(jnp.bfloat16)
        return carry

    lax.fori_loop(0, count, query_block, 0)


def attend(nh, hd, lo, hi, prev, own, after, kid, qid):
    rows, window = own.shape[0], own.shape[0] + 2 * prev.shape[0]
    width = pad_to(hd, LANES)
    return pl.pallas_call(
        functools.partial(attend_kernel, nh, hd),
        out_shape=(
            jax.ShapeDtypeStruct((rows, width), jnp.bfloat16),
            jax.ShapeDtypeStruct((width, rows), jnp.float32),
            jax.ShapeDtypeStruct((8, rows), jnp.float32),
        ),
        in_specs=[SM, SM, VM, VM, VM, VM, VM],
        out_specs=(VM, VM, VM),
        scratch_shapes=[
            pltpu.VMEM((nh, window, LANES), jnp.bfloat16),
            pltpu.VMEM((nh, LANES, window), jnp.bfloat16),
            pltpu.VMEM((nh, BQ, LANES), jnp.bfloat16),
            pltpu.VMEM((nh, LANES, BQ), jnp.float32),
            pltpu.VMEM((2, 8, BQ), jnp.float32),
        ],
        compiler_params=pltpu.CompilerParams(vmem_limit_bytes=VMEM_LIMIT),
    )(lo, hi, prev, own, after, kid, qid)


def attend_back_kernel(
    nh, hd, lo, hi, prev, own, after, kid, qid, do_ref, ot_ref, lse_ref,
    dq_ref, dprev, down, dafter, kh, vh, kt, qh, gh, dk, dv, dqt, delta,
):
    dim = hd // nh
    width = dq_ref.shape[1]
    count = own.shape[0] // BQ
    root = 1.0 / math.sqrt(dim)
    scale = math.log2(math.e) / math.sqrt(dim)

    def load(ref, at, to):
        for h in range(nh):
            k = take_head(ref, rows_at(at, BK), h * dim, dim)
            kh[h, rows_at(to, BK), :] = k.astype(jnp.bfloat16)
            kt[h, :, rows_at(to, BK)] = k.T.astype(jnp.bfloat16)
            vh[h, rows_at(to, BK), :] = take_head(ref, rows_at(at, BK), hd + h * dim, dim).astype(jnp.bfloat16)
            dk[h, rows_at(to, BK), :] = jnp.zeros((BK, LANES), jnp.float32)
            dv[h, rows_at(to, BK), :] = jnp.zeros((BK, LANES), jnp.float32)

    over_window(lo[0], hi[count - 1], prev, own, after, load)

    def query_block(qb, carry):
        rows = rows_at(qb, BQ)
        for h in range(nh):
            qh[h] = take_head(own, rows, 2 * hd + h * dim, dim).astype(jnp.bfloat16)
            gh[h] = take_head(do_ref, rows, h * dim, dim).astype(jnp.bfloat16)
        prod = do_ref[rows, :].astype(jnp.float32).T * ot_ref[:, rows]
        for h in range(nh):
            delta[h : h + 1, :] = jnp.sum(prod[h * dim : (h + 1) * dim], axis=0, keepdims=True)
        dqt[...] = jnp.zeros_like(dqt)
        ids = qid[0:1, rows]

        def key_block(kb, inner):
            keys = rows_at(kb, BK)
            lanes = kid[keys, :]
            same = jnp.concatenate([lanes] * (BQ // LANES), axis=1) == ids
            hs = range(nh)
            scores = [nt_dot(kh[h, keys, :], qh[h]) * scale - lse_ref[h : h + 1, rows] for h in hs]
            dps = [nt_dot(vh[h, keys, :], gh[h]) - delta[h : h + 1, :] for h in hs]
            probs = [jnp.exp2(jnp.where(same, s, NEG)) for s in scores]
            dss = [(p * dp).astype(jnp.bfloat16) for p, dp in zip(probs, dps)]
            lows = [p.astype(jnp.bfloat16) for p in probs]
            for h in hs:
                dv[h, keys, :] += nn_dot(lows[h], gh[h])
            for h in hs:
                dk[h, keys, :] += nn_dot(dss[h], qh[h])
            for h in hs:
                dqt[h] += nn_dot(kt[h, :, keys], dss[h])
            return inner

        lax.fori_loop(lo[qb], hi[qb], key_block, 0)
        parts = [dqt[h, :dim, :] * root for h in range(nh)]
        parts.append(jnp.zeros((width - hd, BQ), jnp.float32))
        dq_ref[rows, :] = jnp.concatenate(parts, axis=0).T.astype(jnp.bfloat16)
        return carry

    lax.fori_loop(0, count, query_block, 0)
    for ref in (dprev, dafter):
        ref[...] = jnp.zeros_like(ref)

    def store(ref, at, to):
        keys = rows_at(to, BK)
        blocks = [dk[h, keys, :] * root for h in range(nh)] + [dv[h, keys, :] for h in range(nh)]
        ref[rows_at(at, BK), :] = put_heads(blocks, [h * dim for h in range(2 * nh)], ref.shape[1]).astype(ref.dtype)

    over_window(lo[0], hi[count - 1], dprev, down, dafter, store)


def attend_back(nh, hd, lo, hi, prev, own, after, kid, qid, grad, ot, lse):
    rows, edge = own.shape[0], prev.shape[0]
    window = rows + 2 * edge
    width, kv = pad_to(hd, LANES), prev.shape[1]
    heads = lambda size, dtype: pltpu.VMEM((nh, size, LANES), dtype)
    return pl.pallas_call(
        functools.partial(attend_back_kernel, nh, hd),
        out_shape=(
            jax.ShapeDtypeStruct((rows, width), jnp.bfloat16),
            jax.ShapeDtypeStruct((edge, kv), jnp.bfloat16),
            jax.ShapeDtypeStruct((rows, kv), jnp.bfloat16),
            jax.ShapeDtypeStruct((edge, kv), jnp.bfloat16),
        ),
        in_specs=[SM, SM] + [VM] * 8,
        out_specs=(VM,) * 4,
        scratch_shapes=[
            heads(window, jnp.bfloat16),
            heads(window, jnp.bfloat16),
            pltpu.VMEM((nh, LANES, window), jnp.bfloat16),
            heads(BQ, jnp.bfloat16),
            heads(BQ, jnp.bfloat16),
            heads(window, jnp.float32),
            heads(window, jnp.float32),
            pltpu.VMEM((nh, LANES, BQ), jnp.float32),
            pltpu.VMEM((8, BQ), jnp.float32),
        ],
        compiler_params=pltpu.CompilerParams(vmem_limit_bytes=VMEM_LIMIT),
    )(lo, hi, prev, own, after, kid, qid, grad, ot, lse)


MESH = pl.DeviceIdType.MESH


def greet(partners, count):
    barrier = pltpu.get_barrier_semaphore()
    for where, there in partners:
        @pl.when(there)
        def _():
            pl.semaphore_signal(barrier, inc=1, device_id=where, device_id_type=MESH)
    pl.semaphore_wait(barrier, count)


def wait_for(ref, sem):
    pltpu.make_async_copy(ref, ref, sem).wait()


def assemble(rows, width, pieces):
    tiles = [None] * (width // LANES)
    for ref, src, dst, count in pieces:
        off, to = src % LANES, dst % LANES
        wide = max(off + count, to + count)
        wide, have = pad_to(wide, LANES), pad_to(off + count, LANES)
        first = src // LANES * LANES
        block = ref[rows, first : first + have].astype(jnp.float32)
        lane = lax.broadcasted_iota(jnp.int32, block.shape, 1)
        block = jnp.where(jnp.logical_and(lane >= off, lane < off + count), block, 0.0)
        if wide > have:
            block = jnp.concatenate([block, jnp.zeros((block.shape[0], wide - have), jnp.float32)], axis=1)
        if off != to:
            block = pltpu.roll(block, (to - off) % wide, 1)
        for step in range(pad_to(to + count, LANES) // LANES):
            part = block[:, step * LANES : (step + 1) * LANES]
            at = dst // LANES + step
            tiles[at] = part if tiles[at] is None else tiles[at] + part
    size = next(t for t in tiles if t is not None).shape
    return jnp.concatenate([jnp.zeros(size, jnp.float32) if t is None else t for t in tiles], axis=1)


def by_rows(size, action, step=64):
    def body(at, carry):
        action(pl.ds(pl.multiple_of(at * step, step), step))
        return carry

    lax.fori_loop(0, size // step, body, 0)


class Gather:
    COPIES = 9

    def __init__(self, shards, fulls, halves, send, recv, load, store, *held):
        self.shards, self.fulls, self.halves, self.held = shards, fulls, halves, held
        self.send, self.recv, self.load, self.store = send, recv, load, store
        self.f, self.r = lax.axis_index("fsdp"), lax.axis_index("replica")
        f = self.f
        c, x, y = lax.rem(f, 2), lax.rem(f // 2, 2), f // 4
        self.core, self.x, self.y = f + 1 - 2 * c, f + 2 - 4 * x, f + 4 - 8 * y
        self.xy = self.x + 4 - 8 * y

    def rows(self, at, which):
        rows, half = self.shards[at][0].shape[0], self.halves[at]
        return {"all": (0, rows), "top": (0, half), "low": (half, rows - half)}[which]

    def part(self, at, place, which):
        first, size = self.rows(at, which)
        rows = self.shards[at][0].shape[0]
        return self.fulls[at].at[pl.ds(pl.multiple_of(place * rows + first, 16), size), :]

    def remote(self, at, kind, src, dst, to):
        return pltpu.make_async_remote_copy(
            src_ref=src, dst_ref=dst, send_sem=self.send.at[at, kind],
            recv_sem=self.recv.at[at, kind], device_id=(to, self.r), device_id_type=MESH,
        )

    def copy(self, at, kind, place, which, to, source=None):
        dst = self.part(at, place, which)
        src = dst if source is None else self.held[at].at[source, pl.ds(*self.rows(at, which)), :]
        return self.remote(at, kind, src, dst, to)

    def hop(self, at, source):
        return self.remote(at, 6 + source, self.held[at].at[0], self.held[at].at[source], (self.x, self.y)[source - 1])

    def keep(self, at, source):
        place = (self.f, self.x, self.y)[source]
        return pltpu.make_async_copy(self.held[at].at[source], self.part(at, place, "all"), self.store.at[at, source])

    def fetch(self, at, source):
        return pltpu.make_async_copy(self.shards[at][source], self.held[at].at[source], self.load.at[at, source])

    def pass_on(self, at, source):
        place = (self.f, self.x, self.y)[source]
        self.copy(at, 2 + source, place, "all", self.core, source).start()
        self.keep(at, source).start()

    def begin(self):
        places = range(len(self.shards))
        for at in places:
            for source in range(len(self.shards[at])):
                self.fetch(at, source).start()
        for at in places:
            self.fetch(at, 0).wait()
            if len(self.shards[at]) == 1:
                self.hop(at, 1).start()
                self.hop(at, 2).start()
        for at in places:
            self.pass_on(at, 0)

    def onward(self, at):
        ahead = len(self.shards[at]) == 3
        self.fetch(at, 1).wait() if ahead else self.hop(at, 1).wait_recv()
        self.copy(at, 0, self.x, "top", self.y, 1).start()
        self.fetch(at, 2).wait() if ahead else self.hop(at, 2).wait_recv()
        self.copy(at, 1, self.y, "low", self.x, 2).start()
        self.pass_on(at, 1)
        self.pass_on(at, 2)

    def across(self, at):
        self.copy(at, 0, self.xy, "top", self.y).wait_recv()
        self.copy(at, 5, self.xy, "top", self.core).start()
        self.copy(at, 1, self.xy, "low", self.x).wait_recv()
        self.copy(at, 6, self.xy, "low", self.core).start()

    def end(self, at):
        for source in range(3):
            self.keep(at, source).wait()
            if source and len(self.shards[at]) == 1:
                self.hop(at, source).wait_send()
        for kind, which in ((0, "top"), (1, "low"), (2, "all"), (3, "all"), (4, "all"), (5, "top"), (6, "low")):
            self.copy(at, kind, self.f, which, self.core).wait_send()
            if kind >= 2:
                self.copy(at, kind, self.f, which, self.core).wait_recv()


def sent_ahead(shards, after):
    shards, _ = lax.optimization_barrier((shards, after))
    hop = lambda shard, step: lax.ppermute(shard, "fsdp", [(at, at ^ step) for at in range(8)])
    return [(shard, hop(shard, 2), hop(shard, 4)) for shard in shards]


def split_shards(refs, sizes):
    shards = []
    for size in sizes:
        shards.append(refs[:size])
        refs = refs[size:]
    return shards, refs


def gather_scratch(shards):
    count = len(shards)
    if not count:
        return []
    return [
        pltpu.SemaphoreType.DMA((count, Gather.COPIES)),
        pltpu.SemaphoreType.DMA((count, Gather.COPIES)),
        pltpu.SemaphoreType.DMA((count, 3)),
        pltpu.SemaphoreType.DMA((count, 3)),
    ] + [pltpu.VMEM((3, *part.shape), part.dtype) for part, *_ in shards]


def gathered_shapes(shards):
    return tuple(jax.ShapeDtypeStruct((8 * part.shape[0], part.shape[1]), part.dtype) for part, *_ in shards)


def halves_of(shards, more=False):
    halves, ahead = [], 0
    for part, *_ in shards:
        rows, size = part.shape
        half = rows // 24 * 16 if more else rows // 32 * 16
        if rows % 32 and ahead <= 0 and not more:
            half += 16
        ahead += (2 * half - rows) * size
        halves.append(half)
    return tuple(halves), tuple(len(shard) for shard in shards)


def start_kernel(plan, part_in, bias_in, *refs):
    halves, sizes = plan
    count = len(halves)
    shards, refs = split_shards(refs, sizes)
    (mod, bias), fulls, refs = refs[:2], refs[2 : count + 2], refs[count + 2 :]
    terms, total, m_s, m_r, b_s, b_r, t_s, t_r, keep, *sems = refs
    f, r = lax.axis_index("fsdp"), lax.axis_index("replica")
    others = [lax.rem(f + d, 8) for d in range(1, 8)]
    greet([((there, r), True) for there in others], 7)

    def remote(src, dst, s_sem, r_sem, there):
        return pltpu.make_async_remote_copy(
            src_ref=src, dst_ref=dst, send_sem=s_sem, recv_sem=r_sem, device_id=(there, r), device_id_type=MESH
        )

    def term_copy(block, source, there):
        return remote(part_in.at[block], terms.at[source], t_s.at[there], t_r.at[source], there)

    def bias_copy(source, there):
        return remote(bias_in, bias.at[source], b_s.at[there], b_r.at[source], there)

    def mod_copy(source, there):
        return remote(total, mod.at[source], m_s.at[there], m_r.at[source], there)

    gather = Gather(shards, fulls, halves, *sems)
    for there in others:
        term_copy(there, f, there).start()
    mine = pltpu.make_async_copy(part_in.at[f], terms.at[f], keep.at[0])
    mine.start()
    gather.begin()
    for there in others:
        bias_copy(f, there).start()
    own_bias = pltpu.make_async_copy(bias_in, bias.at[f], keep.at[1])
    own_bias.start()
    mine.wait()
    for there in others:
        term_copy(f, there, there).wait_recv()
    total[...] = functools.reduce(lambda a, b: a + b, [terms[j] for j in range(8)])
    for there in others:
        mod_copy(f, there).start()
    own_mod = pltpu.make_async_copy(total, mod.at[f], keep.at[2])
    own_mod.start()
    for at in range(count):
        gather.onward(at)
    for at in range(count):
        gather.across(at)
    for at in range(count):
        gather.end(at)
    own_bias.wait()
    own_mod.wait()
    for there in others:
        term_copy(there, f, there).wait_send()
        bias_copy(f, there).wait_send()
        mod_copy(f, there).wait_send()
        bias_copy(there, there).wait_recv()
        mod_copy(there, there).wait_recv()


def start(parts, biases, shards, collective_id):
    sem = lambda: pltpu.SemaphoreType.DMA((8,))
    return pl.pallas_call(
        functools.partial(start_kernel, halves_of(shards)),
        out_shape=(
            jax.ShapeDtypeStruct(parts.shape, parts.dtype),
            jax.ShapeDtypeStruct((8, *biases.shape), biases.dtype),
            *gathered_shapes(shards),
        ),
        in_specs=[HB] * (2 + sum(len(shard) for shard in shards)),
        out_specs=(HB,) * (2 + len(shards)),
        scratch_shapes=[
            pltpu.VMEM(parts.shape, parts.dtype), pltpu.VMEM(parts.shape[1:], parts.dtype),
            sem(), sem(), sem(), sem(), sem(), sem(), pltpu.SemaphoreType.DMA((3,)), *gather_scratch(shards),
        ],
        compiler_params=pltpu.CompilerParams(
            collective_id=collective_id, has_side_effects=True, vmem_limit_bytes=VMEM_LIMIT
        ),
    )(parts, biases, *(part for shard in shards for part in shard))


def to_heads_kernel(reps, size, edge, kv, plan, qkv, *refs):
    halves, sizes = plan
    count = len(halves)
    shards, refs = split_shards(refs, sizes)
    (own, prev, after), fulls, refs = refs[:3], refs[3 : count + 3], refs[count + 3 :]
    x_ref, send, recv, edge_send, edge_recv, *sems = refs
    gather = Gather(shards, fulls, halves, *sems) if count else None
    group, me = lax.axis_index("fsdp"), lax.axis_index("replica")
    groups = lax.axis_size("fsdp")
    wide = x_ref.shape[2]
    width = qkv.shape[1] // 3
    hd = width // reps
    down, up = group > 0, group < groups - 1
    others = [(group, lax.rem(me + d, reps)) for d in range(1, reps)]
    greet(
        [(place, True) for place in others] + [((group - 1, me), down), ((group + 1, me), up)]
        + ([((there, me), True) for there in (gather.core, gather.x, gather.y)] if count else []),
        reps - 1 + down.astype(jnp.int32) + up.astype(jnp.int32) + (3 if count else 0),
    )
    spans = [pl.ds(0, kv), pl.ds(kv, wide - kv)] if wide > kv else [pl.ds(0, kv)]

    def exchange(span, part, there):
        return pltpu.make_async_remote_copy(
            src_ref=x_ref.at[there, :, span], dst_ref=own.at[me, :, span], send_sem=send.at[part, there],
            recv_sem=recv.at[part, me], device_id=(group, there), device_id_type=MESH,
        )

    def depart(place, part):
        span = spans[part]
        pl.when(me != place)(lambda: exchange(span, part, place).start())
        keep = pltpu.make_async_copy(x_ref.at[place, :, span], own.at[place, :, span], recv.at[part, place])
        pl.when(me == place)(keep.start)

    for place in range(reps):
        def pack(rows, place=place):
            at = place * hd
            pieces = [(qkv, width + at, 0, hd), (qkv, 2 * width + at, hd, hd), (qkv, at, 2 * hd, hd)]
            x_ref[place, rows, :] = assemble(rows, wide, pieces).astype(jnp.bfloat16)

        by_rows(size, pack)
        depart(place, 0)
    for part in range(1, len(spans)):
        for place in range(reps):
            depart(place, part)

    if count:
        gather.begin()
    for at in range(count):
        gather.onward(at)

    def edges(piece, action):
        lo, hi = piece * size, (piece + 1) * size
        total = reps * size
        if lo >= total - edge:
            @pl.when(up)
            def _():
                action(0, piece, (group + 1, me), prev.at[pl.ds(lo - (total - edge), size), :])
        if hi <= edge:
            @pl.when(down)
            def _():
                action(1, piece, (group - 1, me), after.at[pl.ds(lo, size), :])

    def start_edge(way, piece, where, target):
        pltpu.make_async_remote_copy(
            src_ref=own.at[piece, :, spans[0]], dst_ref=target, send_sem=edge_send.at[way, piece],
            recv_sem=edge_recv.at[way, piece], device_id=where, device_id_type=MESH,
        ).start()

    def end_send(way, piece, where, target):
        wait_for(own.at[piece, :, spans[0]], edge_send.at[way, piece])

    def end_recv(way, piece, where, target):
        wait_for(target, edge_recv.at[way, piece])

    for piece in range(reps):
        wait_for(own.at[piece, :, spans[0]], recv.at[0, piece])
        edges(piece, start_edge)
    if len(spans) > 1:
        for piece in range(reps):
            wait_for(own.at[piece, :, spans[1]], recv.at[1, piece])
    for at in range(count):
        gather.across(at)
    for part, span in enumerate(spans):
        for _, there in others:
            wait_for(x_ref.at[there, :, span], send.at[part, there])
    for piece in range(reps):
        edges(piece, end_send)
        lo, hi = piece * size, (piece + 1) * size
        total = reps * size
        if lo >= total - edge:
            @pl.when(down)
            def _():
                wait_for(prev.at[pl.ds(lo - (total - edge), size), :], edge_recv.at[0, piece])
        if hi <= edge:
            @pl.when(up)
            def _():
                wait_for(after.at[pl.ds(lo, size), :], edge_recv.at[1, piece])
    for at in range(count):
        gather.end(at)


def to_heads(qkv, reps, edge, kv, shards, collective_id):
    size, wide = qkv.shape[0], pad_to(qkv.shape[1] // reps, LANES)
    sems = pltpu.SemaphoreType.DMA((2, reps))
    own, prev, after, *fulls = pl.pallas_call(
        functools.partial(to_heads_kernel, reps, size, edge, kv, halves_of(shards, True)),
        out_shape=(
            jax.ShapeDtypeStruct((reps, size, wide), qkv.dtype),
            jax.ShapeDtypeStruct((edge, kv), qkv.dtype),
            jax.ShapeDtypeStruct((edge, kv), qkv.dtype),
            *gathered_shapes(shards),
        ),
        in_specs=[VM] + [HB] * sum(len(shard) for shard in shards),
        out_specs=(HB,) * (3 + len(shards)),
        scratch_shapes=[pltpu.VMEM((reps, size, wide), qkv.dtype), sems, sems, sems, sems, *gather_scratch(shards)],
        compiler_params=pltpu.CompilerParams(
            collective_id=collective_id, has_side_effects=True, vmem_limit_bytes=VMEM_LIMIT
        ),
    )(qkv, *(part for shard in shards for part in shard))
    return own.reshape(reps * size, wide), prev, after, fulls


class Tails:
    def __init__(self, hd, size):
        self.main = hd // LANES * LANES
        self.few = hd - self.main
        self.fold = LANES // self.few
        self.band = size // self.fold

    def block(self, values, shift):
        turned = pltpu.roll(values.astype(jnp.float32), shift % LANES, 1) if shift % LANES else values.astype(jnp.float32)
        lane = lax.broadcasted_iota(jnp.int32, turned.shape, 1)
        return jnp.where(lane < self.few, turned, 0.0)

    def folded(self, ref):
        total = None
        for at in range(self.fold):
            part = self.block(ref[at * self.band : (at + 1) * self.band, self.main : self.main + LANES], 0)
            part = pltpu.roll(part, at * self.few, 1) if at else part
            total = part if total is None else total + part
        return total.astype(jnp.bfloat16)

    def unfolded(self, tail, at):
        return self.block(tail, -at * self.few).astype(jnp.bfloat16)


def swap_kernel(reps, out, plan, x_ref, *refs):
    halves, sizes = plan
    count = len(halves)
    shards, refs = split_shards(refs, sizes)
    y_ref, fulls, (held, tail_out, tail_in, opened, send, recv, done, *sems) = refs[0], refs[1 : count + 1], refs[count + 1 :]
    gather = Gather(shards, fulls, halves, *sems) if count else None
    group, me = lax.axis_index("fsdp"), lax.axis_index("replica")
    others = [(group, lax.rem(me + d, reps)) for d in range(1, reps)]
    planar = [(there, me) for there in (gather.core, gather.x, gather.y)] if count else []
    size, lanes = held.shape[1:]
    src, dst = (x_ref, held) if out else (held, y_ref)
    hd = (y_ref if out else x_ref).shape[1] // reps
    tails = Tails(hd, size)
    span = pl.ds(0, tails.main)
    greet([(place, True) for place in others + planar], reps - 1 + len(planar))
    for place in range(reps):
        if not out:
            def pack(rows, place=place):
                held[place, rows, :] = assemble(rows, lanes, [(x_ref, place * hd, 0, hd)]).astype(jnp.bfloat16)

            by_rows(size, pack)
        tail_out[place] = tails.folded(src.at[place])
        parts = ((src.at[place, :, span], lambda to: dst.at[to, :, span]), (tail_out.at[place], lambda to: tail_in.at[to]))
        for at, (part, landing) in enumerate(parts):
            leave = pltpu.make_async_remote_copy(
                src_ref=part, dst_ref=landing(me), send_sem=send.at[at, place], recv_sem=recv.at[at, me],
                device_id=(group, place), device_id_type=MESH,
            )
            keep = pltpu.make_async_copy(part, landing(place), recv.at[at, place])
            pl.when(me != place)(leave.start)
            pl.when(me == place)(keep.start)
    if count:
        gather.begin()
    for at in range(count):
        gather.onward(at)
    for at in range(count):
        gather.across(at)
    for piece in range(reps):
        wait_for(dst.at[piece, :, span], recv.at[0, piece])
        wait_for(tail_in.at[piece], recv.at[1, piece])
        for at in range(tails.fold):
            rows = slice(at * tails.band, (at + 1) * tails.band)
            few = tails.unfolded(tail_in[piece], at)
            if out:
                held[piece, rows, tails.main : tails.main + LANES] = few
            else:
                opened[piece, rows, :] = few
        if not out:
            pltpu.make_async_copy(opened.at[piece], y_ref.at[piece, :, pl.ds(tails.main, LANES)], done.at[piece]).start()
    if out:
        def unpack(rows):
            pieces = [(held.at[place], 0, place * hd, hd) for place in range(reps)]
            y_ref[rows, :] = assemble(rows, y_ref.shape[1], pieces).astype(jnp.bfloat16)

        by_rows(size, unpack)
    else:
        for piece in range(reps):
            wait_for(opened.at[piece], done.at[piece])
    for _, there in others:
        wait_for(src.at[there, :, span], send.at[0, there])
        wait_for(tail_out.at[there], send.at[1, there])
    for at in range(count):
        gather.end(at)


def swap(x, reps, out, shards, collective_id):
    if out:
        size, lanes = x.shape[0] // reps, x.shape[1]
        x = x.reshape(reps, size, lanes)
        shape = (size, HEADS * HEAD_DIM)
    else:
        size, lanes = x.shape[0], pad_to(x.shape[1] // reps, LANES)
        shape = (reps, size, lanes)
    band = Tails(HEADS * HEAD_DIM // reps, size).band
    sems = pltpu.SemaphoreType.DMA((2, reps))
    tail = pltpu.VMEM((reps, band, LANES), x.dtype)
    swapped, *fulls = pl.pallas_call(
        functools.partial(swap_kernel, reps, out, halves_of(shards)),
        out_shape=(jax.ShapeDtypeStruct(shape, x.dtype), *gathered_shapes(shards)),
        in_specs=[VM] + [HB] * sum(len(shard) for shard in shards),
        out_specs=(VM if out else HB,) + (HB,) * len(shards),
        scratch_shapes=[
            pltpu.VMEM((reps, size, lanes), x.dtype), tail, tail, pltpu.VMEM((reps, size, LANES), x.dtype), sems, sems,
            pltpu.SemaphoreType.DMA((reps,)), *gather_scratch(shards),
        ],
        compiler_params=pltpu.CompilerParams(
            collective_id=collective_id, has_side_effects=True, vmem_limit_bytes=VMEM_LIMIT
        ),
    )(x, *(part for shard in shards for part in shard))
    return swapped, fulls


def from_heads_kernel(
    reps, size, edge, dprev, own, dafter, dq, out, out_kv, out_q, dq_tail, from_up, from_down, total, mine,
    sends, recvs, send, recv, tail_sem,
):
    group, me = lax.axis_index("fsdp"), lax.axis_index("replica")
    groups = lax.axis_size("fsdp")
    rows = reps * size
    down, up = group > 0, group < groups - 1
    others = [(group, lax.rem(me + d, reps)) for d in range(1, reps)]
    order = [lax.rem(me + d, reps) for d in range(1, reps + 1)]
    greet(
        [(place, True) for place in others] + [((group - 1, me), down), ((group + 1, me), up)],
        reps - 1 + down.astype(jnp.int32) + up.astype(jnp.int32),
    )
    edges = edge // size
    width = out.shape[1] // 3
    hd = width // reps
    tails = Tails(hd, size)

    def at_piece(piece):
        return pl.ds(pl.multiple_of(piece * size, size), size)

    def to_down(piece):
        return pltpu.make_async_remote_copy(
            src_ref=dprev.at[at_piece(piece), :], dst_ref=from_up.at[at_piece(piece), :], send_sem=sends.at[0, piece],
            recv_sem=recvs.at[0, piece], device_id=(group - 1, me), device_id_type=MESH,
        )

    def to_up(piece):
        return pltpu.make_async_remote_copy(
            src_ref=dafter.at[at_piece(piece), :], dst_ref=from_down.at[at_piece(piece), :], send_sem=sends.at[1, piece],
            recv_sem=recvs.at[1, piece], device_id=(group + 1, me), device_id_type=MESH,
        )

    def edge_pieces(piece, when_up, when_down):
        pl.when(jnp.logical_and(down, piece < edges))(lambda: when_down(piece))
        late = piece - (reps - edges)
        pl.when(jnp.logical_and(up, late >= 0))(lambda: when_up(late))

    for piece in order:
        late = piece - (reps - edges)
        pl.when(jnp.logical_and(down, late >= 0))(lambda late=late: to_down(late).start())
        pl.when(jnp.logical_and(up, piece < edges))(lambda piece=piece: to_up(piece).start())
    tail_load = pltpu.make_async_copy(dq.at[:, pl.ds(tails.main, LANES)], dq_tail, tail_sem)
    tail_load.start()

    def query_copy(piece):
        return pltpu.make_async_remote_copy(
            src_ref=dq.at[at_piece(piece), pl.ds(0, tails.main)], dst_ref=out_q.at[me], send_sem=send.at[0, piece],
            recv_sem=recv.at[0, me], device_id=(group, piece), device_id_type=MESH,
        )

    def sums_copy(piece):
        return pltpu.make_async_remote_copy(
            src_ref=mine.at[at_piece(piece), :], dst_ref=out_kv.at[me], send_sem=send.at[1, piece],
            recv_sem=recv.at[1, me], device_id=(group, piece), device_id_type=MESH,
        )

    for piece in order[:-1]:
        query_copy(piece).start()
    pltpu.make_async_copy(dq.at[at_piece(me), pl.ds(0, tails.main)], out_q.at[me], recv.at[0, me]).start()
    tail_load.wait()
    step = math.gcd(size, 64)

    def sum_up(piece):
        def chunk(at, action):
            here = pl.ds(pl.multiple_of(piece * size + at * step, step), step)
            there = pl.ds(pl.multiple_of(at * step, step), step)
            action(here, there)

        def over(action):
            def body(at, carry):
                chunk(at, action)
                return carry

            lax.fori_loop(0, size // step, body, 0)

        def begin(here, there):
            total[there, :] = own[here, :].astype(jnp.float32)

        over(begin)

        def add(ref, sem, source):
            wait_for(ref.at[at_piece(source), :], sem)

            def body(at, carry):
                there = pl.ds(pl.multiple_of(at * step, step), step)
                here = pl.ds(pl.multiple_of(source * size + at * step, step), step)
                total[there, :] += ref[here, :].astype(jnp.float32)
                return carry

            lax.fori_loop(0, size // step, body, 0)

        edge_pieces(
            piece, lambda late: add(from_up, recvs.at[0, late], late), lambda early: add(from_down, recvs.at[1, early], early)
        )

        def narrow(here, there):
            mine[here, :] = total[there, :].astype(jnp.bfloat16)
            first = 2 * hd // LANES * LANES
            few = pltpu.roll(tails.block(dq_tail[here, :], 0), 2 * hd - first, 1)
            last = slice(first, first + LANES)
            mine[here, last] = (total[there, last] + few).astype(jnp.bfloat16)

        over(narrow)

    for piece in order[:-1]:
        sum_up(piece)
        sums_copy(piece).start()
    sum_up(me)
    pltpu.make_async_copy(mine.at[at_piece(me), :], out_kv.at[me], recv.at[1, me]).start()

    def unpack(section, sources):
        def body(rows):
            pieces = [
                (ref.at[place], first, place * hd + to, lanes) for place in range(reps) for ref, first, to, lanes in sources
            ]
            out[rows, section * width : (section + 1) * width] = assemble(rows, width, pieces).astype(jnp.bfloat16)

        by_rows(size, body)

    for piece in range(reps):
        wait_for(out_q.at[piece], recv.at[0, piece])
        wait_for(out_kv.at[piece], recv.at[1, piece])
    unpack(0, ((out_q, 0, 0, tails.main), (out_kv, 2 * hd, tails.main, tails.few)))
    unpack(1, ((out_kv, 0, 0, hd),))
    unpack(2, ((out_kv, hd, 0, hd),))
    for piece in order[:-1]:
        query_copy(piece).wait_send()
        sums_copy(piece).wait_send()
    for piece in order:
        late = piece - (reps - edges)
        pl.when(jnp.logical_and(down, late >= 0))(lambda late=late: to_down(late).wait_send())
        pl.when(jnp.logical_and(up, piece < edges))(lambda piece=piece: to_up(piece).wait_send())


def from_heads(reps, width, dprev, own, dafter, dq, collective_id):
    rows, kv = own.shape
    edge, size = dprev.shape[0], own.shape[0] // reps
    both = pltpu.SemaphoreType.DMA((2, reps))
    return pl.pallas_call(
        functools.partial(from_heads_kernel, reps, size, edge),
        out_shape=jax.ShapeDtypeStruct((size, 3 * width), own.dtype),
        in_specs=[HB, VM, HB, HB],
        out_specs=VM,
        scratch_shapes=[
            pltpu.VMEM((reps, size, kv), own.dtype),
            pltpu.VMEM((reps, size, width // reps // LANES * LANES), own.dtype),
            pltpu.VMEM((rows, LANES), own.dtype),
            pltpu.VMEM((edge, kv), own.dtype),
            pltpu.VMEM((edge, kv), own.dtype),
            pltpu.VMEM((size, kv), jnp.float32),
            pltpu.VMEM((rows, kv), own.dtype),
            both,
            both,
            both,
            both,
            pltpu.SemaphoreType.DMA,
        ],
        compiler_params=pltpu.CompilerParams(
            collective_id=collective_id, has_side_effects=True, vmem_limit_bytes=VMEM_LIMIT
        ),
    )(dprev, own, dafter, dq)


MATRICES = 12
CHIP_WIDTH, UNIT_WIDTH = 1152, 384
SLACK = 4
LEFT_ROWS = 4
PLACES = ((0, 0), (1, 0), (0, 1), (1, 1))


class Terms:
    def __init__(self, ins, flat, left, right, rows, width, load_sem):
        self.flat, self.left, self.right, self.rows, self.width = flat, left, right, rows, width
        self.unit = right.shape[2]
        self.parts = width // self.unit
        f = lax.axis_index("fsdp")
        self.c, self.x, self.y = lax.rem(f, 2), lax.rem(f // 2, 2), f // 4
        self.core_at, self.x_at, self.y_at = f + 1 - 2 * self.c, f + 2 - 4 * self.x, f + 4 - 8 * self.y
        self.loads, place, slot = [], 0, 0
        for src in ins[:4]:
            self.loads.append((src, flat.at[:, pl.ds(place, src.shape[1])]))
            place += src.shape[1]
        for src in ins[4:]:
            for part in range(src.shape[1] // self.unit):
                self.loads.append((src.at[:, pl.ds(part * self.unit, self.unit)], right.at[slot]))
                slot += 1
        self.load_sem = load_sem

    def start(self):
        for at, (src, dst) in enumerate(self.loads):
            pltpu.make_async_copy(src, dst, self.load_sem.at[at]).start()

    def wait(self):
        for at, (src, dst) in enumerate(self.loads):
            pltpu.make_async_copy(src, dst, self.load_sem.at[at]).wait()

        def turn(at, carry):
            here = pl.ds(pl.multiple_of(at * LANES, LANES), LANES)
            self.left[here, :] = self.flat[:, here].T
            return carry

        lax.fori_loop(0, self.left.shape[0] // LANES, turn, 0)

    def block(self, core, mx, my):
        x, y = self.x + mx * (1 - 2 * self.x), self.y + my * (1 - 2 * self.y)
        return (y * 2 + x) * 2 + (self.c + core * (1 - 2 * self.c))

    def stack(self, u, core):
        rows, width = self.rows, self.width
        m, part = u // self.parts, lax.rem(u, self.parts)
        inside = jnp.where(
            m < 4, rows * m, LEFT_ROWS * width + jnp.where(m < 8, 0, jnp.where(m < 9, width, 2 * width))
        )
        stride = jnp.where(m < 4, 4 * rows, rows)
        other = jnp.maximum(m - 3, 0) * self.parts + part
        blocks = []
        for mx, my in PLACES:
            start = pl.multiple_of(inside + stride * self.block(core, mx, my), 16)
            blocks.append(self.left[pl.ds(start, rows), :])
        return nn_dot(jnp.concatenate(blocks, axis=0), self.right[other])


def term_scratch(ins, unit):
    tokens, width = ins[1].shape
    parts = width // unit
    return [
        pltpu.VMEM((tokens, (LEFT_ROWS + 3) * width), jnp.bfloat16),
        pltpu.VMEM(((LEFT_ROWS + 3) * width, tokens), jnp.bfloat16),
        pltpu.VMEM((9 * parts, tokens, unit), jnp.bfloat16),
        pltpu.SemaphoreType.DMA((4 + 9 * parts,)),
    ]


def remote_copy(src, dst, s_sem, r_sem, where):
    return pltpu.make_async_remote_copy(
        src_ref=src, dst_ref=dst, send_sem=s_sem, recv_sem=r_sem, device_id=where, device_id_type=MESH
    )


def chip_kernel(width, half, *refs):
    ins, (own, xs, ys, tx, ty), refs = refs[:8], refs[8:13], refs[13:]
    flat, left, right, load_sem, csend, crecv, own_b, xs_b, ys_b, tx_b, ty_b, core_s, core_r, out_sem = refs
    r = lax.axis_index("replica")
    count, rows = own.shape[:2]
    terms = Terms(ins, flat, left, right, rows, width, load_sem)
    where = (terms.core_at, r)
    greet([(where, True)], 1)
    terms.start()
    terms.wait()
    bf16, f32 = jnp.bfloat16, jnp.float32

    def core_copy(u):
        pair, four = lax.rem(u, 2), lax.rem(u, 4)
        return remote_copy(csend.at[pair], crecv.at[four], core_s.at[pair], core_r.at[four], where)

    def stores(u):
        pair = lax.rem(u, 2)
        buffers = ((own_b, own), (xs_b, xs), (ys_b, ys), (tx_b, tx), (ty_b, ty))
        return [
            pltpu.make_async_copy(src.at[pair], dst.at[u], out_sem.at[at, pair]) for at, (src, dst) in enumerate(buffers)
        ]

    def close(u):
        for copy in stores(u):
            copy.wait()

    def chip(u):
        pair, four = lax.rem(u, 2), lax.rem(u, 4)
        stacked = terms.stack(u, 0)
        core_copy(u).wait()
        totals = [stacked[m * rows : (m + 1) * rows] + crecv[four, m].astype(f32) for m in range(4)]
        mine, along_x, along_y, opposite = [total.astype(bf16) for total in totals]
        own_b[pair] = mine
        xs_b[pair, 0] = along_x[:half]
        tx_b[pair] = along_x[half:]
        ty_b[pair] = along_y[:half]
        ys_b[pair, 0] = along_y[half:]
        xs_b[pair, 1] = opposite[:half]
        ys_b[pair, 1] = opposite[half:]
        for copy in stores(u):
            copy.start()

    def open_unit(u):
        pair = lax.rem(u, 2)
        csend[pair] = terms.stack(u, 1).astype(bf16).reshape(csend.shape[1:])
        core_copy(u).start()

    def step(t, carry):
        pl.when(t < count)(lambda: open_unit(t))
        pl.when(t >= 3)(lambda: close(t - 3))
        pl.when(jnp.logical_and(t >= 1, t <= count))(lambda: chip(t - 1))
        return carry

    lax.fori_loop(0, count + 3, step, 0)


def chip_sums(lefts, rights, collective_id):
    ins = (*lefts, *rights)
    tokens, width = lefts[1].shape
    rows, unit = width // 8, CHIP_WIDTH
    half = pad_to(rows // 2, 16)
    count = MATRICES * (width // unit)
    bf16 = jnp.bfloat16
    shapes = ((rows, unit), (2, half, unit), (2, rows - half, unit), (rows - half, unit), (half, unit))
    pair = pltpu.SemaphoreType.DMA((2,))
    return pl.pallas_call(
        functools.partial(chip_kernel, width, half),
        out_shape=tuple(jax.ShapeDtypeStruct((count, *shape), bf16) for shape in shapes),
        in_specs=[HB] * 8,
        out_specs=(HB,) * 5,
        scratch_shapes=[
            *term_scratch(ins, unit),
            pltpu.VMEM((2, 4, rows, unit), bf16),
            pltpu.VMEM((4, 4, rows, unit), bf16),
            *(pltpu.VMEM((2, *shape), bf16) for shape in shapes),
            pair,
            pltpu.SemaphoreType.DMA((4,)),
            pltpu.SemaphoreType.DMA((5, 2)),
        ],
        compiler_params=pltpu.CompilerParams(
            collective_id=collective_id, has_side_effects=True, vmem_limit_bytes=VMEM_LIMIT
        ),
        cost_estimate=pl.CostEstimate(flops=2 * 64 * width * width * tokens, bytes_accessed=40 << 20, transcendentals=0),
    )(*ins)


def reduce_kernel(width, half, *refs):
    ins, (extra_in, own_in, xr_in, yr_in, tx_in, ty_in), (out, out_down, mine, shared), refs = refs[:8], refs[8:14], refs[14:18], refs[18:]
    (flat, left, right, load_sem, extra, extra_sem, cx_s, cx_r, cxs_sem, cxr_sem, share_s, share_r,
     csend, crecv, own, xs, xr, ys, yr, tx, ty, x2s, x2r, y2s, y2r, zs, z1r, z2s, z2r, fin,
     own_l, xr_l, yr_l, tx_l, ty_l, ready_sem,
     core_s, core_r, x_s, x_r, y_s, y_r, x2_s, x2_r, y2_s, y2_r, z1_s, z1_r, z2_s, z2_r, fin_l, fin_s, fin_r,
     credit) = refs
    f, r = lax.axis_index("fsdp"), lax.axis_index("replica")
    rows = own.shape[1]
    extras = extra.shape[0]
    unit = own.shape[2]
    slots, pairs, z_slots = xr.shape[0], crecv.shape[0], z1r.shape[0]
    count = extras + 2 * MATRICES * (width // unit)
    terms = Terms(ins, flat, left, right, rows, width, load_sem)
    core_at, x_at, y_at = terms.core_at, terms.x_at, terms.y_at
    inner = jnp.logical_and(r > 0, r < 3)
    outer = jnp.logical_not(inner)
    z_at = r + 1 - 2 * lax.rem(r, 2)
    others = [lax.rem(f + d, 8) for d in range(1, 8)]
    greet(
        [((there, r), True) for there in others] + [((f, r - 1), r > 0), ((f, r + 1), r < 3)],
        7 + (r > 0).astype(jnp.int32) + (r < 3).astype(jnp.int32),
    )
    few = extra.shape[2]
    extra_loads = [
        pltpu.make_async_copy(extra_in.at[:, :, pl.ds(at * unit, unit)], extra.at[at], extra_sem.at[at])
        for at in range(extras)
    ]
    for load in extra_loads:
        load.start()
    terms.start()
    for load in extra_loads:
        load.wait()
    send = remote_copy
    top, low = pl.ds(0, half), pl.ds(half, rows - half)

    def core_copy(slot):
        return send(csend.at[slot], crecv.at[slot], core_s.at[slot], core_r.at[slot], (core_at, r))

    def extra_copy(u):
        return send(cx_s.at[u], cx_r.at[u], cxs_sem.at[u], cxr_sem.at[u], (core_at, r))

    def x_copy(slot):
        return send(xs.at[slot], xr.at[slot], x_s.at[slot], x_r.at[slot], (x_at, r))

    def y_copy(slot):
        return send(ys.at[slot], yr.at[slot], y_s.at[slot], y_r.at[slot], (y_at, r))

    def x2_copy(slot):
        return send(x2s.at[slot], x2r.at[slot], x2_s.at[slot], x2_r.at[slot], (x_at, r))

    def y2_copy(slot):
        return send(y2s.at[slot], y2r.at[slot], y2_s.at[slot], y2_r.at[slot], (y_at, r))

    def z1_copy(slot, to):
        return send(zs.at[slot], z1r.at[to], z1_s.at[slot], z1_r.at[to], (f, z_at))

    def z2_copy(slot):
        return send(z2s.at[slot], z2r.at[slot], z2_s.at[slot], z2_r.at[slot], (f, 3 - r))

    def routed(u, action):
        v = u - extras
        w, layer = v // 2, 1 - lax.rem(v, 2)
        parts = width // unit
        m = w // parts

        @pl.when(m < 4)
        def _():
            row = pl.multiple_of(m * rows, 16)
            column = pl.multiple_of(lax.rem(w, parts) * unit, LANES)
            action(out_down.at[layer, pl.ds(row, rows), pl.ds(column, unit)])

        @pl.when(m >= 4)
        def _():
            column = pl.multiple_of((w - 4 * parts) * unit, LANES)
            action(out.at[layer, :, pl.ds(column, unit)])

    def fin_copy(slot, u, to):
        return send(fin.at[slot], to, fin_s.at[slot], fin_r.at[u], (f, z_at))

    def keep_copy(slot, to):
        return pltpu.make_async_copy(fin.at[slot], to, fin_l.at[slot])

    def columns(u):
        return pl.ds(pl.multiple_of(u * unit, LANES), unit)

    def fin_extra(u):
        slot = lax.rem(u, slots)
        return send(fin.at[slot, pl.ds(0, few), :], mine.at[:, columns(u)], fin_s.at[slot], fin_r.at[u], (f, z_at))

    def keep_extra(u):
        slot = lax.rem(u, slots)
        return pltpu.make_async_copy(fin.at[slot, pl.ds(0, few), :], mine.at[:, columns(u)], fin_l.at[slot])

    def share_copy(u, there, where):
        return send(
            mine.at[:, columns(u)], shared.at[there, :, columns(u)], share_s.at[u, where], share_r.at[u, there], (where, r)
        )

    def piece(src, w):
        whole = src.shape[-1]
        here = pl.ds(pl.multiple_of(lax.rem(w, whole // unit) * unit, LANES), unit)
        at = w // (whole // unit)
        return src.at[at, :, here] if len(src.shape) == 3 else src.at[at, :, :, here]

    def ready_copies(u):
        slot = lax.rem(u, slots)
        buffers = ((own_in, own_l), (xr_in, xr_l), (yr_in, yr_l), (tx_in, tx_l), (ty_in, ty_l))
        return [
            pltpu.make_async_copy(piece(src, (u - extras) // 2), dst.at[slot], ready_sem.at[at, slot])
            for at, (src, dst) in enumerate(buffers)
        ]

    f32, bf16 = jnp.float32, jnp.bfloat16

    def stage(u, condition, body, first=0, last=count):
        live = jnp.logical_and(u >= first, u < last)
        pl.when(live if condition is None else jnp.logical_and(live, condition))(lambda: body(u))

    def share_own(u):
        return pltpu.make_async_copy(mine.at[:, columns(u)], shared.at[f, :, columns(u)], share_r.at[u, f])

    def share(u):
        for there in others:
            share_copy(u, f, there).start()
        share_own(u).start()

    def close(u):
        slot = lax.rem(u, slots)

        def action(to):
            fin_copy(slot, u, to).wait_send()
            keep_copy(slot, to).wait()

        routed(u, action)

    def arrive(u):
        routed(u, lambda to: fin_copy(lax.rem(u, slots), u, to).wait_recv())

    def close_extra(u):
        fin_extra(u).wait_send()
        keep_extra(u).wait()

    def arrive_extra(u):
        fin_extra(u).wait_recv()

    def finish(u):
        slot = lax.rem(u, slots)
        z2_copy(slot).wait()
        fin[slot] = (z2s[slot].astype(f32) + z2r[slot].astype(f32)).astype(bf16)

        @pl.when(u >= extras)
        def _():
            def action(to):
                fin_copy(slot, u, to).start()
                keep_copy(slot, to).start()

            routed(u, action)

        @pl.when(u < extras)
        def _():
            fin_extra(u).start()
            keep_extra(u).start()

    def middle(u):
        slot, z_slot, at = lax.rem(u, slots), lax.rem(u, z_slots), lax.rem(u, own.shape[0])
        z1_copy(slot, z_slot).wait_recv()
        z2s[slot] = (own[at] + z1r[z_slot].astype(f32)).astype(bf16)
        z2_copy(slot).start()

        @pl.when(u + z_slots < count)
        def _():
            pl.semaphore_signal(credit, inc=1, device_id=(f, z_at), device_id_type=MESH)

    def sent(u):
        z1_copy(lax.rem(u, slots), lax.rem(u, z_slots)).wait_send()

    def plane(u):
        slot, at = lax.rem(u, slots), lax.rem(u, own.shape[0])
        x2_copy(slot).wait()
        y2_copy(slot).wait()
        own[at, top, :] += y2r[slot].astype(f32)
        own[at, low, :] += x2r[slot].astype(f32)

        @pl.when(outer)
        def _():
            zs[slot] = own[at].astype(bf16)

            @pl.when(u >= z_slots)
            def _():
                pl.semaphore_wait(credit, 1)

            z1_copy(slot, lax.rem(u, z_slots)).start()

    def cross(u):
        slot, at = lax.rem(u, slots), lax.rem(u, own.shape[0])
        x_copy(slot).wait()
        y_copy(slot).wait()
        y2s[slot] = (ty[slot] + xr[slot, 1].astype(f32)).astype(bf16)
        y2_copy(slot).start()
        x2s[slot] = (tx[slot] + yr[slot, 1].astype(f32)).astype(bf16)
        x2_copy(slot).start()
        own[at, top, :] += xr[slot, 0].astype(f32)
        own[at, low, :] += yr[slot, 0].astype(f32)

    def cross_ready(u):
        slot, at = lax.rem(u, slots), lax.rem(u, own.shape[0])
        for copy in ready_copies(u):
            copy.wait()
        y2s[slot] = (ty_l[slot].astype(f32) + xr_l[slot, 1].astype(f32)).astype(bf16)
        y2_copy(slot).start()
        x2s[slot] = (tx_l[slot].astype(f32) + yr_l[slot, 1].astype(f32)).astype(bf16)
        x2_copy(slot).start()
        own[at, top, :] = own_l[slot, top, :].astype(f32) + xr_l[slot, 0].astype(f32)
        own[at, low, :] = own_l[slot, low, :].astype(f32) + yr_l[slot, 0].astype(f32)

    def chip(u):
        slot, at = lax.rem(u, slots), lax.rem(u, own.shape[0])
        w = (u - extras) // 2
        pair = lax.rem(w, pairs)
        stacked = terms.stack(w, 0)
        core_copy(pair).wait()
        total = stacked[3 * rows :] + crecv[pair, 3].astype(f32)
        xs[slot, 1] = total[:half].astype(bf16)
        ys[slot, 1] = total[half:].astype(bf16)
        total = stacked[rows : 2 * rows] + crecv[pair, 1].astype(f32)
        xs[slot, 0] = total[:half].astype(bf16)
        tx[slot] = total[half:]
        x_copy(slot).start()
        total = stacked[2 * rows : 3 * rows] + crecv[pair, 2].astype(f32)
        ys[slot, 0] = total[half:].astype(bf16)
        ty[slot] = total[:half]
        y_copy(slot).start()
        own[at] = stacked[:rows] + crecv[pair, 0].astype(f32)

    def chip_extra(u):
        slot, at = lax.rem(u, slots), lax.rem(u, own.shape[0])
        extra_copy(u).wait()
        for m, (mx, my) in enumerate(PLACES):
            total = extra[u, terms.block(0, mx, my)] + cx_r[u, m].astype(f32)
            if m == 0:
                own[at, :few, :] = total
            elif m == 2:
                ty[slot, :few, :] = total
            else:
                xs[slot, m // 2, :few, :] = total.astype(bf16)
        x_copy(slot).start()
        y_copy(slot).start()

    def open_extra(u):
        for m, (mx, my) in enumerate(PLACES):
            cx_s[u, m] = extra[u, terms.block(1, mx, my)].astype(bf16)
        extra_copy(u).start()

    def open_ready(u):
        for copy in ready_copies(u):
            copy.start()

    def open_unit(u):
        w = (u - extras) // 2
        pair = lax.rem(w, pairs)
        csend[pair] = terms.stack(w, 1).astype(bf16).reshape(csend.shape[1:])
        core_copy(pair).start()

    def full(u):
        return lax.rem(u - extras, 2) == 1

    def prepared(u):
        return lax.rem(u - extras, 2) == 0

    def step(t, carry):
        at = [t - hop * SLACK for hop in range(7)]
        stage(at[6] - 1, None, share, 0, extras)
        stage(at[6], inner, close, extras)
        stage(at[6], outer, arrive, extras)
        stage(at[6], inner, close_extra, 0, extras)
        stage(at[6], outer, arrive_extra, 0, extras)
        stage(at[5], inner, finish)
        stage(at[4], inner, middle)
        stage(at[4], outer, sent)
        stage(at[3], None, plane)
        stage(at[2], full(at[2]), cross, extras)
        stage(at[2], None, cross, 0, extras)
        stage(at[2], prepared(at[2]), cross_ready, extras)
        stage(at[1], full(at[1]), chip, extras)
        stage(at[1], None, chip_extra, 0, extras)
        pl.when(t == extras + 1)(terms.wait)
        stage(t, full(t), open_unit, extras)
        stage(t, prepared(t), open_ready, extras)
        stage(t, None, open_extra, 0, extras)
        return carry

    lax.fori_loop(0, count + 6 * SLACK + 1, step, 0)
    for u in range(extras):
        for there in others:
            share_copy(u, f, there).wait_send()
            share_copy(u, there, there).wait_recv()
        share_own(u).wait()


def reduce_grads(lefts, rights, ready, extra):
    tokens, width = lefts[1].shape
    rows, unit = width // 8, UNIT_WIDTH
    half = pad_to(rows // 2, 16)
    ins = (*lefts, *rights)
    extras, few = width // unit, extra.shape[1]
    count = extras + 2 * MATRICES * (width // unit)
    bf16, f32 = jnp.bfloat16, jnp.float32
    buf = lambda dtype, *shape: pltpu.VMEM((*shape, unit), dtype)
    sem = lambda *size: pltpu.SemaphoreType.DMA(size)
    slots, z_slots = 2 * SLACK, 3 * SLACK
    rest = rows - half
    return pl.pallas_call(
        functools.partial(reduce_kernel, width, half),
        out_shape=(
            jax.ShapeDtypeStruct((2, rows, (MATRICES - 4) * width), bf16),
            jax.ShapeDtypeStruct((2, 4 * rows, width), bf16),
            jax.ShapeDtypeStruct((few, width), bf16),
            jax.ShapeDtypeStruct(extra.shape, bf16),
        ),
        in_specs=[HB] * 14,
        out_specs=(HB, HB, HB, HB),
        scratch_shapes=[
            *term_scratch(ins, unit),
            buf(f32, extras, 8, few), sem(extras), buf(bf16, extras, 4, few), buf(bf16, extras, 4, few),
            sem(extras), sem(extras), sem(extras, 8), sem(extras, 8),
            buf(bf16, SLACK, 4, rows), buf(bf16, SLACK, 4, rows), buf(f32, 3 * SLACK + 1, rows),
            buf(bf16, slots, 2, half), buf(bf16, slots, 2, half), buf(bf16, slots, 2, rest), buf(bf16, slots, 2, rest),
            buf(f32, slots, rest), buf(f32, slots, half),
            buf(bf16, slots, rest), buf(bf16, slots, rest), buf(bf16, slots, half), buf(bf16, slots, half),
            buf(bf16, slots, rows), buf(bf16, z_slots, rows), buf(bf16, slots, rows), buf(bf16, slots, rows), buf(bf16, slots, rows),
            buf(bf16, slots, rows), buf(bf16, slots, 2, half), buf(bf16, slots, 2, rest), buf(bf16, slots, rest), buf(bf16, slots, half),
            sem(5, slots), sem(SLACK), sem(SLACK), *[sem(slots)] * 8,
            sem(slots), sem(z_slots), *[sem(slots)] * 4, sem(count), pltpu.SemaphoreType.REGULAR,
        ],
        compiler_params=pltpu.CompilerParams(
            collective_id=5, has_side_effects=True, vmem_limit_bytes=60 * 1024 * 1024
        ),
        cost_estimate=pl.CostEstimate(
            flops=2 * 64 * width * width * tokens, bytes_accessed=100 << 20, transcendentals=0
        ),
    )(*ins, extra, *ready)


def pre_norm(stream, shift, scale):
    centred = stream - jnp.mean(stream, axis=-1, keepdims=True)
    spread = jnp.mean(centred * centred, axis=-1, keepdims=True)
    return centred * lax.rsqrt(spread + NORM_EPS) * (1.0 + scale) + shift


def latent_ids(latent_len, positions, token_total):
    starts = jnp.cumsum(latent_len) - latent_len
    found = jnp.sum((starts[None, :] <= positions[:, None]).astype(jnp.int32), axis=1) - 1
    inside = (positions >= 0) & (positions < token_total)
    return jnp.where(inside, found, -1)


def low_dot(left, right):
    return jnp.dot(left, right, preferred_element_type=jnp.float32)


TILE = 512
GELU_ROOT = math.sqrt(2.0 / math.pi)


def thirds(values):
    high = values.astype(jnp.bfloat16)
    rest = values - high.astype(jnp.float32)
    middle = rest.astype(jnp.bfloat16)
    return high, middle, (rest - middle.astype(jnp.float32)).astype(jnp.bfloat16)


def halves_across(width):
    first = pad_to(width // 2, LANES)
    return (pl.ds(0, first), pl.ds(first, width - first))


def at_tile(at, size=TILE):
    return pl.ds(pl.multiple_of(at * size, size), size)


def tiles(count, body):
    def run(at, carry):
        body(at)
        return carry

    lax.fori_loop(0, count, run, 0)


def norm_parts(stream):
    centred = stream - jnp.mean(stream, axis=1, keepdims=True)
    root = lax.rsqrt(jnp.mean(centred * centred, axis=1, keepdims=True) + NORM_EPS)
    return centred * root, root


class FeedForward:
    def __init__(self, pick, mod, weights, held, sems):
        self.pick, self.mod = pick, mod
        self.out_w, self.up_w, self.down_w = held
        self.width, self.hidden = held[1].shape
        self.pieces = sems.shape[0] // 2
        self.piece = self.hidden // self.pieces
        cuts = [pl.ds(at * self.piece, self.piece) for at in range(self.pieces)]
        copy = pltpu.make_async_copy
        self.out_copy = copy(weights[0], held[0], sems.at[0])
        self.up_copies = [copy(weights[1].at[:, cut], held[1].at[:, cut], sems.at[1 + at]) for at, cut in enumerate(cuts)]
        self.down_copies = [
            copy(weights[2].at[cut, :], held[2].at[cut, :], sems.at[1 + self.pieces + at]) for at, cut in enumerate(cuts)
        ]

    def start(self, forth):
        order = [self.out_copy, *self.up_copies, *self.down_copies]
        for part in order if forth else [*self.down_copies, *self.up_copies, self.out_copy]:
            part.start()

    def vector(self, rows, at):
        return nn_dot(self.pick[rows, :], self.mod[:, at * self.width : (at + 1) * self.width])

    def forward(self, stream, mixed, biases, branch, middle, normed, hidden, active, result, after):
        out_b, up_b, down_b = biases
        size, width = stream.shape
        self.out_copy.wait()
        for here in halves_across(width):
            branch[:, here] = nn_dot(mixed[...], self.out_w[:, here]) + out_b[:, here].astype(jnp.float32)

        def first_norm(rows):
            total = stream[rows, :] + self.vector(rows, 2) * branch[rows, :]
            middle[rows, :] = total
            unit, _ = norm_parts(total)
            normed[rows, :] = (unit * (1.0 + self.vector(rows, 4)) + self.vector(rows, 3)).astype(jnp.bfloat16)

        by_rows(size, first_norm)
        for piece in range(self.pieces):
            self.up_copies[piece].wait()

            def widen(at, piece=piece):
                here = at_tile(piece * (self.piece // TILE) + at)
                values = nn_dot(normed[...], self.up_w[:, here]) + up_b[:, here].astype(jnp.float32)
                hidden[:, here] = values
                inner = GELU_ROOT * (values + 0.044715 * values * values * values)
                active[:, here] = (0.5 * values * (1.0 + jnp.tanh(inner))).astype(jnp.bfloat16)

            tiles(self.piece // TILE, widen)
        for part in self.down_copies:
            part.wait()
        for here in halves_across(width):
            result[:, here] = nn_dot(active[...], self.down_w[:, here]) + down_b[:, here].astype(jnp.float32)

        def leave(rows):
            after[rows, :] = (middle[rows, :] + self.vector(rows, 5) * result[rows, :]).astype(after.dtype)

        by_rows(size, leave)

    def backward(self, grad, branch, middle, hidden, result, outs, work, fresh):
        low_result, low_hidden, low_branch, low_mixed, grad_middle, grad_mod, out_sum, up_sum, down_sum = outs
        size, width = middle.shape
        grad_mod[...] = jnp.zeros_like(grad_mod)
        for ref in (out_sum, up_sum, down_sum):
            ref[...] = jnp.zeros_like(ref)

        latents = grad_mod.shape[0] // 4

        def collect(rows, at, values):
            here = slice(at * latents, (at + 1) * latents)
            ones = self.pick[rows, :latents]
            for part in thirds(values)[:2]:
                grad_mod[here, :] += lax.dot_general(
                    ones, part, (((0,), (0,)), ((), ())), preferred_element_type=jnp.float32
                )

        def total(values):
            return jnp.sum(values.astype(jnp.float32), axis=0, keepdims=True)

        def enter(rows):
            values = grad[rows, :].astype(jnp.float32)
            low = (self.vector(rows, 5) * values).astype(jnp.bfloat16)
            low_result[rows, :] = low
            down_sum[...] += total(low)
            collect(rows, 3, values * result[rows, :])

        by_rows(size, enter)

        def widen(at):
            here = at_tile(at)
            values = hidden[:, here]
            square = values * values
            bent = jnp.tanh(GELU_ROOT * (values + 0.044715 * values * square))
            slope = 0.5 * (1.0 + bent) + 0.5 * values * (1.0 - bent * bent) * (GELU_ROOT * (1.0 + 3 * 0.044715 * square))
            low = (nt_dot(low_result[...], self.down_w[here, :]) * slope).astype(jnp.bfloat16)
            low_hidden[:, here] = low
            up_sum[:, here] = total(low)

        for part in self.down_copies if fresh else ():
            part.wait()
        tiles(self.hidden // TILE, widen)
        for part in self.up_copies if fresh else ():
            part.wait()
        for here in halves_across(width):
            work[:, here] = nt_dot(low_hidden[...], self.up_w[here, :])

        def norm_back(rows):
            unit, root = norm_parts(middle[rows, :])
            values = work[rows, :]
            collect(rows, 1, values)
            collect(rows, 2, values * unit)
            scaled = values * (1.0 + self.vector(rows, 4))
            inside = scaled - jnp.mean(scaled, axis=1, keepdims=True)
            inside = inside - unit * jnp.mean(scaled * unit, axis=1, keepdims=True)
            here = grad[rows, :].astype(jnp.float32) + root * inside
            grad_middle[rows, :] = here
            low = (self.vector(rows, 2) * here).astype(jnp.bfloat16)
            low_branch[rows, :] = low
            out_sum[...] += total(low)
            collect(rows, 0, here * branch[rows, :])

        by_rows(size, norm_back)

        if fresh:
            self.out_copy.wait()
        for here in halves_across(width):
            low_mixed[:, here] = nt_dot(low_branch[...], self.out_w[here, :]).astype(jnp.bfloat16)


def feed_kernel(forth, back, *refs):
    pick, mod, out_w, up_w, down_w, out_b, up_b, down_b, *refs = refs
    weights, biases = (out_w, up_w, down_w), (out_b, up_b, down_b)
    if forth and not back:
        stream, mixed, branch, middle, normed, hidden, active, result, after, *refs = refs
        held, sems = refs[:3], refs[3]
    elif back and not forth:
        grad, branch, middle, hidden, result, *refs = refs
        outs, (*held, sems, work) = refs[:9], refs[9:]
    else:
        stream, mixed, grad, normed, active, after, *refs = refs
        outs, (*held, sems, work, branch, middle, hidden, result) = refs[:9], refs[9:]
    feed = FeedForward(pick, mod, weights, held, sems)
    feed.start(forth)
    if forth:
        feed.forward(stream, mixed, biases, branch, middle, normed, hidden, active, result, after)
    if back:
        feed.backward(grad, branch, middle, hidden, result, outs, work, not forth)


def feed_inputs(pick, mod, biases):
    ones = jnp.concatenate([pick.astype(jnp.bfloat16)] * 3, axis=1)
    return (ones, jnp.concatenate(thirds(mod), axis=0), *(part[None] for part in biases[1:]))


def feed_call(forth, back, ins, full, given, dtype):
    qkv_w, qkv_b, out_w, out_b, up_w, up_b, down_w, down_b = full
    size, latents = given[0].shape[0], given[1].shape[0] // 3
    width, hidden = up_w.shape
    bf16, f32 = jnp.bfloat16, jnp.float32
    shape = lambda columns, dtype, rows=size: jax.ShapeDtypeStruct((rows, columns), dtype)
    saved = (shape(width, f32), shape(width, f32), shape(width, bf16), shape(hidden, f32), shape(hidden, bf16), shape(width, f32))
    after = shape(width, dtype)
    outs = (
        shape(width, bf16), shape(hidden, bf16), shape(width, bf16), shape(width, bf16), shape(width, f32),
        shape(width, f32, 4 * latents), shape(width, f32, 1), shape(hidden, f32, 1), shape(width, f32, 1),
    )
    scratch = [pltpu.VMEM(part.shape, part.dtype) for part in (out_w, up_w, down_w)]
    scratch.append(pltpu.SemaphoreType.DMA((1 + 2 * (hidden // (3 * TILE)),)))
    if back:
        scratch.append(pltpu.VMEM((size, width), f32))
    if forth and back:
        scratch += [pltpu.VMEM((size, columns), f32) for columns in (width, width, hidden, width)]
        shapes = (saved[2], saved[4], after, *outs)
    else:
        shapes = (*saved, after) if forth else outs
    return pl.pallas_call(
        functools.partial(feed_kernel, forth, back),
        out_shape=shapes,
        in_specs=[VM, VM, HB, HB, HB, VM, VM, VM] + [VM] * len(ins),
        out_specs=(VM,) * len(shapes),
        scratch_shapes=scratch,
        compiler_params=pltpu.CompilerParams(vmem_limit_bytes=60 * 1024 * 1024),
    )(*given[:2], out_w, up_w, down_w, *given[2:], *ins)


def layer_forward(stream, modulation, full, plan, in_first, shards_first, shards_second, shards_ahead, collective_id, beside):
    qkv_w, qkv_b, out_w, out_b, up_w, up_b, down_w, down_b = full
    reps, edge = plan[:2]
    width = stream.shape[1]
    hd = width // reps
    nh = HEADS // reps
    mod, pick, front = modulation
    shift_one, scale_one = jnp.split(front, 2, axis=1)
    normed = pre_norm(stream, shift_one, scale_one).astype(jnp.bfloat16)
    qkv_bias = qkv_b.astype(jnp.float32)
    bias_full = jnp.concatenate(
        [qkv_bias[:width], jnp.zeros((width,), jnp.float32), qkv_bias[width:]]
    )
    projected = (low_dot(normed, qkv_w) + bias_full).astype(jnp.bfloat16)
    projected, plan, beside = lax.optimization_barrier((projected, plan[2:], beside))
    bounds, ids = plan
    in_second = sent_ahead(shards_first, projected) if shards_first else []
    own, prev, after, fulls = to_heads(projected, reps, edge, pad_to(2 * hd, LANES), in_first, collective_id)
    first_gathered = fulls
    in_second += sent_ahead(shards_second, own) if shards_second else []
    mixed, mixed_t, log_norm = attend(nh, hd, *bounds, prev, own, after, *ids)
    mixed, fulls = swap(mixed, reps, True, in_second, collective_id + 1)
    if in_first:
        (up_w,), (down_w, *fulls) = first_gathered, fulls
    in_next = sent_ahead(shards_ahead, mixed) if shards_ahead else ()
    full = (qkv_w, qkv_b, out_w, out_b, up_w, up_b, down_w, down_b)
    saved = (normed, (prev, own, after), mixed, (mixed_t, log_norm))
    return (saved, full, fulls, in_next, (reps, edge, bounds, ids), beside)


def layer_backward(stream, modulation, full, saved, feed_grads, plan, beside):
    qkv_w = full[0]
    normed, window, mixed, kept = saved
    normed_two, active, grad_result, grad_hidden, grad_branch, grad_mixed, grad_middle, grad_mod, *bias_sums = feed_grads
    reps, edge, bounds, ids = plan
    width = stream.shape[1]
    hd = width // reps
    nh = HEADS // reps
    mod, pick, front = modulation
    shift_one, scale_one = jnp.split(front, 2, axis=1)
    grad_heads, _ = swap(grad_mixed, reps, False, (), 3)
    prev, own, after = window
    grad_q, grad_prev, grad_own, grad_after = attend_back(
        nh, hd, *bounds, prev, own, after, *ids, grad_heads.reshape(own.shape[0], -1), *kept
    )
    grad_projected = from_heads(reps, width, grad_prev, grad_own, grad_after, grad_q, 4)
    grad_projected, beside = lax.optimization_barrier((grad_projected, beside))
    sums = jnp.sum(grad_projected.astype(jnp.float32), axis=0)
    grad_qkv_b = jnp.concatenate([sums[:width], sums[2 * width :]])
    grad_normed = jnp.einsum("te,de->td", grad_projected, qkv_w, preferred_element_type=jnp.float32)
    _, norm_back_one = jax.vjp(pre_norm, stream, shift_one, scale_one)
    grad_stream_part, grad_shift_one, grad_scale_one = norm_back_one(grad_normed)
    grad_stream = grad_middle + grad_stream_part
    grad_mod = jnp.concatenate(
        [
            jnp.einsum("tl,tm->lm", pick, part, precision=HIGH, preferred_element_type=jnp.float32)
            for part in (grad_shift_one, grad_scale_one)
        ]
        + [grad_mod],
    )
    return (
        grad_stream, grad_mod,
        ((active, normed_two, mixed, normed), (grad_result, grad_hidden, grad_branch, grad_projected)),
        (grad_qkv_b, *(part[0] for part in bias_sums)), beside,
    )


def bias_parts(stacked, params):
    return [stacked[:, row, : params[at].shape[0]].reshape(-1) for row, at in enumerate((3, 5, 7, 9))]


def modulation(partial_terms, layers):
    longest = pad_to(max(params[at].shape[0] for params in layers for at in (3, 5, 7, 9)), LANES)
    shares = jnp.stack(
        [jnp.pad(params[at], (0, longest - params[at].shape[0])) for params in layers for at in (3, 5, 7, 9)]
    )
    if not on_planes():
        mods = lax.psum(tuple(partial_terms), "fsdp")
        stacked = lax.all_gather(shares, "fsdp", axis=0)
        fulls = [lax.all_gather(layers[0][at], "fsdp", axis=0, tiled=True) for at in (2, 4)]
    else:
        width = layers[0][4].shape[1]
        parts = partial_terms[0].reshape(8, -1, width)
        some = parts.shape[1]
        parts = jnp.pad(parts, ((0, 0), (0, pad_to(some, 8) - some), (0, 0)))
        mod, stacked, *fulls = start(
            parts, jnp.pad(shares, ((0, 16 - shares.shape[0]), (0, 0))), [(layers[0][at],) for at in (2, 4)], 6
        )
        mods = [mod[:, :some].reshape(partial_terms[0].shape)] + [lax.psum(term, "fsdp") for term in partial_terms[1:]]
    return mods, [bias_parts(stacked[:, 4 * at : 4 * at + 4], params) for at, params in enumerate(layers)], fulls


def on_planes():
    return lax.axis_size("fsdp") == 8 and lax.axis_size("replica") == 4


def first_hop(lefts, rights):
    own, xs, ys, tx, ty = chip_sums(lefts, rights, 11)
    hop = lambda value, step: lax.ppermute(value, "fsdp", [(at, at ^ step) for at in range(8)])
    return (own, hop(xs, 2), hop(ys, 4), tx, ty), own


def owner_sums(pairs, ready, grad_mods, grad_biases):
    groups = lax.axis_size("fsdp")
    width = pairs[0][0][1].shape[1]
    if on_planes():
        mods = jnp.concatenate(grad_mods).reshape(groups, -1, width)
        biases = jnp.stack(
            [jnp.concatenate([part.reshape(groups, -1) for part in parts], axis=1) for parts in grad_biases], axis=1
        )
        used, lines = mods.shape[1], pad_to(mods.shape[1] + 2, 16)
        biases = jnp.pad(biases, ((0, 0), (0, lines - used - 2), (0, 0)))
        out, out_down, mine, shared = reduce_grads(*pairs[0], ready, jnp.concatenate([mods, biases], axis=1))
        mods = shared[:, :used].reshape(2, -1, width)
        shares = mine[used : used + 2].astype(jnp.float32)
        results = []
        for layer_at in range(2):
            columns = lambda first, last: out[layer_at, :, (first - 4) * width : (last - 4) * width].astype(jnp.float32)
            cuts = [0]
            for part in grad_biases[layer_at]:
                cuts.append(cuts[-1] + part.shape[0] // groups)
            weights = (columns(9, 12), columns(8, 9), columns(4, 8), out_down[layer_at].astype(jnp.float32))
            results.append((weights, [shares[layer_at, i:j] for i, j in zip(cuts[:-1], cuts[1:])]))
        return results, mods
    flat = jnp.concatenate([part for parts in grad_biases for part in parts])
    *mods, flat = lax.psum((*grad_mods, flat), ("fsdp", "replica"))
    results, place = [], 0
    for (lefts, rights), parts in zip(pairs, grad_biases):
        grads, biases = [], []
        for left, right in zip(lefts, rights):
            grad = low_dot(left.T, right).astype(jnp.bfloat16)
            part = lax.psum_scatter(grad, "fsdp", scatter_dimension=0, tiled=True)
            grads.append(lax.psum(part, "replica").astype(jnp.float32))
        for part in parts:
            share = part.shape[0] // groups
            biases.append(lax.dynamic_slice_in_dim(flat, place + lax.axis_index("fsdp") * share, share, 0))
            place += part.shape[0]
        results.append((grads[::-1], biases))
    return results, mods


def attention_plan(latent_len, tok_rows, reps, device_at):
    column = tok_rows * reps
    edge = MAXLEN
    total = jnp.sum(latent_len)
    first = lax.axis_index("fsdp") * column
    positions = first - edge + jnp.arange(column + 2 * edge, dtype=jnp.int32)
    ends = jnp.cumsum(latent_len)
    ids = jnp.sum((ends[None, :] <= positions[:, None]).astype(jnp.int32), axis=1)
    ids = jnp.where(positions < 0, -1, ids)
    own = ids[edge : edge + column]
    count = column // BQ
    firsts, lasts = own[::BQ], own[BQ - 1 :: BQ]
    pick = lambda at: (at[:, None] == jnp.arange(latent_len.shape[0], dtype=jnp.int32)[None, :]).astype(jnp.int32)
    low = jnp.sum(pick(firsts) * (ends - latent_len)[None, :], axis=1) - (first - edge)
    high = jnp.sum(pick(lasts) * ends[None, :], axis=1) - (first - edge)
    bounds = ((low // BK).astype(jnp.int32), ((high + BK - 1) // BK).astype(jnp.int32))
    kid = jnp.broadcast_to(ids[:, None], (ids.shape[0], LANES))
    qid = jnp.broadcast_to(own[None, :], (8, column))
    return (reps, edge, bounds, (kid, qid))


def shards(
    tokens,
    cond,
    latent_len,
    first_ada_weight,
    first_ada_bias,
    first_qkv_weight,
    first_qkv_bias,
    first_out_weight,
    first_out_bias,
    first_up_weight,
    first_up_bias,
    first_down_weight,
    first_down_bias,
    second_ada_weight,
    second_ada_bias,
    second_qkv_weight,
    second_qkv_bias,
    second_out_weight,
    second_out_bias,
    second_up_weight,
    second_up_bias,
    second_down_weight,
    second_down_bias,
    cotangent,
):
    tok_rows = tokens.shape[0]
    group_place = lax.axis_index("fsdp")
    device_at = lax.axis_index(("fsdp", "replica"))
    token_total = tok_rows * lax.axis_size(("fsdp", "replica"))
    latent_count = cond.shape[0]
    local_pos = jnp.arange(tok_rows, dtype=jnp.int32)
    own_ids = latent_ids(latent_len, device_at * tok_rows + local_pos, token_total)
    pick = (own_ids[:, None] == jnp.arange(latent_count, dtype=jnp.int32)[None, :]).astype(
        jnp.float32
    )
    plan = attention_plan(latent_len, tok_rows, lax.axis_size("replica"), device_at)
    layers = (
        (
            first_ada_weight,
            first_ada_bias,
            first_qkv_weight,
            first_qkv_bias,
            first_out_weight,
            first_out_bias,
            first_up_weight,
            first_up_bias,
            first_down_weight,
            first_down_bias,
        ),
        (
            second_ada_weight,
            second_ada_bias,
            second_qkv_weight,
            second_qkv_bias,
            second_out_weight,
            second_out_bias,
            second_up_weight,
            second_up_bias,
            second_down_weight,
            second_down_bias,
        ),
    )
    col_width = first_ada_weight.shape[0]
    own_cond = lax.dynamic_slice_in_dim(
        cond.astype(jnp.float32), group_place * col_width, col_width, 1
    )
    own_silu = jax.nn.silu(own_cond).astype(jnp.bfloat16)
    partial_terms = []
    for params in layers:
        term = low_dot(own_silu, params[0])
        bias_share = params[1].astype(jnp.float32)
        spread = lax.dynamic_update_slice_in_dim(
            jnp.zeros((term.shape[1],), jnp.float32),
            bias_share,
            group_place * bias_share.shape[0],
            0,
        )
        partial_terms.append(term + spread[None, :])
    (mod_first, mod_second), biases, attention_weights = modulation(partial_terms, layers)
    mods = [mod_first, mod_second]
    mod_tokens, feeds = [], []
    stream = tokens.astype(jnp.float32)
    inputs = []
    kept = []
    whole = lambda value: lax.all_gather(value, "fsdp", axis=0, tiled=True)
    fulls = []
    in_first = sent_ahead((first_up_weight,), mod_first) if on_planes() else ()
    for layer_at, params in enumerate(layers):
        if layer_at > 0:
            stream, mods[layer_at] = lax.optimization_barrier((stream, mods[layer_at]))
        inputs.append(stream)
        front = jnp.dot(pick, mods[layer_at][:, : 2 * tokens.shape[1]], precision=HIGH, preferred_element_type=jnp.float32)
        mod_tokens.append((mods[layer_at], pick, front))
        feed = feed_inputs(pick, mods[layer_at], biases[layer_at])
        ahead = layers[layer_at + 1] if layer_at + 1 < len(layers) else None
        qkv_w, out_w = attention_weights
        qkv_b, out_b, up_b, down_b = biases[layer_at]
        shards_first, shards_second, shards_ahead, up_w, down_w = (), (), (), None, None
        if on_planes():
            shards_first = (params[8],)
            shards_second = () if ahead is None else (ahead[2], ahead[4])
            shards_ahead = () if ahead is None else (ahead[6],)
        else:
            up_w, down_w = whole(params[6]), whole(params[8])
        full = (qkv_w, qkv_b, out_w, out_b, up_w, up_b, down_w, down_b)
        saved, full, attention_weights, in_first, plan, feed = layer_forward(
            stream, mod_tokens[layer_at], full, plan, in_first, shards_first, shards_second, shards_ahead, 7 + 2 * layer_at,
            feed,
        )
        feeds.append(feed)
        if layer_at == 0:
            *feed_saved, stream = feed_call(
                True, False, (stream, saved[2]), full, feeds[0], jnp.float32
            )
        else:
            normed_two, active, output, *feed_grads = feed_call(
                True, True, (stream, saved[2], cotangent), full, feeds[1], jnp.bfloat16
            )
            feed_grads = [normed_two, active, *feed_grads]
        fulls.append(full)
        if ahead is not None and not on_planes():
            attention_weights = [whole(ahead[at]) for at in (2, 4)]
        kept.append(saved)
    weight_pairs = [None, None]
    ready = ()
    mod_grads = [None, None]
    bias_grads = [None, None]
    for layer_at in (1, 0):
        if layer_at == 0:
            branch, middle, normed_two, hidden, active, result = feed_saved
            feed_grads = feed_call(
                False, True, (grad_stream, branch, middle, hidden, result), fulls[0], feeds[0], jnp.float32
            )
            feed_grads = [normed_two, active, *feed_grads]
        grad_stream, grad_mod, local_grads, local_biases, ready = layer_backward(
            inputs[layer_at], mod_tokens[layer_at], fulls[layer_at], kept[layer_at], feed_grads, plan, ready
        )
        weight_pairs[layer_at] = local_grads
        if layer_at == 1 and on_planes():
            ready, own = first_hop(*local_grads)
            grad_stream, _ = lax.optimization_barrier((grad_stream, own))
        mod_grads[layer_at] = grad_mod
        bias_grads[layer_at] = local_biases
    sums, (grad_mod_first, grad_mod_second) = owner_sums(weight_pairs, ready, mod_grads, bias_grads)
    grad_silu = jnp.zeros(own_cond.shape, jnp.float32)
    ada_grads = []
    for params, grad_mod in zip(layers, (grad_mod_first, grad_mod_second)):
        low_mod = grad_mod.astype(jnp.bfloat16).reshape(6, latent_count, -1).transpose(1, 0, 2).reshape(latent_count, -1)
        weight_grad = jnp.einsum("ld,lm->dm", own_silu, low_mod, preferred_element_type=jnp.float32)
        column_sums = jnp.sum(low_mod.astype(jnp.float32), axis=0)
        bias_rows = params[1].shape[0]
        bias_grad = lax.dynamic_slice_in_dim(column_sums, group_place * bias_rows, bias_rows, 0)
        grad_silu = grad_silu + jnp.einsum(
            "lm,dm->ld", low_mod, params[0], preferred_element_type=jnp.float32
        )
        ada_grads.append((weight_grad, bias_grad))
    _, silu_back = jax.vjp(jax.nn.silu, own_cond)
    cond_grad = silu_back(grad_silu)[0]
    outs = [output, grad_stream, cond_grad]
    for layer_at in range(2):
        outs += list(ada_grads[layer_at])
        for weight, bias in zip(*sums[layer_at]):
            outs += [weight, bias]
    return tuple(outs)


def solution(mesh):
    in_specs = (
        P(("fsdp", "replica"), None),
        P(),
        P(),
        P("fsdp", None),
        P("fsdp"),
        P("fsdp", None),
        P("fsdp"),
        P("fsdp", None),
        P("fsdp"),
        P("fsdp", None),
        P("fsdp"),
        P("fsdp", None),
        P("fsdp"),
        P("fsdp", None),
        P("fsdp"),
        P("fsdp", None),
        P("fsdp"),
        P("fsdp", None),
        P("fsdp"),
        P("fsdp", None),
        P("fsdp"),
        P("fsdp", None),
        P("fsdp"),
        P(("fsdp", "replica"), None),
    )
    out_specs = (
        P(("fsdp", "replica"), None),
        P(("fsdp", "replica"), None),
        P(None, "fsdp"),
        P("fsdp", None),
        P("fsdp"),
        P("fsdp", None),
        P("fsdp"),
        P("fsdp", None),
        P("fsdp"),
        P("fsdp", None),
        P("fsdp"),
        P("fsdp", None),
        P("fsdp"),
        P("fsdp", None),
        P("fsdp"),
        P("fsdp", None),
        P("fsdp"),
        P("fsdp", None),
        P("fsdp"),
        P("fsdp", None),
        P("fsdp"),
        P("fsdp", None),
        P("fsdp"),
    )
    return jax.shard_map(shards, mesh=mesh, in_specs=in_specs, out_specs=out_specs, check_vma=False)
```

```python
import functools
import math

import jax
import jax.numpy as jnp
from jax import lax
from jax.experimental import pallas as pl
from jax.experimental.pallas import tpu as pltpu
from jax.sharding import PartitionSpec as P

HEADS = 16
HEAD_DIM = 72
MAXLEN = 1024
NORM_EPS = 1e-06
HIGH = lax.Precision.HIGHEST
BQ = 256
BK = 256
LANES = 128
NEG = -1e30
VM = pl.BlockSpec(memory_space=pltpu.VMEM)
SM = pl.BlockSpec(memory_space=pltpu.SMEM)
HB = pl.BlockSpec(memory_space=pl.ANY)
VMEM_LIMIT = 56 * 1024 * 1024


def pad_to(size, unit):
    return -(-size // unit) * unit


def take_head(ref, rows, at, dim):
    first, off = at // LANES * LANES, at % LANES
    wide = LANES if off + dim <= LANES else 2 * LANES
    block = ref[rows, first : first + wide].astype(jnp.float32)
    if off:
        block = pltpu.roll(block, wide - off, 1)
    block = block[:, :LANES]
    lane = lax.broadcasted_iota(jnp.int32, block.shape, 1)
    return jnp.where(lane < dim, block, 0.0)


def put_heads(blocks, places, width):
    tiles = [None] * (width // LANES)
    for block, at in zip(blocks, places):
        first, off = at // LANES, at % LANES
        wide = jnp.concatenate([block, jnp.zeros_like(block)], axis=1)
        if off:
            wide = pltpu.roll(wide, off, 1)
        for step in range(2):
            part = wide[:, step * LANES : (step + 1) * LANES]
            if first + step < len(tiles):
                old = tiles[first + step]
                tiles[first + step] = part if old is None else old + part
    rows = blocks[0].shape[0]
    return jnp.concatenate(
        [jnp.zeros((rows, LANES), jnp.float32) if t is None else t for t in tiles], axis=1
    )


def nt_dot(left, right):
    return lax.dot_general(left, right, (((1,), (1,)), ((), ())), preferred_element_type=jnp.float32)


def nn_dot(left, right):
    return jnp.dot(left, right, preferred_element_type=jnp.float32)


def rows_at(block, size):
    return pl.ds(pl.multiple_of(block * size, size), size)


def over_window(lo, hi, prev, own, after, action):
    edge, mid = prev.shape[0] // BK, own.shape[0] // BK

    def run(ref, first, count):
        def body(at, carry):
            action(ref, at - first, at)
            return carry

        lax.fori_loop(jnp.clip(lo, first, first + count), jnp.clip(hi, first, first + count), body, 0)

    run(prev, 0, edge)
    run(own, edge, mid)
    run(after, edge + mid, edge)


def attend_kernel(nh, hd, lo, hi, prev, own, after, kid, qid, o_ref, ot_ref, lse_ref, kh, vt, qh, acc, ml):
    dim = hd // nh
    width = o_ref.shape[1]
    count = own.shape[0] // BQ
    scale = math.log2(math.e) / math.sqrt(dim)

    def load(ref, at, to):
        for h in range(nh):
            kh[h, rows_at(to, BK), :] = take_head(ref, rows_at(at, BK), h * dim, dim).astype(jnp.bfloat16)
            vt[h, :, rows_at(to, BK)] = take_head(ref, rows_at(at, BK), hd + h * dim, dim).T.astype(jnp.bfloat16)

    over_window(lo[0], hi[count - 1], prev, own, after, load)
    lse_ref[...] = jnp.zeros_like(lse_ref)

    def query_block(qb, carry):
        rows = rows_at(qb, BQ)
        for h in range(nh):
            qh[h] = take_head(own, rows, 2 * hd + h * dim, dim).astype(jnp.bfloat16)
        acc[...] = jnp.zeros_like(acc)
        ml[0] = jnp.full(ml.shape[1:], NEG, jnp.float32)
        ml[1] = jnp.zeros(ml.shape[1:], jnp.float32)
        ids = qid[0:1, rows]

        def key_block(kb, inner):
            keys = rows_at(kb, BK)
            lanes = kid[keys, :]
            same = jnp.concatenate([lanes] * (BQ // LANES), axis=1) == ids
            scores = [jnp.where(same, nt_dot(kh[h, keys, :], qh[h]) * scale, NEG) for h in range(nh)]
            olds = [ml[0, h : h + 1, :] for h in range(nh)]
            tops = [jnp.maximum(old, jnp.max(s, axis=0, keepdims=True)) for old, s in zip(olds, scores)]
            probs = [jnp.exp2(s - top) for s, top in zip(scores, tops)]
            outs = [nn_dot(vt[h, :, keys], probs[h].astype(jnp.bfloat16)) for h in range(nh)]
            for h in range(nh):
                alpha = jnp.exp2(olds[h] - tops[h])
                ml[0, h : h + 1, :] = tops[h]
                ml[1, h : h + 1, :] = ml[1, h : h + 1, :] * alpha + jnp.sum(probs[h], axis=0, keepdims=True)
                acc[h] = acc[h] * alpha + outs[h]
            return inner

        lax.fori_loop(lo[qb], hi[qb], key_block, 0)
        parts = []
        for h in range(nh):
            total = ml[1, h : h + 1, :]
            out = acc[h, :dim, :] / total
            parts.append(out)
            lse_ref[h : h + 1, rows] = ml[0, h : h + 1, :] + jnp.log2(total)
        parts.append(jnp.zeros((width - hd, BQ), jnp.float32))
        heads = jnp.concatenate(parts, axis=0)
        ot_ref[:, rows] = heads
        o_ref[rows, :] = heads.T.astype(jnp.bfloat16)
        return carry

    lax.fori_loop(0, count, query_block, 0)


def attend(nh, hd, lo, hi, prev, own, after, kid, qid):
    rows, window = own.shape[0], own.shape[0] + 2 * prev.shape[0]
    width = pad_to(hd, LANES)
    return pl.pallas_call(
        functools.partial(attend_kernel, nh, hd),
        out_shape=(
            jax.ShapeDtypeStruct((rows, width), jnp.bfloat16),
            jax.ShapeDtypeStruct((width, rows), jnp.float32),
            jax.ShapeDtypeStruct((8, rows), jnp.float32),
        ),
        in_specs=[SM, SM, VM, VM, VM, VM, VM],
        out_specs=(VM, VM, VM),
        scratch_shapes=[
            pltpu.VMEM((nh, window, LANES), jnp.bfloat16),
            pltpu.VMEM((nh, LANES, window), jnp.bfloat16),
            pltpu.VMEM((nh, BQ, LANES), jnp.bfloat16),
            pltpu.VMEM((nh, LANES, BQ), jnp.float32),
            pltpu.VMEM((2, 8, BQ), jnp.float32),
        ],
        compiler_params=pltpu.CompilerParams(vmem_limit_bytes=VMEM_LIMIT),
    )(lo, hi, prev, own, after, kid, qid)


def attend_back_kernel(
    nh, hd, lo, hi, prev, own, after, kid, qid, do_ref, ot_ref, lse_ref,
    dq_ref, dprev, down, dafter, kh, vh, kt, qh, gh, dk, dv, dqt, delta,
):
    dim = hd // nh
    width = dq_ref.shape[1]
    count = own.shape[0] // BQ
    root = 1.0 / math.sqrt(dim)
    scale = math.log2(math.e) / math.sqrt(dim)

    def load(ref, at, to):
        for h in range(nh):
            k = take_head(ref, rows_at(at, BK), h * dim, dim)
            kh[h, rows_at(to, BK), :] = k.astype(jnp.bfloat16)
            kt[h, :, rows_at(to, BK)] = k.T.astype(jnp.bfloat16)
            vh[h, rows_at(to, BK), :] = take_head(ref, rows_at(at, BK), hd + h * dim, dim).astype(jnp.bfloat16)
            dk[h, rows_at(to, BK), :] = jnp.zeros((BK, LANES), jnp.float32)
            dv[h, rows_at(to, BK), :] = jnp.zeros((BK, LANES), jnp.float32)

    over_window(lo[0], hi[count - 1], prev, own, after, load)

    def query_block(qb, carry):
        rows = rows_at(qb, BQ)
        for h in range(nh):
            qh[h] = take_head(own, rows, 2 * hd + h * dim, dim).astype(jnp.bfloat16)
            gh[h] = take_head(do_ref, rows, h * dim, dim).astype(jnp.bfloat16)
        prod = do_ref[rows, :].astype(jnp.float32).T * ot_ref[:, rows]
        for h in range(nh):
            delta[h : h + 1, :] = jnp.sum(prod[h * dim : (h + 1) * dim], axis=0, keepdims=True)
        dqt[...] = jnp.zeros_like(dqt)
        ids = qid[0:1, rows]

        def key_block(kb, inner):
            keys = rows_at(kb, BK)
            lanes = kid[keys, :]
            same = jnp.concatenate([lanes] * (BQ // LANES), axis=1) == ids
            hs = range(nh)
            scores = [nt_dot(kh[h, keys, :], qh[h]) * scale - lse_ref[h : h + 1, rows] for h in hs]
            dps = [nt_dot(vh[h, keys, :], gh[h]) - delta[h : h + 1, :] for h in hs]
            probs = [jnp.exp2(jnp.where(same, s, NEG)) for s in scores]
            dss = [(p * dp).astype(jnp.bfloat16) for p, dp in zip(probs, dps)]
            lows = [p.astype(jnp.bfloat16) for p in probs]
            for h in hs:
                dv[h, keys, :] += nn_dot(lows[h], gh[h])
            for h in hs:
                dk[h, keys, :] += nn_dot(dss[h], qh[h])
            for h in hs:
                dqt[h] += nn_dot(kt[h, :, keys], dss[h])
            return inner

        lax.fori_loop(lo[qb], hi[qb], key_block, 0)
        parts = [dqt[h, :dim, :] * root for h in range(nh)]
        parts.append(jnp.zeros((width - hd, BQ), jnp.float32))
        dq_ref[rows, :] = jnp.concatenate(parts, axis=0).T.astype(jnp.bfloat16)
        return carry

    lax.fori_loop(0, count, query_block, 0)
    for ref in (dprev, dafter):
        ref[...] = jnp.zeros_like(ref)

    def store(ref, at, to):
        keys = rows_at(to, BK)
        blocks = [dk[h, keys, :] * root for h in range(nh)] + [dv[h, keys, :] for h in range(nh)]
        ref[rows_at(at, BK), :] = put_heads(blocks, [h * dim for h in range(2 * nh)], ref.shape[1]).astype(ref.dtype)

    over_window(lo[0], hi[count - 1], dprev, down, dafter, store)


def attend_back(nh, hd, lo, hi, prev, own, after, kid, qid, grad, ot, lse):
    rows, edge = own.shape[0], prev.shape[0]
    window = rows + 2 * edge
    width, kv = pad_to(hd, LANES), prev.shape[1]
    heads = lambda size, dtype: pltpu.VMEM((nh, size, LANES), dtype)
    return pl.pallas_call(
        functools.partial(attend_back_kernel, nh, hd),
        out_shape=(
            jax.ShapeDtypeStruct((rows, width), jnp.bfloat16),
            jax.ShapeDtypeStruct((edge, kv), jnp.bfloat16),
            jax.ShapeDtypeStruct((rows, kv), jnp.bfloat16),
            jax.ShapeDtypeStruct((edge, kv), jnp.bfloat16),
        ),
        in_specs=[SM, SM] + [VM] * 8,
        out_specs=(VM,) * 4,
        scratch_shapes=[
            heads(window, jnp.bfloat16),
            heads(window, jnp.bfloat16),
            pltpu.VMEM((nh, LANES, window), jnp.bfloat16),
            heads(BQ, jnp.bfloat16),
            heads(BQ, jnp.bfloat16),
            heads(window, jnp.float32),
            heads(window, jnp.float32),
            pltpu.VMEM((nh, LANES, BQ), jnp.float32),
            pltpu.VMEM((8, BQ), jnp.float32),
        ],
        compiler_params=pltpu.CompilerParams(vmem_limit_bytes=VMEM_LIMIT),
    )(lo, hi, prev, own, after, kid, qid, grad, ot, lse)


MESH = pl.DeviceIdType.MESH


def greet(partners, count):
    barrier = pltpu.get_barrier_semaphore()
    for where, there in partners:
        @pl.when(there)
        def _():
            pl.semaphore_signal(barrier, inc=1, device_id=where, device_id_type=MESH)
    pl.semaphore_wait(barrier, count)


def wait_for(ref, sem):
    pltpu.make_async_copy(ref, ref, sem).wait()


def assemble(rows, width, pieces):
    tiles = [None] * (width // LANES)
    for ref, src, dst, count in pieces:
        off, to = src % LANES, dst % LANES
        wide = max(off + count, to + count)
        wide, have = pad_to(wide, LANES), pad_to(off + count, LANES)
        first = src // LANES * LANES
        block = ref[rows, first : first + have].astype(jnp.float32)
        lane = lax.broadcasted_iota(jnp.int32, block.shape, 1)
        block = jnp.where(jnp.logical_and(lane >= off, lane < off + count), block, 0.0)
        if wide > have:
            block = jnp.concatenate([block, jnp.zeros((block.shape[0], wide - have), jnp.float32)], axis=1)
        if off != to:
            block = pltpu.roll(block, (to - off) % wide, 1)
        for step in range(pad_to(to + count, LANES) // LANES):
            part = block[:, step * LANES : (step + 1) * LANES]
            at = dst // LANES + step
            tiles[at] = part if tiles[at] is None else tiles[at] + part
    size = next(t for t in tiles if t is not None).shape
    return jnp.concatenate([jnp.zeros(size, jnp.float32) if t is None else t for t in tiles], axis=1)


def by_rows(size, action, step=64):
    def body(at, carry):
        action(pl.ds(pl.multiple_of(at * step, step), step))
        return carry

    lax.fori_loop(0, size // step, body, 0)


class Gather:
    COPIES = 9

    def __init__(self, shards, fulls, halves, send, recv, load, store, *held):
        self.shards, self.fulls, self.halves, self.held = shards, fulls, halves, held
        self.send, self.recv, self.load, self.store = send, recv, load, store
        self.f, self.r = lax.axis_index("fsdp"), lax.axis_index("replica")
        f = self.f
        c, x, y = lax.rem(f, 2), lax.rem(f // 2, 2), f // 4
        self.core, self.x, self.y = f + 1 - 2 * c, f + 2 - 4 * x, f + 4 - 8 * y
        self.xy = self.x + 4 - 8 * y

    def rows(self, at, which):
        rows, half = self.shards[at][0].shape[0], self.halves[at]
        return {"all": (0, rows), "top": (0, half), "low": (half, rows - half)}[which]

    def part(self, at, place, which):
        first, size = self.rows(at, which)
        rows = self.shards[at][0].shape[0]
        return self.fulls[at].at[pl.ds(pl.multiple_of(place * rows + first, 16), size), :]

    def remote(self, at, kind, src, dst, to):
        return pltpu.make_async_remote_copy(
            src_ref=src, dst_ref=dst, send_sem=self.send.at[at, kind],
            recv_sem=self.recv.at[at, kind], device_id=(to, self.r), device_id_type=MESH,
        )

    def copy(self, at, kind, place, which, to, source=None):
        dst = self.part(at, place, which)
        src = dst if source is None else self.held[at].at[source, pl.ds(*self.rows(at, which)), :]
        return self.remote(at, kind, src, dst, to)

    def hop(self, at, source):
        return self.remote(at, 6 + source, self.held[at].at[0], self.held[at].at[source], (self.x, self.y)[source - 1])

    def keep(self, at, source):
        place = (self.f, self.x, self.y)[source]
        return pltpu.make_async_copy(self.held[at].at[source], self.part(at, place, "all"), self.store.at[at, source])

    def fetch(self, at, source):
        return pltpu.make_async_copy(self.shards[at][source], self.held[at].at[source], self.load.at[at, source])

    def pass_on(self, at, source):
        place = (self.f, self.x, self.y)[source]
        self.copy(at, 2 + source, place, "all", self.core, source).start()
        self.keep(at, source).start()

    def begin(self):
        places = range(len(self.shards))
        for at in places:
            for source in range(len(self.shards[at])):
                self.fetch(at, source).start()
        for at in places:
            self.fetch(at, 0).wait()
            if len(self.shards[at]) == 1:
                self.hop(at, 1).start()
                self.hop(at, 2).start()
        for at in places:
            self.pass_on(at, 0)

    def onward(self, at):
        ahead = len(self.shards[at]) == 3
        self.fetch(at, 1).wait() if ahead else self.hop(at, 1).wait_recv()
        self.copy(at, 0, self.x, "top", self.y, 1).start()
        self.fetch(at, 2).wait() if ahead else self.hop(at, 2).wait_recv()
        self.copy(at, 1, self.y, "low", self.x, 2).start()
        self.pass_on(at, 1)
        self.pass_on(at, 2)

    def across(self, at):
        self.copy(at, 0, self.xy, "top", self.y).wait_recv()
        self.copy(at, 5, self.xy, "top", self.core).start()
        self.copy(at, 1, self.xy, "low", self.x).wait_recv()
        self.copy(at, 6, self.xy, "low", self.core).start()

    def end(self, at):
        for source in range(3):
            self.keep(at, source).wait()
            if source and len(self.shards[at]) == 1:
                self.hop(at, source).wait_send()
        for kind, which in ((0, "top"), (1, "low"), (2, "all"), (3, "all"), (4, "all"), (5, "top"), (6, "low")):
            self.copy(at, kind, self.f, which, self.core).wait_send()
            if kind >= 2:
                self.copy(at, kind, self.f, which, self.core).wait_recv()


def sent_ahead(shards, after):
    shards, _ = lax.optimization_barrier((shards, after))
    hop = lambda shard, step: lax.ppermute(shard, "fsdp", [(at, at ^ step) for at in range(8)])
    return [(shard, hop(shard, 2), hop(shard, 4)) for shard in shards]


def split_shards(refs, sizes):
    shards = []
    for size in sizes:
        shards.append(refs[:size])
        refs = refs[size:]
    return shards, refs


def gather_scratch(shards):
    count = len(shards)
    if not count:
        return []
    return [
        pltpu.SemaphoreType.DMA((count, Gather.COPIES)),
        pltpu.SemaphoreType.DMA((count, Gather.COPIES)),
        pltpu.SemaphoreType.DMA((count, 3)),
        pltpu.SemaphoreType.DMA((count, 3)),
    ] + [pltpu.VMEM((3, *part.shape), part.dtype) for part, *_ in shards]


def gathered_shapes(shards):
    return tuple(jax.ShapeDtypeStruct((8 * part.shape[0], part.shape[1]), part.dtype) for part, *_ in shards)


def halves_of(shards, more=False):
    halves, ahead = [], 0
    for part, *_ in shards:
        rows, size = part.shape
        half = rows // 24 * 16 if more else rows // 32 * 16
        if rows % 32 and ahead <= 0 and not more:
            half += 16
        ahead += (2 * half - rows) * size
        halves.append(half)
    return tuple(halves), tuple(len(shard) for shard in shards)


def start_kernel(plan, part_in, bias_in, *refs):
    halves, sizes = plan
    count = len(halves)
    shards, refs = split_shards(refs, sizes)
    (mod, bias), fulls, refs = refs[:2], refs[2 : count + 2], refs[count + 2 :]
    terms, total, m_s, m_r, b_s, b_r, t_s, t_r, keep, *sems = refs
    f, r = lax.axis_index("fsdp"), lax.axis_index("replica")
    others = [lax.rem(f + d, 8) for d in range(1, 8)]
    greet([((there, r), True) for there in others], 7)

    def remote(src, dst, s_sem, r_sem, there):
        return pltpu.make_async_remote_copy(
            src_ref=src, dst_ref=dst, send_sem=s_sem, recv_sem=r_sem, device_id=(there, r), device_id_type=MESH
        )

    def term_copy(block, source, there):
        return remote(part_in.at[block], terms.at[source], t_s.at[there], t_r.at[source], there)

    def bias_copy(source, there):
        return remote(bias_in, bias.at[source], b_s.at[there], b_r.at[source], there)

    def mod_copy(source, there):
        return remote(total, mod.at[source], m_s.at[there], m_r.at[source], there)

    gather = Gather(shards, fulls, halves, *sems)
    for there in others:
        term_copy(there, f, there).start()
    mine = pltpu.make_async_copy(part_in.at[f], terms.at[f], keep.at[0])
    mine.start()
    gather.begin()
    for there in others:
        bias_copy(f, there).start()
    own_bias = pltpu.make_async_copy(bias_in, bias.at[f], keep.at[1])
    own_bias.start()
    mine.wait()
    for there in others:
        term_copy(f, there, there).wait_recv()
    total[...] = functools.reduce(lambda a, b: a + b, [terms[j] for j in range(8)])
    for there in others:
        mod_copy(f, there).start()
    own_mod = pltpu.make_async_copy(total, mod.at[f], keep.at[2])
    own_mod.start()
    for at in range(count):
        gather.onward(at)
    for at in range(count):
        gather.across(at)
    for at in range(count):
        gather.end(at)
    own_bias.wait()
    own_mod.wait()
    for there in others:
        term_copy(there, f, there).wait_send()
        bias_copy(f, there).wait_send()
        mod_copy(f, there).wait_send()
        bias_copy(there, there).wait_recv()
        mod_copy(there, there).wait_recv()


def start(parts, biases, shards, collective_id):
    sem = lambda: pltpu.SemaphoreType.DMA((8,))
    return pl.pallas_call(
        functools.partial(start_kernel, halves_of(shards)),
        out_shape=(
            jax.ShapeDtypeStruct(parts.shape, parts.dtype),
            jax.ShapeDtypeStruct((8, *biases.shape), biases.dtype),
            *gathered_shapes(shards),
        ),
        in_specs=[HB] * (2 + sum(len(shard) for shard in shards)),
        out_specs=(HB,) * (2 + len(shards)),
        scratch_shapes=[
            pltpu.VMEM(parts.shape, parts.dtype), pltpu.VMEM(parts.shape[1:], parts.dtype),
            sem(), sem(), sem(), sem(), sem(), sem(), pltpu.SemaphoreType.DMA((3,)), *gather_scratch(shards),
        ],
        compiler_params=pltpu.CompilerParams(
            collective_id=collective_id, has_side_effects=True, vmem_limit_bytes=VMEM_LIMIT
        ),
    )(parts, biases, *(part for shard in shards for part in shard))


def to_heads_kernel(reps, size, edge, kv, plan, qkv, *refs):
    halves, sizes = plan
    count = len(halves)
    shards, refs = split_shards(refs, sizes)
    (own, prev, after), fulls, refs = refs[:3], refs[3 : count + 3], refs[count + 3 :]
    x_ref, send, recv, edge_send, edge_recv, *sems = refs
    gather = Gather(shards, fulls, halves, *sems) if count else None
    group, me = lax.axis_index("fsdp"), lax.axis_index("replica")
    groups = lax.axis_size("fsdp")
    wide = x_ref.shape[2]
    width = qkv.shape[1] // 3
    hd = width // reps
    down, up = group > 0, group < groups - 1
    others = [(group, lax.rem(me + d, reps)) for d in range(1, reps)]
    greet(
        [(place, True) for place in others] + [((group - 1, me), down), ((group + 1, me), up)]
        + ([((there, me), True) for there in (gather.core, gather.x, gather.y)] if count else []),
        reps - 1 + down.astype(jnp.int32) + up.astype(jnp.int32) + (3 if count else 0),
    )
    spans = [pl.ds(0, kv), pl.ds(kv, wide - kv)] if wide > kv else [pl.ds(0, kv)]

    def exchange(span, part, there):
        return pltpu.make_async_remote_copy(
            src_ref=x_ref.at[there, :, span], dst_ref=own.at[me, :, span], send_sem=send.at[part, there],
            recv_sem=recv.at[part, me], device_id=(group, there), device_id_type=MESH,
        )

    def depart(place, part):
        span = spans[part]
        pl.when(me != place)(lambda: exchange(span, part, place).start())
        keep = pltpu.make_async_copy(x_ref.at[place, :, span], own.at[place, :, span], recv.at[part, place])
        pl.when(me == place)(keep.start)

    for place in range(reps):
        def pack(rows, place=place):
            at = place * hd
            pieces = [(qkv, width + at, 0, hd), (qkv, 2 * width + at, hd, hd), (qkv, at, 2 * hd, hd)]
            x_ref[place, rows, :] = assemble(rows, wide, pieces).astype(jnp.bfloat16)

        by_rows(size, pack)
        depart(place, 0)
    for part in range(1, len(spans)):
        for place in range(reps):
            depart(place, part)

    if count:
        gather.begin()
    for at in range(count):
        gather.onward(at)

    def edges(piece, action):
        lo, hi = piece * size, (piece + 1) * size
        total = reps * size
        if lo >= total - edge:
            @pl.when(up)
            def _():
                action(0, piece, (group + 1, me), prev.at[pl.ds(lo - (total - edge), size), :])
        if hi <= edge:
            @pl.when(down)
            def _():
                action(1, piece, (group - 1, me), after.at[pl.ds(lo, size), :])

    def start_edge(way, piece, where, target):
        pltpu.make_async_remote_copy(
            src_ref=own.at[piece, :, spans[0]], dst_ref=target, send_sem=edge_send.at[way, piece],
            recv_sem=edge_recv.at[way, piece], device_id=where, device_id_type=MESH,
        ).start()

    def end_send(way, piece, where, target):
        wait_for(own.at[piece, :, spans[0]], edge_send.at[way, piece])

    def end_recv(way, piece, where, target):
        wait_for(target, edge_recv.at[way, piece])

    for piece in range(reps):
        wait_for(own.at[piece, :, spans[0]], recv.at[0, piece])
        edges(piece, start_edge)
    if len(spans) > 1:
        for piece in range(reps):
            wait_for(own.at[piece, :, spans[1]], recv.at[1, piece])
    for at in range(count):
        gather.across(at)
    for part, span in enumerate(spans):
        for _, there in others:
            wait_for(x_ref.at[there, :, span], send.at[part, there])
    for piece in range(reps):
        edges(piece, end_send)
        lo, hi = piece * size, (piece + 1) * size
        total = reps * size
        if lo >= total - edge:
            @pl.when(down)
            def _():
                wait_for(prev.at[pl.ds(lo - (total - edge), size), :], edge_recv.at[0, piece])
        if hi <= edge:
            @pl.when(up)
            def _():
                wait_for(after.at[pl.ds(lo, size), :], edge_recv.at[1, piece])
    for at in range(count):
        gather.end(at)


def to_heads(qkv, reps, edge, kv, shards, collective_id):
    size, wide = qkv.shape[0], pad_to(qkv.shape[1] // reps, LANES)
    sems = pltpu.SemaphoreType.DMA((2, reps))
    own, prev, after, *fulls = pl.pallas_call(
        functools.partial(to_heads_kernel, reps, size, edge, kv, halves_of(shards, True)),
        out_shape=(
            jax.ShapeDtypeStruct((reps, size, wide), qkv.dtype),
            jax.ShapeDtypeStruct((edge, kv), qkv.dtype),
            jax.ShapeDtypeStruct((edge, kv), qkv.dtype),
            *gathered_shapes(shards),
        ),
        in_specs=[VM] + [HB] * sum(len(shard) for shard in shards),
        out_specs=(HB,) * (3 + len(shards)),
        scratch_shapes=[pltpu.VMEM((reps, size, wide), qkv.dtype), sems, sems, sems, sems, *gather_scratch(shards)],
        compiler_params=pltpu.CompilerParams(
            collective_id=collective_id, has_side_effects=True, vmem_limit_bytes=VMEM_LIMIT
        ),
    )(qkv, *(part for shard in shards for part in shard))
    return own.reshape(reps * size, wide), prev, after, fulls


class Tails:
    def __init__(self, hd, size):
        self.main = hd // LANES * LANES
        self.few = hd - self.main
        self.fold = LANES // self.few
        self.band = size // self.fold

    def block(self, values, shift):
        turned = pltpu.roll(values.astype(jnp.float32), shift % LANES, 1) if shift % LANES else values.astype(jnp.float32)
        lane = lax.broadcasted_iota(jnp.int32, turned.shape, 1)
        return jnp.where(lane < self.few, turned, 0.0)

    def folded(self, ref):
        total = None
        for at in range(self.fold):
            part = self.block(ref[at * self.band : (at + 1) * self.band, self.main : self.main + LANES], 0)
            part = pltpu.roll(part, at * self.few, 1) if at else part
            total = part if total is None else total + part
        return total.astype(jnp.bfloat16)

    def unfolded(self, tail, at):
        return self.block(tail, -at * self.few).astype(jnp.bfloat16)


def swap_kernel(reps, out, plan, chip, x_ref, *refs):
    halves, sizes = plan
    count = len(halves)
    shards, refs = split_shards(refs, sizes)
    have = sum(chip[2]) if chip else 0
    chip_ins, refs = refs[:have], refs[have:]
    y_ref, fulls, refs = refs[0], refs[1 : count + 1], refs[count + 1 :]
    chip_outs, refs = (refs[:5], refs[5:]) if chip else ((), refs)
    (held, tail_out, tail_in, opened, send, recv, done), sems = refs[:7], refs[7:]
    gather = Gather(shards, fulls, halves, *sems) if count else None
    group, me = lax.axis_index("fsdp"), lax.axis_index("replica")
    others = [(group, lax.rem(me + d, reps)) for d in range(1, reps)]
    planar = [(there, me) for there in (gather.core, gather.x, gather.y)] if count else []
    if chip:
        planar.append((group + 1 - 2 * lax.rem(group, 2), me))
    size, lanes = held.shape[1:]
    src, dst = (x_ref, held) if out else (held, y_ref)
    hd = (y_ref if out else x_ref).shape[1] // reps
    tails = Tails(hd, size)
    span = pl.ds(0, tails.main)
    greet([(place, True) for place in others + planar], reps - 1 + len(planar))
    for place in range(reps):
        if not out:
            def pack(rows, place=place):
                held[place, rows, :] = assemble(rows, lanes, [(x_ref, place * hd, 0, hd)]).astype(jnp.bfloat16)

            by_rows(size, pack)
        tail_out[place] = tails.folded(src.at[place])
        parts = ((src.at[place, :, span], lambda to: dst.at[to, :, span]), (tail_out.at[place], lambda to: tail_in.at[to]))
        for at, (part, landing) in enumerate(parts):
            leave = pltpu.make_async_remote_copy(
                src_ref=part, dst_ref=landing(me), send_sem=send.at[at, place], recv_sem=recv.at[at, me],
                device_id=(group, place), device_id_type=MESH,
            )
            keep = pltpu.make_async_copy(part, landing(place), recv.at[at, place])
            pl.when(me != place)(leave.start)
            pl.when(me == place)(keep.start)
    if count:
        gather.begin()
    for at in range(count):
        gather.onward(at)
    for at in range(count):
        gather.across(at)
    if chip:
        terms, run = chip_steps(*chip, (*chip_ins, *chip_outs, *sems))
        terms.start()
        terms.wait()
        run((0, MATRICES + 3))
    for piece in range(reps):
        wait_for(dst.at[piece, :, span], recv.at[0, piece])
        wait_for(tail_in.at[piece], recv.at[1, piece])
        for at in range(tails.fold):
            rows = slice(at * tails.band, (at + 1) * tails.band)
            few = tails.unfolded(tail_in[piece], at)
            if out:
                held[piece, rows, tails.main : tails.main + LANES] = few
            else:
                opened[piece, rows, :] = few
        if not out:
            pltpu.make_async_copy(opened.at[piece], y_ref.at[piece, :, pl.ds(tails.main, LANES)], done.at[piece]).start()
    if out:
        def unpack(rows):
            pieces = [(held.at[place], 0, place * hd, hd) for place in range(reps)]
            y_ref[rows, :] = assemble(rows, y_ref.shape[1], pieces).astype(jnp.bfloat16)

        by_rows(size, unpack)
    else:
        for piece in range(reps):
            wait_for(opened.at[piece], done.at[piece])
    for _, there in others:
        wait_for(src.at[there, :, span], send.at[0, there])
        wait_for(tail_out.at[there], send.at[1, there])
    for at in range(count):
        gather.end(at)


def swap(x, reps, out, shards, collective_id, pair=None):
    if out:
        size, lanes = x.shape[0] // reps, x.shape[1]
        x = x.reshape(reps, size, lanes)
        shape = (size, HEADS * HEAD_DIM)
    else:
        size, lanes = x.shape[0], pad_to(x.shape[1] // reps, LANES)
        shape = (reps, size, lanes)
    band = Tails(HEADS * HEAD_DIM // reps, size).band
    sems = pltpu.SemaphoreType.DMA((2, reps))
    tail = pltpu.VMEM((reps, band, LANES), x.dtype)
    late = ((None, None, None, pair[0][3]), (None, None, None, pair[1][3])) if pair else None
    chip, chip_ins, chip_shapes, chip_scratch = chip_parts(*late, EARLY, MATRICES) if pair else (None, (), (), [])
    swapped, *fulls = pl.pallas_call(
        functools.partial(swap_kernel, reps, out, halves_of(shards), chip),
        out_shape=(jax.ShapeDtypeStruct(shape, x.dtype), *gathered_shapes(shards), *chip_shapes),
        in_specs=[VM] + [HB] * (sum(len(shard) for shard in shards) + len(chip_ins)),
        out_specs=(VM if out else HB,) + (HB,) * (len(shards) + len(chip_shapes)),
        scratch_shapes=[
            pltpu.VMEM((reps, size, lanes), x.dtype), tail, tail, pltpu.VMEM((reps, size, LANES), x.dtype), sems, sems,
            pltpu.SemaphoreType.DMA((reps,)), *gather_scratch(shards), *chip_scratch,
        ],
        compiler_params=pltpu.CompilerParams(
            collective_id=collective_id, has_side_effects=True, vmem_limit_bytes=VMEM_LIMIT
        ),
    )(x, *(part for shard in shards for part in shard), *chip_ins)
    return swapped, fulls


def from_heads_kernel(reps, size, edge, chip, dprev, own, dafter, dq, *refs):
    have = sum(chip[2]) if chip else 0
    chip_ins, out, refs = refs[:have], refs[have], refs[have + 1 :]
    chip_outs, refs = (refs[:5], refs[5:]) if chip else ((), refs)
    (out_kv, out_q, dq_tail, from_up, from_down, total, mine, sends, recvs, send, recv, tail_sem), refs = refs[:12], refs[12:]
    group, me = lax.axis_index("fsdp"), lax.axis_index("replica")
    groups = lax.axis_size("fsdp")
    rows = reps * size
    down, up = group > 0, group < groups - 1
    others = [(group, lax.rem(me + d, reps)) for d in range(1, reps)]
    order = [lax.rem(me + d, reps) for d in range(1, reps + 1)]
    greet(
        [(place, True) for place in others] + [((group - 1, me), down), ((group + 1, me), up)]
        + ([((group + 1 - 2 * lax.rem(group, 2), me), True)] if chip else []),
        reps - 1 + down.astype(jnp.int32) + up.astype(jnp.int32) + (1 if chip else 0),
    )
    terms, run = chip_steps(*chip, (*chip_ins, *chip_outs, *refs)) if chip else (None, lambda some: None)
    if chip:
        terms.start()
    edges = edge // size
    width = out.shape[1] // 3
    hd = width // reps
    tails = Tails(hd, size)

    def at_piece(piece):
        return pl.ds(pl.multiple_of(piece * size, size), size)

    def to_down(piece):
        return pltpu.make_async_remote_copy(
            src_ref=dprev.at[at_piece(piece), :], dst_ref=from_up.at[at_piece(piece), :], send_sem=sends.at[0, piece],
            recv_sem=recvs.at[0, piece], device_id=(group - 1, me), device_id_type=MESH,
        )

    def to_up(piece):
        return pltpu.make_async_remote_copy(
            src_ref=dafter.at[at_piece(piece), :], dst_ref=from_down.at[at_piece(piece), :], send_sem=sends.at[1, piece],
            recv_sem=recvs.at[1, piece], device_id=(group + 1, me), device_id_type=MESH,
        )

    def edge_pieces(piece, when_up, when_down):
        pl.when(jnp.logical_and(down, piece < edges))(lambda: when_down(piece))
        late = piece - (reps - edges)
        pl.when(jnp.logical_and(up, late >= 0))(lambda: when_up(late))

    for piece in order:
        late = piece - (reps - edges)
        pl.when(jnp.logical_and(down, late >= 0))(lambda late=late: to_down(late).start())
        pl.when(jnp.logical_and(up, piece < edges))(lambda piece=piece: to_up(piece).start())
    tail_load = pltpu.make_async_copy(dq.at[:, pl.ds(tails.main, LANES)], dq_tail, tail_sem)
    tail_load.start()

    def query_copy(piece):
        return pltpu.make_async_remote_copy(
            src_ref=dq.at[at_piece(piece), pl.ds(0, tails.main)], dst_ref=out_q.at[me], send_sem=send.at[0, piece],
            recv_sem=recv.at[0, me], device_id=(group, piece), device_id_type=MESH,
        )

    def sums_copy(piece):
        return pltpu.make_async_remote_copy(
            src_ref=mine.at[at_piece(piece), :], dst_ref=out_kv.at[me], send_sem=send.at[1, piece],
            recv_sem=recv.at[1, me], device_id=(group, piece), device_id_type=MESH,
        )

    for piece in order[:-1]:
        query_copy(piece).start()
    pltpu.make_async_copy(dq.at[at_piece(me), pl.ds(0, tails.main)], out_q.at[me], recv.at[0, me]).start()
    tail_load.wait()
    step = math.gcd(size, 64)

    def sum_up(piece):
        def chunk(at, action):
            here = pl.ds(pl.multiple_of(piece * size + at * step, step), step)
            there = pl.ds(pl.multiple_of(at * step, step), step)
            action(here, there)

        def over(action):
            def body(at, carry):
                chunk(at, action)
                return carry

            lax.fori_loop(0, size // step, body, 0)

        def begin(here, there):
            total[there, :] = own[here, :].astype(jnp.float32)

        over(begin)

        def add(ref, sem, source):
            wait_for(ref.at[at_piece(source), :], sem)

            def body(at, carry):
                there = pl.ds(pl.multiple_of(at * step, step), step)
                here = pl.ds(pl.multiple_of(source * size + at * step, step), step)
                total[there, :] += ref[here, :].astype(jnp.float32)
                return carry

            lax.fori_loop(0, size // step, body, 0)

        edge_pieces(
            piece, lambda late: add(from_up, recvs.at[0, late], late), lambda early: add(from_down, recvs.at[1, early], early)
        )

        def narrow(here, there):
            mine[here, :] = total[there, :].astype(jnp.bfloat16)
            first = 2 * hd // LANES * LANES
            few = pltpu.roll(tails.block(dq_tail[here, :], 0), 2 * hd - first, 1)
            last = slice(first, first + LANES)
            mine[here, last] = (total[there, last] + few).astype(jnp.bfloat16)

        over(narrow)

    if chip:
        terms.wait()
    for at, piece in enumerate(order[:-1]):
        run((2 * at, 2 * at + 2))
        sum_up(piece)
        sums_copy(piece).start()
    sum_up(me)
    pltpu.make_async_copy(mine.at[at_piece(me), :], out_kv.at[me], recv.at[1, me]).start()
    run((2 * (reps - 1), MATRICES + 3))

    def unpack(section, sources):
        def body(rows):
            pieces = [
                (ref.at[place], first, place * hd + to, lanes) for place in range(reps) for ref, first, to, lanes in sources
            ]
            out[rows, section * width : (section + 1) * width] = assemble(rows, width, pieces).astype(jnp.bfloat16)

        by_rows(size, body)

    for piece in range(reps):
        wait_for(out_q.at[piece], recv.at[0, piece])
        wait_for(out_kv.at[piece], recv.at[1, piece])
    unpack(0, ((out_q, 0, 0, tails.main), (out_kv, 2 * hd, tails.main, tails.few)))
    unpack(1, ((out_kv, 0, 0, hd),))
    unpack(2, ((out_kv, hd, 0, hd),))
    for piece in order[:-1]:
        query_copy(piece).wait_send()
        sums_copy(piece).wait_send()
    for piece in order:
        late = piece - (reps - edges)
        pl.when(jnp.logical_and(down, late >= 0))(lambda late=late: to_down(late).wait_send())
        pl.when(jnp.logical_and(up, piece < edges))(lambda piece=piece: to_up(piece).wait_send())


def from_heads(reps, width, dprev, own, dafter, dq, collective_id, pair=None):
    rows, kv = own.shape
    edge, size = dprev.shape[0], own.shape[0] // reps
    both = pltpu.SemaphoreType.DMA((2, reps))
    chip, chip_ins, chip_shapes, chip_scratch = chip_parts(*pair, 0, EARLY) if pair else (None, (), (), [])
    return pl.pallas_call(
        functools.partial(from_heads_kernel, reps, size, edge, chip),
        out_shape=(jax.ShapeDtypeStruct((size, 3 * width), own.dtype), *chip_shapes),
        in_specs=[HB, VM, HB, HB] + [HB] * len(chip_ins),
        out_specs=(VM,) + (HB,) * len(chip_shapes),
        scratch_shapes=[
            pltpu.VMEM((reps, size, kv), own.dtype),
            pltpu.VMEM((reps, size, width // reps // LANES * LANES), own.dtype),
            pltpu.VMEM((rows, LANES), own.dtype),
            pltpu.VMEM((edge, kv), own.dtype),
            pltpu.VMEM((edge, kv), own.dtype),
            pltpu.VMEM((size, kv), jnp.float32),
            pltpu.VMEM((rows, kv), own.dtype),
            both,
            both,
            both,
            both,
            pltpu.SemaphoreType.DMA,
            *chip_scratch,
        ],
        compiler_params=pltpu.CompilerParams(
            collective_id=collective_id, has_side_effects=True, vmem_limit_bytes=VMEM_LIMIT
        ),
    )(dprev, own, dafter, dq, *chip_ins)


MATRICES = 12
CHIP_WIDTH, UNIT_WIDTH = 1152, 384
SLACK = 4
LEFT_ROWS = 4
LEFT_SIZES, RIGHT_SIZES = (4, 1, 1, 1), (1, 4, 1, 3)
EARLY = 9
PLACES = ((0, 0), (1, 0), (0, 1), (1, 1))


class Terms:
    def __init__(self, ins, flat, left, right, rows, width, load_sem):
        self.flat, self.left, self.right, self.rows, self.width = flat, left, right, rows, width
        self.unit = right.shape[2]
        self.parts = width // self.unit
        f = lax.axis_index("fsdp")
        self.c, self.x, self.y = lax.rem(f, 2), lax.rem(f // 2, 2), f // 4
        self.core_at, self.x_at, self.y_at = f + 1 - 2 * self.c, f + 2 - 4 * self.x, f + 4 - 8 * self.y
        self.loads, self.turns, place, slot = [], [], 0, 0
        for src, size in zip(ins[:4], LEFT_SIZES):
            if src is not None:
                self.loads.append((src, flat.at[:, pl.ds(place, size * width)]))
                self.turns.append((place // LANES, size * width // LANES))
            place += size * width
        for src, size in zip(ins[4:], RIGHT_SIZES):
            for part in range(size * self.parts):
                if src is not None:
                    self.loads.append((src.at[:, pl.ds(part * self.unit, self.unit)], right.at[slot]))
                slot += 1
        self.load_sem = load_sem

    def start(self):
        for at, (src, dst) in enumerate(self.loads):
            pltpu.make_async_copy(src, dst, self.load_sem.at[at]).start()

    def wait(self):
        for at, (src, dst) in enumerate(self.loads):
            pltpu.make_async_copy(src, dst, self.load_sem.at[at]).wait()

        def turn(at, carry):
            here = pl.ds(pl.multiple_of(at * LANES, LANES), LANES)
            self.left[here, :] = self.flat[:, here].T
            return carry

        for first, count in self.turns:
            lax.fori_loop(first, first + count, turn, 0)

    def block(self, core, mx, my):
        x, y = self.x + mx * (1 - 2 * self.x), self.y + my * (1 - 2 * self.y)
        return (y * 2 + x) * 2 + (self.c + core * (1 - 2 * self.c))

    def stack(self, u, core):
        rows, width = self.rows, self.width
        m, part = u // self.parts, lax.rem(u, self.parts)
        inside = jnp.where(
            m < 4, rows * m, LEFT_ROWS * width + jnp.where(m < 8, 0, jnp.where(m < 9, width, 2 * width))
        )
        stride = jnp.where(m < 4, 4 * rows, rows)
        other = jnp.maximum(m - 3, 0) * self.parts + part
        blocks = []
        for mx, my in PLACES:
            start = pl.multiple_of(inside + stride * self.block(core, mx, my), 16)
            blocks.append(self.left[pl.ds(start, rows), :])
        return nn_dot(jnp.concatenate(blocks, axis=0), self.right[other])


def term_scratch(tokens, width, unit):
    parts = width // unit
    return [
        pltpu.VMEM((tokens, (LEFT_ROWS + 3) * width), jnp.bfloat16),
        pltpu.VMEM(((LEFT_ROWS + 3) * width, tokens), jnp.bfloat16),
        pltpu.VMEM((9 * parts, tokens, unit), jnp.bfloat16),
        pltpu.SemaphoreType.DMA((4 + 9 * parts,)),
    ]


def remote_copy(src, dst, s_sem, r_sem, where):
    return pltpu.make_async_remote_copy(
        src_ref=src, dst_ref=dst, send_sem=s_sem, recv_sem=r_sem, device_id=where, device_id_type=MESH
    )


def chip_steps(width, half, given, first, refs):
    have = sum(given)
    sides, (own, xs, ys, tx, ty), refs = iter(refs[:have]), refs[have : have + 5], refs[have + 5 :]
    ins = [next(sides) if there else None for there in given]
    flat, left, right, load_sem, csend, crecv, own_b, xs_b, ys_b, tx_b, ty_b, core_s, core_r, out_sem = refs
    r = lax.axis_index("replica")
    count, rows = own.shape[:2]
    terms = Terms(ins, flat, left, right, rows, width, load_sem)
    where = (terms.core_at, r)
    bf16, f32 = jnp.bfloat16, jnp.float32

    def core_copy(u):
        pair, four = lax.rem(u, 2), lax.rem(u, 4)
        return remote_copy(csend.at[pair], crecv.at[four], core_s.at[pair], core_r.at[four], where)

    def stores(u):
        pair = lax.rem(u, 2)
        buffers = ((own_b, own), (xs_b, xs), (ys_b, ys), (tx_b, tx), (ty_b, ty))
        return [
            pltpu.make_async_copy(src.at[pair], dst.at[u], out_sem.at[at, pair]) for at, (src, dst) in enumerate(buffers)
        ]

    def close(u):
        for copy in stores(u):
            copy.wait()

    def chip(u):
        pair, four = lax.rem(u, 2), lax.rem(u, 4)
        stacked = terms.stack(first + u, 0)
        core_copy(u).wait()
        totals = [stacked[m * rows : (m + 1) * rows] + crecv[four, m].astype(f32) for m in range(4)]
        mine, along_x, along_y, opposite = [total.astype(bf16) for total in totals]
        own_b[pair] = mine
        xs_b[pair, 0] = along_x[:half]
        tx_b[pair] = along_x[half:]
        ty_b[pair] = along_y[:half]
        ys_b[pair, 0] = along_y[half:]
        xs_b[pair, 1] = opposite[:half]
        ys_b[pair, 1] = opposite[half:]
        for copy in stores(u):
            copy.start()

    def open_unit(u):
        pair = lax.rem(u, 2)
        csend[pair] = terms.stack(first + u, 1).astype(bf16).reshape(csend.shape[1:])
        core_copy(u).start()

    def step(t, carry):
        pl.when(t < count)(lambda: open_unit(t))
        pl.when(t >= 3)(lambda: close(t - 3))
        pl.when(jnp.logical_and(t >= 1, t <= count))(lambda: chip(t - 1))
        return carry

    def run(some):
        lax.fori_loop(min(some[0], count + 3), min(some[1], count + 3), step, 0)

    return terms, run


def chip_parts(lefts, rights, first, last):
    ins = (*lefts, *rights)
    given = tuple(part is not None for part in ins)
    width = next(part for part in rights if part is not None).shape[1] // RIGHT_SIZES[given[4:].index(True)]
    tokens = next(part for part in ins if part is not None).shape[0]
    rows, unit = width // 8, CHIP_WIDTH
    half = pad_to(rows // 2, 16)
    count = last - first
    bf16 = jnp.bfloat16
    shapes = ((rows, unit), (2, half, unit), (2, rows - half, unit), (rows - half, unit), (half, unit))
    scratch = [
        *term_scratch(tokens, width, unit),
        pltpu.VMEM((2, 4, rows, unit), bf16),
        pltpu.VMEM((4, 4, rows, unit), bf16),
        *(pltpu.VMEM((2, *shape), bf16) for shape in shapes),
        pltpu.SemaphoreType.DMA((2,)),
        pltpu.SemaphoreType.DMA((4,)),
        pltpu.SemaphoreType.DMA((5, 2)),
    ]
    ins = tuple(part for part in ins if part is not None)
    return (width, half, given, first), ins, tuple(jax.ShapeDtypeStruct((count, *shape), bf16) for shape in shapes), scratch


def reduce_kernel(width, half, *refs):
    ins, extra_in, early, late, refs = refs[:8], refs[8], refs[9:14], refs[14:19], refs[19:]
    (out, out_down, mine, shared), refs = refs[:4], refs[4:]
    (flat, left, right, load_sem, extra, extra_sem, cx_s, cx_r, cxs_sem, cxr_sem, share_s, share_r,
     csend, crecv, own, xs, xr, ys, yr, tx, ty, x2s, x2r, y2s, y2r, zs, z1r, z2s, z2r, fin,
     own_l, xr_l, yr_l, tx_l, ty_l, ready_sem,
     core_s, core_r, x_s, x_r, y_s, y_r, x2_s, x2_r, y2_s, y2_r, z1_s, z1_r, z2_s, z2_r, fin_l, fin_s, fin_r,
     credit) = refs
    f, r = lax.axis_index("fsdp"), lax.axis_index("replica")
    rows = own.shape[1]
    extras = extra.shape[0]
    unit = own.shape[2]
    slots, pairs, z_slots = xr.shape[0], crecv.shape[0], z1r.shape[0]
    count = extras + 2 * MATRICES * (width // unit)
    terms = Terms(ins, flat, left, right, rows, width, load_sem)
    core_at, x_at, y_at = terms.core_at, terms.x_at, terms.y_at
    inner = jnp.logical_and(r > 0, r < 3)
    outer = jnp.logical_not(inner)
    z_at = r + 1 - 2 * lax.rem(r, 2)
    others = [lax.rem(f + d, 8) for d in range(1, 8)]
    greet(
        [((there, r), True) for there in others] + [((f, r - 1), r > 0), ((f, r + 1), r < 3)],
        7 + (r > 0).astype(jnp.int32) + (r < 3).astype(jnp.int32),
    )
    few = extra.shape[2]
    extra_loads = [
        pltpu.make_async_copy(extra_in.at[:, :, pl.ds(at * unit, unit)], extra.at[at], extra_sem.at[at])
        for at in range(extras)
    ]
    for load in extra_loads:
        load.start()
    terms.start()
    for load in extra_loads:
        load.wait()
    send = remote_copy
    top, low = pl.ds(0, half), pl.ds(half, rows - half)

    def core_copy(slot):
        return send(csend.at[slot], crecv.at[slot], core_s.at[slot], core_r.at[slot], (core_at, r))

    def extra_copy(u):
        return send(cx_s.at[u], cx_r.at[u], cxs_sem.at[u], cxr_sem.at[u], (core_at, r))

    def x_copy(slot):
        return send(xs.at[slot], xr.at[slot], x_s.at[slot], x_r.at[slot], (x_at, r))

    def y_copy(slot):
        return send(ys.at[slot], yr.at[slot], y_s.at[slot], y_r.at[slot], (y_at, r))

    def x2_copy(slot):
        return send(x2s.at[slot], x2r.at[slot], x2_s.at[slot], x2_r.at[slot], (x_at, r))

    def y2_copy(slot):
        return send(y2s.at[slot], y2r.at[slot], y2_s.at[slot], y2_r.at[slot], (y_at, r))

    def z1_copy(slot, to):
        return send(zs.at[slot], z1r.at[to], z1_s.at[slot], z1_r.at[to], (f, z_at))

    def z2_copy(slot):
        return send(z2s.at[slot], z2r.at[slot], z2_s.at[slot], z2_r.at[slot], (f, 3 - r))

    def routed(u, action):
        v = u - extras
        w, layer = v // 2, 1 - lax.rem(v, 2)
        parts = width // unit
        m = w // parts

        @pl.when(m < 4)
        def _():
            row = pl.multiple_of(m * rows, 16)
            column = pl.multiple_of(lax.rem(w, parts) * unit, LANES)
            action(out_down.at[layer, pl.ds(row, rows), pl.ds(column, unit)])

        @pl.when(m >= 4)
        def _():
            column = pl.multiple_of((w - 4 * parts) * unit, LANES)
            action(out.at[layer, :, pl.ds(column, unit)])

    def fin_copy(slot, u, to):
        return send(fin.at[slot], to, fin_s.at[slot], fin_r.at[u], (f, z_at))

    def keep_copy(slot, to):
        return pltpu.make_async_copy(fin.at[slot], to, fin_l.at[slot])

    def columns(u):
        return pl.ds(pl.multiple_of(u * unit, LANES), unit)

    def fin_extra(u):
        slot = lax.rem(u, slots)
        return send(fin.at[slot, pl.ds(0, few), :], mine.at[:, columns(u)], fin_s.at[slot], fin_r.at[u], (f, z_at))

    def keep_extra(u):
        slot = lax.rem(u, slots)
        return pltpu.make_async_copy(fin.at[slot, pl.ds(0, few), :], mine.at[:, columns(u)], fin_l.at[slot])

    def share_copy(u, there, where):
        return send(
            mine.at[:, columns(u)], shared.at[there, :, columns(u)], share_s.at[u, where], share_r.at[u, there], (where, r)
        )

    def piece(src, m, part):
        here = pl.ds(pl.multiple_of(part * unit, LANES), unit)
        return src.at[m, :, here] if len(src.shape) == 3 else src.at[m, :, :, here]

    def ready_copies(u, action):
        slot, w = lax.rem(u, slots), (u - extras) // 2
        parts = width // unit
        m, part = w // parts, lax.rem(w, parts)

        def over(sources, m):
            for at, (src, dst) in enumerate(zip(sources, (own_l, xr_l, yr_l, tx_l, ty_l))):
                action(pltpu.make_async_copy(piece(src, m, part), dst.at[slot], ready_sem.at[at, slot]))

        pl.when(m < EARLY)(lambda: over(early, m))
        pl.when(m >= EARLY)(lambda: over(late, m - EARLY))

    f32, bf16 = jnp.float32, jnp.bfloat16

    def stage(u, condition, body, first=0, last=count):
        live = jnp.logical_and(u >= first, u < last)
        pl.when(live if condition is None else jnp.logical_and(live, condition))(lambda: body(u))

    def share_own(u):
        return pltpu.make_async_copy(mine.at[:, columns(u)], shared.at[f, :, columns(u)], share_r.at[u, f])

    def share(u):
        for there in others:
            share_copy(u, f, there).start()
        share_own(u).start()

    def close(u):
        slot = lax.rem(u, slots)

        def action(to):
            fin_copy(slot, u, to).wait_send()
            keep_copy(slot, to).wait()

        routed(u, action)

    def arrive(u):
        routed(u, lambda to: fin_copy(lax.rem(u, slots), u, to).wait_recv())

    def close_extra(u):
        fin_extra(u).wait_send()
        keep_extra(u).wait()

    def arrive_extra(u):
        fin_extra(u).wait_recv()

    def finish(u):
        slot = lax.rem(u, slots)
        z2_copy(slot).wait()
        fin[slot] = (z2s[slot].astype(f32) + z2r[slot].astype(f32)).astype(bf16)

        @pl.when(u >= extras)
        def _():
            def action(to):
                fin_copy(slot, u, to).start()
                keep_copy(slot, to).start()

            routed(u, action)

        @pl.when(u < extras)
        def _():
            fin_extra(u).start()
            keep_extra(u).start()

    def middle(u):
        slot, z_slot, at = lax.rem(u, slots), lax.rem(u, z_slots), lax.rem(u, own.shape[0])
        z1_copy(slot, z_slot).wait_recv()
        z2s[slot] = (own[at] + z1r[z_slot].astype(f32)).astype(bf16)
        z2_copy(slot).start()

        @pl.when(u + z_slots < count)
        def _():
            pl.semaphore_signal(credit, inc=1, device_id=(f, z_at), device_id_type=MESH)

    def sent(u):
        z1_copy(lax.rem(u, slots), lax.rem(u, z_slots)).wait_send()

    def plane(u):
        slot, at = lax.rem(u, slots), lax.rem(u, own.shape[0])
        x2_copy(slot).wait()
        y2_copy(slot).wait()
        own[at, top, :] += y2r[slot].astype(f32)
        own[at, low, :] += x2r[slot].astype(f32)

        @pl.when(outer)
        def _():
            zs[slot] = own[at].astype(bf16)

            @pl.when(u >= z_slots)
            def _():
                pl.semaphore_wait(credit, 1)

            z1_copy(slot, lax.rem(u, z_slots)).start()

    def cross(u):
        slot, at = lax.rem(u, slots), lax.rem(u, own.shape[0])
        x_copy(slot).wait()
        y_copy(slot).wait()
        y2s[slot] = (ty[slot] + xr[slot, 1].astype(f32)).astype(bf16)
        y2_copy(slot).start()
        x2s[slot] = (tx[slot] + yr[slot, 1].astype(f32)).astype(bf16)
        x2_copy(slot).start()
        own[at, top, :] += xr[slot, 0].astype(f32)
        own[at, low, :] += yr[slot, 0].astype(f32)

    def cross_ready(u):
        slot, at = lax.rem(u, slots), lax.rem(u, own.shape[0])
        ready_copies(u, lambda copy: copy.wait())
        y2s[slot] = (ty_l[slot].astype(f32) + xr_l[slot, 1].astype(f32)).astype(bf16)
        y2_copy(slot).start()
        x2s[slot] = (tx_l[slot].astype(f32) + yr_l[slot, 1].astype(f32)).astype(bf16)
        x2_copy(slot).start()
        own[at, top, :] = own_l[slot, top, :].astype(f32) + xr_l[slot, 0].astype(f32)
        own[at, low, :] = own_l[slot, low, :].astype(f32) + yr_l[slot, 0].astype(f32)

    def chip(u):
        slot, at = lax.rem(u, slots), lax.rem(u, own.shape[0])
        w = (u - extras) // 2
        pair = lax.rem(w, pairs)
        stacked = terms.stack(w, 0)
        core_copy(pair).wait()
        total = stacked[3 * rows :] + crecv[pair, 3].astype(f32)
        xs[slot, 1] = total[:half].astype(bf16)
        ys[slot, 1] = total[half:].astype(bf16)
        total = stacked[rows : 2 * rows] + crecv[pair, 1].astype(f32)
        xs[slot, 0] = total[:half].astype(bf16)
        tx[slot] = total[half:]
        x_copy(slot).start()
        total = stacked[2 * rows : 3 * rows] + crecv[pair, 2].astype(f32)
        ys[slot, 0] = total[half:].astype(bf16)
        ty[slot] = total[:half]
        y_copy(slot).start()
        own[at] = stacked[:rows] + crecv[pair, 0].astype(f32)

    def chip_extra(u):
        slot, at = lax.rem(u, slots), lax.rem(u, own.shape[0])
        extra_copy(u).wait()
        for m, (mx, my) in enumerate(PLACES):
            total = extra[u, terms.block(0, mx, my)] + cx_r[u, m].astype(f32)
            if m == 0:
                own[at, :few, :] = total
            elif m == 2:
                ty[slot, :few, :] = total
            else:
                xs[slot, m // 2, :few, :] = total.astype(bf16)
        x_copy(slot).start()
        y_copy(slot).start()

    def open_extra(u):
        for m, (mx, my) in enumerate(PLACES):
            cx_s[u, m] = extra[u, terms.block(1, mx, my)].astype(bf16)
        extra_copy(u).start()

    def open_ready(u):
        ready_copies(u, lambda copy: copy.start())

    def open_unit(u):
        w = (u - extras) // 2
        pair = lax.rem(w, pairs)
        csend[pair] = terms.stack(w, 1).astype(bf16).reshape(csend.shape[1:])
        core_copy(pair).start()

    def full(u):
        return lax.rem(u - extras, 2) == 1

    def prepared(u):
        return lax.rem(u - extras, 2) == 0

    def step(t, carry):
        at = [t - hop * SLACK for hop in range(7)]
        stage(at[6] - 1, None, share, 0, extras)
        stage(at[6], inner, close, extras)
        stage(at[6], outer, arrive, extras)
        stage(at[6], inner, close_extra, 0, extras)
        stage(at[6], outer, arrive_extra, 0, extras)
        stage(at[5], inner, finish)
        stage(at[4], inner, middle)
        stage(at[4], outer, sent)
        stage(at[3], None, plane)
        stage(at[2], full(at[2]), cross, extras)
        stage(at[2], None, cross, 0, extras)
        stage(at[2], prepared(at[2]), cross_ready, extras)
        stage(at[1], full(at[1]), chip, extras)
        stage(at[1], None, chip_extra, 0, extras)
        pl.when(t == extras + 1)(terms.wait)
        stage(t, full(t), open_unit, extras)
        stage(t, prepared(t), open_ready, extras)
        stage(t, None, open_extra, 0, extras)
        return carry

    lax.fori_loop(0, count + 6 * SLACK + 1, step, 0)
    for u in range(extras):
        for there in others:
            share_copy(u, f, there).wait_send()
            share_copy(u, there, there).wait_recv()
        share_own(u).wait()


def reduce_grads(lefts, rights, ready, extra):
    tokens, width = lefts[1].shape
    rows, unit = width // 8, UNIT_WIDTH
    half = pad_to(rows // 2, 16)
    ins = (*lefts, *rights)
    extras, few = width // unit, extra.shape[1]
    count = extras + 2 * MATRICES * (width // unit)
    bf16, f32 = jnp.bfloat16, jnp.float32
    buf = lambda dtype, *shape: pltpu.VMEM((*shape, unit), dtype)
    sem = lambda *size: pltpu.SemaphoreType.DMA(size)
    slots, z_slots = 2 * SLACK, 3 * SLACK
    rest = rows - half
    return pl.pallas_call(
        functools.partial(reduce_kernel, width, half),
        out_shape=(
            jax.ShapeDtypeStruct((2, rows, (MATRICES - 4) * width), bf16),
            jax.ShapeDtypeStruct((2, 4 * rows, width), bf16),
            jax.ShapeDtypeStruct((few, width), bf16),
            jax.ShapeDtypeStruct(extra.shape, bf16),
        ),
        in_specs=[HB] * 19,
        out_specs=(HB, HB, HB, HB),
        scratch_shapes=[
            *term_scratch(tokens, width, unit),
            buf(f32, extras, 8, few), sem(extras), buf(bf16, extras, 4, few), buf(bf16, extras, 4, few),
            sem(extras), sem(extras), sem(extras, 8), sem(extras, 8),
            buf(bf16, SLACK, 4, rows), buf(bf16, SLACK, 4, rows), buf(f32, 3 * SLACK + 1, rows),
            buf(bf16, slots, 2, half), buf(bf16, slots, 2, half), buf(bf16, slots, 2, rest), buf(bf16, slots, 2, rest),
            buf(f32, slots, rest), buf(f32, slots, half),
            buf(bf16, slots, rest), buf(bf16, slots, rest), buf(bf16, slots, half), buf(bf16, slots, half),
            buf(bf16, slots, rows), buf(bf16, z_slots, rows), buf(bf16, slots, rows), buf(bf16, slots, rows), buf(bf16, slots, rows),
            buf(bf16, slots, rows), buf(bf16, slots, 2, half), buf(bf16, slots, 2, rest), buf(bf16, slots, rest), buf(bf16, slots, half),
            sem(5, slots), sem(SLACK), sem(SLACK), *[sem(slots)] * 8,
            sem(slots), sem(z_slots), *[sem(slots)] * 4, sem(count), pltpu.SemaphoreType.REGULAR,
        ],
        compiler_params=pltpu.CompilerParams(
            collective_id=5, has_side_effects=True, vmem_limit_bytes=60 * 1024 * 1024
        ),
        cost_estimate=pl.CostEstimate(
            flops=2 * 64 * width * width * tokens, bytes_accessed=100 << 20, transcendentals=0
        ),
    )(*ins, extra, *ready)


def pre_norm(stream, shift, scale):
    centred = stream - jnp.mean(stream, axis=-1, keepdims=True)
    spread = jnp.mean(centred * centred, axis=-1, keepdims=True)
    return centred * lax.rsqrt(spread + NORM_EPS) * (1.0 + scale) + shift


def latent_ids(latent_len, positions, token_total):
    starts = jnp.cumsum(latent_len) - latent_len
    found = jnp.sum((starts[None, :] <= positions[:, None]).astype(jnp.int32), axis=1) - 1
    inside = (positions >= 0) & (positions < token_total)
    return jnp.where(inside, found, -1)


def low_dot(left, right):
    return jnp.dot(left, right, preferred_element_type=jnp.float32)


TILE = 512
GELU_ROOT = math.sqrt(2.0 / math.pi)


def thirds(values):
    high = values.astype(jnp.bfloat16)
    rest = values - high.astype(jnp.float32)
    middle = rest.astype(jnp.bfloat16)
    return high, middle, (rest - middle.astype(jnp.float32)).astype(jnp.bfloat16)


def halves_across(width):
    first = pad_to(width // 2, LANES)
    return (pl.ds(0, first), pl.ds(first, width - first))


def at_tile(at, size=TILE):
    return pl.ds(pl.multiple_of(at * size, size), size)


def tiles(count, body):
    def run(at, carry):
        body(at)
        return carry

    lax.fori_loop(0, count, run, 0)


def norm_parts(stream):
    centred = stream - jnp.mean(stream, axis=1, keepdims=True)
    root = lax.rsqrt(jnp.mean(centred * centred, axis=1, keepdims=True) + NORM_EPS)
    return centred * root, root


class FeedForward:
    def __init__(self, pick, mod, weights, held, sems):
        self.pick, self.mod = pick, mod
        self.out_w, self.up_w, self.down_w = held
        self.width, self.hidden = held[1].shape
        self.pieces = sems.shape[0] // 2
        self.piece = self.hidden // self.pieces
        cuts = [pl.ds(at * self.piece, self.piece) for at in range(self.pieces)]
        copy = pltpu.make_async_copy
        self.out_copy = copy(weights[0], held[0], sems.at[0])
        self.up_copies = [copy(weights[1].at[:, cut], held[1].at[:, cut], sems.at[1 + at]) for at, cut in enumerate(cuts)]
        self.down_copies = [
            copy(weights[2].at[cut, :], held[2].at[cut, :], sems.at[1 + self.pieces + at]) for at, cut in enumerate(cuts)
        ]

    def start(self, forth):
        order = [self.out_copy, *self.up_copies, *self.down_copies]
        for part in order if forth else [*self.down_copies, *self.up_copies, self.out_copy]:
            part.start()

    def vector(self, rows, at):
        return nn_dot(self.pick[rows, :], self.mod[:, at * self.width : (at + 1) * self.width])

    def forward(self, stream, mixed, biases, branch, middle, normed, hidden, active, result, after):
        out_b, up_b, down_b = biases
        size, width = stream.shape
        self.out_copy.wait()
        for here in halves_across(width):
            branch[:, here] = nn_dot(mixed[...], self.out_w[:, here]) + out_b[:, here].astype(jnp.float32)

        def first_norm(rows):
            total = stream[rows, :] + self.vector(rows, 2) * branch[rows, :]
            middle[rows, :] = total
            unit, _ = norm_parts(total)
            normed[rows, :] = (unit * (1.0 + self.vector(rows, 4)) + self.vector(rows, 3)).astype(jnp.bfloat16)

        by_rows(size, first_norm)
        for piece in range(self.pieces):
            self.up_copies[piece].wait()

            def widen(at, piece=piece):
                here = at_tile(piece * (self.piece // TILE) + at)
                values = nn_dot(normed[...], self.up_w[:, here]) + up_b[:, here].astype(jnp.float32)
                hidden[:, here] = values
                inner = GELU_ROOT * (values + 0.044715 * values * values * values)
                active[:, here] = (0.5 * values * (1.0 + jnp.tanh(inner))).astype(jnp.bfloat16)

            tiles(self.piece // TILE, widen)
        for part in self.down_copies:
            part.wait()
        for here in halves_across(width):
            result[:, here] = nn_dot(active[...], self.down_w[:, here]) + down_b[:, here].astype(jnp.float32)

        def leave(rows):
            after[rows, :] = (middle[rows, :] + self.vector(rows, 5) * result[rows, :]).astype(after.dtype)

        by_rows(size, leave)

    def backward(self, grad, branch, middle, hidden, result, outs, work, fresh):
        low_result, low_hidden, low_branch, low_mixed, grad_middle, grad_mod, out_sum, up_sum, down_sum = outs
        size, width = middle.shape
        grad_mod[...] = jnp.zeros_like(grad_mod)
        for ref in (out_sum, up_sum, down_sum):
            ref[...] = jnp.zeros_like(ref)

        latents = grad_mod.shape[0] // 4

        def collect(rows, at, values):
            here = slice(at * latents, (at + 1) * latents)
            ones = self.pick[rows, :latents]
            for part in thirds(values)[:2]:
                grad_mod[here, :] += lax.dot_general(
                    ones, part, (((0,), (0,)), ((), ())), preferred_element_type=jnp.float32
                )

        def total(values):
            return jnp.sum(values.astype(jnp.float32), axis=0, keepdims=True)

        def enter(rows):
            values = grad[rows, :].astype(jnp.float32)
            low = (self.vector(rows, 5) * values).astype(jnp.bfloat16)
            low_result[rows, :] = low
            down_sum[...] += total(low)
            collect(rows, 3, values * result[rows, :])

        by_rows(size, enter)

        def widen(at):
            here = at_tile(at)
            values = hidden[:, here]
            square = values * values
            bent = jnp.tanh(GELU_ROOT * (values + 0.044715 * values * square))
            slope = 0.5 * (1.0 + bent) + 0.5 * values * (1.0 - bent * bent) * (GELU_ROOT * (1.0 + 3 * 0.044715 * square))
            low = (nt_dot(low_result[...], self.down_w[here, :]) * slope).astype(jnp.bfloat16)
            low_hidden[:, here] = low
            up_sum[:, here] = total(low)

        for part in self.down_copies if fresh else ():
            part.wait()
        tiles(self.hidden // TILE, widen)
        for part in self.up_copies if fresh else ():
            part.wait()
        for here in halves_across(width):
            work[:, here] = nt_dot(low_hidden[...], self.up_w[here, :])

        def norm_back(rows):
            unit, root = norm_parts(middle[rows, :])
            values = work[rows, :]
            collect(rows, 1, values)
            collect(rows, 2, values * unit)
            scaled = values * (1.0 + self.vector(rows, 4))
            inside = scaled - jnp.mean(scaled, axis=1, keepdims=True)
            inside = inside - unit * jnp.mean(scaled * unit, axis=1, keepdims=True)
            here = grad[rows, :].astype(jnp.float32) + root * inside
            grad_middle[rows, :] = here
            low = (self.vector(rows, 2) * here).astype(jnp.bfloat16)
            low_branch[rows, :] = low
            out_sum[...] += total(low)
            collect(rows, 0, here * branch[rows, :])

        by_rows(size, norm_back)

        if fresh:
            self.out_copy.wait()
        for here in halves_across(width):
            low_mixed[:, here] = nt_dot(low_branch[...], self.out_w[here, :]).astype(jnp.bfloat16)


def feed_kernel(forth, back, *refs):
    pick, mod, out_w, up_w, down_w, out_b, up_b, down_b, *refs = refs
    weights, biases = (out_w, up_w, down_w), (out_b, up_b, down_b)
    if forth and not back:
        stream, mixed, branch, middle, normed, hidden, active, result, after, *refs = refs
        held, sems = refs[:3], refs[3]
    elif back and not forth:
        grad, branch, middle, hidden, result, *refs = refs
        outs, (*held, sems, work) = refs[:9], refs[9:]
    else:
        stream, mixed, grad, normed, active, after, *refs = refs
        outs, (*held, sems, work, branch, middle, hidden, result) = refs[:9], refs[9:]
    feed = FeedForward(pick, mod, weights, held, sems)
    feed.start(forth)
    if forth:
        feed.forward(stream, mixed, biases, branch, middle, normed, hidden, active, result, after)
    if back:
        feed.backward(grad, branch, middle, hidden, result, outs, work, not forth)


def feed_inputs(pick, mod, biases):
    ones = jnp.concatenate([pick.astype(jnp.bfloat16)] * 3, axis=1)
    return (ones, jnp.concatenate(thirds(mod), axis=0), *(part[None] for part in biases[1:]))


def feed_call(forth, back, ins, full, given, dtype):
    qkv_w, qkv_b, out_w, out_b, up_w, up_b, down_w, down_b = full
    size, latents = given[0].shape[0], given[1].shape[0] // 3
    width, hidden = up_w.shape
    bf16, f32 = jnp.bfloat16, jnp.float32
    shape = lambda columns, dtype, rows=size: jax.ShapeDtypeStruct((rows, columns), dtype)
    saved = (shape(width, f32), shape(width, f32), shape(width, bf16), shape(hidden, f32), shape(hidden, bf16), shape(width, f32))
    after = shape(width, dtype)
    outs = (
        shape(width, bf16), shape(hidden, bf16), shape(width, bf16), shape(width, bf16), shape(width, f32),
        shape(width, f32, 4 * latents), shape(width, f32, 1), shape(hidden, f32, 1), shape(width, f32, 1),
    )
    scratch = [pltpu.VMEM(part.shape, part.dtype) for part in (out_w, up_w, down_w)]
    scratch.append(pltpu.SemaphoreType.DMA((1 + 2 * (hidden // (3 * TILE)),)))
    if back:
        scratch.append(pltpu.VMEM((size, width), f32))
    if forth and back:
        scratch += [pltpu.VMEM((size, columns), f32) for columns in (width, width, hidden, width)]
        shapes = (saved[2], saved[4], after, *outs)
    else:
        shapes = (*saved, after) if forth else outs
    return pl.pallas_call(
        functools.partial(feed_kernel, forth, back),
        out_shape=shapes,
        in_specs=[VM, VM, HB, HB, HB, VM, VM, VM] + [VM] * len(ins),
        out_specs=(VM,) * len(shapes),
        scratch_shapes=scratch,
        compiler_params=pltpu.CompilerParams(vmem_limit_bytes=60 * 1024 * 1024),
    )(*given[:2], out_w, up_w, down_w, *given[2:], *ins)


def layer_forward(stream, modulation, full, plan, in_first, shards_first, shards_second, shards_ahead, collective_id, beside):
    qkv_w, qkv_b, out_w, out_b, up_w, up_b, down_w, down_b = full
    reps, edge = plan[:2]
    width = stream.shape[1]
    hd = width // reps
    nh = HEADS // reps
    mod, pick, front = modulation
    shift_one, scale_one = jnp.split(front, 2, axis=1)
    normed = pre_norm(stream, shift_one, scale_one).astype(jnp.bfloat16)
    qkv_bias = qkv_b.astype(jnp.float32)
    bias_full = jnp.concatenate(
        [qkv_bias[:width], jnp.zeros((width,), jnp.float32), qkv_bias[width:]]
    )
    projected = (low_dot(normed, qkv_w) + bias_full).astype(jnp.bfloat16)
    projected, plan, beside = lax.optimization_barrier((projected, plan[2:], beside))
    bounds, ids = plan
    in_second = sent_ahead(shards_first, projected) if shards_first else []
    own, prev, after, fulls = to_heads(projected, reps, edge, pad_to(2 * hd, LANES), in_first, collective_id)
    first_gathered = fulls
    in_second += sent_ahead(shards_second, own) if shards_second else []
    mixed, mixed_t, log_norm = attend(nh, hd, *bounds, prev, own, after, *ids)
    mixed, fulls = swap(mixed, reps, True, in_second, collective_id + 1)
    if in_first:
        (up_w,), (down_w, *fulls) = first_gathered, fulls
    in_next = sent_ahead(shards_ahead, mixed) if shards_ahead else ()
    full = (qkv_w, qkv_b, out_w, out_b, up_w, up_b, down_w, down_b)
    saved = (normed, (prev, own, after), mixed, (mixed_t, log_norm))
    return (saved, full, fulls, in_next, (reps, edge, bounds, ids), beside)


def layer_backward(stream, modulation, full, saved, feed_grads, plan, pair, last, hops):
    qkv_w = full[0]
    normed, window, mixed, kept = saved
    normed_two, active, grad_result, grad_hidden, grad_branch, grad_mixed, grad_middle, grad_mod, *bias_sums = feed_grads
    reps, edge, bounds, ids = plan
    width = stream.shape[1]
    hd = width // reps
    nh = HEADS // reps
    mod, pick, front = modulation
    shift_one, scale_one = jnp.split(front, 2, axis=1)
    grad_heads, sums = swap(grad_mixed, reps, False, (), 13 if pair else 3, pair)
    beside = first_hop(*sums) if pair else ()
    grad_heads, hops = lax.optimization_barrier((grad_heads, hops))
    prev, own, after = window
    grad_q, grad_prev, grad_own, grad_after = attend_back(
        nh, hd, *bounds, prev, own, after, *ids, grad_heads.reshape(own.shape[0], -1), *kept
    )
    early = ((active, normed_two, mixed, None), (grad_result, grad_hidden, grad_branch, None)) if last else None
    grad_projected, *early = from_heads(
        reps, width, grad_prev, grad_own, grad_after, grad_q, 14 if last else 4, early
    )
    beside = first_hop(*early) if last else beside
    if not last:
        grad_projected, beside = lax.optimization_barrier((grad_projected, beside))
    sums = jnp.sum(grad_projected.astype(jnp.float32), axis=0)
    grad_qkv_b = jnp.concatenate([sums[:width], sums[2 * width :]])
    grad_normed = jnp.einsum("te,de->td", grad_projected, qkv_w, preferred_element_type=jnp.float32)
    _, norm_back_one = jax.vjp(pre_norm, stream, shift_one, scale_one)
    grad_stream_part, grad_shift_one, grad_scale_one = norm_back_one(grad_normed)
    grad_stream = grad_middle + grad_stream_part
    grad_mod = jnp.concatenate(
        [
            jnp.einsum("tl,tm->lm", pick, part, precision=HIGH, preferred_element_type=jnp.float32)
            for part in (grad_shift_one, grad_scale_one)
        ]
        + [grad_mod],
    )
    return (
        grad_stream, grad_mod,
        ((active, normed_two, mixed, normed), (grad_result, grad_hidden, grad_branch, grad_projected)),
        (grad_qkv_b, *(part[0] for part in bias_sums)), (*hops, *beside),
    )


def bias_parts(stacked, params):
    return [stacked[:, row, : params[at].shape[0]].reshape(-1) for row, at in enumerate((3, 5, 7, 9))]


def modulation(partial_terms, layers):
    longest = pad_to(max(params[at].shape[0] for params in layers for at in (3, 5, 7, 9)), LANES)
    shares = jnp.stack(
        [jnp.pad(params[at], (0, longest - params[at].shape[0])) for params in layers for at in (3, 5, 7, 9)]
    )
    if not on_planes():
        mods = lax.psum(tuple(partial_terms), "fsdp")
        stacked = lax.all_gather(shares, "fsdp", axis=0)
        fulls = [lax.all_gather(layers[0][at], "fsdp", axis=0, tiled=True) for at in (2, 4)]
    else:
        width = layers[0][4].shape[1]
        parts = partial_terms[0].reshape(8, -1, width)
        some = parts.shape[1]
        parts = jnp.pad(parts, ((0, 0), (0, pad_to(some, 8) - some), (0, 0)))
        mod, stacked, *fulls = start(
            parts, jnp.pad(shares, ((0, 16 - shares.shape[0]), (0, 0))), [(layers[0][at],) for at in (2, 4)], 6
        )
        mods = [mod[:, :some].reshape(partial_terms[0].shape)] + [lax.psum(term, "fsdp") for term in partial_terms[1:]]
    return mods, [bias_parts(stacked[:, 4 * at : 4 * at + 4], params) for at, params in enumerate(layers)], fulls


def on_planes():
    return lax.axis_size("fsdp") == 8 and lax.axis_size("replica") == 4


def first_hop(own, xs, ys, tx, ty):
    hop = lambda value, step: lax.ppermute(value, "fsdp", [(at, at ^ step) for at in range(8)])
    return (own, hop(xs, 2), hop(ys, 4), tx, ty)


def owner_sums(pairs, ready, grad_mods, grad_biases):
    groups = lax.axis_size("fsdp")
    width = pairs[0][0][1].shape[1]
    if on_planes():
        mods = jnp.concatenate(grad_mods).reshape(groups, -1, width)
        biases = jnp.stack(
            [jnp.concatenate([part.reshape(groups, -1) for part in parts], axis=1) for parts in grad_biases], axis=1
        )
        used, lines = mods.shape[1], pad_to(mods.shape[1] + 2, 16)
        biases = jnp.pad(biases, ((0, 0), (0, lines - used - 2), (0, 0)))
        out, out_down, mine, shared = reduce_grads(*pairs[0], ready, jnp.concatenate([mods, biases], axis=1))
        mods = shared[:, :used].reshape(2, -1, width)
        shares = mine[used : used + 2].astype(jnp.float32)
        results = []
        for layer_at in range(2):
            columns = lambda first, last: out[layer_at, :, (first - 4) * width : (last - 4) * width].astype(jnp.float32)
            cuts = [0]
            for part in grad_biases[layer_at]:
                cuts.append(cuts[-1] + part.shape[0] // groups)
            weights = (columns(9, 12), columns(8, 9), columns(4, 8), out_down[layer_at].astype(jnp.float32))
            results.append((weights, [shares[layer_at, i:j] for i, j in zip(cuts[:-1], cuts[1:])]))
        return results, mods
    flat = jnp.concatenate([part for parts in grad_biases for part in parts])
    *mods, flat = lax.psum((*grad_mods, flat), ("fsdp", "replica"))
    results, place = [], 0
    for (lefts, rights), parts in zip(pairs, grad_biases):
        grads, biases = [], []
        for left, right in zip(lefts, rights):
            grad = low_dot(left.T, right).astype(jnp.bfloat16)
            part = lax.psum_scatter(grad, "fsdp", scatter_dimension=0, tiled=True)
            grads.append(lax.psum(part, "replica").astype(jnp.float32))
        for part in parts:
            share = part.shape[0] // groups
            biases.append(lax.dynamic_slice_in_dim(flat, place + lax.axis_index("fsdp") * share, share, 0))
            place += part.shape[0]
        results.append((grads[::-1], biases))
    return results, mods


def attention_plan(latent_len, tok_rows, reps, device_at):
    column = tok_rows * reps
    edge = MAXLEN
    total = jnp.sum(latent_len)
    first = lax.axis_index("fsdp") * column
    positions = first - edge + jnp.arange(column + 2 * edge, dtype=jnp.int32)
    ends = jnp.cumsum(latent_len)
    ids = jnp.sum((ends[None, :] <= positions[:, None]).astype(jnp.int32), axis=1)
    ids = jnp.where(positions < 0, -1, ids)
    own = ids[edge : edge + column]
    count = column // BQ
    firsts, lasts = own[::BQ], own[BQ - 1 :: BQ]
    pick = lambda at: (at[:, None] == jnp.arange(latent_len.shape[0], dtype=jnp.int32)[None, :]).astype(jnp.int32)
    low = jnp.sum(pick(firsts) * (ends - latent_len)[None, :], axis=1) - (first - edge)
    high = jnp.sum(pick(lasts) * ends[None, :], axis=1) - (first - edge)
    bounds = ((low // BK).astype(jnp.int32), ((high + BK - 1) // BK).astype(jnp.int32))
    kid = jnp.broadcast_to(ids[:, None], (ids.shape[0], LANES))
    qid = jnp.broadcast_to(own[None, :], (8, column))
    return (reps, edge, bounds, (kid, qid))


def shards(
    tokens,
    cond,
    latent_len,
    first_ada_weight,
    first_ada_bias,
    first_qkv_weight,
    first_qkv_bias,
    first_out_weight,
    first_out_bias,
    first_up_weight,
    first_up_bias,
    first_down_weight,
    first_down_bias,
    second_ada_weight,
    second_ada_bias,
    second_qkv_weight,
    second_qkv_bias,
    second_out_weight,
    second_out_bias,
    second_up_weight,
    second_up_bias,
    second_down_weight,
    second_down_bias,
    cotangent,
):
    tok_rows = tokens.shape[0]
    group_place = lax.axis_index("fsdp")
    device_at = lax.axis_index(("fsdp", "replica"))
    token_total = tok_rows * lax.axis_size(("fsdp", "replica"))
    latent_count = cond.shape[0]
    local_pos = jnp.arange(tok_rows, dtype=jnp.int32)
    own_ids = latent_ids(latent_len, device_at * tok_rows + local_pos, token_total)
    pick = (own_ids[:, None] == jnp.arange(latent_count, dtype=jnp.int32)[None, :]).astype(
        jnp.float32
    )
    plan = attention_plan(latent_len, tok_rows, lax.axis_size("replica"), device_at)
    layers = (
        (
            first_ada_weight,
            first_ada_bias,
            first_qkv_weight,
            first_qkv_bias,
            first_out_weight,
            first_out_bias,
            first_up_weight,
            first_up_bias,
            first_down_weight,
            first_down_bias,
        ),
        (
            second_ada_weight,
            second_ada_bias,
            second_qkv_weight,
            second_qkv_bias,
            second_out_weight,
            second_out_bias,
            second_up_weight,
            second_up_bias,
            second_down_weight,
            second_down_bias,
        ),
    )
    col_width = first_ada_weight.shape[0]
    own_cond = lax.dynamic_slice_in_dim(
        cond.astype(jnp.float32), group_place * col_width, col_width, 1
    )
    own_silu = jax.nn.silu(own_cond).astype(jnp.bfloat16)
    partial_terms = []
    for params in layers:
        term = low_dot(own_silu, params[0])
        bias_share = params[1].astype(jnp.float32)
        spread = lax.dynamic_update_slice_in_dim(
            jnp.zeros((term.shape[1],), jnp.float32),
            bias_share,
            group_place * bias_share.shape[0],
            0,
        )
        partial_terms.append(term + spread[None, :])
    (mod_first, mod_second), biases, attention_weights = modulation(partial_terms, layers)
    mods = [mod_first, mod_second]
    mod_tokens, feeds = [], []
    stream = tokens.astype(jnp.float32)
    inputs = []
    kept = []
    whole = lambda value: lax.all_gather(value, "fsdp", axis=0, tiled=True)
    fulls = []
    in_first = sent_ahead((first_up_weight,), mod_first) if on_planes() else ()
    for layer_at, params in enumerate(layers):
        if layer_at > 0:
            stream, mods[layer_at] = lax.optimization_barrier((stream, mods[layer_at]))
        inputs.append(stream)
        front = jnp.dot(pick, mods[layer_at][:, : 2 * tokens.shape[1]], precision=HIGH, preferred_element_type=jnp.float32)
        mod_tokens.append((mods[layer_at], pick, front))
        feed = feed_inputs(pick, mods[layer_at], biases[layer_at])
        ahead = layers[layer_at + 1] if layer_at + 1 < len(layers) else None
        qkv_w, out_w = attention_weights
        qkv_b, out_b, up_b, down_b = biases[layer_at]
        shards_first, shards_second, shards_ahead, up_w, down_w = (), (), (), None, None
        if on_planes():
            shards_first = (params[8],)
            shards_second = () if ahead is None else (ahead[2], ahead[4])
            shards_ahead = () if ahead is None else (ahead[6],)
        else:
            up_w, down_w = whole(params[6]), whole(params[8])
        full = (qkv_w, qkv_b, out_w, out_b, up_w, up_b, down_w, down_b)
        saved, full, attention_weights, in_first, plan, feed = layer_forward(
            stream, mod_tokens[layer_at], full, plan, in_first, shards_first, shards_second, shards_ahead, 7 + 2 * layer_at,
            feed,
        )
        feeds.append(feed)
        if layer_at == 0:
            *feed_saved, stream = feed_call(
                True, False, (stream, saved[2]), full, feeds[0], jnp.float32
            )
        else:
            normed_two, active, output, *feed_grads = feed_call(
                True, True, (stream, saved[2], cotangent), full, feeds[1], jnp.bfloat16
            )
            feed_grads = [normed_two, active, *feed_grads]
        fulls.append(full)
        if ahead is not None and not on_planes():
            attention_weights = [whole(ahead[at]) for at in (2, 4)]
        kept.append(saved)
    weight_pairs = [None, None]
    ready = ()
    mod_grads = [None, None]
    bias_grads = [None, None]
    for layer_at in (1, 0):
        if layer_at == 0:
            branch, middle, normed_two, hidden, active, result = feed_saved
            feed_grads = feed_call(
                False, True, (grad_stream, branch, middle, hidden, result), fulls[0], feeds[0], jnp.float32
            )
            feed_grads = [normed_two, active, *feed_grads]
        grad_stream, grad_mod, local_grads, local_biases, ready = layer_backward(
            inputs[layer_at], mod_tokens[layer_at], fulls[layer_at], kept[layer_at], feed_grads, plan,
            weight_pairs[1] if layer_at == 0 and on_planes() else None, layer_at == 1 and on_planes(), ready,
        )
        weight_pairs[layer_at] = local_grads
        mod_grads[layer_at] = grad_mod
        bias_grads[layer_at] = local_biases
    sums, (grad_mod_first, grad_mod_second) = owner_sums(weight_pairs, ready, mod_grads, bias_grads)
    grad_silu = jnp.zeros(own_cond.shape, jnp.float32)
    ada_grads = []
    for params, grad_mod in zip(layers, (grad_mod_first, grad_mod_second)):
        low_mod = grad_mod.astype(jnp.bfloat16).reshape(6, latent_count, -1).transpose(1, 0, 2).reshape(latent_count, -1)
        weight_grad = jnp.einsum("ld,lm->dm", own_silu, low_mod, preferred_element_type=jnp.float32)
        column_sums = jnp.sum(low_mod.astype(jnp.float32), axis=0)
        bias_rows = params[1].shape[0]
        bias_grad = lax.dynamic_slice_in_dim(column_sums, group_place * bias_rows, bias_rows, 0)
        grad_silu = grad_silu + jnp.einsum(
            "lm,dm->ld", low_mod, params[0], preferred_element_type=jnp.float32
        )
        ada_grads.append((weight_grad, bias_grad))
    _, silu_back = jax.vjp(jax.nn.silu, own_cond)
    cond_grad = silu_back(grad_silu)[0]
    outs = [output, grad_stream, cond_grad]
    for layer_at in range(2):
        outs += list(ada_grads[layer_at])
        for weight, bias in zip(*sums[layer_at]):
            outs += [weight, bias]
    return tuple(outs)


def solution(mesh):
    in_specs = (
        P(("fsdp", "replica"), None),
        P(),
        P(),
        P("fsdp", None),
        P("fsdp"),
        P("fsdp", None),
        P("fsdp"),
        P("fsdp", None),
        P("fsdp"),
        P("fsdp", None),
        P("fsdp"),
        P("fsdp", None),
        P("fsdp"),
        P("fsdp", None),
        P("fsdp"),
        P("fsdp", None),
        P("fsdp"),
        P("fsdp", None),
        P("fsdp"),
        P("fsdp", None),
        P("fsdp"),
        P("fsdp", None),
        P("fsdp"),
        P(("fsdp", "replica"), None),
    )
    out_specs = (
        P(("fsdp", "replica"), None),
        P(("fsdp", "replica"), None),
        P(None, "fsdp"),
        P("fsdp", None),
        P("fsdp"),
        P("fsdp", None),
        P("fsdp"),
        P("fsdp", None),
        P("fsdp"),
        P("fsdp", None),
        P("fsdp"),
        P("fsdp", None),
        P("fsdp"),
        P("fsdp", None),
        P("fsdp"),
        P("fsdp", None),
        P("fsdp"),
        P("fsdp", None),
        P("fsdp"),
        P("fsdp", None),
        P("fsdp"),
        P("fsdp", None),
        P("fsdp"),
    )
    return jax.shard_map(shards, mesh=mesh, in_specs=in_specs, out_specs=out_specs, check_vma=False)
```
